32 devices in a mesh: dp: 4 (over x, core), ep: 2 (over y), tp: 4 (over z).
Axes of the slice: x: 2, y: 2, z: 4, core: 2. Of those that a mesh axis runs over, the one named last changes fastest.
Arguments:
- tokens: bfloat16 [4096, 2048], P(('dp', 'ep'), 'tp'), may hold values from -6 to 6
- norm_attn: bfloat16 [2048], P('tp'), may hold values from 0.5 to 1.5
- w_query: bfloat16 [2048, 2048], P(None, 'tp'), may hold values from -0.125 to 0.125
- w_key: bfloat16 [2048, 2048], P(None, 'tp'), may hold values from -0.125 to 0.125
- w_value: bfloat16 [2048, 2048], P(None, 'tp'), may hold values from -0.125 to 0.125
- w_output: bfloat16 [2048, 2048], P('tp'), may hold values from -2 to 2
- norm_ffn: bfloat16 [2048], P('tp'), may hold values from 0.5 to 1.5
- w_router: bfloat16 [2048, 8], replicated, may hold values from -0.0625 to 0.0625
- shared_switch: bfloat16 [2048], replicated, may hold values from -0.125 to 0.125
- shared_gate: bfloat16 [2048, 5632], P(None, 'tp'), may hold values from -0.125 to 0.125
- shared_up: bfloat16 [2048, 5632], P(None, 'tp'), may hold values from -0.125 to 0.125
- shared_down: bfloat16 [5632, 2048], P('tp'), may hold values from -0.15625 to 0.15625
- expert_gate: bfloat16 [8, 2048, 1408], P('ep', None, 'tp'), may hold values from -0.125 to 0.125
- expert_up: bfloat16 [8, 2048, 1408], P('ep', None, 'tp'), may hold values from -0.125 to 0.125
- expert_down: bfloat16 [8, 1408, 2048], P('ep', 'tp'), may hold values from -0.625 to 0.625
- routes: int32 [4096, 4], P(('dp', 'ep')), may hold values from 0 to 7, all different within a row; in each aligned block of 512 rows (0 to 511, 512 to 1023, ...) at most 320 rows name the same one
- segments: int32 [4096], P('dp'), may hold values from 0 to 4, as said below
- output_gradient: bfloat16 [4096, 2048], P(('dp', 'ep'), 'tp'), may hold values from -6 to 6
Outputs:
- layer_out: bfloat16 [4096, 2048], P(('dp', 'ep'), 'tp')
- tokens_grad: float32 [4096, 2048], P(('dp', 'ep'), 'tp')
- norm_attn_grad: float32 [2048], P('tp')
- w_query_grad: float32 [2048, 2048], P(None, 'tp')
- w_key_grad: float32 [2048, 2048], P(None, 'tp')
- w_value_grad: float32 [2048, 2048], P(None, 'tp')
- w_output_grad: float32 [2048, 2048], P('tp')
- norm_ffn_grad: float32 [2048], P('tp')
- w_router_grad: float32 [2048, 8], replicated
- shared_switch_grad: float32 [2048], replicated
- shared_gate_grad: float32 [2048, 5632], P(None, 'tp')
- shared_up_grad: float32 [2048, 5632], P(None, 'tp')
- shared_down_grad: float32 [5632, 2048], P('tp')
- expert_gate_grad: float32 [8, 2048, 1408], P('ep', None, 'tp')
- expert_up_grad: float32 [8, 2048, 1408], P('ep', None, 'tp')
- expert_down_grad: float32 [8, 1408, 2048], P('ep', 'tp')
The draws below stay inside these ranges and needn't reach their ends.
Inputs may be any that keep to these rules, and one draw needn't show every extreme that they name: `routes`: in the rows of one device no expert is named by more than 320 rows. `segments`: within each sequence of 1024 tokens the ids never fall and start at 0; each sequence holds five documents.
All inputs are finite; a program needn't handle non-finite values.
Results may differ from the reference program's by a relative error of at most 0.02.
Values may be sent and summed in bfloat16 or wider, within the bound.
A program may use at most 448 MiB of HBM per device.

```python
import math
from functools import partial
import jax
import jax.numpy as jnp
import numpy as np
from jax import lax

D = 2048
HEADS = 16
HD = 128
FE = 1408
FS = 5632
TOP = 4
TOK_DEV = 512
EXPERTS = 8
CAP = 320
SEQ = 1024
TOKENS = 4096


def draw_segments(key, part):
    key = jax.random.fold_in(key, 7)
    seq_count = TOKENS // SEQ
    half_seq = SEQ // 2
    sub_keys = jax.random.split(key, 4)
    mid_start = half_seq - jax.random.randint(sub_keys[0], (seq_count,), half_seq // 4, half_seq // 2 + 1)
    mid_end = half_seq + jax.random.randint(sub_keys[1], (seq_count,), half_seq // 4, half_seq // 2 + 1)
    first_cut = jax.random.randint(sub_keys[2], (seq_count,), mid_start // 4, 3 * mid_start // 4 + 1)
    tail_len = SEQ - mid_end
    last_cut = mid_end + jax.random.randint(sub_keys[3], (seq_count,), tail_len // 4, 3 * tail_len // 4 + 1)
    spots = jnp.arange(SEQ, dtype=jnp.int32)[None, :]
    seg_ids = (spots >= first_cut[:, None]).astype(jnp.int32) + (spots >= mid_start[:, None]).astype(jnp.int32) + (spots >= mid_end[:, None]).astype(jnp.int32) + (spots >= last_cut[:, None]).astype(jnp.int32)
    return seg_ids.reshape(TOKENS)


def block_levels(key, extent, shards, least, largest):
    gain = 1.0
    for dim, shards_of in shards:
        heights = jax.random.uniform(jax.random.fold_in(jax.random.fold_in(key, 6), dim), (shards_of,), jnp.float32, least / len(shards), largest / len(shards))
        gain = gain * jnp.repeat(jnp.exp(heights), extent[dim] // shards_of).reshape((-1,) + (1,) * (len(extent) - 1 - dim))
    return gain


def deal_out(stream_key, own, number, rows, amount, top, limit, skew):
    ranking = jax.random.permutation(stream_key, amount)
    heavy_load, common = portions_of(amount, rows * top, limit, skew, True), portions_of(amount, rows * top, limit, skew, False)
    places = jnp.arange(amount)

    def named(lengths, turn):
        used = int((lengths > 0).sum())
        fixed = max(1, used // 4)
        passed = fixed + (places - fixed + turn * (used - fixed)) % max(1, amount - fixed)
        return jnp.zeros((amount,), jnp.int32).at[ranking[jnp.where(places < fixed, places, passed)]].set(jnp.asarray(lengths, jnp.int32))

    lengths = jnp.where(number % 4 == 0, named(heavy_load, number // 4), named(common, number - number // 4 - 1))
    mixed = jax.random.permutation(jax.random.fold_in(own, 3), amount)
    source_of, taker = mixed[0:amount // 2 * 2:2], mixed[1:amount // 2 * 2:2]
    room = jnp.minimum(lengths[source_of] - 1, limit - lengths[taker]) // 2
    room = jnp.where((source_of == ranking[0]) | (taker == ranking[0]) | (lengths[taker] == 0), 0, jnp.maximum(room, 0))
    passed = jax.random.randint(jax.random.fold_in(own, 4), (amount // 2,), 0, 1 << 20) % (room + 1)
    lengths = lengths.at[source_of].add(-passed).at[taker].add(passed)
    items = jnp.searchsorted(jnp.cumsum(lengths), jnp.arange(rows * top), side="right").astype(jnp.int32)
    grid = items.reshape(top, rows).T
    grid = grid[jax.random.permutation(jax.random.fold_in(own, 1), rows)]
    turn = jax.random.randint(jax.random.fold_in(own, 2), (rows, 1), 0, top)
    return jnp.take_along_axis(grid, (jnp.arange(top)[None, :] + turn) % top, axis=1)


def portions_of(number_of, total, most, lean, full):
    portions = [(1 << 20) // math.isqrt(rank ** lean) + 1 for rank in range(1, number_of + 1)]
    largest = most if full else min(most, max(-(-total // number_of), total * portions[0] // sum(portions)))
    least = 1 if total - largest >= number_of - 1 else 0
    counts, spare = [largest] + [least] * (number_of - 1), total - largest - least * (number_of - 1)
    while spare > 0:
        candidates = [i for i in range(1, number_of) if counts[i] < largest] or [i for i in range(1, number_of) if counts[i] < most]
        whole, remaining = sum([portions[i] for i in candidates]), spare
        for i in candidates:
            extra = min(most - counts[i], max(1, remaining * portions[i] // whole), spare)
            counts[i] = counts[i] + extra
            spare = spare - extra
    return np.array(counts)


def scatter_about(rng, extent, scale, most, cuts=(), kind=jnp.bfloat16):
    array = scale * jax.random.normal(rng, extent, jnp.float32)
    if cuts:
        array = array * block_levels(rng, extent, cuts, -0.22, 0.18)
    return jnp.clip(array, -most, most).astype(kind)


def setup_inputs(seed: int = 0) -> dict:
    keys = jax.random.split(jax.random.key(seed), 19)
    tokens = scatter_about(keys[0], (TOKENS, D), 1.0, 6.0, ((0, 8), (1, 4)))
    norm_attn = jnp.clip(1.0 + 0.1 * jax.random.normal(keys[1], (D,), jnp.float32), 0.5, 1.5).astype(jnp.bfloat16)
    w_query = scatter_about(keys[2], (D, HEADS * HD), D ** -0.5, 0.125, ((1, 4),))
    w_key = scatter_about(keys[3], (D, HEADS * HD), D ** -0.5, 0.125, ((1, 4),))
    w_value = scatter_about(keys[4], (D, HEADS * HD), D ** -0.5, 0.125, ((1, 4),))
    w_output = scatter_about(keys[5], (HEADS * HD, D), (max(HEADS * HD // 256, 8)) ** -0.5, 2.0, ((0, 4),))
    norm_ffn = jnp.clip(1.0 + 0.1 * jax.random.normal(keys[6], (D,), jnp.float32), 0.5, 1.5).astype(jnp.bfloat16)
    w_router = scatter_about(keys[7], (D, EXPERTS), (4 * D) ** -0.5, 0.0625)
    shared_switch = scatter_about(keys[8], (D,), D ** -0.5, 0.125)
    shared_gate = scatter_about(keys[9], (D, FS), D ** -0.5, 0.125, ((1, 4),))
    shared_up = scatter_about(keys[10], (D, FS), D ** -0.5, 0.125, ((1, 4),))
    shared_down = scatter_about(keys[11], (FS, D), (FS // 4) ** -0.5, 0.15625, ((0, 4),))
    expert_gate = scatter_about(keys[12], (EXPERTS, D, FE), D ** -0.5, 0.125, ((0, 2), (2, 4)))
    expert_up = scatter_about(keys[13], (EXPERTS, D, FE), D ** -0.5, 0.125, ((0, 2), (2, 4)))
    expert_down = scatter_about(keys[14], (EXPERTS, FE, D), (max(FE // 16, 2)) ** -0.5, 0.625, ((0, 2), (1, 4)))
    routes_keys = jax.random.split(jax.random.fold_in(keys[15], 1), TOKENS // TOK_DEV)
    routes_turns = jax.random.permutation(jax.random.fold_in(keys[15], 3), TOKENS // TOK_DEV)
    routes = jax.vmap(lambda own, number: deal_out(jax.random.fold_in(keys[15], 2), own, number, TOK_DEV, EXPERTS, TOP, CAP, 1))(routes_keys, routes_turns).reshape((TOKENS, TOP))
    segments = draw_segments(jax.random.fold_in(keys[18], 71), 0)
    output_gradient = scatter_about(keys[17], (TOKENS, D), 1.0, 6.0, ((0, 8), (1, 4)))
    return {"tokens": tokens, "norm_attn": norm_attn, "w_query": w_query, "w_key": w_key, "w_value": w_value, "w_output": w_output, "norm_ffn": norm_ffn, "w_router": w_router, "shared_switch": shared_switch, "shared_gate": shared_gate, "shared_up": shared_up, "shared_down": shared_down, "expert_gate": expert_gate, "expert_up": expert_up, "expert_down": expert_down, "routes": routes, "segments": segments, "output_gradient": output_gradient}


EPS = 1e-06
ROPE_BASE = 1000000.0
NEG = -1e+30
HIGH = lax.Precision.HIGHEST

@jax.custom_vjp
def low(v):
    return lax.optimization_barrier(v.astype(jnp.bfloat16)).astype(jnp.float32)

@jax.custom_vjp
def low_back(v):
    return v

def reduced_precision_keep(v):
    return (low(v), None)

def low_pass(kept, grad):
    return (grad,)

def back_keep(v):
    return (v, None)

def back_low(kept, grad):
    return (low(grad),)
low.defvjp(reduced_precision_keep, low_pass)
low_back.defvjp(back_keep, back_low)

def matmul(left, right):
    return jnp.dot(left, right, precision=HIGH, preferred_element_type=jnp.float32)

def rope_tables(positions, feat_width):
    half_width = feat_width // 2
    inv_freq = ROPE_BASE ** (-(jnp.arange(half_width, dtype=jnp.float32) * 2.0) / feat_width)
    angles = positions.astype(jnp.float32)[:, None] * inv_freq[None, :]
    return (jnp.cos(angles), jnp.sin(angles))

def rotate(tensor, cos_table, sin_table):
    half_width = tensor.shape[-1] // 2
    first_half = tensor[..., :half_width]
    second_half = tensor[..., half_width:]
    cos_b = cos_table[:, None, :]
    sin_b = sin_table[:, None, :]
    return jnp.concatenate([first_half * cos_b - second_half * sin_b, second_half * cos_b + first_half * sin_b], axis=-1)

def attend_sequence(inputs):
    query, key_rows, value_rows, seg_ids = inputs
    q_block = min(512, TOK_DEV)
    score_scale = 1.0 / math.sqrt(HD)
    key_pos = jnp.arange(SEQ, dtype=jnp.int32)

    def one_block(blk_start):
        q_piece = lax.dynamic_slice_in_dim(query, blk_start, q_block, 0)
        piece_pos = blk_start + jnp.arange(q_block, dtype=jnp.int32)
        piece_seg = lax.dynamic_slice_in_dim(seg_ids, blk_start, q_block, 0)
        allowed = (piece_seg[:, None] == seg_ids[None, :]) & (key_pos[None, :] <= piece_pos[:, None])
        scores = low_back(jnp.einsum('qhd,khd->hqk', q_piece, key_rows, precision=HIGH) * score_scale)
        scores = jnp.where(allowed[None], scores, NEG)
        row_top = lax.optimization_barrier(jnp.max(scores, axis=2, keepdims=True))
        shifted_exp = jnp.exp(scores - row_top)
        weights = low(shifted_exp / lax.optimization_barrier(jnp.sum(shifted_exp, axis=2, keepdims=True)))
        return jnp.einsum('hqk,khd->qhd', weights, value_rows, precision=HIGH)
    starts = jnp.arange(SEQ // q_block, dtype=jnp.int32) * q_block
    return lax.map(jax.checkpoint(one_block), starts).reshape(SEQ, HEADS, HD)

def layer_forward(tok_f, norm_attn, w_query, w_key, w_value, w_output, norm_ffn, w_router, shared_switch, shared_gate, shared_up, shared_down, expert_gate, expert_up, expert_down, routes, segments):
    inv_one = lax.rsqrt(lax.optimization_barrier(jnp.mean(tok_f * tok_f, axis=1, keepdims=True)) + EPS)
    normed = low(tok_f * inv_one * norm_attn)
    q_pre = low_back(matmul(normed, w_query))
    k_pre = low_back(matmul(normed, w_key))
    value_all = low(low_back(matmul(normed, w_value))).reshape(TOKENS, HEADS, HD)
    positions = jnp.arange(TOKENS, dtype=jnp.int32) % SEQ
    cos_table, sin_table = rope_tables(positions, HD)
    query = low(rotate(q_pre.reshape(TOKENS, HEADS, HD), cos_table, sin_table))
    key_all = low(rotate(k_pre.reshape(TOKENS, HEADS, HD), cos_table, sin_table))
    seq_count = TOKENS // SEQ
    attended = lax.map(attend_sequence, (query.reshape(seq_count, SEQ, HEADS, HD), key_all.reshape(seq_count, SEQ, HEADS, HD), value_all.reshape(seq_count, SEQ, HEADS, HD), segments.reshape(seq_count, SEQ)))
    attended = low(low_back(attended.reshape(TOKENS, HEADS * HD)))
    resid = tok_f + low_back(matmul(attended, w_output))
    inv_two = lax.rsqrt(lax.optimization_barrier(jnp.mean(resid * resid, axis=1, keepdims=True)) + EPS)
    mixed = low(resid * inv_two * norm_ffn)
    logits = low_back(matmul(mixed, w_router))
    router_prob = jax.nn.softmax(logits, axis=1)
    route_hot = (routes[:, :, None] == jnp.arange(EXPERTS, dtype=jnp.int32)[None, None, :]).astype(jnp.float32)
    combine = router_prob * lax.optimization_barrier(jnp.sum(route_hot, axis=1))
    switch = jax.nn.sigmoid(low_back(matmul(mixed, shared_switch)))
    gate_shared = low_back(matmul(mixed, shared_gate))
    up_shared = low_back(matmul(mixed, shared_up))
    hidden_shared = low(jax.nn.silu(gate_shared) * up_shared)
    shared_out = low_back(matmul(hidden_shared, shared_down))

    def expert_step(running, inputs):
        gate_w, up_w, down_w, weight_col = inputs
        gate_pre = low_back(matmul(mixed, gate_w))
        up_pre = low_back(matmul(mixed, up_w))
        hidden = low(jax.nn.silu(gate_pre) * up_pre)
        expert_out = low_back(matmul(hidden, down_w))
        return (running + weight_col[:, None] * expert_out, None)
    expert_mix, _ = lax.scan(jax.checkpoint(expert_step), jnp.zeros((TOKENS, D), jnp.float32), (expert_gate, expert_up, expert_down, combine.T))
    return resid + expert_mix + switch[:, None] * shared_out

def reference(tokens, norm_attn, w_query, w_key, w_value, w_output, norm_ffn, w_router, shared_switch, shared_gate, shared_up, shared_down, expert_gate, expert_up, expert_down, routes, segments, output_gradient):
    params = tuple((param.astype(jnp.float32) for param in (tokens, norm_attn, w_query, w_key, w_value, w_output, norm_ffn, w_router, shared_switch, shared_gate, shared_up, shared_down, expert_gate, expert_up, expert_down)))
    forward = partial(layer_forward, routes=routes, segments=segments)
    result, pullback = jax.vjp(forward, *params)
    grads = pullback(output_gradient.astype(jnp.float32))
    return (result.astype(jnp.bfloat16), grads[0], grads[1], grads[2], grads[3], grads[4], grads[5], grads[6], grads[7], grads[8], grads[9], grads[10], grads[11], grads[12], grads[13], grads[14])
```

```python
import math

import jax
import jax.numpy as jnp
from jax import lax
from jax.sharding import PartitionSpec as P

HD = 128
EPS = 1e-06
ROPE_BASE = 1000000.0
NEG = -1e30
F32 = jnp.float32
BF16 = jnp.bfloat16


def mm(left, right):
    return lax.dot_general(left, right, (((1,), (0,)), ((), ())), preferred_element_type=F32)


def mm_nt(left, right):
    return lax.dot_general(left, right, (((1,), (1,)), ((), ())), preferred_element_type=F32)


def mm_tn(left, right):
    return lax.dot_general(left, right, (((0,), (0,)), ((), ())), preferred_element_type=F32)


def swap(value, axis, bit):
    count = lax.axis_size(axis)
    return lax.ppermute(value, axis, [(i, i ^ bit) for i in range(count)])


def bit_of(axis, bit):
    return (lax.axis_index(axis) // bit) % 2


def half(value, which, dim):
    size = value.shape[dim] // 2
    return lax.dynamic_slice_in_dim(value, which * size, size, dim)


def halve(value, axis, bit, dim):
    mine = bit_of(axis, bit)
    got = swap(half(value, 1 - mine, dim), axis, bit)
    return (half(value, mine, dim).astype(F32) + got.astype(F32)).astype(BF16)


def double(value, axis, bit, dim):
    got = swap(value, axis, bit)
    mine = bit_of(axis, bit) == 0
    return jnp.concatenate([jnp.where(mine, value, got), jnp.where(mine, got, value)], axis=dim)


def rope_tables(positions, feat_width):
    half_width = feat_width // 2
    inv_freq = ROPE_BASE ** (-(jnp.arange(half_width, dtype=F32) * 2.0) / feat_width)
    angles = positions.astype(F32)[:, None] * inv_freq[None, :]
    return (jnp.cos(angles), jnp.sin(angles))


def rotate(tensor, cos_table, sin_table):
    half_width = tensor.shape[-1] // 2
    first_half = tensor[..., :half_width]
    second_half = tensor[..., half_width:]
    cos_b = cos_table[:, None, :]
    sin_b = sin_table[:, None, :]
    return jnp.concatenate(
        [first_half * cos_b - second_half * sin_b, second_half * cos_b + first_half * sin_b],
        axis=-1,
    )


def ffn_pieces(rows, grads, scale, gate_w, up_w, down_w, groups):
    count = rows.shape[0]
    hidden_width = gate_w.shape[1]
    gate_pre = mm(rows, gate_w)
    up_pre = mm(rows, up_w)
    grad_hidden = mm_nt(grads, down_w)
    sig = jax.nn.sigmoid(gate_pre)
    act = gate_pre * sig
    slope = sig * (1.0 + gate_pre * (1.0 - sig))
    hidden = (act * up_pre).astype(BF16).astype(F32)
    wide = jnp.repeat(scale, hidden_width // groups, axis=1, total_repeat_length=hidden_width)
    scaled_hidden = (hidden * wide).astype(BF16)
    dots = jnp.sum((hidden * grad_hidden).reshape(count, groups, -1), axis=2)
    grad_scaled = grad_hidden * wide
    grad_gate = (grad_scaled * up_pre * slope).astype(BF16)
    grad_up = (grad_scaled * act).astype(BF16)
    along = jnp.sum(grad_gate.astype(F32) * gate_pre + grad_up.astype(F32) * up_pre, axis=1)
    return scaled_hidden, grad_gate, grad_up, dots, along


def body(
    tokens,
    norm_attn,
    w_query,
    w_key,
    w_value,
    w_output,
    norm_ffn,
    w_router,
    shared_switch,
    shared_gate,
    shared_up,
    shared_down,
    expert_gate,
    expert_up,
    expert_down,
    routes,
    segments,
    output_gradient,
):
    tp_count = lax.axis_size("tp")
    ep_count = lax.axis_size("ep")
    dp_count = lax.axis_size("dp")
    tp_rank = lax.axis_index("tp")
    ep_rank = lax.axis_index("ep")
    rows = tokens.shape[0]
    width_own = tokens.shape[1]
    width = width_own * tp_count
    heads = w_query.shape[1] // HD
    experts_own = expert_gate.shape[0]
    experts = experts_own * ep_count
    expert_width = expert_gate.shape[2]
    score_scale = 1.0 / math.sqrt(HD)
    far_bits = [1 << b for b in range(1, dp_count.bit_length() - 1)]

    def own_columns(value):
        return lax.dynamic_slice_in_dim(value, tp_rank * width_own, width_own, value.ndim - 1)

    def total_dense(value, dims):
        stages = [("ep", 1)] + [("dp", b) for b in far_bits]
        for axis, bit in stages:
            value = halve(value, axis, bit, dims)
        for axis, bit in reversed(stages):
            value = double(value, axis, bit, dims)
        return value

    def total_expert(value, dims):
        stages = [("dp", b) for b in far_bits]
        for axis, bit in stages:
            value = halve(value, axis, bit, dims)
        for axis, bit in reversed(stages):
            value = double(value, axis, bit, dims)
        return value

    near = bit_of("dp", 1)

    def pair_rows(left, right):
        send = mm_tn(half(left, 1 - near, 1), right).astype(BF16)
        got = swap(send, "dp", 1)
        return (mm_tn(half(left, near, 1), right) + got.astype(F32)).astype(BF16)

    def pair_columns(left, right):
        send = mm_tn(left, half(right, 1 - near, 1)).astype(BF16)
        got = swap(send, "dp", 1)
        return (mm_tn(left, half(right, near, 1)) + got.astype(F32)).astype(BF16)

    def spread(value, dim):
        got = swap(value, "dp", 1)
        first = near == 0
        return (
            jnp.concatenate([jnp.where(first, value, got), jnp.where(first, got, value)], axis=dim)
        ).astype(F32)

    packed = jnp.concatenate(
        [tokens, norm_attn[None, :], norm_ffn[None, :], jnp.zeros((14, width_own), BF16)], axis=0
    )
    packed = lax.all_gather(packed, "tp", axis=1, tiled=True)
    x_full = packed[:rows].astype(F32)
    gain_one = packed[rows].astype(F32)
    gain_two = packed[rows + 1].astype(F32)
    grad_rows = lax.all_gather(output_gradient, "tp", axis=1, tiled=True)
    grad_peer = swap(grad_rows, "ep", 1)
    route_hot = jnp.sum(
        (routes[:, :, None] == jnp.arange(experts, dtype=jnp.int32)[None, None, :]).astype(F32),
        axis=1,
    )
    route_hot_peer = swap(route_hot, "ep", 1)

    inv_one = lax.rsqrt(jnp.mean(x_full * x_full, axis=1, keepdims=True) + EPS)
    normed = (x_full * inv_one * gain_one).astype(BF16)
    q_pre = mm(normed, w_query)
    k_pre = mm(normed, w_key)
    v_pre = mm(normed, w_value)
    positions = ep_rank * rows + jnp.arange(rows, dtype=jnp.int32)
    cos_table, sin_table = rope_tables(positions, HD)
    query = rotate(q_pre.reshape(rows, heads, HD), cos_table, sin_table).astype(BF16)
    key_own = rotate(k_pre.reshape(rows, heads, HD), cos_table, sin_table).astype(BF16)
    value_own = v_pre.astype(BF16).reshape(rows, heads, HD)
    forth = [(i, i + 1) for i in range(ep_count - 1)]
    back = [(i + 1, i) for i in range(ep_count - 1)]
    earlier = lax.ppermute(jnp.stack([key_own, value_own]), "ep", forth)
    key_rows = jnp.concatenate([earlier[0], key_own], axis=0)
    value_rows = jnp.concatenate([earlier[1], value_own], axis=0)
    key_pos = (ep_rank - 1) * rows + jnp.arange(2 * rows, dtype=jnp.int32)
    seg_rows = segments.reshape(ep_count, rows)
    query_seg = lax.dynamic_index_in_dim(seg_rows, ep_rank, 0, keepdims=False)
    before_seg = lax.dynamic_index_in_dim(
        seg_rows, jnp.maximum(ep_rank - 1, 0), 0, keepdims=False
    )
    key_seg = jnp.concatenate([jnp.where(ep_rank > 0, before_seg, -1), query_seg])
    allowed = (query_seg[:, None] == key_seg[None, :]) & (key_pos[None, :] <= positions[:, None])

    def masked_scores():
        scores = (
            jnp.einsum("qhd,khd->hqk", query, key_rows, preferred_element_type=F32) * score_scale
        )
        return jnp.where(allowed[None], scores, NEG)

    scores = masked_scores()
    row_top = jnp.max(scores, axis=2, keepdims=True)
    shifted = jnp.exp(scores - row_top)
    row_total = jnp.sum(shifted, axis=2, keepdims=True)
    weights = (shifted / row_total).astype(BF16)
    attended = jnp.einsum("hqk,khd->qhd", weights, value_rows, preferred_element_type=F32)
    attn_rows = attended.astype(BF16).reshape(rows, heads * HD)
    log_norm = row_top + jnp.log(row_total)

    attn_part = mm(attn_rows, w_output).astype(BF16)
    attn_own = lax.psum_scatter(attn_part, "tp", scatter_dimension=1, tiled=True)
    attn_total = lax.all_gather(attn_own, "tp", axis=1, tiled=True)
    resid = x_full + attn_total.astype(F32)
    inv_two = lax.rsqrt(jnp.mean(resid * resid, axis=1, keepdims=True) + EPS)
    mixed = (resid * inv_two * gain_two).astype(BF16)
    mixed_peer = swap(mixed, "ep", 1)
    resid_own = own_columns(resid)

    def router(values):
        logits = mm(values, w_router)
        return logits, jax.nn.softmax(logits, axis=1)

    logits, router_prob = router(mixed)
    combine = router_prob * route_hot
    combine_peer = router(mixed_peer)[1] * route_hot_peer
    switch_logit = mm(mixed, shared_switch[:, None])
    switch = jax.nn.sigmoid(switch_logit)

    def own_experts(value):
        return lax.dynamic_slice_in_dim(value, ep_rank * experts_own, experts_own, 1)

    hidden_s, gate_s, up_s, dots_s, along_s = ffn_pieces(
        mixed, grad_rows, switch, shared_gate, shared_up, shared_down, 1
    )
    gate_up_s = jnp.concatenate([gate_s, up_s], axis=1)
    total_s = pair_rows(mixed, gate_up_s)
    total_sd = pair_columns(hidden_s, grad_rows)
    grad_s = mm_nt(gate_s, shared_gate) + mm_nt(up_s, shared_up)
    out_s = mm(hidden_s, shared_down)

    hidden_width = experts_own * expert_width
    gate_w = jnp.transpose(expert_gate, (1, 0, 2)).reshape(width, hidden_width)
    up_w = jnp.transpose(expert_up, (1, 0, 2)).reshape(width, hidden_width)
    down_w = expert_down.reshape(hidden_width, width)
    both = jnp.concatenate([mixed, mixed_peer], axis=0)
    both_grad = jnp.concatenate([grad_rows, grad_peer], axis=0)
    scale_e = jnp.concatenate([own_experts(combine), own_experts(combine_peer)], axis=0)
    hidden_e, gate_e, up_e, dots_e, along_e = ffn_pieces(
        both, both_grad, scale_e, gate_w, up_w, down_w, experts_own
    )
    grad_e = mm_nt(gate_e, gate_w) + mm_nt(up_e, up_w)
    grad_e_back = swap(grad_e[rows:].astype(BF16), "ep", 1)
    small_e = jnp.concatenate([dots_e, along_e[:, None]], axis=1)
    small_back = swap(small_e[rows:], "ep", 1)
    grad_part = (grad_s + grad_e[:rows] + grad_back_f32(grad_e_back)).astype(BF16)
    grad_own = lax.psum_scatter(grad_part, "tp", scatter_dimension=1, tiled=True).astype(F32)

    gate_up_e = jnp.concatenate([gate_e, up_e], axis=1)
    total_e = pair_rows(both, gate_up_e)
    total_ed = pair_columns(hidden_e, both_grad)
    out_e = mm(hidden_e, down_w)
    out_e_back = swap(out_e[rows:].astype(BF16), "ep", 1)

    first = ep_rank == 0
    dots_here, dots_there = dots_e[:rows], small_back[:, :experts_own]
    dots_all = jnp.concatenate(
        [jnp.where(first, dots_here, dots_there), jnp.where(first, dots_there, dots_here)], axis=1
    )
    along = along_s + along_e[:rows] + small_back[:, experts_own]
    small = lax.psum(jnp.concatenate([dots_all, dots_s, along[:, None]], axis=1), "tp")
    grad_prob = small[:, :experts] * route_hot
    grad_switch = small[:, experts : experts + 1]
    along = small[:, experts + 1 : experts + 2]
    grad_logits = (
        router_prob * (grad_prob - jnp.sum(router_prob * grad_prob, axis=1, keepdims=True))
    ).astype(BF16)
    grad_slogit = (grad_switch * switch * (1.0 - switch)).astype(BF16)
    grad_router = mm_tn(mixed, grad_logits)
    grad_switch_w = mm_tn(mixed, grad_slogit)
    tp_rows = lax.dynamic_slice_in_dim(w_router, tp_rank * width_own, width_own, 0)
    grad_own = (
        grad_own
        + mm_nt(grad_logits, tp_rows)
        + grad_slogit.astype(F32) * own_columns(shared_switch).astype(F32)[None, :]
    )
    along = (
        along
        + jnp.sum(grad_logits.astype(F32) * logits, axis=1, keepdims=True)
        + grad_slogit.astype(F32) * switch_logit
    )
    gain_two_own = norm_ffn.astype(F32)
    grad_resid = (
        output_gradient.astype(F32)
        + inv_two * gain_two_own * grad_own
        - resid_own * (inv_two * inv_two) * (along / width)
    )
    grad_gain_two = jnp.sum(grad_own * resid_own * inv_two, axis=0)
    resid_low = lax.all_gather(grad_resid.astype(BF16), "tp", axis=1, tiled=True)

    ffn_part = (out_s + out_e[:rows] + out_e_back.astype(F32)).astype(BF16)
    ffn_own = lax.psum_scatter(ffn_part, "tp", scatter_dimension=1, tiled=True)
    layer_out = (resid_own + ffn_own.astype(F32)).astype(BF16)

    total_wo = pair_columns(attn_rows, resid_low)
    grad_attn = mm_nt(resid_low, w_output).astype(BF16).reshape(rows, heads, HD)
    probs = jnp.exp(masked_scores() - log_norm)
    grad_probs = jnp.einsum("qhd,khd->hqk", grad_attn, value_rows, preferred_element_type=F32)
    grad_scores = (
        probs * (grad_probs - jnp.sum(probs * grad_probs, axis=2, keepdims=True))
    ).astype(BF16)
    grad_query = (
        jnp.einsum("hqk,khd->qhd", grad_scores, key_rows, preferred_element_type=F32) * score_scale
    )
    grad_keys = (
        jnp.einsum("hqk,qhd->khd", grad_scores, query, preferred_element_type=F32) * score_scale
    )
    grad_values = jnp.einsum(
        "hqk,qhd->khd", probs.astype(BF16), grad_attn, preferred_element_type=F32
    )
    later = lax.ppermute(
        jnp.stack([grad_keys[:rows], grad_values[:rows]]).astype(BF16), "ep", back
    ).astype(F32)
    grad_key = grad_keys[rows:] + later[0]
    grad_value = grad_values[rows:] + later[1]
    shape = (rows, heads * HD)
    grad_qpre = rotate(grad_query, cos_table, -sin_table).astype(BF16).reshape(shape)
    grad_kpre = rotate(grad_key, cos_table, -sin_table).astype(BF16).reshape(shape)
    grad_vpre = grad_value.astype(BF16).reshape(shape)
    grad_normed = (
        mm_nt(grad_qpre, w_query) + mm_nt(grad_kpre, w_key) + mm_nt(grad_vpre, w_value)
    ).astype(BF16)
    normed_own = lax.psum_scatter(grad_normed, "tp", scatter_dimension=1, tiled=True).astype(F32)
    row_part = jnp.sum(
        grad_qpre.astype(F32) * q_pre
        + grad_kpre.astype(F32) * k_pre
        + grad_vpre.astype(F32) * v_pre,
        axis=1,
        keepdims=True,
    )
    row_total = lax.psum(row_part, "tp")
    total_qkv = pair_rows(normed, jnp.concatenate([grad_qpre, grad_kpre, grad_vpre], axis=1))
    x_own = tokens.astype(F32)
    grad_tokens = (
        grad_resid
        + inv_one * norm_attn.astype(F32) * normed_own
        - x_own * (inv_one * inv_one) * (row_total / width)
    )
    grad_gain_one = jnp.sum(normed_own * x_own * inv_one, axis=0)

    flat = jnp.concatenate(
        [grad_gain_two, grad_router.reshape(-1), grad_switch_w.reshape(-1), grad_gain_one]
    )
    flat = lax.psum(flat, ("dp", "ep"))
    grad_gain_two = flat[:width_own]
    grad_router = flat[width_own : width_own + width * experts].reshape(width, experts)
    grad_switch_w = flat[width_own + width * experts : width_own + width * (experts + 1)]
    grad_gain_one = flat[width_own + width * (experts + 1) :]

    shared_gu = spread(total_dense(total_s, 0), 0)
    shared_d = spread(total_dense(total_sd, 0), 1)
    expert_gu = spread(total_expert(total_e, 0), 0)
    expert_d = spread(total_expert(total_ed, 0), 1)
    wo_grad = spread(total_dense(total_wo, 0), 1)
    qkv_grad = spread(total_dense(total_qkv, 0), 0)
    qkv = heads * HD

    def per_expert(value):
        return jnp.transpose(value.reshape(width, experts_own, expert_width), (1, 0, 2))

    return (
        layer_out,
        grad_tokens,
        grad_gain_one,
        qkv_grad[:, :qkv],
        qkv_grad[:, qkv : 2 * qkv],
        qkv_grad[:, 2 * qkv :],
        wo_grad,
        grad_gain_two,
        grad_router,
        grad_switch_w,
        shared_gu[:, : shared_gate.shape[1]],
        shared_gu[:, shared_gate.shape[1] :],
        shared_d,
        per_expert(expert_gu[:, :hidden_width]),
        per_expert(expert_gu[:, hidden_width:]),
        expert_d.reshape(experts_own, expert_width, width),
    )


def grad_back_f32(value):
    return value.astype(F32)


def solution(mesh):
    placed = (
        P(("dp", "ep"), "tp"),
        P("tp"),
        P(None, "tp"),
        P(None, "tp"),
        P(None, "tp"),
        P("tp", None),
        P("tp"),
        P(),
        P(),
        P(None, "tp"),
        P(None, "tp"),
        P("tp", None),
        P("ep", None, "tp"),
        P("ep", None, "tp"),
        P("ep", "tp", None),
        P(("dp", "ep"), None),
        P("dp"),
        P(("dp", "ep"), "tp"),
    )
    return jax.shard_map(
        body,
        mesh=mesh,
        in_specs=placed,
        out_specs=(
            P(("dp", "ep"), "tp"),
            P(("dp", "ep"), "tp"),
            P("tp"),
            P(None, "tp"),
            P(None, "tp"),
            P(None, "tp"),
            P("tp", None),
            P("tp"),
            P(),
            P(),
            P(None, "tp"),
            P(None, "tp"),
            P("tp", None),
            P("ep", None, "tp"),
            P("ep", None, "tp"),
            P("ep", "tp", None),
        ),
        check_vma=False,
    )
```

```python
import functools
import math

import jax
import jax.numpy as jnp
from jax import lax
from jax.experimental import pallas as pl
from jax.experimental.pallas import tpu as pltpu
from jax.sharding import PartitionSpec as P

HD = 128
EPS = 1e-06
ROPE_BASE = 1000000.0
NEG = -1e30
F32 = jnp.float32
BF16 = jnp.bfloat16


def mm(left, right):
    return lax.dot_general(left, right, (((1,), (0,)), ((), ())), preferred_element_type=F32)


def mm_nt(left, right):
    return lax.dot_general(left, right, (((1,), (1,)), ((), ())), preferred_element_type=F32)


def mm_tn(left, right):
    return lax.dot_general(left, right, (((0,), (0,)), ((), ())), preferred_element_type=F32)


def swap(value, axis, bit):
    count = lax.axis_size(axis)
    return lax.ppermute(value, axis, [(i, i ^ bit) for i in range(count)])


def bit_of(axis, bit):
    return (lax.axis_index(axis) // bit) % 2


def half(value, which, dim):
    size = value.shape[dim] // 2
    return lax.dynamic_slice_in_dim(value, which * size, size, dim)


def halve(value, axis, bit, dim):
    mine = bit_of(axis, bit)
    got = swap(half(value, 1 - mine, dim), axis, bit)
    return (half(value, mine, dim).astype(F32) + got.astype(F32)).astype(BF16)


def after(value, *others):
    return lax.optimization_barrier((value, *others))[0]


def reduce_send(value, axis, bit):
    return swap(half(value, 1 - bit_of(axis, bit), 0), axis, bit)


def reduce_add(value, got, axis, bit):
    return (half(value, bit_of(axis, bit), 0).astype(F32) + got.astype(F32)).astype(BF16)


def gather_pieces(pieces, axis, bit):
    return pieces + [(mask | {(axis, bit)}, swap(rows, axis, bit)) for mask, rows in pieces]


def assemble_kernel(count, widths, row_of, column_of, *refs):
    inputs, outputs = refs[:count], refs[count:]
    for p in range(count):

        @pl.when(pl.program_id(0) == p)
        def _(p=p):
            start = 0
            for out, width in zip(outputs, widths):
                out[...] = inputs[p][:, start : start + width].astype(F32)
                start += width


def assemble(pieces, stages, column_stage, widths):
    count = len(pieces)
    rows, columns = pieces[0][1].shape
    row_of, column_of = [], []
    for mask, _ in pieces:
        place = jnp.int32(0)
        for stage in stages:
            bit = bit_of(*stage)
            place = place * 2 + (1 - bit if stage in mask else bit)
        row_of.append(place)
        bit = bit_of(*column_stage) if column_stage else jnp.int32(0)
        column_of.append(1 - bit if column_stage in mask else bit)
    row_of, column_of = jnp.stack(row_of), jnp.stack(column_of)
    parts = 1
    while rows // parts * columns > (1 << 18) and rows % (32 * parts) == 0:
        parts *= 2
    step = rows // parts

    def source(p):
        def at(i, s, row_of, column_of):
            return (jnp.where(i < p, 0, jnp.where(i == p, s, parts - 1)), 0)

        return pl.BlockSpec((step, columns), at)

    total_rows = rows << len(stages)
    if column_stage:
        specs = [pl.BlockSpec((step, columns), lambda i, s, r, c: (r[i] * parts + s, c[i]))]
        shapes = [jax.ShapeDtypeStruct((total_rows, 2 * columns), F32)]
    else:
        specs = [
            pl.BlockSpec((step, width), lambda i, s, r, c: (r[i] * parts + s, 0))
            for width in widths
        ]
        shapes = [jax.ShapeDtypeStruct((total_rows, width), F32) for width in widths]
    moved = count * rows * columns
    return pl.pallas_call(
        functools.partial(assemble_kernel, count, widths),
        grid_spec=pltpu.PrefetchScalarGridSpec(
            num_scalar_prefetch=2,
            grid=(count, parts),
            in_specs=[source(p) for p in range(count)],
            out_specs=specs,
        ),
        out_shape=shapes,
        compiler_params=pltpu.CompilerParams(vmem_limit_bytes=32 << 20),
        cost_estimate=pl.CostEstimate(flops=moved, bytes_accessed=6 * moved, transcendentals=0),
    )(row_of, column_of, *[rows for _, rows in pieces])


def rope_tables(positions, feat_width):
    half_width = feat_width // 2
    inv_freq = ROPE_BASE ** (-(jnp.arange(half_width, dtype=F32) * 2.0) / feat_width)
    angles = positions.astype(F32)[:, None] * inv_freq[None, :]
    return (jnp.cos(angles), jnp.sin(angles))


def rotate(tensor, cos_table, sin_table):
    half_width = tensor.shape[-1] // 2
    first_half = tensor[..., :half_width]
    second_half = tensor[..., half_width:]
    cos_b = cos_table[:, None, :]
    sin_b = sin_table[:, None, :]
    return jnp.concatenate(
        [first_half * cos_b - second_half * sin_b, second_half * cos_b + first_half * sin_b],
        axis=-1,
    )


def ffn_kernel(groups, with_base, flipped, *refs):
    rows, grads, scale, gate_w, up_w, down_w = refs[:6]
    refs = refs[6:]
    if with_base:
        base_out, base_dx = refs[:2]
        refs = refs[2:]
    hid_ref, dgate_ref, dup_ref, out_ref, dx_ref, small_ref = refs
    width = down_w.shape[0]
    into, back = (mm_nt, mm) if flipped else (mm, mm_nt)
    gate_pre = into(rows[...], gate_w[...])
    up_pre = into(rows[...], up_w[...])
    grad_hidden = mm_nt(grads[...], down_w[...])
    sig = 1.0 / (1.0 + jnp.exp(-gate_pre))
    act = gate_pre * sig
    slope = sig + act * (1.0 - sig)
    hidden = (act * up_pre).astype(BF16).astype(F32)
    each = width // groups
    column = lax.broadcasted_iota(jnp.int32, (1, width), 1)
    wide = scale[:, 0:1]
    for e in range(1, groups):
        wide = jnp.where(column >= e * each, scale[:, e:e+1], wide)
    prod = hidden * grad_hidden
    for e in range(groups):
        part = prod if groups == 1 else jnp.where((column >= e*each) & (column < (e+1)*each), prod, 0.0)
        small_ref[:, e:e+1] = jnp.sum(part, axis=1, keepdims=True)
    hid = (hidden * wide).astype(BF16)
    hid_ref[...] = hid
    scaled = grad_hidden * wide
    dgate = (scaled * up_pre * slope).astype(BF16)
    dup = (scaled * act).astype(BF16)
    dgate_ref[...] = dgate
    dup_ref[...] = dup
    small_ref[:, groups:groups+1] = jnp.sum(dgate.astype(F32)*gate_pre + dup.astype(F32)*up_pre, axis=1, keepdims=True)
    out = mm(hid, down_w[...])
    dx = back(dgate, gate_w[...]) + back(dup, up_w[...])
    if with_base:
        out = out + base_out[...].astype(F32)
        dx = dx + base_dx[...].astype(F32)
    out_ref[...] = out.astype(BF16)
    dx_ref[...] = dx.astype(BF16)

def ffn(rows, grads, scale, gate_w, up_w, down_w, base=(), flipped=False, block=256):
    count, width = rows.shape
    hidden = down_w.shape[0]
    groups = scale.shape[1]
    block = min(block, count)
    def by_row(n): return pl.BlockSpec((block, n), lambda i: (i, 0))
    def held(a): return pl.BlockSpec(a.shape, lambda i: (0, 0), pipeline_mode=pl.Buffered(1))
    return pl.pallas_call(
        functools.partial(ffn_kernel, groups, bool(base), flipped),
        grid=(count // block,),
        in_specs=[by_row(width), by_row(width), by_row(groups), held(gate_w), held(up_w), held(down_w)] + [by_row(width)] * len(base),
        out_specs=[by_row(hidden)] * 3 + [by_row(width)] * 2 + [by_row(groups + 1)],
        out_shape=[jax.ShapeDtypeStruct((count, hidden), BF16)] * 3 + [jax.ShapeDtypeStruct((count, width), BF16)] * 2 + [jax.ShapeDtypeStruct((count, groups + 1), F32)],
        compiler_params=pltpu.CompilerParams(vmem_limit_bytes=62 << 20),
        cost_estimate=pl.CostEstimate(flops=12*count*width*hidden, bytes_accessed=6*width*hidden + 12*count*width, transcendentals=count*hidden),
    )(rows, grads, scale, gate_w, up_w, down_w, *base)


def line_sum(rows, width_own, depth, prepare, settle, gathered, part, came, came_two, spread, sems):
    n = lax.axis_size("tp")
    me = lax.axis_index("tp")
    chunks, _, step, _ = part.shape
    sum_send, sum_recv, two_recv, out_send, out_recv = sems

    def send(source, target, send_sem, recv_sem, to):
        return pltpu.make_async_remote_copy(
            src_ref=source, dst_ref=target, send_sem=send_sem, recv_sem=recv_sem,
            device_id={"tp": to}, device_id_type=pl.DeviceIdType.MESH,
        )

    def sum_copy(c, s, to_right, two):
        target = came_two.at[c] if two else came.at[c, s]
        sem = two_recv.at[c] if two else sum_recv.at[c, s]
        return send(part.at[c, s], target, sum_send.at[c, s], sem, me + 1 if to_right else me - 1)

    def out_copy(c, s, to_right):
        return send(
            spread.at[c, s], spread.at[c, s], out_send.at[c, s, 1 if to_right else 0],
            out_recv.at[c, s], me + 1 if to_right else me - 1,
        )

    def within(c):
        return (c >= 0) & (c < chunks)

    def pass_sums(t):
        @pl.when(within(t))
        def _():
            prepare(t)

        for s in range(n):
            c = t - me * depth

            @pl.when((me < s) & within(c))
            def _(s=s, c=c):
                @pl.when(me > 0)
                def _():
                    sum_copy(c, s, True, False).wait_recv()
                    part[c, s] = (part[c, s].astype(F32) + came[c, s].astype(F32)).astype(BF16)

                sum_copy(c, s, True, False).start()

        for s in range(n):
            c = t - (n - 1 - me) * depth

            @pl.when((me > s) & within(c))
            def _(s=s, c=c):
                @pl.when(me < n - 1)
                def _():
                    sum_copy(c, s, False, False).wait_recv()
                    part[c, s] = (part[c, s].astype(F32) + came[c, s].astype(F32)).astype(BF16)

                @pl.when(me - 1 == s)
                def _():
                    sum_copy(c, s, False, True).start()

                @pl.when(me - 1 > s)
                def _():
                    sum_copy(c, s, False, False).start()

    def pass_own(t):
        c = t - (n - 1) * depth
        for s in range(n):

            @pl.when((me == s) & within(c))
            def _(s=s):
                if s > 0:
                    sum_copy(c, s, True, False).wait_recv()
                if s < n - 1:
                    sum_copy(c, s, False, True).wait_recv()
                total = part[c, s].astype(F32)
                if s > 0:
                    total = total + came[c, s].astype(F32)
                if s < n - 1:
                    total = total + came_two[c].astype(F32)
                spread[c, s] = settle(c, total)
                if s > 0:
                    out_copy(c, s, False).start()
                if s < n - 1:
                    out_copy(c, s, True).start()

    def pass_out(t):
        for s in range(n):
            right = t - (n - 1 + me - s) * depth
            left = t - (n - 1 + s - me) * depth

            @pl.when((me > s) & within(right))
            def _(s=s, c=right):
                out_copy(c, s, True).wait_recv()

                @pl.when(me < n - 1)
                def _():
                    out_copy(c, s, True).start()

            @pl.when((me < s) & within(left))
            def _(s=s, c=left):
                out_copy(c, s, False).wait_recv()

                @pl.when(me > 0)
                def _():
                    out_copy(c, s, False).start()

        last = t - 2 * (n - 1) * depth

        @pl.when(within(last))
        def _():
            gathered(last)

    def turn(t, carry):
        pass_sums(t)
        pass_own(t)
        pass_out(t)
        return carry

    lax.fori_loop(0, chunks + 2 * (n - 1) * depth, turn, 0)

    def drain(c, carry):
        for s in range(n):

            @pl.when(me != s)
            def _(s=s):
                sum_copy(c, s, True, False).wait_send()

            @pl.when((me < n - 1) & (s <= me))
            def _(s=s):
                out_copy(c, s, True).wait_send()

            @pl.when((me > 0) & (s >= me))
            def _(s=s):
                out_copy(c, s, False).wait_send()

        return carry

    lax.fori_loop(0, chunks, drain, 0)


def line_scratch(rows, width_own):
    n = lax.axis_size("tp")
    chunks = max(1, min(16, 128 // n))
    step = rows // chunks
    slots = pltpu.VMEM((chunks, n, step, width_own), BF16)
    dma = pltpu.SemaphoreType.DMA
    return chunks, step, [
        slots, slots, pltpu.VMEM((chunks, step, width_own), BF16), slots,
        dma((chunks, n)), dma((chunks, n)), dma((chunks,)), dma((chunks, n, 2)), dma((chunks, n)),
    ]


def greet(peers):
    n = lax.axis_size("tp")
    me = lax.axis_index("tp")
    barrier = pltpu.get_barrier_semaphore()

    def signal(where):
        pl.semaphore_signal(barrier, inc=1, device_id=where, device_id_type=pl.DeviceIdType.MESH)

    @pl.when(me > 0)
    def _():
        signal({"tp": me - 1})

    @pl.when(me < n - 1)
    def _():
        signal({"tp": me + 1})

    for where in peers:
        signal(where)

    beside = jnp.where(me > 0, 1, 0) + jnp.where(me < n - 1, 1, 0)
    pl.semaphore_wait(barrier, beside + len(peers))


def attend_out_kernel(
    chunks, step, depth, eps, attn, w_out, x, gain,
    mixed, mixed_peer, resid_own, inv_out,
    part, came, came_two, spread, s0, s1, s2, s3, s4, y_send, y_recv,
):
    n = lax.axis_size("tp")
    me = lax.axis_index("tp")
    own = part.shape[3]
    rows = attn.shape[0]
    other = {"ep": 1 - lax.axis_index("ep")}
    greet([other])
    block = max(step, min(rows, 128))

    def product(b, carry):
        start = pl.multiple_of(b * block, block)
        value = mm(attn[pl.ds(start, block), :], w_out[...]).astype(BF16)
        for s in range(n):
            for k in range(block // step):
                part[b * (block // step) + k, s] = value[k * step:(k + 1) * step, s * own:(s + 1) * own]
        return carry

    lax.fori_loop(0, rows // block, product, 0)

    def at(c):
        return pl.ds(pl.multiple_of(c * step, step), step)

    def peer_copy(c):
        return pltpu.make_async_remote_copy(
            src_ref=mixed.at[at(c)], dst_ref=mixed_peer.at[at(c)], send_sem=y_send.at[c], recv_sem=y_recv.at[c],
            device_id=other, device_id_type=pl.DeviceIdType.MESH,
        )

    def prepare(c):
        pass

    def settle(c, total):
        return total.astype(BF16)

    def gathered(c):
        resid = []
        square = jnp.zeros((step, 1), F32)
        for s in range(n):
            piece = x[at(c), s * own:(s + 1) * own].astype(F32) + spread[c, s].astype(F32)
            resid.append(piece)
            square = square + jnp.sum(piece * piece, axis=1, keepdims=True)
        inv = lax.rsqrt(square / (n * own) + eps)
        inv_out[at(c), :] = inv
        for s in range(n):
            mixed[at(c), s * own:(s + 1) * own] = (resid[s] * inv * gain[:, s * own:(s + 1) * own]).astype(BF16)

            @pl.when(me == s)
            def _(s=s):
                resid_own[at(c), :] = resid[s]

        peer_copy(c).start()

    line_sum(rows, own, depth, prepare, settle, gathered, part, came, came_two, spread, (s0, s1, s2, s3, s4))

    def last(c, carry):
        peer_copy(c).wait_recv()
        peer_copy(c).wait_send()
        return carry

    lax.fori_loop(0, chunks, last, 0)


def attend_out(attn, w_out, x, gain, width_own, depth=1):
    rows, width = x.shape
    chunks, step, scratch = line_scratch(rows, width_own)
    vmem = pl.BlockSpec(memory_space=pltpu.VMEM)
    dma = pltpu.SemaphoreType.DMA
    return pl.pallas_call(
        functools.partial(attend_out_kernel, chunks, step, depth, EPS),
        out_shape=[
            jax.ShapeDtypeStruct((rows, width), BF16), jax.ShapeDtypeStruct((rows, width), BF16),
            jax.ShapeDtypeStruct((rows, width_own), F32), jax.ShapeDtypeStruct((rows, 1), F32),
        ],
        in_specs=[vmem] * 4,
        out_specs=[vmem] * 4,
        scratch_shapes=scratch + [dma((chunks,)), dma((chunks,))],
        compiler_params=pltpu.CompilerParams(collective_id=1, has_side_effects=True, vmem_limit_bytes=40 << 20),
        cost_estimate=pl.CostEstimate(flops=0, bytes_accessed=0, transcendentals=0),
    )(attn, w_out, x, gain)


def resid_grad_kernel(
    chunks, step, depth, grad, grad_p, out_p, router, along, g_own, resid_own, inv_two, gain,
    low, grad_resid, gain_grad, out_back,
    part, came, came_two, spread, s0, s1, s2, s3, s4, back, y_send, y_recv, o_send, o_recv,
):
    n = lax.axis_size("tp")
    own = part.shape[3]
    rows = grad.shape[0]
    other = {"ep": 1 - lax.axis_index("ep")}

    def at(c):
        return pl.ds(pl.multiple_of(c * step, step), step)

    def peer_copy(c):
        return pltpu.make_async_remote_copy(
            src_ref=grad_p.at[at(c)], dst_ref=back.at[at(c)], send_sem=y_send.at[c], recv_sem=y_recv.at[c],
            device_id=other, device_id_type=pl.DeviceIdType.MESH,
        )

    def out_copy():
        return pltpu.make_async_remote_copy(
            src_ref=out_p, dst_ref=out_back, send_sem=o_send, recv_sem=o_recv,
            device_id=other, device_id_type=pl.DeviceIdType.MESH,
        )

    greet([other])

    def begin(c, carry):
        peer_copy(c).start()
        return carry

    lax.fori_loop(0, chunks, begin, 0)
    out_copy().start()
    gain_grad[...] = jnp.zeros_like(gain_grad)

    def prepare(c):
        peer_copy(c).wait_recv()
        for s in range(n):
            columns = slice(s * own, (s + 1) * own)
            part[c, s] = (grad[at(c), columns].astype(F32) + back[at(c), columns].astype(F32)).astype(BF16)

    def settle(c, total):
        total = total + router[at(c), :]
        inv = inv_two[at(c), :]
        resid = resid_own[at(c), :]
        gain_grad[...] += jnp.sum(total * resid * inv, axis=0, keepdims=True)
        result = g_own[at(c), :].astype(F32) + inv * gain[...] * total - resid * (inv * inv * along[at(c), :] / (n * own))
        grad_resid[at(c), :] = result
        return result.astype(BF16)

    def gathered(c):
        for s in range(n):
            low[at(c), s * own:(s + 1) * own] = spread[c, s]

    line_sum(rows, own, depth, prepare, settle, gathered, part, came, came_two, spread, (s0, s1, s2, s3, s4))

    def last(c, carry):
        peer_copy(c).wait_send()
        return carry

    lax.fori_loop(0, chunks, last, 0)
    out_copy().wait()


def resid_grad(grad, grad_p, out_p, router, along, g_own, resid_own, inv_two, gain, depth=1):
    rows, width = grad.shape
    width_own = g_own.shape[1]
    chunks, step, scratch = line_scratch(rows, width_own)
    vmem = pl.BlockSpec(memory_space=pltpu.VMEM)
    far = pl.BlockSpec(memory_space=pl.ANY)
    dma = pltpu.SemaphoreType.DMA
    return pl.pallas_call(
        functools.partial(resid_grad_kernel, chunks, step, depth),
        out_shape=[
            jax.ShapeDtypeStruct((rows, width), BF16), jax.ShapeDtypeStruct((rows, width_own), F32),
            jax.ShapeDtypeStruct((1, width_own), F32), jax.ShapeDtypeStruct((rows, width), BF16),
        ],
        in_specs=[vmem] + [far] * 2 + [vmem] * 6,
        out_specs=[vmem] * 3 + [far],
        scratch_shapes=scratch + [pltpu.VMEM((rows, width), BF16), dma((chunks,)), dma((chunks,)), dma, dma],
        compiler_params=pltpu.CompilerParams(collective_id=2, has_side_effects=True, vmem_limit_bytes=40 << 20),
        cost_estimate=pl.CostEstimate(flops=0, bytes_accessed=0, transcendentals=0),
    )(grad, grad_p, out_p, router, along, g_own, resid_own, inv_two, gain)


def body(
    tokens,
    norm_attn,
    w_query,
    w_key,
    w_value,
    w_output,
    norm_ffn,
    w_router,
    shared_switch,
    shared_gate,
    shared_up,
    shared_down,
    expert_gate,
    expert_up,
    expert_down,
    routes,
    segments,
    output_gradient,
):
    tp_count = lax.axis_size("tp")
    ep_count = lax.axis_size("ep")
    dp_count = lax.axis_size("dp")
    tp_rank = lax.axis_index("tp")
    ep_rank = lax.axis_index("ep")
    rows = tokens.shape[0]
    width_own = tokens.shape[1]
    width = width_own * tp_count
    heads = w_query.shape[1] // HD
    experts_own = expert_gate.shape[0]
    experts = experts_own * ep_count
    expert_width = expert_gate.shape[2]
    score_scale = 1.0 / math.sqrt(HD)
    far_bits = [1 << b for b in range(1, dp_count.bit_length() - 1)]

    def own_columns(value):
        return lax.dynamic_slice_in_dim(value, tp_rank * width_own, width_own, value.ndim - 1)

    near = bit_of("dp", 1)

    def pair_send(left, right, columns):
        if columns:
            right = half(right, 1 - near, 1)
        else:
            left = half(left, 1 - near, 1)
        return swap(mm_tn(left, right).astype(BF16), "dp", 1)

    def pair_keep(left, right, columns, got):
        if columns:
            right = half(right, near, 1)
        else:
            left = half(left, near, 1)
        return (mm_tn(left, right) + got.astype(F32)).astype(BF16)

    core = ("dp", 1)
    far = [("dp", b) for b in far_bits]
    line = [("ep", 1)]

    def alone(value):
        return [(frozenset(), value)]

    def whole(pieces, stages, columns, widths):
        if columns:
            return assemble(pieces, stages, core, widths)
        return assemble(pieces, [core] + stages, None, widths)

    def over_tp(value):
        bit = 1
        while bit < tp_count:
            value = value + swap(value, "tp", bit)
            bit *= 2
        return value

    def over_rows(value):
        for axis, bit in [core] + far + line:
            value = value + swap(value, axis, bit)
        return value

    packed = jnp.concatenate(
        [tokens, norm_attn[None, :], norm_ffn[None, :], jnp.zeros((14, width_own), BF16)], axis=0
    )
    packed = lax.all_gather(packed, "tp", axis=1, tiled=True)
    x_full = packed[:rows].astype(F32)
    gain_one = packed[rows].astype(F32)
    gain_two = packed[rows + 1].astype(F32)
    grad_rows = lax.all_gather(output_gradient, "tp", axis=1, tiled=True)
    grad_peer = swap(grad_rows, "ep", 1)
    route_hot = jnp.sum(
        (routes[:, :, None] == jnp.arange(experts, dtype=jnp.int32)[None, None, :]).astype(F32),
        axis=1,
    )
    route_hot_peer = swap(route_hot, "ep", 1)

    inv_one = lax.rsqrt(jnp.mean(x_full * x_full, axis=1, keepdims=True) + EPS)
    normed = (x_full * inv_one * gain_one).astype(BF16)
    q_pre = mm(normed, w_query)
    k_pre = mm(normed, w_key)
    v_pre = mm(normed, w_value)
    positions = ep_rank * rows + jnp.arange(rows, dtype=jnp.int32)
    cos_table, sin_table = rope_tables(positions, HD)
    query = rotate(q_pre.reshape(rows, heads, HD), cos_table, sin_table).astype(BF16)
    key_own = rotate(k_pre.reshape(rows, heads, HD), cos_table, sin_table).astype(BF16)
    value_own = v_pre.astype(BF16).reshape(rows, heads, HD)
    forth = [(i, i + 1) for i in range(ep_count - 1)]
    back = [(i + 1, i) for i in range(ep_count - 1)]
    earlier = lax.ppermute(jnp.stack([key_own, value_own]), "ep", forth)
    earlier = after(earlier, grad_rows)
    key_rows = jnp.concatenate([earlier[0], key_own], axis=0)
    value_rows = jnp.concatenate([earlier[1], value_own], axis=0)
    key_pos = (ep_rank - 1) * rows + jnp.arange(2 * rows, dtype=jnp.int32)
    seg_rows = segments.reshape(ep_count, rows)
    query_seg = lax.dynamic_index_in_dim(seg_rows, ep_rank, 0, keepdims=False)
    before_seg = lax.dynamic_index_in_dim(
        seg_rows, jnp.maximum(ep_rank - 1, 0), 0, keepdims=False
    )
    key_seg = jnp.concatenate([jnp.where(ep_rank > 0, before_seg, -1), query_seg])
    allowed = (query_seg[:, None] == key_seg[None, :]) & (key_pos[None, :] <= positions[:, None])

    def masked_scores():
        scores = (
            jnp.einsum("qhd,khd->hqk", query, key_rows, preferred_element_type=F32) * score_scale
        )
        return jnp.where(allowed[None], scores, NEG)

    scores = masked_scores()
    row_top = jnp.max(scores, axis=2, keepdims=True)
    shifted = jnp.exp(scores - row_top)
    row_total = jnp.sum(shifted, axis=2, keepdims=True)
    weights = (shifted / row_total).astype(BF16)
    attended = jnp.einsum("hqk,khd->qhd", weights, value_rows, preferred_element_type=F32)
    attn_rows = attended.astype(BF16).reshape(rows, heads * HD)
    log_norm = row_top + jnp.log(row_total)

    mixed, mixed_peer, resid_own, inv_two = attend_out(
        attn_rows, w_output, after(packed[:rows], grad_peer), gain_two[None, :], width_own
    )

    def router(values):
        logits = mm(values, w_router)
        return logits, jax.nn.softmax(logits, axis=1)

    logits, router_prob = router(mixed)
    combine = router_prob * route_hot
    combine_peer = router(mixed_peer)[1] * route_hot_peer
    switch_logit = mm(mixed, shared_switch[:, None])
    switch = jax.nn.sigmoid(switch_logit)

    def own_experts(value):
        return lax.dynamic_slice_in_dim(value, ep_rank * experts_own, experts_own, 1)

    x_link = far[0]
    y_link = line[0]

    hid_s, gate_s, up_s, out_s, grad_s, small_s = ffn(
        mixed, grad_rows, switch, shared_gate, shared_up, shared_down
    )
    got_sg = pair_send(mixed, gate_s, False)
    got_sd = pair_send(hid_s, after(grad_rows, got_sg), True)
    got_su = pair_send(after(mixed, got_sd), up_s, False)
    sum_sg = pair_keep(mixed, gate_s, False, got_sg)
    got_sg = reduce_send(sum_sg, *x_link)
    sum_sd = pair_keep(hid_s, after(grad_rows, sum_sg), True, got_sd)
    got_sd = reduce_send(sum_sd, *x_link)
    sum_su = pair_keep(after(mixed, sum_sd), up_s, False, got_su)
    got_su = reduce_send(sum_su, *y_link)

    hidden_width = experts_own * expert_width
    gate_w = jnp.transpose(expert_gate, (0, 2, 1)).reshape(hidden_width, width)
    up_w = jnp.transpose(expert_up, (0, 2, 1)).reshape(hidden_width, width)
    down_w = expert_down.reshape(hidden_width, width)
    peer_rows = after(mixed_peer, sum_su)
    hid_p, gate_p, up_p, out_p, grad_p, small_p = ffn(
        peer_rows, grad_peer, own_experts(combine_peer), gate_w, up_w, down_w, (), True
    )
    small_back = swap(small_p.T, "ep", 1)
    sum_sg = reduce_add(sum_sg, after(got_sg, grad_p), *x_link)
    got_sg = reduce_send(sum_sg, *y_link)
    own_rows = after(mixed, sum_sg)
    hid_e, gate_e, up_e, out_e, grad_e, small_e = ffn(
        own_rows, grad_rows, own_experts(combine), gate_w, up_w, down_w, (out_s, grad_s), True
    )

    first = ep_rank == 0
    small_e = small_e.T
    dots_here, dots_there = small_e[:experts_own], small_back[:experts_own]
    small = jnp.concatenate(
        [
            jnp.where(first, dots_here, dots_there),
            jnp.where(first, dots_there, dots_here),
            small_s.T[:1],
            small_s.T[1:] + small_e[experts_own:] + small_back[experts_own:],
        ],
        axis=0,
    )
    small = over_tp(small)

    sum_su = reduce_add(sum_su, after(got_su, grad_e), *y_link)
    got_su = reduce_send(sum_su, *x_link)
    sum_sd = reduce_add(sum_sd, after(got_sd, sum_su), *x_link)
    got_sd = reduce_send(sum_sd, *y_link)

    both = after(jnp.concatenate([mixed, mixed_peer], axis=0), sum_sd)
    both_grad = jnp.concatenate([grad_rows, grad_peer], axis=0)
    gate_b = jnp.concatenate([gate_e, gate_p], axis=0)
    up_b = jnp.concatenate([up_e, up_p], axis=0)
    hid_b = jnp.concatenate([hid_e, hid_p], axis=0)
    got_eg = pair_send(gate_b, both, True)
    got_eu = pair_send(up_b, after(both, got_eg), True)
    got_ed = pair_send(hid_b, after(both_grad, got_eu), True)
    sum_eg = pair_keep(gate_b, both, True, got_eg)
    got_eg = reduce_send(sum_eg, *x_link)
    sum_eu = pair_keep(up_b, after(both, sum_eg), True, got_eu)
    got_eu = reduce_send(sum_eu, *x_link)
    sum_ed = pair_keep(hid_b, after(both_grad, sum_eu), True, got_ed)
    got_ed = reduce_send(sum_ed, *x_link)
    sum_su = reduce_add(sum_su, after(got_su, sum_ed), *x_link)
    piece_su = gather_pieces(alone(sum_su), *x_link)
    sum_sg = reduce_add(sum_sg, after(got_sg, sum_su), *y_link)
    piece_sg = gather_pieces(alone(sum_sg), *x_link)
    sum_sd = reduce_add(sum_sd, after(got_sd, sum_sg), *y_link)
    piece_sd = gather_pieces(alone(sum_sd), *x_link)

    small = small.T
    grad_prob = small[:, :experts] * route_hot
    grad_switch = small[:, experts : experts + 1]
    along = small[:, experts + 1 : experts + 2]
    grad_logits = (
        router_prob * (grad_prob - jnp.sum(router_prob * grad_prob, axis=1, keepdims=True))
    ).astype(BF16)
    grad_slogit = (grad_switch * switch * (1.0 - switch)).astype(BF16)
    tp_rows = lax.dynamic_slice_in_dim(w_router, tp_rank * width_own, width_own, 0)
    router_part = (
        mm_nt(grad_logits, tp_rows)
        + grad_slogit.astype(F32) * own_columns(shared_switch).astype(F32)[None, :]
    )
    grad_router = mm_tn(grad_logits, mixed)
    grad_switch_w = mm_tn(grad_slogit, mixed)
    along = (
        along
        + jnp.sum(grad_logits.astype(F32) * logits, axis=1, keepdims=True)
        + grad_slogit.astype(F32) * switch_logit
    )
    resid_low, grad_resid, grad_gain_two, out_back = resid_grad(
        after(grad_e, sum_sd), grad_p, out_p, router_part, along, output_gradient, resid_own, inv_two, norm_ffn.astype(F32)[None, :]
    )
    flat = jnp.concatenate(
        [grad_gain_two.reshape(-1), grad_router.reshape(-1), grad_switch_w.reshape(-1)]
    ).reshape(-1, 128)
    ffn_part = (out_e.astype(F32) + out_back.astype(F32)).astype(BF16)

    grad_attn = mm_nt(resid_low, w_output).astype(BF16).reshape(rows, heads, HD)
    probs = jnp.exp(masked_scores() - log_norm)
    grad_probs = jnp.einsum("qhd,khd->hqk", grad_attn, value_rows, preferred_element_type=F32)
    grad_scores = (
        probs * (grad_probs - jnp.sum(probs * grad_probs, axis=2, keepdims=True))
    ).astype(BF16)
    grad_query = (
        jnp.einsum("hqk,khd->qhd", grad_scores, key_rows, preferred_element_type=F32) * score_scale
    )
    grad_keys = (
        jnp.einsum("hqk,qhd->khd", grad_scores, query, preferred_element_type=F32) * score_scale
    )
    grad_values = jnp.einsum(
        "hqk,qhd->khd", probs.astype(BF16), grad_attn, preferred_element_type=F32
    )
    later = lax.ppermute(
        jnp.stack([grad_keys[:rows], grad_values[:rows]]).astype(BF16), "ep", back
    )
    ffn_own = lax.psum_scatter(
        after(ffn_part, grad_keys), "tp", scatter_dimension=1, tiled=True
    )
    layer_out = (resid_own + ffn_own.astype(F32)).astype(BF16)
    flat = over_rows(after(flat, grad_keys))
    sum_eg = reduce_add(sum_eg, after(got_eg, grad_keys), *x_link)
    piece_eg = gather_pieces(alone(sum_eg), *x_link)
    sum_eu = reduce_add(sum_eu, after(got_eu, sum_eg), *x_link)
    piece_eu = gather_pieces(alone(sum_eu), *x_link)
    sum_ed = reduce_add(sum_ed, after(got_ed, sum_eu), *x_link)
    piece_ed = gather_pieces(alone(sum_ed), *x_link)
    got_wo = pair_send(after(attn_rows, sum_ed), resid_low, True)
    sum_wo = pair_keep(after(attn_rows, got_wo), resid_low, True, got_wo)
    got_wo = reduce_send(sum_wo, *y_link)
    later = after(later, sum_wo).astype(F32)
    grad_key = grad_keys[rows:] + later[0]
    grad_value = grad_values[rows:] + later[1]
    shape = (rows, heads * HD)
    grad_qpre = rotate(grad_query, cos_table, -sin_table).astype(BF16).reshape(shape)
    grad_kpre = rotate(grad_key, cos_table, -sin_table).astype(BF16).reshape(shape)
    grad_vpre = grad_value.astype(BF16).reshape(shape)
    grad_qkv = jnp.concatenate([grad_qpre, grad_kpre, grad_vpre], axis=1)
    got_qkv = pair_send(normed, grad_qkv, False)
    grad_qkv = after(grad_qkv, got_qkv)
    sum_qkv = pair_keep(normed, grad_qkv, False, got_qkv)
    got_qkv = reduce_send(sum_qkv, *y_link)
    grad_normed = (
        mm_nt(after(grad_qpre, sum_qkv), w_query)
        + mm_nt(grad_kpre, w_key)
        + mm_nt(grad_vpre, w_value)
    ).astype(BF16)
    normed_own = lax.psum_scatter(grad_normed, "tp", scatter_dimension=1, tiled=True).astype(F32)
    row_part = jnp.sum(
        grad_qpre.astype(F32) * q_pre
        + grad_kpre.astype(F32) * k_pre
        + grad_vpre.astype(F32) * v_pre,
        axis=1,
    )
    row_total = over_tp(row_part[None, :]).T

    y_then_x, x_then_y = line + far, far + line
    qkv = heads * HD
    inner = shared_gate.shape[1]

    def later_pieces(pieces, other, stage):
        (mask, rows_), *rest = pieces
        return gather_pieces([(mask, after(rows_, other))] + rest, *stage)

    piece_su = later_pieces(piece_su, grad_normed, y_link)
    piece_sg = later_pieces(piece_sg, piece_su[1][1], y_link)
    piece_sd = later_pieces(piece_sd, piece_sg[1][1], y_link)
    sum_wo = reduce_add(sum_wo, after(got_wo, grad_normed), *y_link)
    got_wo = reduce_send(sum_wo, *x_link)
    sum_qkv = reduce_add(sum_qkv, after(got_qkv, sum_wo), *y_link)
    got_qkv = reduce_send(sum_qkv, *x_link)
    piece_su = later_pieces(piece_su, sum_qkv, core)
    piece_sg = later_pieces(piece_sg, piece_su[3][1], core)
    (su_grad,) = whole(piece_su, y_then_x, False, (inner,))
    piece_sd = later_pieces(piece_sd, piece_sg[3][1], core)
    (sg_grad,) = whole(piece_sg, x_then_y, False, (inner,))
    (sd_grad,) = whole(piece_sd, x_then_y, True, (width // 2,))
    piece_eg = later_pieces(piece_eg, sum_qkv, core)
    (eg_grad,) = whole(piece_eg, far, True, (width // 2,))
    piece_eu = later_pieces(piece_eu, piece_eg[1][1], core)
    (eu_grad,) = whole(piece_eu, far, True, (width // 2,))
    piece_ed = later_pieces(piece_ed, piece_eu[1][1], core)
    (ed_grad,) = whole(piece_ed, far, True, (width // 2,))
    sum_wo = reduce_add(sum_wo, after(got_wo, piece_ed[1][1]), *x_link)
    sum_qkv = reduce_add(sum_qkv, after(got_qkv, sum_wo), *x_link)
    piece_qkv = gather_pieces(alone(sum_qkv), *x_link)
    piece_wo = gather_pieces(alone(sum_wo), *x_link)
    piece_qkv = gather_pieces(piece_qkv, *y_link)
    piece_wo = gather_pieces(piece_wo, *y_link)
    piece_wo = gather_pieces(piece_wo, *core)
    piece_qkv = gather_pieces(piece_qkv, *core)
    (wo_grad,) = whole(piece_wo, y_then_x, True, (width // 2,))
    wq_grad, wk_grad, wv_grad = whole(piece_qkv, y_then_x, False, (qkv,) * 3)

    x_own = tokens.astype(F32)
    grad_tokens = (
        grad_resid
        + inv_one * norm_attn.astype(F32) * normed_own
        - x_own * (inv_one * inv_one) * (row_total / width)
    )
    grad_gain_one = jnp.sum(normed_own * x_own * inv_one, axis=0)

    flat = flat.reshape(-1)
    grad_gain_two = flat[:width_own]
    grad_router = flat[width_own : width_own + width * experts].reshape(experts, width).T
    grad_switch_w = flat[width_own + width * experts :]
    grad_gain_one = over_rows(grad_gain_one.reshape(-1, 128)).reshape(-1)

    def per_expert(value):
        return value.reshape(experts_own, expert_width, width)

    return (
        layer_out,
        grad_tokens,
        grad_gain_one,
        wq_grad,
        wk_grad,
        wv_grad,
        wo_grad,
        grad_gain_two,
        grad_router,
        grad_switch_w,
        sg_grad,
        su_grad,
        sd_grad,
        jnp.transpose(per_expert(eg_grad), (0, 2, 1)),
        jnp.transpose(per_expert(eu_grad), (0, 2, 1)),
        per_expert(ed_grad),
    )


def solution(mesh):
    placed = (
        P(("dp", "ep"), "tp"),
        P("tp"),
        P(None, "tp"),
        P(None, "tp"),
        P(None, "tp"),
        P("tp", None),
        P("tp"),
        P(),
        P(),
        P(None, "tp"),
        P(None, "tp"),
        P("tp", None),
        P("ep", None, "tp"),
        P("ep", None, "tp"),
        P("ep", "tp", None),
        P(("dp", "ep"), None),
        P("dp"),
        P(("dp", "ep"), "tp"),
    )
    return jax.shard_map(
        body,
        mesh=mesh,
        in_specs=placed,
        out_specs=(
            P(("dp", "ep"), "tp"),
            P(("dp", "ep"), "tp"),
            P("tp"),
            P(None, "tp"),
            P(None, "tp"),
            P(None, "tp"),
            P("tp", None),
            P("tp"),
            P(),
            P(),
            P(None, "tp"),
            P(None, "tp"),
            P("tp", None),
            P("ep", None, "tp"),
            P("ep", None, "tp"),
            P("ep", "tp", None),
        ),
        check_vma=False,
    )
```

```python
import functools
import math

import jax
import jax.numpy as jnp
from jax import lax
from jax.experimental import pallas as pl
from jax.experimental.pallas import tpu as pltpu
from jax.sharding import PartitionSpec as P

HD = 128
EPS = 1e-06
ROPE_BASE = 1000000.0
NEG = -1e30
F32 = jnp.float32
BF16 = jnp.bfloat16


def mm(left, right):
    return lax.dot_general(left, right, (((1,), (0,)), ((), ())), preferred_element_type=F32)


def mm_nt(left, right):
    return lax.dot_general(left, right, (((1,), (1,)), ((), ())), preferred_element_type=F32)


def mm_tn(left, right):
    return lax.dot_general(left, right, (((0,), (0,)), ((), ())), preferred_element_type=F32)


def swap(value, axis, bit):
    count = lax.axis_size(axis)
    return lax.ppermute(value, axis, [(i, i ^ bit) for i in range(count)])


def bit_of(axis, bit):
    return (lax.axis_index(axis) // bit) % 2


def half(value, which, dim):
    size = value.shape[dim] // 2
    return lax.dynamic_slice_in_dim(value, which * size, size, dim)


def after(value, *others):
    return lax.optimization_barrier((value, *others))[0]


def reduce_send(value, axis, bit):
    return swap(half(value, 1 - bit_of(axis, bit), 0), axis, bit)


def reduce_add(value, got, axis, bit):
    return (half(value, bit_of(axis, bit), 0).astype(F32) + got.astype(F32)).astype(BF16)


def places():
    count = lax.axis_size("dp")
    dp, ep = lax.axis_index("dp"), lax.axis_index("ep")
    core, x = dp % 2, dp // (count // 2)
    where = (
        {"dp": dp + 1 - 2 * core},
        {"dp": (dp + count // 2) % count},
        {"ep": 1 - ep},
    )
    return core, x, ep, where


def greet_all(peers):
    barrier = pltpu.get_barrier_semaphore()
    for where in peers:
        pl.semaphore_signal(
            barrier, inc=1, device_id=where, device_id_type=pl.DeviceIdType.MESH
        )
    pl.semaphore_wait(barrier, len(peers))


def add_rows(total, more, start, count, out=None):
    step = 32 if count % 32 == 0 else 16

    def turn(k, carry):
        here = pl.ds(pl.multiple_of(k * step, step), step)
        there = pl.ds(pl.multiple_of(start + k * step, step), step)
        value = (total[there, :].astype(F32) + more[here, :].astype(F32)).astype(BF16)
        if out is None:
            total[there, :] = value
        else:
            out[here, :] = value
        return carry

    lax.fori_loop(0, count // step, turn, 0)


def sums_kernel(
    sgu, sd, egu, ed, qkv, wo, flat,
    sgu_f, sd_f, egu_f, ed_f, qkv_f, wo_f, flat_f,
    q_own, q_in, q_in2, q_out, w_own, w_in, w_in2, w_out, flat_in, l_sem, s_sem, r_sem,
):
    core, x, y, (to_core, to_x, to_y) = places()
    used = [0, 0]

    def here(source, target):
        k = used[0]
        used[0] += 1
        copy = pltpu.make_async_copy(source, target, l_sem.at[k])
        copy.start()
        return copy

    def there(source, target, where):
        k = used[1]
        used[1] += 1
        copy = pltpu.make_async_remote_copy(
            src_ref=source, dst_ref=target, send_sem=s_sem.at[k], recv_sem=r_sem.at[k],
            device_id=where, device_id_type=pl.DeviceIdType.MESH,
        )
        copy.start()
        return copy

    greet_all((to_core, to_x, to_y))
    q_rows, w_rows = q_own.shape[0], w_own.shape[0]
    load_q = here(qkv.at[pl.ds(y * q_rows, q_rows)], q_own)
    load_w = here(wo.at[pl.ds(y * w_rows, w_rows)], w_own)
    a1 = there(qkv.at[pl.ds((1 - y) * q_rows, q_rows)], q_in, to_y)
    a2 = there(wo.at[pl.ds((1 - y) * w_rows, w_rows)], w_in, to_y)
    b1 = there(sgu, sgu_f.at[core, x, y], to_x)
    b2 = there(sd, sd_f.at[core, y, x], to_x)
    f1 = there(flat, flat_in.at[0], to_core)
    own_s = here(sgu, sgu_f.at[core, x, y])
    own_sd = here(sd, sd_f.at[core, y, x])
    own_e = here(egu, egu_f.at[core, x])
    own_ed = here(ed, ed_f.at[core, x])

    b1.wait_recv()
    d1 = there(sgu, sgu_f.at[core, x, y], to_y)
    d2 = there(sgu_f.at[core, 1 - x, y], sgu_f.at[core, 1 - x, y], to_y)
    f1.wait()
    flat_f[...] = flat[...] + flat_in[0]
    f2 = there(flat_f, flat_in.at[1], to_x)

    load_q.wait()
    a1.wait_recv()
    add_rows(q_own, q_in, 0, q_rows)
    a3 = there(q_own.at[pl.ds((1 - x) * (q_rows // 2), q_rows // 2)], q_in2, to_x)
    load_w.wait()
    a2.wait_recv()
    add_rows(w_own, w_in, 0, w_rows)
    a4 = there(w_own.at[pl.ds((1 - x) * (w_rows // 2), w_rows // 2)], w_in2, to_x)
    cut = egu.shape[0] // 2
    b3 = there(egu.at[pl.ds(0, cut)], egu_f.at[core, x, pl.ds(0, cut)], to_x)
    b2.wait_recv()
    own_sd.wait()
    d3 = there(sd_f.at[core, y], sd_f.at[core, y], to_y)
    f2.wait()
    flat_f[...] = flat_f[...] + flat_in[1]
    f3 = there(flat_f, flat_in.at[2], to_y)

    a3.wait_recv()
    add_rows(q_own, q_in2, x * (q_rows // 2), q_rows // 2, q_out)
    a5 = there(q_out, qkv_f.at[core, y, x], to_x)
    own_q = here(q_out, qkv_f.at[core, y, x])
    a4.wait_recv()
    add_rows(w_own, w_in2, x * (w_rows // 2), w_rows // 2, w_out)
    a6 = there(w_out, wo_f.at[core, y, x], to_x)
    own_w = here(w_out, wo_f.at[core, y, x])
    b4 = there(egu.at[pl.ds(cut, cut)], egu_f.at[core, x, pl.ds(cut, cut)], to_x)
    b5 = there(ed, ed_f.at[core, x], to_x)

    d1.wait_recv()
    d2.wait_recv()
    own_s.wait()
    c1 = there(sgu_f.at[core], sgu_f.at[core], to_core)
    a5.wait_recv()
    own_q.wait()
    a7 = there(qkv_f.at[core, y], qkv_f.at[core, y], to_y)
    a6.wait_recv()
    own_w.wait()
    a8 = there(wo_f.at[core, y], wo_f.at[core, y], to_y)
    d3.wait_recv()
    c2 = there(sd_f.at[core], sd_f.at[core], to_core)
    f3.wait()
    flat_f[...] = flat_f[...] + flat_in[2]
    b3.wait_recv()
    b4.wait_recv()
    own_e.wait()
    c3 = there(egu_f.at[core], egu_f.at[core], to_core)
    a7.wait_recv()
    c4 = there(qkv_f.at[core], qkv_f.at[core], to_core)
    a8.wait_recv()
    c5 = there(wo_f.at[core], wo_f.at[core], to_core)
    b5.wait_recv()
    own_ed.wait()
    c6 = there(ed_f.at[core], ed_f.at[core], to_core)
    for copy in (c1, c2, c3, c4, c5, c6):
        copy.wait_recv()
    for copy in (a1, a2, a3, a4, a5, a6, a7, a8, b1, b2, b3, b4, b5, d1, d2, d3, c1, c2, c3, c4, c5, c6):
        copy.wait_send()


def sums(sgu, sd, egu, ed, qkv, wo, flat):
    def pieces(count, value, cut=1):
        return jax.ShapeDtypeStruct(
            (2,) * count + (value.shape[0] // cut, value.shape[1]), BF16
        )

    far = pl.BlockSpec(memory_space=pl.ANY)
    vmem = pl.BlockSpec(memory_space=pltpu.VMEM)

    def room(value, cut):
        return pltpu.VMEM((value.shape[0] // cut, value.shape[1]), BF16)

    dma = pltpu.SemaphoreType.DMA
    return pl.pallas_call(
        sums_kernel,
        out_shape=[
            pieces(3, sgu), pieces(3, sd), pieces(2, egu), pieces(2, ed),
            pieces(3, qkv, 4), pieces(3, wo, 4), jax.ShapeDtypeStruct(flat.shape, F32),
        ],
        in_specs=[far] * 6 + [vmem],
        out_specs=[far] * 6 + [vmem],
        scratch_shapes=[room(qkv, 2), room(qkv, 2), room(qkv, 4), room(qkv, 4)]
        + [room(wo, 2), room(wo, 2), room(wo, 4), room(wo, 4)]
        + [pltpu.VMEM((3,) + flat.shape, F32), dma((8,)), dma((25,)), dma((25,))],
        compiler_params=pltpu.CompilerParams(
            collective_id=3, has_side_effects=True, vmem_limit_bytes=32 << 20
        ),
        cost_estimate=pl.CostEstimate(flops=0, bytes_accessed=0, transcendentals=0),
    )(sgu, sd, egu, ed, qkv, wo, flat)


def widen_kernel(source, *outputs):
    value = source[...]
    value = value.reshape(value.shape[-2:])
    start = 0
    for out in outputs:
        width = out.shape[1]
        out[...] = value[:, start : start + width].astype(F32)
        start += width


def widen(value, widths=(), kinds=1, kind=0):
    columns = value.shape[-1]
    if widths:
        value = value.reshape(-1, columns)
        rows = value.shape[0]
        step = min(rows, 256)
        source = pl.BlockSpec((step, columns), lambda i: (i, 0))
        grid = (rows // step,)
        specs = [pl.BlockSpec((step, width), lambda i: (i, 0)) for width in widths]
        shapes = [jax.ShapeDtypeStruct((rows, width), F32) for width in widths]
    else:
        value = value.reshape(2, kinds, -1, columns)
        rows = value.shape[2]
        step = rows
        while step * columns > (1 << 19) and step % 32 == 0:
            step //= 2
        steps = rows // step
        source = pl.BlockSpec((1, 1, step, columns), lambda i, c: (c, kind, i, 0))
        grid = (steps, 2)
        specs = [pl.BlockSpec((step, columns), lambda i, c: (i, c))]
        shapes = [jax.ShapeDtypeStruct((rows, 2 * columns), F32)]
    return pl.pallas_call(
        widen_kernel,
        grid=grid,
        in_specs=[source],
        out_specs=specs,
        out_shape=shapes,
        compiler_params=pltpu.CompilerParams(vmem_limit_bytes=32 << 20),
        cost_estimate=pl.CostEstimate(flops=0, bytes_accessed=0, transcendentals=0),
    )(value)


def weight_kernel(added, part, left, right, *refs):
    total = mm_tn(left[...], right[...])
    if added:
        total = total + refs[0][...].astype(F32)
    refs[-1][...] = total.astype(BF16)


def weight_half(left, right, which, columns, got=None, rows=None, block=1408):
    rows = rows or left.shape[0]
    height, wide = left.shape[1], right.shape[1]
    if columns:
        wide = wide // 2
    else:
        height = height // 2
    step = height
    while step > block and step % 256 == 0:
        step //= 2
    steps = height // step
    extra = [] if got is None else [got]
    out_spec = pl.BlockSpec((step, wide), lambda i, part: (i, 0))
    if columns:
        left_at, right_at = (lambda i, part: (0, i)), (lambda i, part: (0, part[0]))
    else:
        left_at, right_at = (lambda i, part: (0, part[0] * steps + i)), (lambda i, part: (0, 0))
    return pl.pallas_call(
        functools.partial(weight_kernel, bool(extra)),
        grid_spec=pltpu.PrefetchScalarGridSpec(
            num_scalar_prefetch=1,
            grid=(steps,),
            in_specs=[pl.BlockSpec((rows, step), left_at), pl.BlockSpec((rows, wide), right_at)]
            + [out_spec] * len(extra),
            out_specs=out_spec,
        ),
        out_shape=jax.ShapeDtypeStruct((height, wide), BF16),
        compiler_params=pltpu.CompilerParams(vmem_limit_bytes=48 << 20),
        cost_estimate=pl.CostEstimate(flops=0, bytes_accessed=0, transcendentals=0),
    )(which.reshape(1).astype(jnp.int32), left, right, *extra)


def rope_tables(positions, feat_width):
    half_width = feat_width // 2
    inv_freq = ROPE_BASE ** (-(jnp.arange(half_width, dtype=F32) * 2.0) / feat_width)
    angles = positions.astype(F32)[:, None] * inv_freq[None, :]
    return (jnp.cos(angles), jnp.sin(angles))


def rotate(tensor, cos_table, sin_table):
    half_width = tensor.shape[-1] // 2
    first_half = tensor[..., :half_width]
    second_half = tensor[..., half_width:]
    cos_b = cos_table[:, None, :]
    sin_b = sin_table[:, None, :]
    return jnp.concatenate(
        [first_half * cos_b - second_half * sin_b, second_half * cos_b + first_half * sin_b],
        axis=-1,
    )


def ffn_kernel(groups, base, into, flipped, *refs):
    rows, grads, scale, gate_w, up_w, down_w = refs[:6]
    refs = refs[6:]
    if base:
        base_out, base_dx = refs[:2]
        refs = refs[2:]
    hid_ref, dgu_ref, out_ref, dx_ref, small_ref = refs[2:] if into else refs
    width = down_w.shape[0]
    to, back = (mm_nt, mm) if flipped else (mm, mm_nt)
    gate_pre = to(rows[...], gate_w[...])
    up_pre = to(rows[...], up_w[...])
    grad_hidden = mm_nt(grads[...], down_w[...])
    sig = 1.0 / (1.0 + jnp.exp(-gate_pre))
    act = gate_pre * sig
    slope = sig + act * (1.0 - sig)
    hidden = (act * up_pre).astype(BF16).astype(F32)
    each = width // groups
    column = lax.broadcasted_iota(jnp.int32, (1, width), 1)
    wide = scale[:, 0:1]
    for e in range(1, groups):
        wide = jnp.where(column >= e * each, scale[:, e : e + 1], wide)
    prod = hidden * grad_hidden
    for e in range(groups):
        part = prod
        if groups > 1:
            part = jnp.where((column >= e * each) & (column < (e + 1) * each), prod, 0.0)
        small_ref[:, e : e + 1] = jnp.sum(part, axis=1, keepdims=True)
    hid = (hidden * wide).astype(BF16)
    hid_ref[...] = hid
    scaled = grad_hidden * wide
    dgate = (scaled * up_pre * slope).astype(BF16)
    dup = (scaled * act).astype(BF16)
    dgu_ref[:, :width] = dgate
    dgu_ref[:, width:] = dup
    small_ref[:, groups : groups + 1] = jnp.sum(
        dgate.astype(F32) * gate_pre + dup.astype(F32) * up_pre, axis=1, keepdims=True
    )
    out = mm(hid, down_w[...])
    dx = back(dgate, gate_w[...]) + back(dup, up_w[...])
    if base:
        out = out + base_out[...].astype(F32)
        dx = dx + base_dx[...].astype(F32)
    out_ref[...] = out.astype(BF16)
    dx_ref[...] = dx.astype(BF16)


def ffn(rows, grads, scale, gate_w, up_w, down_w, start=0, total=0, base=(), into=(), flipped=False):
    count, groups = scale.shape
    width = rows.shape[1]
    hidden = down_w.shape[0]
    block = min(256, count)
    first = start // block
    total = total or count
    place = first if total > count else 0

    def at(n, offset):
        return pl.BlockSpec((block, n), lambda i: (i + offset, 0))

    def held(a):
        return pl.BlockSpec(a.shape, lambda i: (0, 0), pipeline_mode=pl.Buffered(1))

    far = pl.BlockSpec(memory_space=pl.ANY)
    return pl.pallas_call(
        functools.partial(ffn_kernel, groups, bool(base), bool(into), flipped),
        grid=(count // block,),
        in_specs=[at(width, first), at(width, first), at(groups, 0)]
        + [held(gate_w), held(up_w), held(down_w)]
        + [at(width, 0)] * len(base)
        + [far] * len(into),
        out_specs=[
            at(hidden, place),
            at(2 * hidden, place),
            at(width, 0),
            at(width, 0),
            at(groups + 1, 0),
        ],
        out_shape=[
            jax.ShapeDtypeStruct((total, hidden), BF16),
            jax.ShapeDtypeStruct((total, 2 * hidden), BF16),
            jax.ShapeDtypeStruct((count, width), BF16),
            jax.ShapeDtypeStruct((count, width), BF16),
            jax.ShapeDtypeStruct((count, groups + 1), F32),
        ],
        input_output_aliases={6 + len(base) + k: k for k in range(len(into))},
        compiler_params=pltpu.CompilerParams(vmem_limit_bytes=62 << 20),
        cost_estimate=pl.CostEstimate(flops=0, bytes_accessed=0, transcendentals=0),
    )(rows, grads, scale, gate_w, up_w, down_w, *base, *into)


def line_sum(rows, width_own, depth, prepare, settle, gathered, part, came, came_two, spread, sems):
    n = lax.axis_size("tp")
    me = lax.axis_index("tp")
    chunks, _, step, _ = part.shape
    sum_send, sum_recv, two_recv, out_send, out_recv = sems

    def send(source, target, send_sem, recv_sem, to):
        return pltpu.make_async_remote_copy(
            src_ref=source, dst_ref=target, send_sem=send_sem, recv_sem=recv_sem,
            device_id={"tp": to}, device_id_type=pl.DeviceIdType.MESH,
        )

    def sum_copy(c, s, to_right, two):
        target = came_two.at[c] if two else came.at[c, s]
        sem = two_recv.at[c] if two else sum_recv.at[c, s]
        return send(part.at[c, s], target, sum_send.at[c, s], sem, me + 1 if to_right else me - 1)

    def out_copy(c, s, to_right):
        return send(
            spread.at[c, s], spread.at[c, s], out_send.at[c, s, 1 if to_right else 0],
            out_recv.at[c, s], me + 1 if to_right else me - 1,
        )

    def within(c):
        return (c >= 0) & (c < chunks)

    def pass_sums(t):
        @pl.when(within(t))
        def _():
            prepare(t)

        for s in range(n):
            c = t - me * depth

            @pl.when((me < s) & within(c))
            def _(s=s, c=c):
                @pl.when(me > 0)
                def _():
                    sum_copy(c, s, True, False).wait_recv()
                    part[c, s] = (part[c, s].astype(F32) + came[c, s].astype(F32)).astype(BF16)

                sum_copy(c, s, True, False).start()

        for s in range(n):
            c = t - (n - 1 - me) * depth

            @pl.when((me > s) & within(c))
            def _(s=s, c=c):
                @pl.when(me < n - 1)
                def _():
                    sum_copy(c, s, False, False).wait_recv()
                    part[c, s] = (part[c, s].astype(F32) + came[c, s].astype(F32)).astype(BF16)

                @pl.when(me - 1 == s)
                def _():
                    sum_copy(c, s, False, True).start()

                @pl.when(me - 1 > s)
                def _():
                    sum_copy(c, s, False, False).start()

    def pass_own(t):
        c = t - (n - 1) * depth
        for s in range(n):

            @pl.when((me == s) & within(c))
            def _(s=s):
                if s > 0:
                    sum_copy(c, s, True, False).wait_recv()
                if s < n - 1:
                    sum_copy(c, s, False, True).wait_recv()
                total = part[c, s].astype(F32)
                if s > 0:
                    total = total + came[c, s].astype(F32)
                if s < n - 1:
                    total = total + came_two[c].astype(F32)
                spread[c, s] = settle(c, total)
                if s > 0:
                    out_copy(c, s, False).start()
                if s < n - 1:
                    out_copy(c, s, True).start()

    def pass_out(t):
        for s in range(n):
            right = t - (n - 1 + me - s) * depth
            left = t - (n - 1 + s - me) * depth

            @pl.when((me > s) & within(right))
            def _(s=s, c=right):
                out_copy(c, s, True).wait_recv()

                @pl.when(me < n - 1)
                def _():
                    out_copy(c, s, True).start()

            @pl.when((me < s) & within(left))
            def _(s=s, c=left):
                out_copy(c, s, False).wait_recv()

                @pl.when(me > 0)
                def _():
                    out_copy(c, s, False).start()

        last = t - 2 * (n - 1) * depth

        @pl.when(within(last))
        def _():
            gathered(last)

    def turn(t, carry):
        pass_sums(t)
        pass_own(t)
        pass_out(t)
        return carry

    lax.fori_loop(0, chunks + 2 * (n - 1) * depth, turn, 0)

    def drain(c, carry):
        for s in range(n):

            @pl.when(me != s)
            def _(s=s):
                sum_copy(c, s, True, False).wait_send()

            @pl.when((me < n - 1) & (s <= me))
            def _(s=s):
                out_copy(c, s, True).wait_send()

            @pl.when((me > 0) & (s >= me))
            def _(s=s):
                out_copy(c, s, False).wait_send()

        return carry

    lax.fori_loop(0, chunks, drain, 0)


def line_scratch(rows, width_own):
    n = lax.axis_size("tp")
    chunks = max(1, min(16, 128 // n))
    step = rows // chunks
    slots = pltpu.VMEM((chunks, n, step, width_own), BF16)
    dma = pltpu.SemaphoreType.DMA
    return chunks, step, [
        slots, slots, pltpu.VMEM((chunks, step, width_own), BF16), slots,
        dma((chunks, n)), dma((chunks, n)), dma((chunks,)), dma((chunks, n, 2)), dma((chunks, n)),
    ]


def greet(peers):
    n = lax.axis_size("tp")
    me = lax.axis_index("tp")
    barrier = pltpu.get_barrier_semaphore()

    def signal(where):
        pl.semaphore_signal(barrier, inc=1, device_id=where, device_id_type=pl.DeviceIdType.MESH)

    @pl.when(me > 0)
    def _():
        signal({"tp": me - 1})

    @pl.when(me < n - 1)
    def _():
        signal({"tp": me + 1})

    for where in peers:
        signal(where)

    beside = jnp.where(me > 0, 1, 0) + jnp.where(me < n - 1, 1, 0)
    pl.semaphore_wait(barrier, beside + len(peers))


def attend_out_kernel(
    chunks, step, depth, eps, attn, w_out, x, gain,
    mixed, resid_own, inv_out,
    part, came, came_two, spread, s0, s1, s2, s3, s4, y_send, y_recv,
):
    n = lax.axis_size("tp")
    me = lax.axis_index("tp")
    own = part.shape[3]
    rows = attn.shape[0]
    other = {"ep": 1 - lax.axis_index("ep")}
    greet([other])
    block = max(step, min(rows, 128))

    def product(b, carry):
        start = pl.multiple_of(b * block, block)
        value = mm(attn[pl.ds(start, block), :], w_out[...]).astype(BF16)
        for s in range(n):
            for k in range(block // step):
                part[b * (block // step) + k, s] = value[k * step:(k + 1) * step, s * own:(s + 1) * own]
        return carry

    lax.fori_loop(0, rows // block, product, 0)

    def at(c):
        return pl.ds(pl.multiple_of(c * step, step), step)

    def peer_copy(c):
        return pltpu.make_async_remote_copy(
            src_ref=mixed.at[at(c)], dst_ref=mixed.at[pl.ds(pl.multiple_of(rows + c * step, step), step)], send_sem=y_send.at[c], recv_sem=y_recv.at[c],
            device_id=other, device_id_type=pl.DeviceIdType.MESH,
        )

    def prepare(c):
        pass

    def settle(c, total):
        return total.astype(BF16)

    def gathered(c):
        resid = []
        square = jnp.zeros((step, 1), F32)
        for s in range(n):
            piece = x[at(c), s * own:(s + 1) * own].astype(F32) + spread[c, s].astype(F32)
            resid.append(piece)
            square = square + jnp.sum(piece * piece, axis=1, keepdims=True)
        inv = lax.rsqrt(square / (n * own) + eps)
        inv_out[at(c), :] = inv
        for s in range(n):
            mixed[at(c), s * own:(s + 1) * own] = (resid[s] * inv * gain[:, s * own:(s + 1) * own]).astype(BF16)

            @pl.when(me == s)
            def _(s=s):
                resid_own[at(c), :] = resid[s]

        peer_copy(c).start()

    line_sum(rows, own, depth, prepare, settle, gathered, part, came, came_two, spread, (s0, s1, s2, s3, s4))

    def last(c, carry):
        peer_copy(c).wait_recv()
        peer_copy(c).wait_send()
        return carry

    lax.fori_loop(0, chunks, last, 0)


def attend_out(attn, w_out, x, gain, width_own, depth=1):
    rows, width = x.shape
    chunks, step, scratch = line_scratch(rows, width_own)
    vmem = pl.BlockSpec(memory_space=pltpu.VMEM)
    dma = pltpu.SemaphoreType.DMA
    return pl.pallas_call(
        functools.partial(attend_out_kernel, chunks, step, depth, EPS),
        out_shape=[
            jax.ShapeDtypeStruct((2 * rows, width), BF16),
            jax.ShapeDtypeStruct((rows, width_own), F32), jax.ShapeDtypeStruct((rows, 1), F32),
        ],
        in_specs=[vmem] * 4,
        out_specs=[vmem] * 3,
        scratch_shapes=scratch + [dma((chunks,)), dma((chunks,))],
        compiler_params=pltpu.CompilerParams(collective_id=1, has_side_effects=True, vmem_limit_bytes=40 << 20),
        cost_estimate=pl.CostEstimate(flops=0, bytes_accessed=0, transcendentals=0),
    )(attn, w_out, x, gain)


def resid_grad_kernel(
    chunks, step, depth, grad, grad_p, out_p, sum_egu, sum_ed, router, along, g_own, resid_own, inv_two, gain,
    low, grad_resid, gain_grad, out_back, got_egu, got_ed,
    part, came, came_two, spread, s0, s1, s2, s3, s4, back, y_send, y_recv, o_send, o_recv,
    x_send, x_recv,
):
    n = lax.axis_size("tp")
    own = part.shape[3]
    rows = grad.shape[0]
    _, x_bit, _, (_, to_x, other) = places()

    def at(c):
        return pl.ds(pl.multiple_of(c * step, step), step)

    def peer_copy(c):
        return pltpu.make_async_remote_copy(
            src_ref=grad_p.at[at(c)], dst_ref=back.at[at(c)], send_sem=y_send.at[c], recv_sem=y_recv.at[c],
            device_id=other, device_id_type=pl.DeviceIdType.MESH,
        )

    def out_copy():
        return pltpu.make_async_remote_copy(
            src_ref=out_p, dst_ref=out_back, send_sem=o_send, recv_sem=o_recv,
            device_id=other, device_id_type=pl.DeviceIdType.MESH,
        )

    def half_copy(source, target, k):
        return pltpu.make_async_remote_copy(
            src_ref=source.at[pl.ds((1 - x_bit) * target.shape[0], target.shape[0])], dst_ref=target,
            send_sem=x_send.at[k], recv_sem=x_recv.at[k],
            device_id=to_x, device_id_type=pl.DeviceIdType.MESH,
        )

    greet([other, to_x])
    half_copy(sum_egu, got_egu, 0).start()
    half_copy(sum_ed, got_ed, 1).start()

    def begin(c, carry):
        peer_copy(c).start()
        return carry

    lax.fori_loop(0, chunks, begin, 0)
    out_copy().start()
    gain_grad[...] = jnp.zeros_like(gain_grad)

    def prepare(c):
        peer_copy(c).wait_recv()
        for s in range(n):
            columns = slice(s * own, (s + 1) * own)
            part[c, s] = (grad[at(c), columns].astype(F32) + back[at(c), columns].astype(F32)).astype(BF16)

    def settle(c, total):
        total = total + router[at(c), :]
        inv = inv_two[at(c), :]
        resid = resid_own[at(c), :]
        gain_grad[...] += jnp.sum(total * resid * inv, axis=0, keepdims=True)
        result = g_own[at(c), :].astype(F32) + inv * gain[...] * total - resid * (inv * inv * along[at(c), :] / (n * own))
        grad_resid[at(c), :] = result
        return result.astype(BF16)

    def gathered(c):
        for s in range(n):
            low[at(c), s * own:(s + 1) * own] = spread[c, s]

    line_sum(rows, own, depth, prepare, settle, gathered, part, came, came_two, spread, (s0, s1, s2, s3, s4))

    def last(c, carry):
        peer_copy(c).wait_send()
        return carry

    lax.fori_loop(0, chunks, last, 0)
    out_copy().wait()
    half_copy(sum_egu, got_egu, 0).wait()
    half_copy(sum_ed, got_ed, 1).wait()


def resid_grad(grad, grad_p, out_p, sum_egu, sum_ed, router, along, g_own, resid_own, inv_two, gain, depth=1):
    rows, width = grad.shape
    width_own = g_own.shape[1]
    chunks, step, scratch = line_scratch(rows, width_own)
    vmem = pl.BlockSpec(memory_space=pltpu.VMEM)
    far = pl.BlockSpec(memory_space=pl.ANY)
    dma = pltpu.SemaphoreType.DMA
    return pl.pallas_call(
        functools.partial(resid_grad_kernel, chunks, step, depth),
        out_shape=[
            jax.ShapeDtypeStruct((rows, width), BF16), jax.ShapeDtypeStruct((rows, width_own), F32),
            jax.ShapeDtypeStruct((1, width_own), F32), jax.ShapeDtypeStruct((rows, width), BF16),
        ]
        + [jax.ShapeDtypeStruct((v.shape[0] // 2, v.shape[1]), BF16) for v in (sum_egu, sum_ed)],
        in_specs=[vmem] + [far] * 4 + [vmem] * 6,
        out_specs=[vmem] * 3 + [far] * 3,
        scratch_shapes=scratch + [pltpu.VMEM((rows, width), BF16), dma((chunks,)), dma((chunks,)), dma, dma, dma((2,)), dma((2,))],
        compiler_params=pltpu.CompilerParams(collective_id=2, has_side_effects=True, vmem_limit_bytes=40 << 20),
        cost_estimate=pl.CostEstimate(flops=0, bytes_accessed=0, transcendentals=0),
    )(grad, grad_p, out_p, sum_egu, sum_ed, router, along, g_own, resid_own, inv_two, gain)


def body(
    tokens,
    norm_attn,
    w_query,
    w_key,
    w_value,
    w_output,
    norm_ffn,
    w_router,
    shared_switch,
    shared_gate,
    shared_up,
    shared_down,
    expert_gate,
    expert_up,
    expert_down,
    routes,
    segments,
    output_gradient,
):
    tp_count = lax.axis_size("tp")
    ep_count = lax.axis_size("ep")
    dp_count = lax.axis_size("dp")
    tp_rank = lax.axis_index("tp")
    ep_rank = lax.axis_index("ep")
    rows = tokens.shape[0]
    width_own = tokens.shape[1]
    width = width_own * tp_count
    heads = w_query.shape[1] // HD
    experts_own = expert_gate.shape[0]
    experts = experts_own * ep_count
    expert_width = expert_gate.shape[2]
    score_scale = 1.0 / math.sqrt(HD)
    far_bits = [1 << b for b in range(1, dp_count.bit_length() - 1)]

    def own_columns(value):
        return lax.dynamic_slice_in_dim(value, tp_rank * width_own, width_own, value.ndim - 1)

    near = bit_of("dp", 1)

    def pair_send(left, right, columns, used=None):
        return swap(weight_half(left, right, 1 - near, columns, rows=used), "dp", 1)

    def pair_keep(left, right, columns, got, used=None):
        return weight_half(left, right, near, columns, got, rows=used)

    core = ("dp", 1)
    far = [("dp", b) for b in far_bits]
    line = [("ep", 1)]
    x_link, y_link = far[0], line[0]

    def over_tp(value):
        bit = 1
        while bit < tp_count:
            value = value + swap(value, "tp", bit)
            bit *= 2
        return value

    def over_rows(value):
        for axis, bit in [core] + far + line:
            value = value + swap(value, axis, bit)
        return value

    packed = jnp.concatenate(
        [tokens, norm_attn[None, :], norm_ffn[None, :], jnp.zeros((14, width_own), BF16)], axis=0
    )
    packed = lax.all_gather(packed, "tp", axis=1, tiled=True)
    x_full = packed[:rows].astype(F32)
    gain_one = packed[rows].astype(F32)
    gain_two = packed[rows + 1].astype(F32)
    grad_rows = lax.all_gather(after(output_gradient, packed), "tp", axis=1, tiled=True)
    part = rows // 2
    grad_peer_a = swap(grad_rows[:part], "ep", 1)
    grad_peer_b = swap(grad_rows[part:], "ep", 1)
    route_hot = jnp.sum(
        (routes[:, :, None] == jnp.arange(experts, dtype=jnp.int32)[None, None, :]).astype(F32),
        axis=1,
    )
    route_hot_peer = swap(route_hot, "ep", 1)

    inv_one = lax.rsqrt(jnp.mean(x_full * x_full, axis=1, keepdims=True) + EPS)
    normed = (x_full * inv_one * gain_one).astype(BF16)
    q_pre = mm(normed, w_query)
    k_pre = mm(normed, w_key)
    v_pre = mm(normed, w_value)
    positions = ep_rank * rows + jnp.arange(rows, dtype=jnp.int32)
    cos_table, sin_table = rope_tables(positions, HD)
    query = rotate(q_pre.reshape(rows, heads, HD), cos_table, sin_table).astype(BF16)
    key_own = rotate(k_pre.reshape(rows, heads, HD), cos_table, sin_table).astype(BF16)
    value_own = v_pre.astype(BF16).reshape(rows, heads, HD)
    forth = [(i, i + 1) for i in range(ep_count - 1)]
    back = [(i + 1, i) for i in range(ep_count - 1)]
    earlier = lax.ppermute(jnp.stack([key_own, value_own]), "ep", forth)
    earlier = after(earlier, grad_rows)
    key_rows = jnp.concatenate([earlier[0], key_own], axis=0)
    value_rows = jnp.concatenate([earlier[1], value_own], axis=0)
    key_pos = (ep_rank - 1) * rows + jnp.arange(2 * rows, dtype=jnp.int32)
    seg_rows = segments.reshape(ep_count, rows)
    query_seg = lax.dynamic_index_in_dim(seg_rows, ep_rank, 0, keepdims=False)
    before_seg = lax.dynamic_index_in_dim(
        seg_rows, jnp.maximum(ep_rank - 1, 0), 0, keepdims=False
    )
    key_seg = jnp.concatenate([jnp.where(ep_rank > 0, before_seg, -1), query_seg])
    allowed = (query_seg[:, None] == key_seg[None, :]) & (key_pos[None, :] <= positions[:, None])

    def masked_scores():
        scores = (
            jnp.einsum("qhd,khd->hqk", query, key_rows, preferred_element_type=F32) * score_scale
        )
        return jnp.where(allowed[None], scores, NEG)

    scores = masked_scores()
    row_top = jnp.max(scores, axis=2, keepdims=True)
    shifted = jnp.exp(scores - row_top)
    row_total = jnp.sum(shifted, axis=2, keepdims=True)
    weights = (shifted / row_total).astype(BF16)
    attended = jnp.einsum("hqk,khd->qhd", weights, value_rows, preferred_element_type=F32)
    attn_rows = attended.astype(BF16).reshape(rows, heads * HD)
    log_norm = row_top + jnp.log(row_total)

    both, resid_own, inv_two = attend_out(
        attn_rows, w_output, after(packed[:rows], grad_peer_a), gain_two[None, :], width_own
    )
    mixed = both[:rows]

    def router(values):
        logits = mm(values, w_router)
        return logits, jax.nn.softmax(logits, axis=1)

    logits, router_prob = router(mixed)
    combine = router_prob * route_hot
    combine_peer = router(both[rows:])[1] * route_hot_peer
    switch_logit = mm(mixed, shared_switch[:, None])
    switch = jax.nn.sigmoid(switch_logit)

    def own_experts(value):
        return lax.dynamic_slice_in_dim(value, ep_rank * experts_own, experts_own, 1)

    hid_s, dgu_s, out_s, grad_s, small_s = ffn(
        both, grad_rows, switch, shared_gate, shared_up, shared_down
    )
    both_grad = jnp.concatenate([grad_rows, grad_peer_a, after(grad_peer_b, grad_s)], axis=0)
    got_sgu = pair_send(both, after(dgu_s, both_grad), False, rows)
    got_sd = pair_send(hid_s, after(grad_rows, got_sgu), True)
    sum_sgu = pair_keep(both, dgu_s, False, after(got_sgu, got_sd), rows)
    got_sgu = reduce_send(sum_sgu, *x_link)
    sum_sd = pair_keep(hid_s, after(grad_rows, sum_sgu), True, got_sd)
    got_sd = reduce_send(sum_sd, *y_link)

    hidden_width = experts_own * expert_width
    gate_w = jnp.transpose(expert_gate, (0, 2, 1)).reshape(hidden_width, width)
    up_w = jnp.transpose(expert_up, (0, 2, 1)).reshape(hidden_width, width)
    down_w = expert_down.reshape(hidden_width, width)
    hid_p, dgu_p, out_p, grad_p, small_p = ffn(
        both,
        after(both_grad, sum_sd),
        own_experts(combine_peer),
        gate_w,
        up_w,
        down_w,
        start=rows,
        total=2 * rows,
        flipped=True,
    )
    small_back = swap(small_p.T, "ep", 1)
    hid_e, dgu_e, out_e, grad_e, small_e = ffn(
        both,
        both_grad,
        after(own_experts(combine), grad_p),
        gate_w,
        up_w,
        down_w,
        total=2 * rows,
        base=(out_s, grad_s),
        into=(hid_p, dgu_p),
        flipped=True,
    )
    sum_sgu = reduce_add(sum_sgu, after(got_sgu, grad_e), *x_link)
    got_sgu = reduce_send(sum_sgu, *y_link)
    sum_sd = reduce_add(sum_sd, after(got_sd, sum_sgu), *y_link)
    got_sd = reduce_send(sum_sd, *x_link)

    first = ep_rank == 0
    small_e = small_e.T
    small_back = after(small_back, grad_e)
    dots_here, dots_there = small_e[:experts_own], small_back[:experts_own]
    small = jnp.concatenate(
        [
            jnp.where(first, dots_here, dots_there),
            jnp.where(first, dots_there, dots_here),
            small_s.T[:1],
            small_s.T[1:] + small_e[experts_own:] + small_back[experts_own:],
        ],
        axis=0,
    )
    got_small = swap(small, "tp", 1)
    got_egu = pair_send(after(dgu_e, sum_sd), both, True)
    small = small + after(got_small, got_egu)
    bit = 2
    got_ed = pair_send(hid_e, after(both_grad, small), True)
    sum_egu = dgu_e
    while bit < tp_count:
        got_small = swap(small, "tp", bit)
        if bit == 2:
            sum_egu = pair_keep(dgu_e, both, True, after(got_egu, got_ed))
        small = small + after(got_small, sum_egu)
        bit *= 2
    sum_ed = pair_keep(hid_e, after(both_grad, sum_egu), True, got_ed)
    small = after(small.T, sum_ed)
    grad_prob = small[:, :experts] * route_hot
    grad_switch = small[:, experts : experts + 1]
    along = small[:, experts + 1 : experts + 2]
    grad_logits = (
        router_prob * (grad_prob - jnp.sum(router_prob * grad_prob, axis=1, keepdims=True))
    ).astype(BF16)
    grad_slogit = (grad_switch * switch * (1.0 - switch)).astype(BF16)
    tp_rows = lax.dynamic_slice_in_dim(w_router, tp_rank * width_own, width_own, 0)
    router_part = (
        mm_nt(grad_logits, tp_rows)
        + grad_slogit.astype(F32) * own_columns(shared_switch).astype(F32)[None, :]
    )
    along = (
        along
        + jnp.sum(grad_logits.astype(F32) * logits, axis=1, keepdims=True)
        + grad_slogit.astype(F32) * switch_logit
    )
    sum_sgu = reduce_add(sum_sgu, after(got_sgu, sum_ed), *y_link)
    sum_sd = reduce_add(sum_sd, after(got_sd, sum_sgu), *x_link)
    resid_low, grad_resid, grad_gain_two, out_back, got_egu, got_ed = resid_grad(
        after(grad_e, sum_sd),
        grad_p,
        out_p,
        sum_egu,
        sum_ed,
        router_part,
        along,
        output_gradient,
        resid_own,
        inv_two,
        norm_ffn.astype(F32)[None, :],
    )

    grad_attn = mm_nt(resid_low, w_output).astype(BF16).reshape(rows, heads, HD)
    probs = jnp.exp(masked_scores() - log_norm)
    grad_probs = jnp.einsum("qhd,khd->hqk", grad_attn, value_rows, preferred_element_type=F32)
    grad_scores = (
        probs * (grad_probs - jnp.sum(probs * grad_probs, axis=2, keepdims=True))
    ).astype(BF16)
    grad_keys = (
        jnp.einsum("hqk,qhd->khd", grad_scores, query, preferred_element_type=F32) * score_scale
    )
    grad_values = jnp.einsum(
        "hqk,qhd->khd", probs.astype(BF16), grad_attn, preferred_element_type=F32
    )
    later = lax.ppermute(
        jnp.stack([grad_keys[:rows], grad_values[:rows]]).astype(BF16), "ep", back
    )
    grad_query = (
        jnp.einsum("hqk,khd->qhd", grad_scores, key_rows, preferred_element_type=F32) * score_scale
    )
    got_wo = pair_send(after(attn_rows, grad_keys, grad_values), resid_low, True)
    sum_egu = reduce_add(sum_egu, after(got_egu, got_wo), *x_link)
    sum_ed = reduce_add(sum_ed, after(got_ed, sum_egu), *x_link)
    sum_wo = pair_keep(after(attn_rows, sum_ed), resid_low, True, got_wo)
    grad_router = mm_tn(after(grad_logits, sum_wo), mixed)
    grad_switch_w = mm_tn(grad_slogit, mixed)
    flat = jnp.concatenate(
        [grad_gain_two.reshape(-1), grad_router.reshape(-1), grad_switch_w.reshape(-1)]
    ).reshape(-1, 128)
    ffn_part = (out_e.astype(F32) + after(out_back, sum_wo).astype(F32)).astype(BF16)
    ffn_own = lax.psum_scatter(ffn_part, "tp", scatter_dimension=1, tiled=True)
    later = after(later, sum_wo, ffn_part, flat).astype(F32)
    grad_key = grad_keys[rows:] + later[0]
    grad_value = grad_values[rows:] + later[1]
    shape = (rows, heads * HD)
    grad_qpre = rotate(grad_query, cos_table, -sin_table).astype(BF16).reshape(shape)
    grad_kpre = rotate(grad_key, cos_table, -sin_table).astype(BF16).reshape(shape)
    grad_vpre = grad_value.astype(BF16).reshape(shape)
    grad_qkv = jnp.concatenate([grad_qpre, grad_kpre, grad_vpre], axis=1)
    got_qkv = pair_send(normed, grad_qkv, False)
    grad_qkv = after(grad_qkv, got_qkv)
    sum_qkv = pair_keep(normed, grad_qkv, False, got_qkv)
    row_part = jnp.sum(
        grad_qpre.astype(F32) * q_pre
        + grad_kpre.astype(F32) * k_pre
        + grad_vpre.astype(F32) * v_pre,
        axis=1,
    )
    grad_normed = (
        mm_nt(after(grad_qpre, sum_qkv), w_query)
        + mm_nt(grad_kpre, w_key)
        + mm_nt(grad_vpre, w_value)
    ).astype(BF16)
    extra = max(1, rows // width_own)
    below = jnp.tile(row_part.reshape(extra, -1), (1, tp_count)).astype(BF16)
    below = jnp.pad(below, ((0, -extra % 16), (0, 0)))
    normed_own = lax.psum_scatter(
        jnp.concatenate([grad_normed, below], axis=0), "tp", scatter_dimension=1, tiled=True
    ).astype(F32)

    qkv = heads * HD
    inner = shared_gate.shape[1]
    sgu_f, sd_f, egu_f, ed_f, qkv_f, wo_f, flat = sums(
        sum_sgu, sum_sd, sum_egu, sum_ed, after(sum_qkv, grad_normed), sum_wo, flat
    )
    sg_grad, su_grad = widen(sgu_f, (inner, inner))
    (sd_grad,) = widen(sd_f)
    (eg_grad,) = widen(egu_f, kinds=2, kind=0)
    (eu_grad,) = widen(egu_f, kinds=2, kind=1)
    (ed_grad,) = widen(ed_f)
    wq_grad, wk_grad, wv_grad = widen(qkv_f, (qkv,) * 3)
    (wo_grad,) = widen(wo_f)

    x_own = tokens.astype(F32)
    normed_own = after(normed_own, flat)
    row_total = normed_own[rows : rows + extra].reshape(rows, 1)
    normed_own = normed_own[:rows]
    grad_tokens = (
        grad_resid
        + inv_one * norm_attn.astype(F32) * normed_own
        - x_own * (inv_one * inv_one) * (row_total / width)
    )
    grad_gain_one = jnp.sum(normed_own * x_own * inv_one, axis=0)
    grad_gain_one = over_rows(grad_gain_one.reshape(-1, 128)).reshape(-1)
    layer_out = (resid_own + after(ffn_own, flat).astype(F32)).astype(BF16)
    flat = flat.reshape(-1)
    grad_gain_two = flat[:width_own]
    grad_router = flat[width_own : width_own + width * experts].reshape(experts, width).T
    grad_switch_w = flat[width_own + width * experts :]

    def per_expert(value):
        return value.reshape(experts_own, expert_width, width)

    return (
        layer_out,
        grad_tokens,
        grad_gain_one,
        wq_grad,
        wk_grad,
        wv_grad,
        wo_grad,
        grad_gain_two,
        grad_router,
        grad_switch_w,
        sg_grad,
        su_grad,
        sd_grad,
        jnp.transpose(per_expert(eg_grad), (0, 2, 1)),
        jnp.transpose(per_expert(eu_grad), (0, 2, 1)),
        per_expert(ed_grad),
    )


def solution(mesh):
    placed = (
        P(("dp", "ep"), "tp"),
        P("tp"),
        P(None, "tp"),
        P(None, "tp"),
        P(None, "tp"),
        P("tp", None),
        P("tp"),
        P(),
        P(),
        P(None, "tp"),
        P(None, "tp"),
        P("tp", None),
        P("ep", None, "tp"),
        P("ep", None, "tp"),
        P("ep", "tp", None),
        P(("dp", "ep"), None),
        P("dp"),
        P(("dp", "ep"), "tp"),
    )
    return jax.shard_map(
        body,
        mesh=mesh,
        in_specs=placed,
        out_specs=(
            P(("dp", "ep"), "tp"),
            P(("dp", "ep"), "tp"),
            P("tp"),
            P(None, "tp"),
            P(None, "tp"),
            P(None, "tp"),
            P("tp", None),
            P("tp"),
            P(),
            P(),
            P(None, "tp"),
            P(None, "tp"),
            P("tp", None),
            P("ep", None, "tp"),
            P("ep", None, "tp"),
            P("ep", "tp", None),
        ),
        check_vma=False,
    )
```

```python
import functools
import math

import jax
import jax.numpy as jnp
from jax import lax
from jax.experimental import pallas as pl
from jax.experimental.pallas import tpu as pltpu
from jax.sharding import PartitionSpec as P

HD = 128
EPS = 1e-06
ROPE_BASE = 1000000.0
NEG = -1e30
F32 = jnp.float32
BF16 = jnp.bfloat16


def mm(left, right):
    return lax.dot_general(left, right, (((1,), (0,)), ((), ())), preferred_element_type=F32)


def mm_nt(left, right):
    return lax.dot_general(left, right, (((1,), (1,)), ((), ())), preferred_element_type=F32)


def mm_tn(left, right):
    return lax.dot_general(left, right, (((0,), (0,)), ((), ())), preferred_element_type=F32)


def swap(value, axis, bit):
    count = lax.axis_size(axis)
    return lax.ppermute(value, axis, [(i, i ^ bit) for i in range(count)])


def bit_of(axis, bit):
    return (lax.axis_index(axis) // bit) % 2


def half(value, which, dim):
    size = value.shape[dim] // 2
    return lax.dynamic_slice_in_dim(value, which * size, size, dim)


def after(value, *others):
    return lax.optimization_barrier((value, *others))[0]


def reduce_send(value, axis, bit):
    return swap(half(value, 1 - bit_of(axis, bit), 0), axis, bit)


def reduce_add(value, got, axis, bit):
    return (half(value, bit_of(axis, bit), 0).astype(F32) + got.astype(F32)).astype(BF16)


def places():
    count = lax.axis_size("dp")
    dp, ep = lax.axis_index("dp"), lax.axis_index("ep")
    core, x = dp % 2, dp // (count // 2)
    where = (
        {"dp": dp + 1 - 2 * core},
        {"dp": (dp + count // 2) % count},
        {"ep": 1 - ep},
    )
    return core, x, ep, where


def greet_all(peers):
    barrier = pltpu.get_barrier_semaphore()
    for where in peers:
        pl.semaphore_signal(
            barrier, inc=1, device_id=where, device_id_type=pl.DeviceIdType.MESH
        )
    pl.semaphore_wait(barrier, len(peers))


def add_rows(total, more, start, count, out=None):
    step = 32 if count % 32 == 0 else 16

    def turn(k, carry):
        here = pl.ds(pl.multiple_of(k * step, step), step)
        there = pl.ds(pl.multiple_of(start + k * step, step), step)
        value = (total[there, :].astype(F32) + more[here, :].astype(F32)).astype(BF16)
        if out is None:
            total[there, :] = value
        else:
            out[here, :] = value
        return carry

    lax.fori_loop(0, count // step, turn, 0)


def tail_kernel(
    scale,
    sgu, sd, egu, ed, flat, normed, w_query, w_key, w_value, attn,
    low, w_out, query, keys, values, lse, query_seg, key_seg, cos, sin,
    sgu_f, sd_f, egu_f, ed_f, qkv_f, wo_f, flat_f, grad_normed, row_part,
    normed_v, wq_v, wk_v, wv_v, attn_v, grad_attn, grad_key, grad_value, early, came, grad_qkv,
    q_sent, q_half, q_in, q_in2, q_out, w_sent, w_half, w_in, w_in2, w_out_v,
    e_own, e_in, d_own, d_in, flat_in, l_sem, s_sem, r_sem,
):
    core, x, y, (to_core, to_x, to_y) = places()
    used = [0, 0]
    sent = []

    def here(source, target):
        k = used[0]
        used[0] += 1
        copy = pltpu.make_async_copy(source, target, l_sem.at[k])
        copy.start()
        return copy

    def remote(source, target, where):
        k = used[1]
        used[1] += 1
        return pltpu.make_async_remote_copy(
            src_ref=source, dst_ref=target, send_sem=s_sem.at[k], recv_sem=r_sem.at[k],
            device_id=where, device_id_type=pl.DeviceIdType.MESH,
        )

    def there(source, target, where):
        copy = remote(source, target, where)
        copy.start()
        sent.append(copy)
        return copy

    rows = query.shape[0]
    heads = query.shape[1] // HD
    mine = heads * HD
    q_rows, w_rows = q_in.shape[0], w_in.shape[0]
    e_rows, d_rows = e_own.shape[0], d_own.shape[0]
    greet_all((to_core, to_x, to_y))

    b3 = there(egu.at[pl.ds((1 - x) * e_rows, e_rows)], e_in, to_x)
    b4 = there(ed.at[pl.ds((1 - x) * d_rows, d_rows)], d_in, to_x)
    f1 = there(flat, flat_in.at[0], to_core)
    load_attn = here(attn, attn_v)
    load_normed = here(normed, normed_v)
    loads = [here(w_query, wq_v), here(w_key, wk_v), here(w_value, wv_v)]
    load_e = here(egu.at[pl.ds(x * e_rows, e_rows)], e_own)
    load_d = here(ed.at[pl.ds(x * d_rows, d_rows)], d_own)
    own_s = here(sgu, sgu_f.at[core, y])
    own_sd = [here(sd.at[p], sd_f.at[core, p, y]) for p in range(2)]

    grad_attn[...] = mm_nt(low[...], w_out[...]).astype(BF16)
    key_at = (y - 1) * rows + lax.broadcasted_iota(jnp.int32, (1, 2 * rows), 1)
    query_at = y * rows + lax.broadcasted_iota(jnp.int32, (rows, 1), 0)
    allowed = (query_seg[...] == key_seg[...]) & (key_at <= query_at)
    sums_of = jnp.zeros((rows, 1), F32)
    early_copies = []
    for h in range(heads):
        own = slice(h * HD, (h + 1) * HD)
        q, k, v, g = query[:, own], keys[:, own], values[:, own], grad_attn[:, own]
        scores = jnp.where(allowed, mm_nt(q, k) * scale, NEG)
        probs = jnp.exp(scores - lse[:, h : h + 1])
        grad_probs = mm_nt(g, v)
        weighted = probs * grad_probs
        grad_scores = (weighted - probs * jnp.sum(weighted, axis=1, keepdims=True)).astype(BF16)
        grad_q = mm(grad_scores, k) * scale
        grad_k = mm_tn(grad_scores, q) * scale
        grad_v = mm_tn(probs.astype(BF16), g)
        grad_key[:, own] = grad_k[rows:]
        grad_value[:, own] = grad_v[rows:]
        early[h, 0] = grad_k[:rows].astype(BF16)
        early[h, 1] = grad_v[:rows].astype(BF16)
        copy = remote(early.at[h], came.at[h], to_y)
        early_copies.append(copy)

        @pl.when(y == 1)
        def _(copy=copy):
            copy.start()

        sums_of = sums_of + jnp.sum(grad_q * q.astype(F32), axis=1, keepdims=True)
        turned = grad_q * cos[...] + pltpu.roll(grad_q, HD // 2, 1) * sin[...]
        grad_qkv[:, own] = turned.astype(BF16)

    d1 = there(sgu.at[0], sgu_f.at[core, y, 0], to_y)
    load_attn.wait()
    half_of = low.shape[1] // 2
    w_sent[...] = mm_tn(attn_v[...], low[:, pl.ds(pl.multiple_of((1 - core) * half_of, half_of), half_of)]).astype(BF16)
    a0 = there(w_sent, w_half, to_core)
    w_own = mm_tn(attn_v[...], low[:, pl.ds(pl.multiple_of(core * half_of, half_of), half_of)])
    f1.wait_recv()
    flat_f[...] = flat[...] + flat_in[0]
    f2 = there(flat_f, flat_in.at[1], to_x)
    a0.wait_recv()
    w_half[...] = (w_own + w_half[...].astype(F32)).astype(BF16)
    a2 = there(w_half.at[pl.ds((1 - y) * w_rows, w_rows)], w_in, to_y)

    for h in range(heads):
        own = slice(h * HD, (h + 1) * HD)

        @pl.when(y == 0)
        def _(h=h, own=own):
            early_copies[h].wait_recv()
            grad_key[:, own] = grad_key[:, own] + came[h, 0].astype(F32)
            grad_value[:, own] = grad_value[:, own] + came[h, 1].astype(F32)

        @pl.when(y == 1)
        def _(h=h):
            early_copies[h].wait_send()

        grad_k, grad_v = grad_key[:, own], grad_value[:, own]
        sums_of = sums_of + jnp.sum(
            grad_k * keys[rows:, own].astype(F32) + grad_v * values[rows:, own].astype(F32),
            axis=1, keepdims=True,
        )
        turned = grad_k * cos[...] + pltpu.roll(grad_k, HD // 2, 1) * sin[...]
        grad_qkv[:, mine + h * HD : mine + (h + 1) * HD] = turned.astype(BF16)
        grad_qkv[:, 2 * mine + h * HD : 2 * mine + (h + 1) * HD] = grad_v.astype(BF16)
    row_part[...] = sums_of

    load_normed.wait()
    tall = q_half.shape[0]
    step = tall // 4

    def product(i, which):
        start = pl.multiple_of(which * tall + i * step, step)
        return mm_tn(normed_v[:, pl.ds(start, step)], grad_qkv[...])

    a0q = []
    for i in range(4):
        q_sent[i * step : (i + 1) * step, :] = product(i, 1 - core).astype(BF16)
        a0q.append(there(q_sent.at[pl.ds(i * step, step)], q_half.at[pl.ds(i * step, step)], to_core))
    for i in range(4):
        value = product(i, core)
        a0q[i].wait_recv()
        here_rows = slice(i * step, (i + 1) * step)
        q_half[here_rows, :] = (value + q_half[here_rows, :].astype(F32)).astype(BF16)
    a1 = there(q_half.at[pl.ds((1 - y) * q_rows, q_rows)], q_in, to_y)
    d2 = there(sgu.at[1], sgu_f.at[core, y, 1], to_y)
    for copy in loads:
        copy.wait()
    grad_normed[...] = (
        mm_nt(grad_qkv[:, :mine], wq_v[...])
        + mm_nt(grad_qkv[:, mine : 2 * mine], wk_v[...])
        + mm_nt(grad_qkv[:, 2 * mine :], wv_v[...])
    ).astype(BF16)

    load_e.wait()
    b3.wait_recv()
    add_rows(e_own, e_in, 0, e_rows)
    f2.wait_recv()
    f2.wait_send()
    flat_f[...] = flat_f[...] + flat_in[1]
    f3 = there(flat_f, flat_in.at[2], to_y)
    a2.wait_recv()
    add_rows(w_half, w_in, y * w_rows, w_rows)
    a4 = there(w_half.at[pl.ds(y * w_rows + (1 - x) * (w_rows // 2), w_rows // 2)], w_in2, to_x)
    load_d.wait()
    b4.wait_recv()
    add_rows(d_own, d_in, 0, d_rows)
    a1.wait_recv()
    add_rows(q_half, q_in, y * q_rows, q_rows)
    a3 = there(q_half.at[pl.ds(y * q_rows + (1 - x) * (q_rows // 2), q_rows // 2)], q_in2, to_x)
    cut = e_rows // 2
    b5 = there(e_own.at[pl.ds(0, cut)], egu_f.at[core, x, pl.ds(0, cut)], to_x)
    own_e = here(e_own, egu_f.at[core, x])
    own_ed = here(d_own, ed_f.at[core, x])
    d3 = [there(sd.at[p], sd_f.at[core, p, y], to_y) for p in range(2)]
    a4.wait_recv()
    add_rows(w_half, w_in2, y * w_rows + x * (w_rows // 2), w_rows // 2, w_out_v)
    a6 = there(w_out_v, wo_f.at[core, y, x], to_x)
    own_w = here(w_out_v, wo_f.at[core, y, x])
    a3.wait_recv()
    add_rows(q_half, q_in2, y * q_rows + x * (q_rows // 2), q_rows // 2, q_out)
    a5 = there(q_out, qkv_f.at[core, y, x], to_x)
    own_q = here(q_out, qkv_f.at[core, y, x])
    b7 = there(e_own.at[pl.ds(cut, cut)], egu_f.at[core, x, pl.ds(cut, cut)], to_x)
    b6 = there(d_own, ed_f.at[core, x], to_x)
    own_s.wait()
    d1.wait_recv()
    d2.wait_recv()
    c1 = there(sgu_f.at[core], sgu_f.at[core], to_core)
    a6.wait_recv()
    own_w.wait()
    a8 = there(wo_f.at[core, y], wo_f.at[core, y], to_y)
    a5.wait_recv()
    own_q.wait()
    a7 = there(qkv_f.at[core, y], qkv_f.at[core, y], to_y)
    for copy in own_sd:
        copy.wait()
    for copy in d3:
        copy.wait_recv()
    c2 = there(sd_f.at[core], sd_f.at[core], to_core)
    f3.wait_recv()
    f3.wait_send()
    flat_f[...] = flat_f[...] + flat_in[2]
    own_e.wait()
    b5.wait_recv()
    b7.wait_recv()
    c3 = there(egu_f.at[core], egu_f.at[core], to_core)
    a8.wait_recv()
    c5 = there(wo_f.at[core], wo_f.at[core], to_core)
    a7.wait_recv()
    c4 = there(qkv_f.at[core], qkv_f.at[core], to_core)
    own_ed.wait()
    b6.wait_recv()
    c6 = there(ed_f.at[core], ed_f.at[core], to_core)
    for copy in (c1, c2, c3, c4, c5, c6):
        copy.wait_recv()
    for copy in sent:
        if copy is not f2 and copy is not f3:
            copy.wait_send()


def tail(sgu, sd, egu, ed, flat, normed, w_query, w_key, w_value, attn, low, w_out, query, keys, values, lse, query_seg, key_seg, cos, sin):
    rows, width = low.shape
    mine = query.shape[1]
    heads = mine // HD

    def pieces(count, height, wide):
        return jax.ShapeDtypeStruct((2,) * count + (height, wide), BF16)

    far = pl.BlockSpec(memory_space=pl.ANY)
    vmem = pl.BlockSpec(memory_space=pltpu.VMEM)

    def room(*shape, kind=BF16):
        return pltpu.VMEM(shape, kind)

    half_of = width // 2
    dma = pltpu.SemaphoreType.DMA
    return pl.pallas_call(
        functools.partial(tail_kernel, 1.0 / math.sqrt(HD)),
        out_shape=[
            pieces(3, *sgu.shape[1:]), pieces(3, *sd.shape[1:]),
            pieces(2, egu.shape[0] // 2, egu.shape[1]), pieces(2, ed.shape[0] // 2, ed.shape[1]),
            pieces(3, half_of // 4, 3 * mine), pieces(3, mine // 4, half_of),
            jax.ShapeDtypeStruct(flat.shape, F32), jax.ShapeDtypeStruct((rows, width), BF16),
            jax.ShapeDtypeStruct((rows, 1), F32),
        ],
        in_specs=[far] * 4 + [vmem] + [far] * 5 + [vmem] * 10,
        out_specs=[far] * 6 + [vmem] * 3,
        scratch_shapes=[
            room(rows, width), room(width, mine), room(width, mine), room(width, mine), room(rows, mine),
            room(rows, mine), room(rows, mine, kind=F32), room(rows, mine, kind=F32),
            room(heads, 2, rows, HD), room(heads, 2, rows, HD), room(rows, 3 * mine),
            room(half_of, 3 * mine), room(half_of, 3 * mine), room(half_of // 2, 3 * mine),
            room(half_of // 4, 3 * mine), room(half_of // 4, 3 * mine),
            room(mine, half_of), room(mine, half_of), room(mine // 2, half_of),
            room(mine // 4, half_of), room(mine // 4, half_of),
            room(egu.shape[0] // 2, egu.shape[1]), room(egu.shape[0] // 2, egu.shape[1]),
            room(ed.shape[0] // 2, ed.shape[1]), room(ed.shape[0] // 2, ed.shape[1]),
            room(3, *flat.shape, kind=F32), dma((16,)), dma((40,)), dma((40,)),
        ],
        compiler_params=pltpu.CompilerParams(
            collective_id=3, has_side_effects=True, vmem_limit_bytes=62 << 20
        ),
        cost_estimate=pl.CostEstimate(flops=0, bytes_accessed=0, transcendentals=0),
    )(sgu, sd, egu, ed, flat, normed, w_query, w_key, w_value, attn, low, w_out, query, keys, values, lse, query_seg, key_seg, cos, sin)


def widen_kernel(source, *outputs):
    value = source[...]
    value = value.reshape(value.shape[-2:])
    start = 0
    for out in outputs:
        width = out.shape[1]
        out[...] = value[:, start : start + width].astype(F32)
        start += width


def widen(value, widths=(), kinds=1, kind=0):
    columns = value.shape[-1]
    if widths:
        value = value.reshape(-1, columns)
        rows = value.shape[0]
        step = min(rows, 256)
        source = pl.BlockSpec((step, columns), lambda i: (i, 0))
        grid = (rows // step,)
        specs = [pl.BlockSpec((step, width), lambda i: (i, 0)) for width in widths]
        shapes = [jax.ShapeDtypeStruct((rows, width), F32) for width in widths]
    else:
        value = value.reshape(2, kinds, -1, columns)
        rows = value.shape[2]
        step = rows
        while step * columns > (1 << 19) and step % 32 == 0:
            step //= 2
        steps = rows // step
        source = pl.BlockSpec((1, 1, step, columns), lambda i, c: (c, kind, i, 0))
        grid = (steps, 2)
        specs = [pl.BlockSpec((step, columns), lambda i, c: (i, c))]
        shapes = [jax.ShapeDtypeStruct((rows, 2 * columns), F32)]
    return pl.pallas_call(
        widen_kernel,
        grid=grid,
        in_specs=[source],
        out_specs=specs,
        out_shape=shapes,
        compiler_params=pltpu.CompilerParams(vmem_limit_bytes=32 << 20),
        cost_estimate=pl.CostEstimate(flops=0, bytes_accessed=0, transcendentals=0),
    )(value)


def weight_kernel(added, part, left, right, *refs):
    total = mm_tn(left[...], right[...])
    if added:
        total = total + refs[0][...].astype(F32)
    refs[-1][...] = total.astype(BF16)


def weight_half(left, right, which, columns, got=None, rows=None, block=1408):
    rows = rows or left.shape[0]
    height, wide = left.shape[1], right.shape[1]
    if columns:
        wide = wide // 2
    else:
        height = height // 2
    step = height
    while step > block and step % 256 == 0:
        step //= 2
    steps = height // step
    extra = [] if got is None else [got]
    out_spec = pl.BlockSpec((step, wide), lambda i, part: (i, 0))
    if columns:
        left_at, right_at = (lambda i, part: (0, i)), (lambda i, part: (0, part[0]))
    else:
        left_at, right_at = (lambda i, part: (0, part[0] * steps + i)), (lambda i, part: (0, 0))
    return pl.pallas_call(
        functools.partial(weight_kernel, bool(extra)),
        grid_spec=pltpu.PrefetchScalarGridSpec(
            num_scalar_prefetch=1,
            grid=(steps,),
            in_specs=[pl.BlockSpec((rows, step), left_at), pl.BlockSpec((rows, wide), right_at)]
            + [out_spec] * len(extra),
            out_specs=out_spec,
        ),
        out_shape=jax.ShapeDtypeStruct((height, wide), BF16),
        compiler_params=pltpu.CompilerParams(vmem_limit_bytes=48 << 20),
        cost_estimate=pl.CostEstimate(flops=0, bytes_accessed=0, transcendentals=0),
    )(which.reshape(1).astype(jnp.int32), left, right, *extra)


def rope_tables(positions, feat_width):
    half_width = feat_width // 2
    inv_freq = ROPE_BASE ** (-(jnp.arange(half_width, dtype=F32) * 2.0) / feat_width)
    angles = positions.astype(F32)[:, None] * inv_freq[None, :]
    return (jnp.cos(angles), jnp.sin(angles))


def rotate(tensor, cos_table, sin_table):
    half_width = tensor.shape[-1] // 2
    first_half = tensor[..., :half_width]
    second_half = tensor[..., half_width:]
    cos_b = cos_table[:, None, :]
    sin_b = sin_table[:, None, :]
    return jnp.concatenate(
        [first_half * cos_b - second_half * sin_b, second_half * cos_b + first_half * sin_b],
        axis=-1,
    )


def ffn_kernel(groups, base, into, flipped, carry, *refs):
    rows, grads, scale, gate_w, up_w, down_w = refs[:6]
    refs = refs[6:]
    if base:
        base_out, base_dx = refs[:2]
        refs = refs[2:]
    if into:
        refs = refs[2:]
    sources, refs = refs[: len(carry)], refs[len(carry) :]
    hid_ref, dgu_ref, out_ref, dx_ref, small_ref, *refs = refs
    copies = []
    if carry:
        send_sem, recv_sem = refs[-2:]
        _, x, y, where = places()
        for m, (link, count, start, stride) in enumerate(carry):
            first = start + (1 - (x, y)[link - 1]) * stride
            copies.append(
                pltpu.make_async_remote_copy(
                    src_ref=sources[m].at[pl.ds(first, count)], dst_ref=refs[m],
                    send_sem=send_sem.at[m], recv_sem=recv_sem.at[m],
                    device_id=where[link], device_id_type=pl.DeviceIdType.MESH,
                )
            )
        links = sorted({link for link, _, _, _ in carry})

        @pl.when(pl.program_id(0) == 0)
        def _():
            greet_all([where[link] for link in links])
            for copy in copies:
                copy.start()

    width = down_w.shape[0]
    to, back = (mm_nt, mm) if flipped else (mm, mm_nt)
    gate_pre = to(rows[...], gate_w[...])
    up_pre = to(rows[...], up_w[...])
    grad_hidden = mm_nt(grads[...], down_w[...])
    sig = 1.0 / (1.0 + jnp.exp(-gate_pre))
    act = gate_pre * sig
    slope = sig + act * (1.0 - sig)
    hidden = (act * up_pre).astype(BF16).astype(F32)
    each = width // groups
    column = lax.broadcasted_iota(jnp.int32, (1, width), 1)
    wide = scale[:, 0:1]
    for e in range(1, groups):
        wide = jnp.where(column >= e * each, scale[:, e : e + 1], wide)
    prod = hidden * grad_hidden
    for e in range(groups):
        part = prod
        if groups > 1:
            part = jnp.where((column >= e * each) & (column < (e + 1) * each), prod, 0.0)
        small_ref[:, e : e + 1] = jnp.sum(part, axis=1, keepdims=True)
    hid = (hidden * wide).astype(BF16)
    hid_ref[...] = hid
    scaled = grad_hidden * wide
    dgate = (scaled * up_pre * slope).astype(BF16)
    dup = (scaled * act).astype(BF16)
    dgu_ref[:, :width] = dgate
    dgu_ref[:, width:] = dup
    small_ref[:, groups : groups + 1] = jnp.sum(
        dgate.astype(F32) * gate_pre + dup.astype(F32) * up_pre, axis=1, keepdims=True
    )
    out = mm(hid, down_w[...])
    dx = back(dgate, gate_w[...]) + back(dup, up_w[...])
    if base:
        out = out + base_out[...].astype(F32)
        dx = dx + base_dx[...].astype(F32)
    out_ref[...] = out.astype(BF16)
    dx_ref[...] = dx.astype(BF16)
    if carry:

        @pl.when(pl.program_id(0) == pl.num_programs(0) - 1)
        def _():
            for copy in copies:
                copy.wait()


def ffn(rows, grads, scale, gate_w, up_w, down_w, start=0, total=0, base=(), into=(), flipped=False, carry=(), number=None):
    count, groups = scale.shape
    width = rows.shape[1]
    hidden = down_w.shape[0]
    block = min(256, count)
    first = start // block
    total = total or count
    place = first if total > count else 0

    def at(n, offset):
        return pl.BlockSpec((block, n), lambda i: (i + offset, 0))

    def held(a):
        return pl.BlockSpec(a.shape, lambda i: (0, 0), pipeline_mode=pl.Buffered(1))

    far = pl.BlockSpec(memory_space=pl.ANY)
    return pl.pallas_call(
        functools.partial(
            ffn_kernel, groups, bool(base), bool(into), flipped, tuple(c[1:] for c in carry)
        ),
        grid=(count // block,),
        in_specs=[at(width, first), at(width, first), at(groups, 0)]
        + [held(gate_w), held(up_w), held(down_w)]
        + [at(width, 0)] * len(base)
        + [far] * (len(into) + len(carry)),
        out_specs=[
            at(hidden, place),
            at(2 * hidden, place),
            at(width, 0),
            at(width, 0),
            at(groups + 1, 0),
        ]
        + [far] * len(carry),
        out_shape=[
            jax.ShapeDtypeStruct((total, hidden), BF16),
            jax.ShapeDtypeStruct((total, 2 * hidden), BF16),
            jax.ShapeDtypeStruct((count, width), BF16),
            jax.ShapeDtypeStruct((count, width), BF16),
            jax.ShapeDtypeStruct((count, groups + 1), F32),
        ]
        + [jax.ShapeDtypeStruct((c[2], c[0].shape[1]), BF16) for c in carry],
        scratch_shapes=[pltpu.SemaphoreType.DMA((len(carry),))] * 2 if carry else [],
        input_output_aliases={6 + len(base) + k: k for k in range(len(into))},
        compiler_params=pltpu.CompilerParams(
            vmem_limit_bytes=62 << 20, collective_id=number, has_side_effects=bool(carry)
        ),
        cost_estimate=pl.CostEstimate(flops=0, bytes_accessed=0, transcendentals=0),
    )(rows, grads, scale, gate_w, up_w, down_w, *base, *into, *[c[0] for c in carry])


def line_sum(depth, prepare, settle, gathered, beside, part, came, came_two, spread, sems):
    n = lax.axis_size("tp")
    me = lax.axis_index("tp")
    chunks, _, step, _ = part.shape
    sum_send, sum_recv, two_recv, out_send, out_recv = sems

    def send(source, target, send_sem, recv_sem, to):
        return pltpu.make_async_remote_copy(
            src_ref=source, dst_ref=target, send_sem=send_sem, recv_sem=recv_sem,
            device_id={"tp": to}, device_id_type=pl.DeviceIdType.MESH,
        )

    def sum_copy(c, s, to_right, two):
        target = came_two.at[c] if two else came.at[c, s]
        sem = two_recv.at[c] if two else sum_recv.at[c, s]
        return send(part.at[c, s], target, sum_send.at[c, s], sem, me + 1 if to_right else me - 1)

    def out_copy(c, s, to_right):
        return send(
            spread.at[c, s], spread.at[c, s], out_send.at[c, s, 1 if to_right else 0],
            out_recv.at[c, s], me + 1 if to_right else me - 1,
        )

    def within(c):
        return (c >= 0) & (c < chunks)

    def pass_sums(t):
        @pl.when(within(t))
        def _():
            prepare(t)

        for s in range(n):
            c = t - me * depth

            @pl.when((me < s) & within(c))
            def _(s=s, c=c):
                @pl.when(me > 0)
                def _():
                    sum_copy(c, s, True, False).wait_recv()
                    part[c, s] = (part[c, s].astype(F32) + came[c, s].astype(F32)).astype(BF16)

                sum_copy(c, s, True, False).start()

        for s in range(n):
            c = t - (n - 1 - me) * depth

            @pl.when((me > s) & within(c))
            def _(s=s, c=c):
                @pl.when(me < n - 1)
                def _():
                    sum_copy(c, s, False, False).wait_recv()
                    part[c, s] = (part[c, s].astype(F32) + came[c, s].astype(F32)).astype(BF16)

                @pl.when(me - 1 == s)
                def _():
                    sum_copy(c, s, False, True).start()

                @pl.when(me - 1 > s)
                def _():
                    sum_copy(c, s, False, False).start()

    def pass_own(t):
        c = t - (n - 1) * depth
        for s in range(n):

            @pl.when((me == s) & within(c))
            def _(s=s):
                if s > 0:
                    sum_copy(c, s, True, False).wait_recv()
                if s < n - 1:
                    sum_copy(c, s, False, True).wait_recv()
                total = part[c, s].astype(F32)
                if s > 0:
                    total = total + came[c, s].astype(F32)
                if s < n - 1:
                    total = total + came_two[c].astype(F32)
                spread[c, s] = settle(c, total)
                if s > 0:
                    out_copy(c, s, False).start()
                if s < n - 1:
                    out_copy(c, s, True).start()

    def pass_out(t):
        for s in range(n):
            right = t - (n - 1 + me - s) * depth
            left = t - (n - 1 + s - me) * depth

            @pl.when((me > s) & within(right))
            def _(s=s, c=right):
                out_copy(c, s, True).wait_recv()

                @pl.when(me < n - 1)
                def _():
                    out_copy(c, s, True).start()

            @pl.when((me < s) & within(left))
            def _(s=s, c=left):
                out_copy(c, s, False).wait_recv()

                @pl.when(me > 0)
                def _():
                    out_copy(c, s, False).start()

        last = t - 2 * (n - 1) * depth

        @pl.when(within(last))
        def _():
            gathered(last)

    def turn(t, carry):
        pass_sums(t)
        pass_own(t)
        pass_out(t)
        if beside is not None:
            beside(t)
        return carry

    lax.fori_loop(0, chunks + 2 * (n - 1) * depth, turn, 0)

    def drain(c, carry):
        for s in range(n):

            @pl.when(me != s)
            def _(s=s):
                sum_copy(c, s, True, False).wait_send()

            @pl.when((me < n - 1) & (s <= me))
            def _(s=s):
                out_copy(c, s, True).wait_send()

            @pl.when((me > 0) & (s >= me))
            def _(s=s):
                out_copy(c, s, False).wait_send()

        return carry

    lax.fori_loop(0, chunks, drain, 0)


def line_scratch(rows, width_own):
    n = lax.axis_size("tp")
    chunks = max(1, min(16, 128 // n))
    step = rows // chunks
    slots = pltpu.VMEM((chunks, n, step, width_own), BF16)
    dma = pltpu.SemaphoreType.DMA
    return chunks, step, [
        slots, slots, pltpu.VMEM((chunks, step, width_own), BF16), slots,
        dma((chunks, n)), dma((chunks, n)), dma((chunks,)), dma((chunks, n, 2)), dma((chunks, n)),
    ]


def greet(peers):
    n = lax.axis_size("tp")
    me = lax.axis_index("tp")
    barrier = pltpu.get_barrier_semaphore()

    def signal(where):
        pl.semaphore_signal(barrier, inc=1, device_id=where, device_id_type=pl.DeviceIdType.MESH)

    @pl.when(me > 0)
    def _():
        signal({"tp": me - 1})

    @pl.when(me < n - 1)
    def _():
        signal({"tp": me + 1})

    for where in peers:
        signal(where)

    beside = jnp.where(me > 0, 1, 0) + jnp.where(me < n - 1, 1, 0)
    pl.semaphore_wait(barrier, beside + len(peers))


def attend_out_kernel(
    chunks, step, depth, eps, attn, w_out, x, gain, grads,
    mixed, resid_own, inv_out, grads_peer,
    part, came, came_two, spread, s0, s1, s2, s3, s4, y_send, y_recv, g_send, g_recv,
):
    n = lax.axis_size("tp")
    me = lax.axis_index("tp")
    own = part.shape[3]
    rows = attn.shape[0]
    other = {"ep": 1 - lax.axis_index("ep")}
    greet([other])
    grads_copy = pltpu.make_async_remote_copy(
        src_ref=grads.at[pl.ds(0, grads_peer.shape[0])], dst_ref=grads_peer, send_sem=g_send, recv_sem=g_recv,
        device_id=other, device_id_type=pl.DeviceIdType.MESH,
    )
    grads_copy.start()
    block = max(step, min(rows, 128))

    def product(b, carry):
        start = pl.multiple_of(b * block, block)
        value = mm(attn[pl.ds(start, block), :], w_out[...]).astype(BF16)
        for s in range(n):
            for k in range(block // step):
                part[b * (block // step) + k, s] = value[k * step:(k + 1) * step, s * own:(s + 1) * own]
        return carry

    lax.fori_loop(0, rows // block, product, 0)

    def at(c):
        return pl.ds(pl.multiple_of(c * step, step), step)

    def peer_copy(c):
        return pltpu.make_async_remote_copy(
            src_ref=mixed.at[at(c)], dst_ref=mixed.at[pl.ds(pl.multiple_of(rows + c * step, step), step)], send_sem=y_send.at[c], recv_sem=y_recv.at[c],
            device_id=other, device_id_type=pl.DeviceIdType.MESH,
        )

    def prepare(c):
        pass

    def settle(c, total):
        return total.astype(BF16)

    def gathered(c):
        resid = []
        square = jnp.zeros((step, 1), F32)
        for s in range(n):
            piece = x[at(c), s * own:(s + 1) * own].astype(F32) + spread[c, s].astype(F32)
            resid.append(piece)
            square = square + jnp.sum(piece * piece, axis=1, keepdims=True)
        inv = lax.rsqrt(square / (n * own) + eps)
        inv_out[at(c), :] = inv
        for s in range(n):
            mixed[at(c), s * own:(s + 1) * own] = (resid[s] * inv * gain[:, s * own:(s + 1) * own]).astype(BF16)

            @pl.when(me == s)
            def _(s=s):
                resid_own[at(c), :] = resid[s]

        peer_copy(c).start()

    line_sum(depth, prepare, settle, gathered, None, part, came, came_two, spread, (s0, s1, s2, s3, s4))

    def last(c, carry):
        peer_copy(c).wait_recv()
        peer_copy(c).wait_send()
        return carry

    lax.fori_loop(0, chunks, last, 0)
    grads_copy.wait()


def attend_out(attn, w_out, x, gain, grads, width_own, depth=1):
    rows, width = x.shape
    chunks, step, scratch = line_scratch(rows, width_own)
    vmem = pl.BlockSpec(memory_space=pltpu.VMEM)
    far = pl.BlockSpec(memory_space=pl.ANY)
    dma = pltpu.SemaphoreType.DMA
    return pl.pallas_call(
        functools.partial(attend_out_kernel, chunks, step, depth, EPS),
        out_shape=[
            jax.ShapeDtypeStruct((2 * rows, width), BF16),
            jax.ShapeDtypeStruct((rows, width_own), F32), jax.ShapeDtypeStruct((rows, 1), F32),
            jax.ShapeDtypeStruct((rows // 2, width), BF16),
        ],
        in_specs=[vmem] * 4 + [far],
        out_specs=[vmem] * 3 + [far],
        scratch_shapes=scratch + [dma((chunks,)), dma((chunks,)), dma, dma],
        compiler_params=pltpu.CompilerParams(collective_id=1, has_side_effects=True, vmem_limit_bytes=40 << 20),
        cost_estimate=pl.CostEstimate(flops=0, bytes_accessed=0, transcendentals=0),
    )(attn, w_out, x, gain, grads)


def resid_grad_kernel(
    chunks, step, depth, tiles, grad, grad_p, out_p, dgu, hid, both, both_grad, sgu, sd, router, along, g_own, resid_own, inv_two, gain,
    low, grad_resid, gain_grad, out_back, sum_egu, sum_ed, sgu_x, sd_x,
    part, came, came_two, spread, s0, s1, s2, s3, s4, back, y_send, y_recv, o_send, o_recv,
    dgu_v, hid_v, both_v, both_grad_v, sent_egu, sent_ed, came_egu, came_ed,
    s_own, s_in, d_own, d_in, l_sem, w_send, w_recv, w_out, r_send, r_recv, r_out,
):
    n = lax.axis_size("tp")
    own = part.shape[3]
    rows = grad.shape[0]
    core, x, y, (to_core, to_x, other) = places()

    def at(c):
        return pl.ds(pl.multiple_of(c * step, step), step)

    def peer_copy(c):
        return pltpu.make_async_remote_copy(
            src_ref=grad_p.at[at(c)], dst_ref=back.at[at(c)], send_sem=y_send.at[c], recv_sem=y_recv.at[c],
            device_id=other, device_id_type=pl.DeviceIdType.MESH,
        )

    def out_copy():
        return pltpu.make_async_remote_copy(
            src_ref=out_p, dst_ref=out_back, send_sem=o_send, recv_sem=o_recv,
            device_id=other, device_id_type=pl.DeviceIdType.MESH,
        )

    loads = [
        pltpu.make_async_copy(source, target, l_sem.at[m])
        for m, (source, target) in enumerate(
            (
                (dgu, dgu_v),
                (both, both_v),
                (hid, hid_v),
                (both_grad, both_grad_v),
                (sgu.at[pl.ds(x * s_own.shape[0], s_own.shape[0])], s_own),
                (sd.at[pl.ds(y * d_own.shape[0], d_own.shape[0])], d_own),
            )
        )
    ]
    kinds = ((dgu_v, both_v, sent_egu, came_egu, sum_egu), (hid_v, both_grad_v, sent_ed, came_ed, sum_ed))

    def sum_copies(m):
        source, target, where = (
            (sgu.at[pl.ds((1 - x) * s_own.shape[0], s_own.shape[0])], s_in, to_x),
            (sd.at[pl.ds((1 - y) * d_own.shape[0], d_own.shape[0])], d_in, other),
            (s_own, sgu_x.at[x], to_x),
            (d_own, sd_x.at[x], to_x),
        )[m]
        return pltpu.make_async_remote_copy(
            src_ref=source, dst_ref=target, send_sem=r_send.at[m], recv_sem=r_recv.at[m],
            device_id=where, device_id_type=pl.DeviceIdType.MESH,
        )

    def own_out(m):
        return pltpu.make_async_copy((s_own, d_own)[m], (sgu_x, sd_x)[m].at[x], r_out.at[m])

    def shared(m):
        sum_copies(m).wait_recv()
        add_rows((s_own, d_own)[m], (s_in, d_in)[m], 0, (s_own, d_own)[m].shape[0])
        sum_copies(2 + m).start()
        own_out(m).start()

    def tile_copy(m, b):
        return pltpu.make_async_remote_copy(
            src_ref=kinds[m][2].at[b], dst_ref=kinds[m][3].at[b], send_sem=w_send.at[b, m], recv_sem=w_recv.at[b, m],
            device_id=to_core, device_id_type=pl.DeviceIdType.MESH,
        )

    def tile_out(m, b):
        tall = kinds[m][3].shape[1]
        return pltpu.make_async_copy(
            kinds[m][3].at[b], kinds[m][4].at[pl.ds(pl.multiple_of(b * tall, tall), tall)], w_out.at[b, m]
        )

    def tile(m, b, which):
        left, right = kinds[m][:2]
        tall, wide = kinds[m][3].shape[1:]
        return mm_tn(
            left[...] if tiles == 1 else left[:, pl.ds(pl.multiple_of(b * tall, tall), tall)],
            right[:, pl.ds(pl.multiple_of(which * wide, wide), wide)],
        )

    def weights(t):
        @pl.when(t == 0)
        def _():
            for copy in loads:
                copy.wait()

        @pl.when(t < tiles)
        def _():
            for m in range(2):
                kinds[m][2][t] = tile(m, t, 1 - core).astype(BF16)
                tile_copy(m, t).start()

        @pl.when(t == tiles)
        def _():
            shared(0)

        @pl.when(t == tiles + tiles // 2 + 1)
        def _():
            shared(1)

        @pl.when((t >= tiles) & (t < 2 * tiles))
        def _():
            b = t - tiles
            for m in range(2):
                value = tile(m, b, core)
                tile_copy(m, b).wait_recv()
                kinds[m][3][b] = (value + kinds[m][3][b].astype(F32)).astype(BF16)
                tile_out(m, b).start()

    for copy in loads:
        copy.start()
    greet([other, to_core, to_x])
    sum_copies(0).start()

    def begin(c, carry):
        peer_copy(c).start()
        return carry

    lax.fori_loop(0, chunks, begin, 0)
    sum_copies(1).start()
    out_copy().start()
    gain_grad[...] = jnp.zeros_like(gain_grad)

    def prepare(c):
        peer_copy(c).wait_recv()
        for s in range(n):
            columns = slice(s * own, (s + 1) * own)
            part[c, s] = (grad[at(c), columns].astype(F32) + back[at(c), columns].astype(F32)).astype(BF16)

    def settle(c, total):
        total = total + router[at(c), :]
        inv = inv_two[at(c), :]
        resid = resid_own[at(c), :]
        gain_grad[...] += jnp.sum(total * resid * inv, axis=0, keepdims=True)
        result = g_own[at(c), :].astype(F32) + inv * gain[...] * total - resid * (inv * inv * along[at(c), :] / (n * own))
        grad_resid[at(c), :] = result
        return result.astype(BF16)

    def gathered(c):
        for s in range(n):
            low[at(c), s * own:(s + 1) * own] = spread[c, s]

    line_sum(depth, prepare, settle, gathered, weights, part, came, came_two, spread, (s0, s1, s2, s3, s4))

    def last(c, carry):
        peer_copy(c).wait_send()
        return carry

    lax.fori_loop(0, chunks, last, 0)
    out_copy().wait()

    def done(b, carry):
        for m in range(2):
            tile_copy(m, b).wait_send()
            tile_out(m, b).wait()
        return carry

    lax.fori_loop(0, tiles, done, 0)
    for m in range(2):
        sum_copies(m).wait_send()
        sum_copies(2 + m).wait()
        own_out(m).wait()


def resid_grad(grad, grad_p, out_p, dgu, hid, both, both_grad, sgu, sd, router, along, g_own, resid_own, inv_two, gain, depth=1):
    rows, width = grad.shape
    width_own = g_own.shape[1]
    chunks, step, scratch = line_scratch(rows, width_own)
    hidden = hid.shape[1]
    tiles = 11 if hidden % (11 * 128) == 0 else 1
    vmem = pl.BlockSpec(memory_space=pltpu.VMEM)
    far = pl.BlockSpec(memory_space=pl.ANY)
    dma = pltpu.SemaphoreType.DMA
    return pl.pallas_call(
        functools.partial(resid_grad_kernel, chunks, step, depth, tiles),
        out_shape=[
            jax.ShapeDtypeStruct((rows, width), BF16), jax.ShapeDtypeStruct((rows, width_own), F32),
            jax.ShapeDtypeStruct((1, width_own), F32), jax.ShapeDtypeStruct((rows, width), BF16),
        ]
        + [jax.ShapeDtypeStruct((k * hidden, width // 2), BF16) for k in (2, 1)]
        + [jax.ShapeDtypeStruct((2, v.shape[0] // 2, v.shape[1]), BF16) for v in (sgu, sd)],
        in_specs=[vmem] + [far] * 8 + [vmem] * 6,
        out_specs=[vmem] * 3 + [far] * 5,
        scratch_shapes=scratch + [pltpu.VMEM((rows, width), BF16), dma((chunks,)), dma((chunks,)), dma, dma]
        + [pltpu.VMEM(v.shape, BF16) for v in (dgu, hid, both, both_grad)]
        + [pltpu.VMEM((tiles, k * hidden // tiles, width // 2), BF16) for k in (2, 1, 2, 1)]
        + [pltpu.VMEM((v.shape[0] // 2, v.shape[1]), BF16) for v in (sgu, sgu, sd, sd)]
        + [dma((6,)), dma((tiles, 2)), dma((tiles, 2)), dma((tiles, 2)), dma((4,)), dma((4,)), dma((2,))],
        compiler_params=pltpu.CompilerParams(collective_id=2, has_side_effects=True, vmem_limit_bytes=63 << 20),
        cost_estimate=pl.CostEstimate(flops=0, bytes_accessed=0, transcendentals=0),
    )(grad, grad_p, out_p, dgu, hid, both, both_grad, sgu, sd, router, along, g_own, resid_own, inv_two, gain)


def body(
    tokens,
    norm_attn,
    w_query,
    w_key,
    w_value,
    w_output,
    norm_ffn,
    w_router,
    shared_switch,
    shared_gate,
    shared_up,
    shared_down,
    expert_gate,
    expert_up,
    expert_down,
    routes,
    segments,
    output_gradient,
):
    tp_count = lax.axis_size("tp")
    ep_count = lax.axis_size("ep")
    dp_count = lax.axis_size("dp")
    tp_rank = lax.axis_index("tp")
    ep_rank = lax.axis_index("ep")
    rows = tokens.shape[0]
    width_own = tokens.shape[1]
    width = width_own * tp_count
    heads = w_query.shape[1] // HD
    experts_own = expert_gate.shape[0]
    experts = experts_own * ep_count
    expert_width = expert_gate.shape[2]
    score_scale = 1.0 / math.sqrt(HD)
    far_bits = [1 << b for b in range(1, dp_count.bit_length() - 1)]

    def own_columns(value):
        return lax.dynamic_slice_in_dim(value, tp_rank * width_own, width_own, value.ndim - 1)

    near = bit_of("dp", 1)

    def pair_send(left, right, columns, used=None):
        sent = weight_half(left, right, 1 - near, columns, rows=used)
        return sent, swap(sent, "dp", 1)

    def pair_keep(left, right, columns, got, used=None):
        return weight_half(left, right, near, columns, got, rows=used)

    core = ("dp", 1)
    far = [("dp", b) for b in far_bits]
    line = [("ep", 1)]
    x_link, y_link = far[0], line[0]

    def over_tp(value):
        if tp_count <= 4:
            others = [
                lax.ppermute(value, "tp", [(i, (i + d) % tp_count) for i in range(tp_count)])
                for d in range(1, tp_count)
            ]
            return sum(others, value)
        bit = 1
        while bit < tp_count:
            value = value + swap(value, "tp", bit)
            bit *= 2
        return value

    def over_rows(value):
        for axis, bit in [core] + far + line:
            value = value + swap(value, axis, bit)
        return value

    packed = jnp.concatenate(
        [tokens, norm_attn[None, :], norm_ffn[None, :], jnp.zeros((14, width_own), BF16)], axis=0
    )
    packed = lax.all_gather(packed, "tp", axis=1, tiled=True)
    x_full = packed[:rows].astype(F32)
    gain_one = packed[rows].astype(F32)
    gain_two = packed[rows + 1].astype(F32)
    grad_rows = lax.all_gather(after(output_gradient, packed), "tp", axis=1, tiled=True)
    route_hot = jnp.sum(
        (routes[:, :, None] == jnp.arange(experts, dtype=jnp.int32)[None, None, :]).astype(F32),
        axis=1,
    )
    route_hot_peer = swap(route_hot, "ep", 1)

    inv_one = lax.rsqrt(jnp.mean(x_full * x_full, axis=1, keepdims=True) + EPS)
    normed = (x_full * inv_one * gain_one).astype(BF16)
    q_pre = mm(normed, w_query)
    k_pre = mm(normed, w_key)
    v_pre = mm(normed, w_value)
    positions = ep_rank * rows + jnp.arange(rows, dtype=jnp.int32)
    cos_table, sin_table = rope_tables(positions, HD)
    query = rotate(q_pre.reshape(rows, heads, HD), cos_table, sin_table).astype(BF16)
    key_own = rotate(k_pre.reshape(rows, heads, HD), cos_table, sin_table).astype(BF16)
    value_own = v_pre.astype(BF16).reshape(rows, heads, HD)
    forth = [(i, i + 1) for i in range(ep_count - 1)]
    back = [(i + 1, i) for i in range(ep_count - 1)]
    earlier = lax.ppermute(jnp.stack([key_own, value_own]), "ep", forth)
    earlier = after(earlier, grad_rows)
    key_rows = jnp.concatenate([earlier[0], key_own], axis=0)
    value_rows = jnp.concatenate([earlier[1], value_own], axis=0)
    key_pos = (ep_rank - 1) * rows + jnp.arange(2 * rows, dtype=jnp.int32)
    seg_rows = segments.reshape(ep_count, rows)
    query_seg = lax.dynamic_index_in_dim(seg_rows, ep_rank, 0, keepdims=False)
    before_seg = lax.dynamic_index_in_dim(
        seg_rows, jnp.maximum(ep_rank - 1, 0), 0, keepdims=False
    )
    key_seg = jnp.concatenate([jnp.where(ep_rank > 0, before_seg, -1), query_seg])
    allowed = (query_seg[:, None] == key_seg[None, :]) & (key_pos[None, :] <= positions[:, None])

    def masked_scores():
        scores = (
            jnp.einsum("qhd,khd->hqk", query, key_rows, preferred_element_type=F32) * score_scale
        )
        return jnp.where(allowed[None], scores, NEG)

    scores = masked_scores()
    row_top = jnp.max(scores, axis=2, keepdims=True)
    shifted = jnp.exp(scores - row_top)
    row_total = jnp.sum(shifted, axis=2, keepdims=True)
    weights = (shifted / row_total).astype(BF16)
    attended = jnp.einsum("hqk,khd->qhd", weights, value_rows, preferred_element_type=F32)
    attn_rows = attended.astype(BF16).reshape(rows, heads * HD)
    log_norm = row_top + jnp.log(row_total)

    both, resid_own, inv_two, grad_peer_a = attend_out(
        attn_rows, w_output, packed[:rows], gain_two[None, :], grad_rows, width_own
    )
    mixed = both[:rows]

    def router(values):
        logits = mm(values, w_router)
        return logits, jax.nn.softmax(logits, axis=1)

    logits, router_prob = router(mixed)
    combine = router_prob * route_hot
    combine_peer = router(both[rows:])[1] * route_hot_peer
    switch_logit = mm(mixed, shared_switch[:, None])
    switch = jax.nn.sigmoid(switch_logit)

    def own_experts(value):
        return lax.dynamic_slice_in_dim(value, ep_rank * experts_own, experts_own, 1)

    hid_s, dgu_s, out_s, grad_s, small_s, grad_peer_b = ffn(
        both,
        grad_rows,
        switch,
        shared_gate,
        shared_up,
        shared_down,
        carry=[(grad_rows, 2, rows // 2, rows // 2, 0)],
        number=4,
    )
    both_grad = jnp.concatenate([grad_rows, grad_peer_a, grad_peer_b], axis=0)
    sent, got_sgu = pair_send(both, dgu_s, False, rows)
    sent, got_sd = pair_send(hid_s, after(grad_rows, sent), True)
    sum_sgu = pair_keep(both, after(dgu_s, sent, both_grad), False, got_sgu, rows)
    sum_sd = pair_keep(hid_s, after(grad_rows, sum_sgu), True, got_sd)
    quarter = sum_sgu.shape[0] // 4

    hidden_width = experts_own * expert_width
    gate_w = jnp.transpose(expert_gate, (0, 2, 1)).reshape(hidden_width, width)
    up_w = jnp.transpose(expert_up, (0, 2, 1)).reshape(hidden_width, width)
    down_w = expert_down.reshape(hidden_width, width)
    hid_p, dgu_p, out_p, grad_p, small_p, got_sgu_a, got_sd = ffn(
        both,
        after(both_grad, sum_sd),
        own_experts(combine_peer),
        gate_w,
        up_w,
        down_w,
        start=rows,
        total=2 * rows,
        flipped=True,
        carry=[
            (sum_sgu, 2, quarter, 0, 2 * quarter),
            (sum_sd, 1, sum_sd.shape[0] // 2, 0, sum_sd.shape[0] // 2),
        ],
        number=5,
    )
    small_back = swap(small_p.T, "ep", 1)
    hid_e, dgu_e, out_e, grad_e, small_e, got_sgu_b = ffn(
        both,
        both_grad,
        after(own_experts(combine), grad_p),
        gate_w,
        up_w,
        down_w,
        total=2 * rows,
        base=(out_s, grad_s),
        into=(hid_p, dgu_p),
        flipped=True,
        carry=[(sum_sgu, 2, quarter, quarter, 2 * quarter)],
        number=6,
    )
    got_sgu = jnp.concatenate([got_sgu_a, got_sgu_b], axis=0)

    first = ep_rank == 0
    small_e = small_e.T
    small_back = after(small_back, grad_e)
    dots_here, dots_there = small_e[:experts_own], small_back[:experts_own]
    small = jnp.concatenate(
        [
            jnp.where(first, dots_here, dots_there),
            jnp.where(first, dots_there, dots_here),
            small_s.T[:1],
            small_s.T[1:] + small_e[experts_own:] + small_back[experts_own:],
        ],
        axis=0,
    )
    small = over_tp(small).T
    grad_prob = small[:, :experts] * route_hot
    grad_switch = small[:, experts : experts + 1]
    along = small[:, experts + 1 : experts + 2]
    grad_logits = (
        router_prob * (grad_prob - jnp.sum(router_prob * grad_prob, axis=1, keepdims=True))
    ).astype(BF16)
    grad_slogit = (grad_switch * switch * (1.0 - switch)).astype(BF16)
    tp_rows = lax.dynamic_slice_in_dim(w_router, tp_rank * width_own, width_own, 0)
    router_part = (
        mm_nt(grad_logits, tp_rows)
        + grad_slogit.astype(F32) * own_columns(shared_switch).astype(F32)[None, :]
    )
    along = (
        along
        + jnp.sum(grad_logits.astype(F32) * logits, axis=1, keepdims=True)
        + grad_slogit.astype(F32) * switch_logit
    )
    grad_router = mm_tn(grad_logits, mixed)
    grad_switch_w = mm_tn(grad_slogit, mixed)
    sum_sgu = reduce_add(sum_sgu, got_sgu, *y_link)
    sum_sd = reduce_add(sum_sd, got_sd, *x_link)

    resid_low, grad_resid, grad_gain_two, out_back, sum_egu, sum_ed, sgu_x, sd_x = resid_grad(
        grad_e,
        grad_p,
        out_p,
        dgu_e,
        hid_e,
        both,
        both_grad,
        sum_sgu,
        sum_sd,
        router_part,
        along,
        output_gradient,
        resid_own,
        inv_two,
        norm_ffn.astype(F32)[None, :],
    )

    flat = jnp.concatenate(
        [grad_gain_two.reshape(-1), grad_router.reshape(-1), grad_switch_w.reshape(-1)]
    ).reshape(-1, 128)
    qkv = heads * HD
    inner = shared_gate.shape[1]
    ffn_part = (out_e.astype(F32) + out_back.astype(F32)).astype(BF16)
    ffn_own = lax.psum_scatter(
        ffn_part, "tp", scatter_dimension=1, tiled=True
    )
    flat = after(flat, ffn_part)
    sgu_f, sd_f, egu_f, ed_f, qkv_f, wo_f, flat, grad_normed, row_part = tail(
        sgu_x,
        sd_x,
        sum_egu,
        sum_ed,
        flat,
        normed,
        w_query,
        w_key,
        w_value,
        attn_rows,
        resid_low,
        w_output,
        query.reshape(rows, qkv),
        key_rows.reshape(2 * rows, qkv),
        value_rows.reshape(2 * rows, qkv),
        log_norm[:, :, 0].T,
        query_seg[:, None],
        key_seg[None, :],
        jnp.concatenate([cos_table, cos_table], axis=1),
        jnp.concatenate([sin_table, -sin_table], axis=1),
    )

    extra = max(1, rows // width_own)
    below = jnp.tile(row_part.reshape(extra, -1), (1, tp_count)).astype(BF16)
    below = jnp.pad(below, ((0, -extra % 16), (0, 0)))
    normed_own = lax.psum_scatter(
        jnp.concatenate([grad_normed, below], axis=0), "tp", scatter_dimension=1, tiled=True
    ).astype(F32)

    sg_grad, su_grad = widen(sgu_f, (inner, inner))
    (sd_grad,) = widen(sd_f)
    (eg_grad,) = widen(egu_f, kinds=2, kind=0)
    (eu_grad,) = widen(egu_f, kinds=2, kind=1)
    (ed_grad,) = widen(ed_f)
    wq_grad, wk_grad, wv_grad = widen(qkv_f, (qkv,) * 3)
    (wo_grad,) = widen(wo_f)

    x_own = tokens.astype(F32)
    normed_own = after(normed_own, sg_grad, sd_grad, eg_grad, eu_grad, ed_grad)
    row_total = normed_own[rows : rows + extra].reshape(rows, 1)
    normed_own = normed_own[:rows]
    grad_tokens = (
        grad_resid
        + inv_one * norm_attn.astype(F32) * normed_own
        - x_own * (inv_one * inv_one) * (row_total / width)
    )
    grad_gain_one = jnp.sum(normed_own * x_own * inv_one, axis=0)
    grad_gain_one = over_rows(grad_gain_one.reshape(-1, 128)).reshape(-1)
    layer_out = (resid_own + after(ffn_own, flat).astype(F32)).astype(BF16)
    flat = flat.reshape(-1)
    grad_gain_two = flat[:width_own]
    grad_router = flat[width_own : width_own + width * experts].reshape(experts, width).T
    grad_switch_w = flat[width_own + width * experts :]

    def per_expert(value):
        return value.reshape(experts_own, expert_width, width)

    return (
        layer_out,
        grad_tokens,
        grad_gain_one,
        wq_grad,
        wk_grad,
        wv_grad,
        wo_grad,
        grad_gain_two,
        grad_router,
        grad_switch_w,
        sg_grad,
        su_grad,
        sd_grad,
        jnp.transpose(per_expert(eg_grad), (0, 2, 1)),
        jnp.transpose(per_expert(eu_grad), (0, 2, 1)),
        per_expert(ed_grad),
    )


def solution(mesh):
    placed = (
        P(("dp", "ep"), "tp"),
        P("tp"),
        P(None, "tp"),
        P(None, "tp"),
        P(None, "tp"),
        P("tp", None),
        P("tp"),
        P(),
        P(),
        P(None, "tp"),
        P(None, "tp"),
        P("tp", None),
        P("ep", None, "tp"),
        P("ep", None, "tp"),
        P("ep", "tp", None),
        P(("dp", "ep"), None),
        P("dp"),
        P(("dp", "ep"), "tp"),
    )
    return jax.shard_map(
        body,
        mesh=mesh,
        in_specs=placed,
        out_specs=(
            P(("dp", "ep"), "tp"),
            P(("dp", "ep"), "tp"),
            P("tp"),
            P(None, "tp"),
            P(None, "tp"),
            P(None, "tp"),
            P("tp", None),
            P("tp"),
            P(),
            P(),
            P(None, "tp"),
            P(None, "tp"),
            P("tp", None),
            P("ep", None, "tp"),
            P("ep", None, "tp"),
            P("ep", "tp", None),
        ),
        check_vma=False,
    )
```

```python
import functools
import math

import jax
import jax.numpy as jnp
from jax import lax
from jax.experimental import pallas as pl
from jax.experimental.pallas import tpu as pltpu
from jax.sharding import PartitionSpec as P

HD = 128
EPS = 1e-06
ROPE_BASE = 1000000.0
NEG = -1e30
F32 = jnp.float32
BF16 = jnp.bfloat16


def mm(left, right):
    return lax.dot_general(left, right, (((1,), (0,)), ((), ())), preferred_element_type=F32)


def mm_nt(left, right):
    return lax.dot_general(left, right, (((1,), (1,)), ((), ())), preferred_element_type=F32)


def mm_tn(left, right):
    return lax.dot_general(left, right, (((0,), (0,)), ((), ())), preferred_element_type=F32)


def swap(value, axis, bit):
    count = lax.axis_size(axis)
    return lax.ppermute(value, axis, [(i, i ^ bit) for i in range(count)])


def bit_of(axis, bit):
    return (lax.axis_index(axis) // bit) % 2


def half(value, which, dim):
    size = value.shape[dim] // 2
    return lax.dynamic_slice_in_dim(value, which * size, size, dim)


def after(value, *others):
    return lax.optimization_barrier((value, *others))[0]


def reduce_send(value, axis, bit):
    return swap(half(value, 1 - bit_of(axis, bit), 0), axis, bit)


def reduce_add(value, got, axis, bit):
    return (half(value, bit_of(axis, bit), 0).astype(F32) + got.astype(F32)).astype(BF16)


def places():
    count = lax.axis_size("dp")
    dp, ep = lax.axis_index("dp"), lax.axis_index("ep")
    core, x = dp % 2, dp // (count // 2)
    where = (
        {"dp": dp + 1 - 2 * core},
        {"dp": (dp + count // 2) % count},
        {"ep": 1 - ep},
    )
    return core, x, ep, where


def greet_all(peers):
    barrier = pltpu.get_barrier_semaphore()
    for where in peers:
        pl.semaphore_signal(
            barrier, inc=1, device_id=where, device_id_type=pl.DeviceIdType.MESH
        )
    pl.semaphore_wait(barrier, len(peers))


def add_rows(total, more, start, count, out=None):
    step = 32 if count % 32 == 0 else 16

    def turn(k, carry):
        here = pl.ds(pl.multiple_of(k * step, step), step)
        there = pl.ds(pl.multiple_of(start + k * step, step), step)
        value = (total[there, :].astype(F32) + more[here, :].astype(F32)).astype(BF16)
        if out is None:
            total[there, :] = value
        else:
            out[here, :] = value
        return carry

    lax.fori_loop(0, count // step, turn, 0)


def tail_kernel(
    scale,
    sgu, sd, egu, ed, flat, normed, w_query, w_key, w_value, attn, ffn,
    tokens, inv_one, low, w_out, query, keys, values, lse, query_seg, key_seg, cos, sin,
    sgu_f, sd_f, egu_f, ed_f, qkv_f, wo_f, flat_f, ffn_own, normed_own, row_total, gain_f,
    normed_v, wq_v, wk_v, wv_v, attn_v, grad_attn, grad_key, grad_value, early, came, grad_qkv,
    q_sent, q_half, q_in, q_in2, q_out, w_sent, w_half, w_in, w_in2, w_out_v,
    e_own, e_in, flat_in, ffn_in, grad_normed, normed_in, row_in, gain_in, l_sem, s_sem, r_sem,
):
    core, x, y, (to_core, to_x, to_y) = places()
    used = [0, 0]
    sent = []

    def here(source, target):
        k = used[0]
        used[0] += 1
        copy = pltpu.make_async_copy(source, target, l_sem.at[k])
        copy.start()
        return copy

    def remote(source, target, where):
        k = used[1]
        used[1] += 1
        return pltpu.make_async_remote_copy(
            src_ref=source, dst_ref=target, send_sem=s_sem.at[k], recv_sem=r_sem.at[k],
            device_id=where, device_id_type=pl.DeviceIdType.MESH,
        )

    def there(source, target, where):
        copy = remote(source, target, where)
        copy.start()
        sent.append(copy)
        return copy

    rows = query.shape[0]
    heads = query.shape[1] // HD
    mine = heads * HD
    q_rows, w_rows = q_in.shape[0], w_in.shape[0]
    e_rows = e_own.shape[0]
    n, me = lax.axis_size("tp"), lax.axis_index("tp")
    tp = [{"tp": (me + d) % n} for d in range(1, n)]
    own_width = ffn_own.shape[1]

    def columns(d):
        return pl.ds(pl.multiple_of(((me + d) % n) * own_width, own_width), own_width)

    greet_all([to_core, to_x, to_y] + tp)

    b3 = there(egu.at[pl.ds((1 - x) * e_rows, e_rows)], e_in, to_x)
    b6 = there(ed, ed_f.at[core, x], to_x)
    f1 = there(flat, flat_in.at[0], to_core)
    z_ffn = [there(ffn.at[:, columns(d)], ffn_in.at[d], tp[d - 1]) for d in range(1, n)]
    own_ffn = here(ffn.at[:, columns(0)], ffn_in.at[0])
    load_attn = here(attn, attn_v)
    load_normed = here(normed, normed_v)
    loads = [here(w_query, wq_v), here(w_key, wk_v), here(w_value, wv_v)]
    load_e = here(egu.at[pl.ds(x * e_rows, e_rows)], e_own)
    own_ed = here(ed, ed_f.at[core, x])
    own_s = here(sgu, sgu_f.at[core, y])
    own_sd = [here(sd.at[p], sd_f.at[core, p, y]) for p in range(2)]

    grad_attn[...] = mm_nt(low[...], w_out[...]).astype(BF16)
    key_at = (y - 1) * rows + lax.broadcasted_iota(jnp.int32, (1, 2 * rows), 1)
    query_at = y * rows + lax.broadcasted_iota(jnp.int32, (rows, 1), 0)
    allowed = (query_seg[...] == key_seg[...]) & (key_at <= query_at)
    sums_of = jnp.zeros((rows, 1), F32)
    early_copies = []
    for h in range(heads):
        own = slice(h * HD, (h + 1) * HD)
        q, k, v, g = query[:, own], keys[:, own], values[:, own], grad_attn[:, own]
        scores = jnp.where(allowed, mm_nt(q, k) * scale, NEG)
        probs = jnp.exp(scores - lse[:, h : h + 1])
        grad_probs = mm_nt(g, v)
        weighted = probs * grad_probs
        grad_scores = (weighted - probs * jnp.sum(weighted, axis=1, keepdims=True)).astype(BF16)
        grad_q = mm(grad_scores, k) * scale
        grad_k = mm_tn(grad_scores, q) * scale
        grad_v = mm_tn(probs.astype(BF16), g)
        grad_key[:, own] = grad_k[rows:]
        grad_value[:, own] = grad_v[rows:]
        early[h, 0] = grad_k[:rows].astype(BF16)
        early[h, 1] = grad_v[:rows].astype(BF16)
        copy = remote(early.at[h], came.at[h], to_y)
        early_copies.append(copy)

        @pl.when(y == 1)
        def _(copy=copy):
            copy.start()

        sums_of = sums_of + jnp.sum(grad_q * q.astype(F32), axis=1, keepdims=True)
        turned = grad_q * cos[...] + pltpu.roll(grad_q, HD // 2, 1) * sin[...]
        grad_qkv[:, own] = turned.astype(BF16)

    d1 = there(sgu.at[0], sgu_f.at[core, y, 0], to_y)
    load_attn.wait()
    half_of = low.shape[1] // 2
    w_sent[...] = mm_tn(attn_v[...], low[:, pl.ds(pl.multiple_of((1 - core) * half_of, half_of), half_of)]).astype(BF16)
    a0 = there(w_sent, w_half, to_core)
    w_own = mm_tn(attn_v[...], low[:, pl.ds(pl.multiple_of(core * half_of, half_of), half_of)])
    f1.wait_recv()
    flat_f[...] = flat[...] + flat_in[0]
    f2 = there(flat_f, flat_in.at[1], to_x)
    a0.wait_recv()
    w_half[...] = (w_own + w_half[...].astype(F32)).astype(BF16)
    a2 = there(w_half.at[pl.ds((1 - y) * w_rows, w_rows)], w_in, to_y)

    for h in range(heads):
        own = slice(h * HD, (h + 1) * HD)

        @pl.when(y == 0)
        def _(h=h, own=own):
            early_copies[h].wait_recv()
            grad_key[:, own] = grad_key[:, own] + came[h, 0].astype(F32)
            grad_value[:, own] = grad_value[:, own] + came[h, 1].astype(F32)

        @pl.when(y == 1)
        def _(h=h):
            early_copies[h].wait_send()

        grad_k, grad_v = grad_key[:, own], grad_value[:, own]
        sums_of = sums_of + jnp.sum(
            grad_k * keys[rows:, own].astype(F32) + grad_v * values[rows:, own].astype(F32),
            axis=1, keepdims=True,
        )
        turned = grad_k * cos[...] + pltpu.roll(grad_k, HD // 2, 1) * sin[...]
        grad_qkv[:, mine + h * HD : mine + (h + 1) * HD] = turned.astype(BF16)
        grad_qkv[:, 2 * mine + h * HD : 2 * mine + (h + 1) * HD] = grad_v.astype(BF16)
    row_in[0] = jnp.broadcast_to(sums_of, (rows, 128)).T[:8]
    z_rows = [there(row_in.at[0], row_in.at[d], tp[d - 1]) for d in range(1, n)]

    load_normed.wait()
    tall = q_half.shape[0]
    step = tall // 4

    def product(i, which):
        start = pl.multiple_of(which * tall + i * step, step)
        return mm_tn(normed_v[:, pl.ds(start, step)], grad_qkv[...])

    a0q = []
    for i in range(4):
        q_sent[i * step : (i + 1) * step, :] = product(i, 1 - core).astype(BF16)
        a0q.append(there(q_sent.at[pl.ds(i * step, step)], q_half.at[pl.ds(i * step, step)], to_core))
    for i in range(4):
        value = product(i, core)
        a0q[i].wait_recv()
        here_rows = slice(i * step, (i + 1) * step)
        q_half[here_rows, :] = (value + q_half[here_rows, :].astype(F32)).astype(BF16)
    a1 = there(q_half.at[pl.ds((1 - y) * q_rows, q_rows)], q_in, to_y)
    d2 = there(sgu.at[1], sgu_f.at[core, y, 1], to_y)
    for copy in loads:
        copy.wait()
    grad_normed[...] = (
        mm_nt(grad_qkv[:, :mine], wq_v[...])
        + mm_nt(grad_qkv[:, mine : 2 * mine], wk_v[...])
        + mm_nt(grad_qkv[:, 2 * mine :], wv_v[...])
    ).astype(BF16)
    z_normed = [there(grad_normed.at[:, columns(d)], normed_in.at[d], tp[d - 1]) for d in range(1, n)]

    load_e.wait()
    b3.wait_recv()
    add_rows(e_own, e_in, 0, e_rows)
    f2.wait_recv()
    f2.wait_send()
    flat_f[...] = flat_f[...] + flat_in[1]
    f3 = there(flat_f, flat_in.at[2], to_y)
    a2.wait_recv()
    add_rows(w_half, w_in, y * w_rows, w_rows)
    a4 = there(w_half.at[pl.ds(y * w_rows + (1 - x) * (w_rows // 2), w_rows // 2)], w_in2, to_x)
    a1.wait_recv()
    add_rows(q_half, q_in, y * q_rows, q_rows)
    a3 = there(q_half.at[pl.ds(y * q_rows + (1 - x) * (q_rows // 2), q_rows // 2)], q_in2, to_x)
    cut = e_rows // 2
    b5 = there(e_own.at[pl.ds(0, cut)], egu_f.at[core, x, pl.ds(0, cut)], to_x)
    own_e = here(e_own, egu_f.at[core, x])
    d3 = [there(sd.at[p], sd_f.at[core, p, y], to_y) for p in range(2)]
    for copy in z_normed + z_rows:
        copy.wait_recv()
    total = grad_normed[:, columns(0)].astype(F32)
    row_sum = row_in[0]
    for d in range(1, n):
        total = total + normed_in[d].astype(F32)
        row_sum = row_sum + row_in[d]
    normed_own[...] = total
    row_total[...] = row_sum
    gain = jnp.sum(total * tokens[...].astype(F32) * inv_one[...], axis=0, keepdims=True)
    gain_f[...] = jnp.broadcast_to(gain, gain_f.shape)
    g1 = there(gain_f, gain_in.at[0], to_core)
    a4.wait_recv()
    add_rows(w_half, w_in2, y * w_rows + x * (w_rows // 2), w_rows // 2, w_out_v)
    a6 = there(w_out_v, wo_f.at[core, y, x], to_x)
    own_w = here(w_out_v, wo_f.at[core, y, x])
    g1.wait_recv()
    g1.wait_send()
    gain_f[...] = gain_f[...] + gain_in[0]
    g2 = there(gain_f, gain_in.at[1], to_x)
    a3.wait_recv()
    add_rows(q_half, q_in2, y * q_rows + x * (q_rows // 2), q_rows // 2, q_out)
    a5 = there(q_out, qkv_f.at[core, y, x], to_x)
    own_q = here(q_out, qkv_f.at[core, y, x])
    b7 = there(e_own.at[pl.ds(cut, cut)], egu_f.at[core, x, pl.ds(cut, cut)], to_x)
    own_ffn.wait()
    for copy in z_ffn:
        copy.wait_recv()
    total = ffn_in[0].astype(F32)
    for d in range(1, n):
        total = total + ffn_in[d].astype(F32)
    ffn_own[...] = total
    own_s.wait()
    d1.wait_recv()
    d2.wait_recv()
    c1 = there(sgu_f.at[core], sgu_f.at[core], to_core)
    g2.wait_recv()
    g2.wait_send()
    gain_f[...] = gain_f[...] + gain_in[1]
    g3 = there(gain_f, gain_in.at[2], to_y)
    a6.wait_recv()
    own_w.wait()
    a8 = there(wo_f.at[core, y], wo_f.at[core, y], to_y)
    a5.wait_recv()
    own_q.wait()
    a7 = there(qkv_f.at[core, y], qkv_f.at[core, y], to_y)
    for copy in own_sd:
        copy.wait()
    for copy in d3:
        copy.wait_recv()
    c2 = there(sd_f.at[core], sd_f.at[core], to_core)
    f3.wait_recv()
    f3.wait_send()
    flat_f[...] = flat_f[...] + flat_in[2]
    own_e.wait()
    b5.wait_recv()
    b7.wait_recv()
    c3 = there(egu_f.at[core], egu_f.at[core], to_core)
    a8.wait_recv()
    c5 = there(wo_f.at[core], wo_f.at[core], to_core)
    a7.wait_recv()
    c4 = there(qkv_f.at[core], qkv_f.at[core], to_core)
    own_ed.wait()
    b6.wait_recv()
    c6 = there(ed_f.at[core], ed_f.at[core], to_core)
    g3.wait_recv()
    g3.wait_send()
    gain_f[...] = gain_f[...] + gain_in[2]
    for copy in (c1, c2, c3, c4, c5, c6):
        copy.wait_recv()
    for copy in sent:
        if all(copy is not other for other in (f2, f3, g1, g2, g3)):
            copy.wait_send()


def tail(sgu, sd, egu, ed, flat, normed, w_query, w_key, w_value, attn, ffn, tokens, inv_one, low, w_out, query, keys, values, lse, query_seg, key_seg, cos, sin):
    rows, width = low.shape
    mine = query.shape[1]
    heads = mine // HD

    def pieces(count, height, wide):
        return jax.ShapeDtypeStruct((2,) * count + (height, wide), BF16)

    far = pl.BlockSpec(memory_space=pl.ANY)
    vmem = pl.BlockSpec(memory_space=pltpu.VMEM)

    def room(*shape, kind=BF16):
        return pltpu.VMEM(shape, kind)

    half_of = width // 2
    n = lax.axis_size("tp")
    dma = pltpu.SemaphoreType.DMA
    return pl.pallas_call(
        functools.partial(tail_kernel, 1.0 / math.sqrt(HD)),
        out_shape=[
            pieces(3, *sgu.shape[1:]), pieces(3, *sd.shape[1:]),
            pieces(2, egu.shape[0] // 2, egu.shape[1]), pieces(2, *ed.shape),
            pieces(3, half_of // 4, 3 * mine), pieces(3, mine // 4, half_of),
            jax.ShapeDtypeStruct(flat.shape, F32), jax.ShapeDtypeStruct(tokens.shape, F32),
            jax.ShapeDtypeStruct(tokens.shape, F32), jax.ShapeDtypeStruct((8, rows), F32),
            jax.ShapeDtypeStruct((8, tokens.shape[1]), F32),
        ],
        in_specs=[far] * 4 + [vmem] + [far] * 6 + [vmem] * 12,
        out_specs=[far] * 6 + [vmem] * 5,
        scratch_shapes=[
            room(rows, width), room(width, mine), room(width, mine), room(width, mine), room(rows, mine),
            room(rows, mine), room(rows, mine, kind=F32), room(rows, mine, kind=F32),
            room(heads, 2, rows, HD), room(heads, 2, rows, HD), room(rows, 3 * mine),
            room(half_of, 3 * mine), room(half_of, 3 * mine), room(half_of // 2, 3 * mine),
            room(half_of // 4, 3 * mine), room(half_of // 4, 3 * mine),
            room(mine, half_of), room(mine, half_of), room(mine // 2, half_of),
            room(mine // 4, half_of), room(mine // 4, half_of),
            room(egu.shape[0] // 2, egu.shape[1]), room(egu.shape[0] // 2, egu.shape[1]),
            room(3, *flat.shape, kind=F32), room(n, *tokens.shape), room(rows, width), room(n, *tokens.shape),
            room(n, 8, rows, kind=F32), room(3, 8, tokens.shape[1], kind=F32),
            dma((16,)), dma((36 + heads + 3 * n,)), dma((36 + heads + 3 * n,)),
        ],
        compiler_params=pltpu.CompilerParams(
            collective_id=3, has_side_effects=True, vmem_limit_bytes=62 << 20
        ),
        cost_estimate=pl.CostEstimate(flops=0, bytes_accessed=0, transcendentals=0),
    )(sgu, sd, egu, ed, flat, normed, w_query, w_key, w_value, attn, ffn, tokens, inv_one, low, w_out, query, keys, values, lse, query_seg, key_seg, cos, sin)


def widen_kernel(source, *outputs):
    value = source[...]
    value = value.reshape(value.shape[-2:])
    start = 0
    for out in outputs:
        width = out.shape[1]
        out[...] = value[:, start : start + width].astype(F32)
        start += width


def widen(value, widths=(), kinds=1, kind=0, across=2):
    columns = value.shape[-1]
    if widths:
        value = value.reshape(-1, columns)
        rows = value.shape[0]
        step = min(rows, 256)
        source = pl.BlockSpec((step, columns), lambda i: (i, 0))
        grid = (rows // step,)
        specs = [pl.BlockSpec((step, width), lambda i: (i, 0)) for width in widths]
        shapes = [jax.ShapeDtypeStruct((rows, width), F32) for width in widths]
    else:
        value = value.reshape(across, kinds, -1, columns)
        rows = value.shape[2]
        step = rows
        while step * columns > (1 << 19) and step % 32 == 0:
            step //= 2
        steps = rows // step
        source = pl.BlockSpec((1, 1, step, columns), lambda i, c: (c, kind, i, 0))
        grid = (steps, across)
        specs = [pl.BlockSpec((step, columns), lambda i, c: (i, c))]
        shapes = [jax.ShapeDtypeStruct((rows, across * columns), F32)]
    return pl.pallas_call(
        widen_kernel,
        grid=grid,
        in_specs=[source],
        out_specs=specs,
        out_shape=shapes,
        compiler_params=pltpu.CompilerParams(vmem_limit_bytes=32 << 20),
        cost_estimate=pl.CostEstimate(flops=0, bytes_accessed=0, transcendentals=0),
    )(value)


def weight_kernel(added, part, left, right, *refs):
    total = mm_tn(left[...], right[...])
    if added:
        total = total + refs[0][...].astype(F32)
    refs[-1][...] = total.astype(BF16)


def weight_half(left, right, which, columns, got=None, rows=None, block=1408):
    rows = rows or left.shape[0]
    height, wide = left.shape[1], right.shape[1]
    if columns:
        wide = wide // 2
    else:
        height = height // 2
    step = height
    while step > block and step % 256 == 0:
        step //= 2
    steps = height // step
    extra = [] if got is None else [got]
    out_spec = pl.BlockSpec((step, wide), lambda i, part: (i, 0))
    if columns:
        left_at, right_at = (lambda i, part: (0, i)), (lambda i, part: (0, part[0]))
    else:
        left_at, right_at = (lambda i, part: (0, part[0] * steps + i)), (lambda i, part: (0, 0))
    return pl.pallas_call(
        functools.partial(weight_kernel, bool(extra)),
        grid_spec=pltpu.PrefetchScalarGridSpec(
            num_scalar_prefetch=1,
            grid=(steps,),
            in_specs=[pl.BlockSpec((rows, step), left_at), pl.BlockSpec((rows, wide), right_at)]
            + [out_spec] * len(extra),
            out_specs=out_spec,
        ),
        out_shape=jax.ShapeDtypeStruct((height, wide), BF16),
        compiler_params=pltpu.CompilerParams(vmem_limit_bytes=48 << 20),
        cost_estimate=pl.CostEstimate(flops=0, bytes_accessed=0, transcendentals=0),
    )(which.reshape(1).astype(jnp.int32), left, right, *extra)


def rope_tables(positions, feat_width):
    half_width = feat_width // 2
    inv_freq = ROPE_BASE ** (-(jnp.arange(half_width, dtype=F32) * 2.0) / feat_width)
    angles = positions.astype(F32)[:, None] * inv_freq[None, :]
    return (jnp.cos(angles), jnp.sin(angles))


def rotate(tensor, cos_table, sin_table):
    half_width = tensor.shape[-1] // 2
    first_half = tensor[..., :half_width]
    second_half = tensor[..., half_width:]
    cos_b = cos_table[:, None, :]
    sin_b = sin_table[:, None, :]
    return jnp.concatenate(
        [first_half * cos_b - second_half * sin_b, second_half * cos_b + first_half * sin_b],
        axis=-1,
    )


def ffn_kernel(groups, base, into, flipped, carry, *refs):
    rows, grads, scale, *stored = refs[:6]
    refs = refs[6:]
    if base:
        base_out, base_dx = refs[:2]
        refs = refs[2:]
    if into:
        refs = refs[2:]
    sources, refs = refs[: len(carry)], refs[len(carry) :]
    hid_ref, dgu_ref, out_ref, dx_ref, small_ref, *refs = refs
    *refs, gate_w, up_w, down_w, w_sem = refs
    weights = [
        pltpu.make_async_copy(source, target, w_sem.at[m])
        for m, (source, target) in enumerate(zip(stored, (gate_w, up_w, down_w)))
    ]

    @pl.when(pl.program_id(0) == 0)
    def _():
        for copy in weights:
            copy.start()

    copies = []
    if carry:
        send_sem, recv_sem = refs[-2:]
        _, x, y, where = places()
        for m, (link, count, start, stride) in enumerate(carry):
            first = start + (1 - (x, y)[link - 1]) * stride
            copies.append(
                pltpu.make_async_remote_copy(
                    src_ref=sources[m].at[pl.ds(first, count)], dst_ref=refs[m],
                    send_sem=send_sem.at[m], recv_sem=recv_sem.at[m],
                    device_id=where[link], device_id_type=pl.DeviceIdType.MESH,
                )
            )
        links = sorted({link for link, _, _, _ in carry})

        @pl.when(pl.program_id(0) == 0)
        def _():
            greet_all([where[link] for link in links])
            for copy in copies:
                copy.start()

    @pl.when(pl.program_id(0) == 0)
    def _():
        for copy in weights:
            copy.wait()

    width = down_w.shape[0]
    to, back = (mm_nt, mm) if flipped else (mm, mm_nt)
    gate_pre = to(rows[...], gate_w[...])
    up_pre = to(rows[...], up_w[...])
    grad_hidden = mm_nt(grads[...], down_w[...])
    sig = 1.0 / (1.0 + jnp.exp(-gate_pre))
    act = gate_pre * sig
    slope = sig + act * (1.0 - sig)
    hidden = (act * up_pre).astype(BF16).astype(F32)
    each = width // groups
    column = lax.broadcasted_iota(jnp.int32, (1, width), 1)
    wide = scale[:, 0:1]
    for e in range(1, groups):
        wide = jnp.where(column >= e * each, scale[:, e : e + 1], wide)
    prod = hidden * grad_hidden
    for e in range(groups):
        part = prod
        if groups > 1:
            part = jnp.where((column >= e * each) & (column < (e + 1) * each), prod, 0.0)
        small_ref[:, e : e + 1] = jnp.sum(part, axis=1, keepdims=True)
    hid = (hidden * wide).astype(BF16)
    hid_ref[...] = hid
    scaled = grad_hidden * wide
    dgate = (scaled * up_pre * slope).astype(BF16)
    dup = (scaled * act).astype(BF16)
    dgu_ref[:, :width] = dgate
    dgu_ref[:, width:] = dup
    small_ref[:, groups : groups + 1] = jnp.sum(
        dgate.astype(F32) * gate_pre + dup.astype(F32) * up_pre, axis=1, keepdims=True
    )
    out = mm(hid, down_w[...])
    dx = back(dgate, gate_w[...]) + back(dup, up_w[...])
    if base:
        out = out + base_out[...].astype(F32)
        dx = dx + base_dx[...].astype(F32)
    out_ref[...] = out.astype(BF16)
    dx_ref[...] = dx.astype(BF16)
    if carry:

        @pl.when(pl.program_id(0) == pl.num_programs(0) - 1)
        def _():
            for copy in copies:
                copy.wait()


def ffn(rows, grads, scale, gate_w, up_w, down_w, start=0, total=0, base=(), into=(), flipped=False, carry=(), number=None):
    count, groups = scale.shape
    width = rows.shape[1]
    hidden = down_w.shape[0]
    block = min(256, count)
    first = start // block
    total = total or count
    place = first if total > count else 0

    def at(n, offset):
        return pl.BlockSpec((block, n), lambda i: (i + offset, 0))

    far = pl.BlockSpec(memory_space=pl.ANY)
    return pl.pallas_call(
        functools.partial(
            ffn_kernel, groups, bool(base), bool(into), flipped, tuple(c[1:] for c in carry)
        ),
        grid=(count // block,),
        in_specs=[at(width, first), at(width, first), at(groups, 0)]
        + [far] * 3
        + [at(width, 0)] * len(base)
        + [far] * (len(into) + len(carry)),
        out_specs=[
            at(hidden, place),
            at(2 * hidden, place),
            at(width, 0),
            at(width, 0),
            at(groups + 1, 0),
        ]
        + [far] * len(carry),
        out_shape=[
            jax.ShapeDtypeStruct((total, hidden), BF16),
            jax.ShapeDtypeStruct((total, 2 * hidden), BF16),
            jax.ShapeDtypeStruct((count, width), BF16),
            jax.ShapeDtypeStruct((count, width), BF16),
            jax.ShapeDtypeStruct((count, groups + 1), F32),
        ]
        + [jax.ShapeDtypeStruct((c[2], c[0].shape[1]), BF16) for c in carry],
        scratch_shapes=([pltpu.SemaphoreType.DMA((len(carry),))] * 2 if carry else [])
        + [pltpu.VMEM(w.shape, BF16) for w in (gate_w, up_w, down_w)]
        + [pltpu.SemaphoreType.DMA((3,))],
        input_output_aliases={6 + len(base) + k: k for k in range(len(into))},
        compiler_params=pltpu.CompilerParams(
            vmem_limit_bytes=62 << 20, collective_id=number, has_side_effects=bool(carry)
        ),
        cost_estimate=pl.CostEstimate(flops=0, bytes_accessed=0, transcendentals=0),
    )(rows, grads, scale, gate_w, up_w, down_w, *base, *into, *[c[0] for c in carry])


def line_sum(depth, prepare, settle, gathered, beside, part, came, came_two, spread, sems):
    n = lax.axis_size("tp")
    me = lax.axis_index("tp")
    chunks, _, step, _ = part.shape
    sum_send, sum_recv, two_recv, out_send, out_recv = sems

    def send(source, target, send_sem, recv_sem, to):
        return pltpu.make_async_remote_copy(
            src_ref=source, dst_ref=target, send_sem=send_sem, recv_sem=recv_sem,
            device_id={"tp": to}, device_id_type=pl.DeviceIdType.MESH,
        )

    def sum_copy(c, s, to_right, two):
        target = came_two.at[c] if two else came.at[c, s]
        sem = two_recv.at[c] if two else sum_recv.at[c, s]
        return send(part.at[c, s], target, sum_send.at[c, s], sem, me + 1 if to_right else me - 1)

    def out_copy(c, s, to_right):
        return send(
            spread.at[c, s], spread.at[c, s], out_send.at[c, s, 1 if to_right else 0],
            out_recv.at[c, s], me + 1 if to_right else me - 1,
        )

    def within(c):
        return (c >= 0) & (c < chunks)

    def pass_sums(t):
        @pl.when(within(t))
        def _():
            prepare(t)

        for s in range(n):
            c = t - me * depth

            @pl.when((me < s) & within(c))
            def _(s=s, c=c):
                @pl.when(me > 0)
                def _():
                    sum_copy(c, s, True, False).wait_recv()
                    part[c, s] = (part[c, s].astype(F32) + came[c, s].astype(F32)).astype(BF16)

                sum_copy(c, s, True, False).start()

        for s in range(n):
            c = t - (n - 1 - me) * depth

            @pl.when((me > s) & within(c))
            def _(s=s, c=c):
                @pl.when(me < n - 1)
                def _():
                    sum_copy(c, s, False, False).wait_recv()
                    part[c, s] = (part[c, s].astype(F32) + came[c, s].astype(F32)).astype(BF16)

                @pl.when(me - 1 == s)
                def _():
                    sum_copy(c, s, False, True).start()

                @pl.when(me - 1 > s)
                def _():
                    sum_copy(c, s, False, False).start()

    def pass_own(t):
        c = t - (n - 1) * depth
        for s in range(n):

            @pl.when((me == s) & within(c))
            def _(s=s):
                if s > 0:
                    sum_copy(c, s, True, False).wait_recv()
                if s < n - 1:
                    sum_copy(c, s, False, True).wait_recv()
                total = part[c, s].astype(F32)
                if s > 0:
                    total = total + came[c, s].astype(F32)
                if s < n - 1:
                    total = total + came_two[c].astype(F32)
                spread[c, s] = settle(c, total)
                if s > 0:
                    out_copy(c, s, False).start()
                if s < n - 1:
                    out_copy(c, s, True).start()

    def pass_out(t):
        for s in range(n):
            right = t - (n - 1 + me - s) * depth
            left = t - (n - 1 + s - me) * depth

            @pl.when((me > s) & within(right))
            def _(s=s, c=right):
                out_copy(c, s, True).wait_recv()

                @pl.when(me < n - 1)
                def _():
                    out_copy(c, s, True).start()

            @pl.when((me < s) & within(left))
            def _(s=s, c=left):
                out_copy(c, s, False).wait_recv()

                @pl.when(me > 0)
                def _():
                    out_copy(c, s, False).start()

        last = t - 2 * (n - 1) * depth

        @pl.when(within(last))
        def _():
            gathered(last)

    def turn(t, carry):
        pass_sums(t)
        pass_own(t)
        pass_out(t)
        if beside is not None:
            beside(t)
        return carry

    lax.fori_loop(0, chunks + 2 * (n - 1) * depth, turn, 0)

    def drain(c, carry):
        for s in range(n):

            @pl.when(me != s)
            def _(s=s):
                sum_copy(c, s, True, False).wait_send()

            @pl.when((me < n - 1) & (s <= me))
            def _(s=s):
                out_copy(c, s, True).wait_send()

            @pl.when((me > 0) & (s >= me))
            def _(s=s):
                out_copy(c, s, False).wait_send()

        return carry

    lax.fori_loop(0, chunks, drain, 0)


def line_scratch(rows, width_own):
    n = lax.axis_size("tp")
    chunks = max(1, min(16, 128 // n))
    step = rows // chunks
    slots = pltpu.VMEM((chunks, n, step, width_own), BF16)
    dma = pltpu.SemaphoreType.DMA
    return chunks, step, [
        slots, slots, pltpu.VMEM((chunks, step, width_own), BF16), slots,
        dma((chunks, n)), dma((chunks, n)), dma((chunks,)), dma((chunks, n, 2)), dma((chunks, n)),
    ]


def greet(peers):
    n = lax.axis_size("tp")
    me = lax.axis_index("tp")
    barrier = pltpu.get_barrier_semaphore()

    def signal(where):
        pl.semaphore_signal(barrier, inc=1, device_id=where, device_id_type=pl.DeviceIdType.MESH)

    @pl.when(me > 0)
    def _():
        signal({"tp": me - 1})

    @pl.when(me < n - 1)
    def _():
        signal({"tp": me + 1})

    for where in peers:
        signal(where)

    beside = jnp.where(me > 0, 1, 0) + jnp.where(me < n - 1, 1, 0)
    pl.semaphore_wait(barrier, beside + len(peers))


def attend_out_kernel(
    chunks, step, depth, eps, attn, w_out, x, gain, grads,
    mixed, resid_own, inv_out, grads_peer,
    part, came, came_two, spread, s0, s1, s2, s3, s4, y_send, y_recv, g_send, g_recv,
):
    n = lax.axis_size("tp")
    me = lax.axis_index("tp")
    own = part.shape[3]
    rows = attn.shape[0]
    other = {"ep": 1 - lax.axis_index("ep")}
    greet([other])
    grads_copy = pltpu.make_async_remote_copy(
        src_ref=grads.at[pl.ds(0, grads_peer.shape[0])], dst_ref=grads_peer, send_sem=g_send, recv_sem=g_recv,
        device_id=other, device_id_type=pl.DeviceIdType.MESH,
    )
    grads_copy.start()
    block = max(step, min(rows, 128))

    def product(b, carry):
        start = pl.multiple_of(b * block, block)
        value = mm(attn[pl.ds(start, block), :], w_out[...]).astype(BF16)
        for s in range(n):
            for k in range(block // step):
                part[b * (block // step) + k, s] = value[k * step:(k + 1) * step, s * own:(s + 1) * own]
        return carry

    lax.fori_loop(0, rows // block, product, 0)

    def at(c):
        return pl.ds(pl.multiple_of(c * step, step), step)

    def peer_copy(c):
        return pltpu.make_async_remote_copy(
            src_ref=mixed.at[at(c)], dst_ref=mixed.at[pl.ds(pl.multiple_of(rows + c * step, step), step)], send_sem=y_send.at[c], recv_sem=y_recv.at[c],
            device_id=other, device_id_type=pl.DeviceIdType.MESH,
        )

    def prepare(c):
        pass

    def settle(c, total):
        return total.astype(BF16)

    def gathered(c):
        resid = []
        square = jnp.zeros((step, 1), F32)
        for s in range(n):
            piece = x[at(c), s * own:(s + 1) * own].astype(F32) + spread[c, s].astype(F32)
            resid.append(piece)
            square = square + jnp.sum(piece * piece, axis=1, keepdims=True)
        inv = lax.rsqrt(square / (n * own) + eps)
        inv_out[at(c), :] = inv
        for s in range(n):
            mixed[at(c), s * own:(s + 1) * own] = (resid[s] * inv * gain[:, s * own:(s + 1) * own]).astype(BF16)

            @pl.when(me == s)
            def _(s=s):
                resid_own[at(c), :] = resid[s]

        peer_copy(c).start()

    line_sum(depth, prepare, settle, gathered, None, part, came, came_two, spread, (s0, s1, s2, s3, s4))

    def last(c, carry):
        peer_copy(c).wait_recv()
        peer_copy(c).wait_send()
        return carry

    lax.fori_loop(0, chunks, last, 0)
    grads_copy.wait()


def attend_out(attn, w_out, x, gain, grads, width_own, depth=1):
    rows, width = x.shape
    chunks, step, scratch = line_scratch(rows, width_own)
    vmem = pl.BlockSpec(memory_space=pltpu.VMEM)
    far = pl.BlockSpec(memory_space=pl.ANY)
    dma = pltpu.SemaphoreType.DMA
    return pl.pallas_call(
        functools.partial(attend_out_kernel, chunks, step, depth, EPS),
        out_shape=[
            jax.ShapeDtypeStruct((2 * rows, width), BF16),
            jax.ShapeDtypeStruct((rows, width_own), F32), jax.ShapeDtypeStruct((rows, 1), F32),
            jax.ShapeDtypeStruct((rows // 2, width), BF16),
        ],
        in_specs=[vmem] * 4 + [far],
        out_specs=[vmem] * 3 + [far],
        scratch_shapes=scratch + [dma((chunks,)), dma((chunks,)), dma, dma],
        compiler_params=pltpu.CompilerParams(collective_id=1, has_side_effects=True, vmem_limit_bytes=40 << 20),
        cost_estimate=pl.CostEstimate(flops=0, bytes_accessed=0, transcendentals=0),
    )(attn, w_out, x, gain, grads)


def resid_grad_kernel(
    chunks, step, depth, tiles, grad, grad_p, out_p, dgu, hid, both, both_grad, sgu, sd,
    small_e, small_p, small_s, prob, hot, logits, switch, w_small, g_own, resid_own, inv_two, gain,
    low, grad_resid, gain_grad, out_back, sum_egu, sum_ed, sgu_x, sd_x, grad_small,
    part, came, came_two, spread, s0, s1, s2, s3, s4, back, y_send, y_recv, o_send, o_recv,
    dgu_v, hid_v, both_v, both_grad_v, sent_egu, sent_ed, came_egu, came_ed,
    s_own, s_in, d_own, d_in, l_sem, w_send, w_recv, w_out, r_send, r_recv, r_out,
    router, along, small_y, small_z, ed_in, ed_out, t_send, t_recv, e_send, e_recv, e_out,
):
    n = lax.axis_size("tp")
    own = part.shape[3]
    rows = grad.shape[0]
    core, x, y, (to_core, to_x, other) = places()

    def at(c):
        return pl.ds(pl.multiple_of(c * step, step), step)

    def peer_copy(c):
        return pltpu.make_async_remote_copy(
            src_ref=grad_p.at[at(c)], dst_ref=back.at[at(c)], send_sem=y_send.at[c], recv_sem=y_recv.at[c],
            device_id=other, device_id_type=pl.DeviceIdType.MESH,
        )

    def out_copy():
        return pltpu.make_async_remote_copy(
            src_ref=out_p, dst_ref=out_back, send_sem=o_send, recv_sem=o_recv,
            device_id=other, device_id_type=pl.DeviceIdType.MESH,
        )

    loads = [
        pltpu.make_async_copy(source, target, l_sem.at[m])
        for m, (source, target) in enumerate(
            (
                (dgu, dgu_v),
                (both, both_v),
                (hid, hid_v),
                (both_grad, both_grad_v),
                (sgu.at[pl.ds(x * s_own.shape[0], s_own.shape[0])], s_own),
                (sd.at[pl.ds(y * d_own.shape[0], d_own.shape[0])], d_own),
            )
        )
    ]
    kinds = ((dgu_v, both_v, sent_egu, came_egu, sum_egu), (hid_v, both_grad_v, sent_ed, came_ed, sum_ed))

    def sum_copies(m):
        source, target, where = (
            (sgu.at[pl.ds((1 - x) * s_own.shape[0], s_own.shape[0])], s_in, to_x),
            (sd.at[pl.ds((1 - y) * d_own.shape[0], d_own.shape[0])], d_in, other),
            (s_own, sgu_x.at[x], to_x),
            (d_own, sd_x.at[x], to_x),
        )[m]
        return pltpu.make_async_remote_copy(
            src_ref=source, dst_ref=target, send_sem=r_send.at[m], recv_sem=r_recv.at[m],
            device_id=where, device_id_type=pl.DeviceIdType.MESH,
        )

    def own_out(m):
        return pltpu.make_async_copy((s_own, d_own)[m], (sgu_x, sd_x)[m].at[x], r_out.at[m])

    def shared(m):
        sum_copies(m).wait_recv()
        add_rows((s_own, d_own)[m], (s_in, d_in)[m], 0, (s_own, d_own)[m].shape[0])
        sum_copies(2 + m).start()
        own_out(m).start()

    def tile_copy(m, b):
        return pltpu.make_async_remote_copy(
            src_ref=kinds[m][2].at[b], dst_ref=kinds[m][3].at[b], send_sem=w_send.at[b, m], recv_sem=w_recv.at[b, m],
            device_id=to_core, device_id_type=pl.DeviceIdType.MESH,
        )

    def x_copy(b):
        wide = ed_in.shape[2]
        return pltpu.make_async_remote_copy(
            src_ref=came_ed.at[b, :, pl.ds(pl.multiple_of((1 - x) * wide, wide), wide)], dst_ref=ed_in.at[b],
            send_sem=e_send.at[b], recv_sem=e_recv.at[b],
            device_id=to_x, device_id_type=pl.DeviceIdType.MESH,
        )

    def x_out(b):
        tall = ed_in.shape[1]
        return pltpu.make_async_copy(
            ed_out.at[b], sum_ed.at[pl.ds(pl.multiple_of(b * tall, tall), tall)], e_out.at[b]
        )

    def tile_out(m, b):
        tall = kinds[m][3].shape[1]
        return pltpu.make_async_copy(
            kinds[m][3].at[b], kinds[m][4].at[pl.ds(pl.multiple_of(b * tall, tall), tall)], w_out.at[b, m]
        )

    def tile(m, b, which):
        left, right = kinds[m][:2]
        tall, wide = kinds[m][3].shape[1:]
        return mm_tn(
            left[...] if tiles == 1 else left[:, pl.ds(pl.multiple_of(b * tall, tall), tall)],
            right[:, pl.ds(pl.multiple_of(which * wide, wide), wide)],
        )

    def weights(t):
        @pl.when(t == 0)
        def _():
            for copy in loads:
                copy.wait()

        @pl.when(t == 1)
        def _():
            gates()

        @pl.when(t < tiles)
        def _():
            for m in range(2):
                kinds[m][2][t] = tile(m, t, 1 - core).astype(BF16)
                tile_copy(m, t).start()

        @pl.when(t == tiles * 8 // 11)
        def _():
            shared(0)

        @pl.when(t == tiles * 14 // 11)
        def _():
            shared(1)

        @pl.when((t >= tiles) & (t < 2 * tiles))
        def _():
            b = t - tiles
            for m in range(2):
                value = tile(m, b, core)
                tile_copy(m, b).wait_recv()
                kinds[m][3][b] = (value + kinds[m][3][b].astype(F32)).astype(BF16)
                if m == 0:
                    tile_out(m, b).start()
                else:
                    x_copy(b).start()

    for copy in loads:
        copy.start()
    me = lax.axis_index("tp")

    def small_copy(d):
        return pltpu.make_async_remote_copy(
            src_ref=small_z.at[0] if d else small_p, dst_ref=small_z.at[d] if d else small_y,
            send_sem=t_send.at[d], recv_sem=t_recv.at[d],
            device_id={"tp": (me + d) % n} if d else other, device_id_type=pl.DeviceIdType.MESH,
        )

    greet_all([other, to_core, to_x] + [{"tp": (me + d) % n} for d in range(1, n)])
    small_copy(0).start()
    sum_copies(0).start()

    def begin(c, carry):
        peer_copy(c).start()
        return carry

    lax.fori_loop(0, chunks, begin, 0)
    sum_copies(1).start()
    out_copy().start()
    gain_grad[...] = jnp.zeros_like(gain_grad)
    experts_own = small_e.shape[0] - 1
    experts = 2 * experts_own
    small_copy(0).wait_recv()
    here, there = small_e[:experts_own, :], small_y[:experts_own, :]
    small_z[0] = jnp.zeros_like(small_z[0])
    small_z[0, :experts_own] = jnp.where(y == 0, here, there)
    small_z[0, experts_own:experts] = jnp.where(y == 0, there, here)
    small_z[0, experts : experts + 1] = small_s[:1, :]
    small_z[0, experts + 1 : experts + 2] = small_s[1:, :] + small_e[experts_own:, :] + small_y[experts_own:, :]
    for d in range(1, n):
        small_copy(d).start()

    def gates():
        total = small_z[0]
        for d in range(1, n):
            small_copy(d).wait_recv()
            total = total + small_z[d]
        slots = prob.shape[1]
        total = jnp.concatenate([total, jnp.zeros((128 - total.shape[0], rows), F32)], axis=0).T
        grad_prob = total[:, :slots] * hot[...]
        inner = jnp.sum(prob[...] * grad_prob, axis=1, keepdims=True)
        sw = switch[...]
        grad_switch = total[:, experts : experts + 1] * sw * (1.0 - sw)
        place = lax.broadcasted_iota(jnp.int32, (1, slots), 1)
        grads = jnp.where(place == experts, grad_switch, prob[...] * (grad_prob - inner)).astype(BF16)
        router[...] = mm_nt(grads, w_small[...])
        along[...] = total[:, experts + 1 : experts + 2] + jnp.sum(
            grads.astype(F32) * logits[...], axis=1, keepdims=True
        )
        grad_small[...] = mm_tn(grads, both_v[:rows, :])

    def prepare(c):
        peer_copy(c).wait_recv()
        for s in range(n):
            columns = slice(s * own, (s + 1) * own)
            part[c, s] = (grad[at(c), columns].astype(F32) + back[at(c), columns].astype(F32)).astype(BF16)

    def settle(c, total):
        total = total + router[at(c), :]
        inv = inv_two[at(c), :]
        resid = resid_own[at(c), :]
        gain_grad[...] += jnp.sum(total * resid * inv, axis=0, keepdims=True)
        result = g_own[at(c), :].astype(F32) + inv * gain[...] * total - resid * (inv * inv * along[at(c), :] / (n * own))
        grad_resid[at(c), :] = result
        return result.astype(BF16)

    def gathered(c):
        for s in range(n):
            low[at(c), s * own:(s + 1) * own] = spread[c, s]

    line_sum(depth, prepare, settle, gathered, weights, part, came, came_two, spread, (s0, s1, s2, s3, s4))

    def last(c, carry):
        peer_copy(c).wait_send()
        return carry

    lax.fori_loop(0, chunks, last, 0)
    out_copy().wait()

    def done(b, carry):
        x_copy(b).wait_recv()
        wide = ed_in.shape[2]
        own = came_ed[b, :, pl.ds(pl.multiple_of(x * wide, wide), wide)]
        ed_out[b] = (own.astype(F32) + ed_in[b].astype(F32)).astype(BF16)
        x_out(b).start()
        tile_copy(0, b).wait_send()
        tile_copy(1, b).wait_send()
        tile_out(0, b).wait()
        x_copy(b).wait_send()
        return carry

    lax.fori_loop(0, tiles, done, 0)

    def written(b, carry):
        x_out(b).wait()
        return carry

    lax.fori_loop(0, tiles, written, 0)
    for m in range(2):
        sum_copies(m).wait_send()
        sum_copies(2 + m).wait()
        own_out(m).wait()
    for d in range(n):
        small_copy(d).wait_send()


def resid_grad(grad, grad_p, out_p, dgu, hid, both, both_grad, sgu, sd, small_e, small_p, small_s, prob, hot, logits, switch, w_small, g_own, resid_own, inv_two, gain, depth=1):
    rows, width = grad.shape
    width_own = g_own.shape[1]
    chunks, step, scratch = line_scratch(rows, width_own)
    hidden = hid.shape[1]
    tiles = 11 if hidden % (11 * 128) == 0 else 1
    vmem = pl.BlockSpec(memory_space=pltpu.VMEM)
    far = pl.BlockSpec(memory_space=pl.ANY)
    dma = pltpu.SemaphoreType.DMA
    return pl.pallas_call(
        functools.partial(resid_grad_kernel, chunks, step, depth, tiles),
        out_shape=[
            jax.ShapeDtypeStruct((rows, width), BF16), jax.ShapeDtypeStruct((rows, width_own), F32),
            jax.ShapeDtypeStruct((1, width_own), F32), jax.ShapeDtypeStruct((rows, width), BF16),
        ]
        + [jax.ShapeDtypeStruct((2 * hidden, width // 2), BF16), jax.ShapeDtypeStruct((hidden, width // 4), BF16)]
        + [jax.ShapeDtypeStruct((2, v.shape[0] // 2, v.shape[1]), BF16) for v in (sgu, sd)]
        + [jax.ShapeDtypeStruct((prob.shape[1], width), F32)],
        in_specs=[vmem] + [far] * 8 + [vmem] * 12,
        out_specs=[vmem] * 3 + [far] * 5 + [vmem],
        scratch_shapes=scratch + [pltpu.VMEM((rows, width), BF16), dma((chunks,)), dma((chunks,)), dma, dma]
        + [pltpu.VMEM(v.shape, BF16) for v in (dgu, hid, both, both_grad)]
        + [pltpu.VMEM((tiles, k * hidden // tiles, width // 2), BF16) for k in (2, 1, 2, 1)]
        + [pltpu.VMEM((v.shape[0] // 2, v.shape[1]), BF16) for v in (sgu, sgu, sd, sd)]
        + [dma((6,)), dma((tiles, 2)), dma((tiles, 2)), dma((tiles, 2)), dma((4,)), dma((4,)), dma((2,))]
        + [pltpu.VMEM((rows, width_own), F32), pltpu.VMEM((rows, 1), F32)]
        + [pltpu.VMEM(small_e.shape, F32), pltpu.VMEM((lax.axis_size("tp"), 16, rows), F32)]
        + [pltpu.VMEM((tiles, hidden // tiles, width // 4), BF16)] * 2
        + [dma((lax.axis_size("tp"),))] * 2 + [dma((tiles,))] * 3,
        compiler_params=pltpu.CompilerParams(collective_id=2, has_side_effects=True, vmem_limit_bytes=63 << 20),
        cost_estimate=pl.CostEstimate(flops=0, bytes_accessed=0, transcendentals=0),
    )(grad, grad_p, out_p, dgu, hid, both, both_grad, sgu, sd, small_e, small_p, small_s, prob, hot, logits, switch, w_small, g_own, resid_own, inv_two, gain)


def body(
    tokens,
    norm_attn,
    w_query,
    w_key,
    w_value,
    w_output,
    norm_ffn,
    w_router,
    shared_switch,
    shared_gate,
    shared_up,
    shared_down,
    expert_gate,
    expert_up,
    expert_down,
    routes,
    segments,
    output_gradient,
):
    tp_count = lax.axis_size("tp")
    ep_count = lax.axis_size("ep")
    dp_count = lax.axis_size("dp")
    tp_rank = lax.axis_index("tp")
    ep_rank = lax.axis_index("ep")
    rows = tokens.shape[0]
    width_own = tokens.shape[1]
    width = width_own * tp_count
    heads = w_query.shape[1] // HD
    experts_own = expert_gate.shape[0]
    experts = experts_own * ep_count
    expert_width = expert_gate.shape[2]
    score_scale = 1.0 / math.sqrt(HD)
    far_bits = [1 << b for b in range(1, dp_count.bit_length() - 1)]

    def own_columns(value):
        return lax.dynamic_slice_in_dim(value, tp_rank * width_own, width_own, value.ndim - 1)

    near = bit_of("dp", 1)

    def pair_send(left, right, columns, used=None):
        sent = weight_half(left, right, 1 - near, columns, rows=used)
        return sent, swap(sent, "dp", 1)

    def pair_keep(left, right, columns, got, used=None):
        return weight_half(left, right, near, columns, got, rows=used)

    core = ("dp", 1)
    far = [("dp", b) for b in far_bits]
    line = [("ep", 1)]
    x_link, y_link = far[0], line[0]

    def over_tp(value):
        if tp_count <= 4:
            others = [
                lax.ppermute(value, "tp", [(i, (i + d) % tp_count) for i in range(tp_count)])
                for d in range(1, tp_count)
            ]
            return sum(others, value)
        bit = 1
        while bit < tp_count:
            value = value + swap(value, "tp", bit)
            bit *= 2
        return value

    def over_rows(value):
        for axis, bit in [core] + far + line:
            value = value + swap(value, axis, bit)
        return value

    packed = jnp.concatenate(
        [tokens, norm_attn[None, :], norm_ffn[None, :], jnp.zeros((14, width_own), BF16)], axis=0
    )
    packed = lax.all_gather(packed, "tp", axis=1, tiled=True)
    x_full = packed[:rows].astype(F32)
    gain_one = packed[rows].astype(F32)
    gain_two = packed[rows + 1].astype(F32)
    grad_rows = lax.all_gather(after(output_gradient, packed), "tp", axis=1, tiled=True)
    route_hot = jnp.sum(
        (routes[:, :, None] == jnp.arange(experts, dtype=jnp.int32)[None, None, :]).astype(F32),
        axis=1,
    )
    route_hot_peer = swap(route_hot, "ep", 1)

    inv_one = lax.rsqrt(jnp.mean(x_full * x_full, axis=1, keepdims=True) + EPS)
    normed = (x_full * inv_one * gain_one).astype(BF16)
    q_pre = mm(normed, w_query)
    k_pre = mm(normed, w_key)
    v_pre = mm(normed, w_value)
    positions = ep_rank * rows + jnp.arange(rows, dtype=jnp.int32)
    cos_table, sin_table = rope_tables(positions, HD)
    query = rotate(q_pre.reshape(rows, heads, HD), cos_table, sin_table).astype(BF16)
    key_own = rotate(k_pre.reshape(rows, heads, HD), cos_table, sin_table).astype(BF16)
    value_own = v_pre.astype(BF16).reshape(rows, heads, HD)
    forth = [(i, i + 1) for i in range(ep_count - 1)]
    back = [(i + 1, i) for i in range(ep_count - 1)]
    earlier = lax.ppermute(jnp.stack([key_own, value_own]), "ep", forth)
    earlier = after(earlier, grad_rows)
    key_rows = jnp.concatenate([earlier[0], key_own], axis=0)
    value_rows = jnp.concatenate([earlier[1], value_own], axis=0)
    key_pos = (ep_rank - 1) * rows + jnp.arange(2 * rows, dtype=jnp.int32)
    seg_rows = segments.reshape(ep_count, rows)
    query_seg = lax.dynamic_index_in_dim(seg_rows, ep_rank, 0, keepdims=False)
    before_seg = lax.dynamic_index_in_dim(
        seg_rows, jnp.maximum(ep_rank - 1, 0), 0, keepdims=False
    )
    key_seg = jnp.concatenate([jnp.where(ep_rank > 0, before_seg, -1), query_seg])
    allowed = (query_seg[:, None] == key_seg[None, :]) & (key_pos[None, :] <= positions[:, None])

    def masked_scores():
        scores = (
            jnp.einsum("qhd,khd->hqk", query, key_rows, preferred_element_type=F32) * score_scale
        )
        return jnp.where(allowed[None], scores, NEG)

    scores = masked_scores()
    row_top = jnp.max(scores, axis=2, keepdims=True)
    shifted = jnp.exp(scores - row_top)
    row_total = jnp.sum(shifted, axis=2, keepdims=True)
    weights = (shifted / row_total).astype(BF16)
    attended = jnp.einsum("hqk,khd->qhd", weights, value_rows, preferred_element_type=F32)
    attn_rows = attended.astype(BF16).reshape(rows, heads * HD)
    log_norm = row_top + jnp.log(row_total)

    both, resid_own, inv_two, grad_peer_a = attend_out(
        attn_rows, w_output, packed[:rows], gain_two[None, :], grad_rows, width_own
    )
    mixed = both[:rows]

    def router(values):
        logits = mm(values, w_router)
        return logits, jax.nn.softmax(logits, axis=1)

    logits, router_prob = router(mixed)
    combine = router_prob * route_hot
    combine_peer = router(both[rows:])[1] * route_hot_peer
    switch_logit = mm(mixed, shared_switch[:, None])
    switch = jax.nn.sigmoid(switch_logit)

    def own_experts(value):
        return lax.dynamic_slice_in_dim(value, ep_rank * experts_own, experts_own, 1)

    hid_s, dgu_s, out_s, grad_s, small_s, grad_peer_b = ffn(
        both,
        grad_rows,
        switch,
        shared_gate,
        shared_up,
        shared_down,
        carry=[(grad_rows, 2, rows // 2, rows // 2, 0)],
        number=4,
    )
    both_grad = jnp.concatenate([grad_rows, grad_peer_a, grad_peer_b], axis=0)
    sent, got_sgu = pair_send(both, dgu_s, False, rows)
    sent, got_sd = pair_send(hid_s, after(grad_rows, sent), True)
    sum_sgu = pair_keep(both, after(dgu_s, sent, both_grad), False, got_sgu, rows)
    sum_sd = pair_keep(hid_s, after(grad_rows, sum_sgu), True, got_sd)
    quarter = sum_sgu.shape[0] // 4

    hidden_width = experts_own * expert_width
    gate_w = jnp.transpose(expert_gate, (0, 2, 1)).reshape(hidden_width, width)
    up_w = jnp.transpose(expert_up, (0, 2, 1)).reshape(hidden_width, width)
    down_w = expert_down.reshape(hidden_width, width)
    hid_p, dgu_p, out_p, grad_p, small_p, got_sgu_a, got_sd = ffn(
        both,
        after(both_grad, sum_sd),
        own_experts(combine_peer),
        gate_w,
        up_w,
        down_w,
        start=rows,
        total=2 * rows,
        flipped=True,
        carry=[
            (sum_sgu, 2, quarter, 0, 2 * quarter),
            (sum_sd, 1, sum_sd.shape[0] // 2, 0, sum_sd.shape[0] // 2),
        ],
        number=5,
    )
    hid_e, dgu_e, out_e, grad_e, small_e, got_sgu_b = ffn(
        both,
        both_grad,
        after(own_experts(combine), grad_p),
        gate_w,
        up_w,
        down_w,
        total=2 * rows,
        base=(out_s, grad_s),
        into=(hid_p, dgu_p),
        flipped=True,
        carry=[(sum_sgu, 2, quarter, quarter, 2 * quarter)],
        number=6,
    )
    got_sgu = jnp.concatenate([got_sgu_a, got_sgu_b], axis=0)

    sum_sgu = reduce_add(sum_sgu, got_sgu, *y_link)
    sum_sd = reduce_add(sum_sd, got_sd, *x_link)

    tp_rows = lax.dynamic_slice_in_dim(w_router, tp_rank * width_own, width_own, 0)
    spare = 16 - experts - 1

    def slots(value, more=None):
        more = jnp.zeros((value.shape[0], 1), value.dtype) if more is None else more
        return jnp.pad(jnp.concatenate([value, more], axis=1), ((0, 0), (0, spare)))

    resid_low, grad_resid, grad_gain_two, out_back, sum_egu, sum_ed, sgu_x, sd_x, grad_small = resid_grad(
        grad_e,
        grad_p,
        out_p,
        dgu_e,
        hid_e,
        both,
        both_grad,
        sum_sgu,
        sum_sd,
        small_e.T,
        small_p.T,
        small_s.T,
        slots(router_prob),
        slots(route_hot),
        slots(logits, switch_logit),
        switch,
        slots(tp_rows, own_columns(shared_switch)[:, None]),
        output_gradient,
        resid_own,
        inv_two,
        norm_ffn.astype(F32)[None, :],
    )

    flat = jnp.concatenate(
        [grad_gain_two.reshape(-1), grad_small[: experts + 1].reshape(-1)]
    ).reshape(-1, 128)
    qkv = heads * HD
    inner = shared_gate.shape[1]
    ffn_part = (out_e.astype(F32) + out_back.astype(F32)).astype(BF16)
    sgu_f, sd_f, egu_f, ed_f, qkv_f, wo_f, flat, ffn_own, normed_own, row_total, grad_gain_one = tail(
        sgu_x,
        sd_x,
        sum_egu,
        sum_ed,
        flat,
        normed,
        w_query,
        w_key,
        w_value,
        attn_rows,
        ffn_part,
        tokens,
        inv_one,
        resid_low,
        w_output,
        query.reshape(rows, qkv),
        key_rows.reshape(2 * rows, qkv),
        value_rows.reshape(2 * rows, qkv),
        log_norm[:, :, 0].T,
        query_seg[:, None],
        key_seg[None, :],
        jnp.concatenate([cos_table, cos_table], axis=1),
        jnp.concatenate([sin_table, -sin_table], axis=1),
    )

    sg_grad, su_grad = widen(sgu_f, (inner, inner))
    (sd_grad,) = widen(sd_f)
    (eg_grad,) = widen(egu_f, kinds=2, kind=0)
    (eu_grad,) = widen(egu_f, kinds=2, kind=1)
    (ed_grad,) = widen(ed_f, across=4)
    wq_grad, wk_grad, wv_grad = widen(qkv_f, (qkv,) * 3)
    (wo_grad,) = widen(wo_f)

    x_own = tokens.astype(F32)
    grad_tokens = (
        grad_resid
        + inv_one * norm_attn.astype(F32) * normed_own
        - x_own * (inv_one * inv_one) * (row_total[0][:, None] / width)
    )
    grad_gain_one = grad_gain_one[0]
    layer_out = (resid_own + ffn_own).astype(BF16)
    flat = flat.reshape(-1)
    grad_gain_two = flat[:width_own]
    grad_router = flat[width_own : width_own + width * experts].reshape(experts, width).T
    grad_switch_w = flat[width_own + width * experts :]

    def per_expert(value):
        return value.reshape(experts_own, expert_width, width)

    return (
        layer_out,
        grad_tokens,
        grad_gain_one,
        wq_grad,
        wk_grad,
        wv_grad,
        wo_grad,
        grad_gain_two,
        grad_router,
        grad_switch_w,
        sg_grad,
        su_grad,
        sd_grad,
        jnp.transpose(per_expert(eg_grad), (0, 2, 1)),
        jnp.transpose(per_expert(eu_grad), (0, 2, 1)),
        per_expert(ed_grad),
    )


def solution(mesh):
    placed = (
        P(("dp", "ep"), "tp"),
        P("tp"),
        P(None, "tp"),
        P(None, "tp"),
        P(None, "tp"),
        P("tp", None),
        P("tp"),
        P(),
        P(),
        P(None, "tp"),
        P(None, "tp"),
        P("tp", None),
        P("ep", None, "tp"),
        P("ep", None, "tp"),
        P("ep", "tp", None),
        P(("dp", "ep"), None),
        P("dp"),
        P(("dp", "ep"), "tp"),
    )
    return jax.shard_map(
        body,
        mesh=mesh,
        in_specs=placed,
        out_specs=(
            P(("dp", "ep"), "tp"),
            P(("dp", "ep"), "tp"),
            P("tp"),
            P(None, "tp"),
            P(None, "tp"),
            P(None, "tp"),
            P("tp", None),
            P("tp"),
            P(),
            P(),
            P(None, "tp"),
            P(None, "tp"),
            P("tp", None),
            P("ep", None, "tp"),
            P("ep", None, "tp"),
            P("ep", "tp", None),
        ),
        check_vma=False,
    )
```

```python
import functools
import math

import jax
import jax.numpy as jnp
import numpy as np
from jax import lax
from jax.experimental import pallas as pl
from jax.experimental.pallas import tpu as pltpu
from jax.sharding import PartitionSpec as P

HD = 128
EPS = 1e-06
ROPE_BASE = 1000000.0
NEG = -1e30
F32 = jnp.float32
BF16 = jnp.bfloat16


def mm(left, right):
    return lax.dot_general(left, right, (((1,), (0,)), ((), ())), preferred_element_type=F32)


def mm_nt(left, right):
    return lax.dot_general(left, right, (((1,), (1,)), ((), ())), preferred_element_type=F32)


def mm_tn(left, right):
    return lax.dot_general(left, right, (((0,), (0,)), ((), ())), preferred_element_type=F32)


def swap(value, axis, bit):
    count = lax.axis_size(axis)
    return lax.ppermute(value, axis, [(i, i ^ bit) for i in range(count)])


def bit_of(axis, bit):
    return (lax.axis_index(axis) // bit) % 2


def half(value, which, dim):
    size = value.shape[dim] // 2
    return lax.dynamic_slice_in_dim(value, which * size, size, dim)


def after(value, *others):
    return lax.optimization_barrier((value, *others))[0]


def reduce_send(value, axis, bit):
    return swap(half(value, 1 - bit_of(axis, bit), 0), axis, bit)


def reduce_add(value, got, axis, bit):
    return (half(value, bit_of(axis, bit), 0).astype(F32) + got.astype(F32)).astype(BF16)


def places():
    count = lax.axis_size("dp")
    dp, ep = lax.axis_index("dp"), lax.axis_index("ep")
    core, x = dp % 2, dp // (count // 2)
    where = (
        {"dp": dp + 1 - 2 * core},
        {"dp": (dp + count // 2) % count},
        {"ep": 1 - ep},
    )
    return core, x, ep, where


def greet_all(peers):
    barrier = pltpu.get_barrier_semaphore()
    for where in peers:
        pl.semaphore_signal(
            barrier, inc=1, device_id=where, device_id_type=pl.DeviceIdType.MESH
        )
    pl.semaphore_wait(barrier, len(peers))


def add_rows(total, more, start, count, out=None):
    step = 32 if count % 32 == 0 else 16

    def turn(k, carry):
        here = pl.ds(pl.multiple_of(k * step, step), step)
        there = pl.ds(pl.multiple_of(start + k * step, step), step)
        value = (total[there, :].astype(F32) + more[here, :].astype(F32)).astype(BF16)
        if out is None:
            total[there, :] = value
        else:
            out[here, :] = value
        return carry

    lax.fori_loop(0, count // step, turn, 0)


def front_kernel(
    scale, chunks, tokens, gains, cotangent, w_query, w_key, w_value, segments, freq,
    x, normed, inv_one, gain_two, grads, query, keys, values, attn, lse, query_seg, key_seg, cos, sin,
    wq_v, wk_v, wv_v, gains_in, l_sem, x_send, x_recv, s_sem, r_sem, kv_send, kv_recv,
):
    n, me = lax.axis_size("tp"), lax.axis_index("tp")
    y = lax.axis_index("ep")
    rows, own = tokens.shape
    heads = query.shape[1] // HD
    step = rows // chunks
    to_y = {"ep": 1 - y}
    tp = [{"tp": (me + d) % n} for d in range(1, n)]

    def remote(source, target, send_sem, recv_sem, where):
        return pltpu.make_async_remote_copy(
            src_ref=source, dst_ref=target, send_sem=send_sem, recv_sem=recv_sem,
            device_id=where, device_id_type=pl.DeviceIdType.MESH,
        )

    def piece(c, s):
        return (pl.ds(c * step, step), pl.ds(pl.multiple_of(s * own, own), own))

    def x_copy(c, s, to_right):
        return remote(
            x.at[piece(c, s)], x.at[piece(c, s)], x_send.at[c, s, 1 if to_right else 0], x_recv.at[c, s],
            {"tp": me + 1 if to_right else me - 1},
        )

    loads = [
        pltpu.make_async_copy(a, b, l_sem.at[m])
        for m, (a, b) in enumerate(((w_key, wk_v), (w_value, wv_v), (w_query, wq_v)))
    ]
    for copy in loads:
        copy.start()
    x[:, pl.ds(pl.multiple_of(me * own, own), own)] = tokens[...]
    gains_in[0] = gains[...]
    greet_all([to_y] + tp)
    for c in range(chunks):

        @pl.when(me > 0)
        def _(c=c):
            x_copy(c, me, False).start()

        @pl.when(me < n - 1)
        def _(c=c):
            x_copy(c, me, True).start()

    g_copies = [remote(gains_in.at[0], gains_in.at[d], s_sem.at[d - 1], r_sem.at[d - 1], tp[d - 1]) for d in range(1, n)]
    for copy in g_copies:
        copy.start()

    at = (y * rows + lax.broadcasted_iota(jnp.int32, (rows, 1), 0)).astype(F32)
    angle = at * freq[...]
    cos[...] = jnp.cos(angle)
    lane = lax.broadcasted_iota(jnp.int32, (1, HD), 1)
    sin[...] = jnp.where(lane < HD // 2, 1.0, -1.0) * jnp.sin(angle)
    whole = segments[...].astype(F32)
    mine = jnp.where(y == 0, whole[:, :rows], whole[:, rows : 2 * rows])
    query_seg[...] = jnp.broadcast_to(mine, (128, rows)).T[:, :1]
    key_seg[:, :rows] = jnp.where(y == 0, -1.0, whole[:, :rows])
    key_seg[:, rows:] = mine

    for d in range(1, n):
        for c in range(chunks):

            @pl.when(me >= d)
            def _(c=c, d=d):
                x_copy(c, me - d, True).wait_recv()

                @pl.when(me < n - 1)
                def _():
                    x_copy(c, me - d, True).start()

            @pl.when(me + d < n)
            def _(c=c, d=d):
                x_copy(c, me + d, False).wait_recv()

                @pl.when(me > 0)
                def _():
                    x_copy(c, me + d, False).start()

    mine_at = pl.ds(pl.multiple_of(me * own, own), own)
    c_copies = [
        remote(cotangent, grads.at[:, mine_at], s_sem.at[n - 2 + d], r_sem.at[n - 2 + d], tp[d - 1]) for d in range(1, n)
    ]
    handed = n == 4
    for d, copy in enumerate(c_copies, 1):

        @pl.when(((me + d) % n - me != n - 1) & (me - (me + d) % n != n - 1) if handed else me >= 0)
        def _(copy=copy):
            copy.start()

    inner = (me > 0) & (me < n - 1)

    def hand_on():
        upward = me == n - 2
        origin = pl.ds(pl.multiple_of(jnp.where(upward, 0, n - 1) * own, own), own)
        arrival = jnp.where(upward, n - 2 + n - 1, n - 2 + 1)
        return remote(
            grads.at[:, origin], grads.at[:, origin], s_sem.at[2 * n - 2], r_sem.at[arrival],
            {"tp": jnp.where(upward, n - 1, 0)},
        )
    own_grads = pltpu.make_async_copy(cotangent, grads.at[:, mine_at], l_sem.at[3])
    own_grads.start()
    for copy in g_copies:
        copy.wait_recv()
    gain_one = []
    for s in range(n):
        row = gains_in[0, :2, :].astype(F32) * jnp.where(me == s, 1.0, 0.0)
        for d in range(1, n):
            row = row + gains_in[d, :2, :].astype(F32) * jnp.where((me - d + n) % n == s, 1.0, 0.0)
        gain_one.append(row[:1])
        gain_two[:, s * own : (s + 1) * own] = row[1:]

    block = min(rows, 128)
    for b in range(rows // block):
        here = slice(b * block, (b + 1) * block)
        square = jnp.zeros((block, 1), F32)
        for s in range(n):
            part = x[here, s * own : (s + 1) * own].astype(F32)
            square = square + jnp.sum(part * part, axis=1, keepdims=True)
        inv = lax.rsqrt(square / (n * own) + EPS)
        inv_one[here, :] = inv
        for s in range(n):
            columns = slice(s * own, (s + 1) * own)
            normed[here, columns] = (x[here, columns].astype(F32) * inv * gain_one[s]).astype(BF16)

    def rope(value):
        return value * cos[...] - pltpu.roll(value, HD // 2, 1) * sin[...]

    loads[0].wait()
    loads[1].wait()
    key_pre = mm(normed[...], wk_v[...])
    value_pre = mm(normed[...], wv_v[...])

    @pl.when(y == 0)
    def _():
        keys[:rows, :] = jnp.zeros((rows, heads * HD), BF16)
        values[:rows, :] = jnp.zeros((rows, heads * HD), BF16)

    def kv_copy(h, m):
        array = (keys, values)[m]
        part = pl.ds(h * HD, HD)
        return remote(
            array.at[pl.ds(rows, rows), part], array.at[pl.ds(0, rows), part], kv_send.at[h, m], kv_recv.at[h, m], to_y
        )

    for h in range(heads):
        part = slice(h * HD, (h + 1) * HD)
        keys[rows:, part] = rope(key_pre[:, part]).astype(BF16)
        values[rows:, part] = value_pre[:, part].astype(BF16)

        @pl.when(y == 0)
        def _(h=h):
            kv_copy(h, 0).start()
            kv_copy(h, 1).start()

    loads[2].wait()
    query_pre = mm(normed[...], wq_v[...])
    for h in range(heads):
        part = slice(h * HD, (h + 1) * HD)
        query[:, part] = rope(query_pre[:, part]).astype(BF16)

    if handed:

        @pl.when(inner)
        def _():
            c_copies[1].wait_recv()
            hand_on().start()

    key_at = (y - 1) * rows + lax.broadcasted_iota(jnp.int32, (1, 2 * rows), 1)
    query_at = y * rows + lax.broadcasted_iota(jnp.int32, (rows, 1), 0)
    allowed = (query_seg[...] == key_seg[...]) & (key_at <= query_at)
    for h in range(heads):
        part = slice(h * HD, (h + 1) * HD)

        @pl.when(y == 1)
        def _(h=h):
            kv_copy(h, 0).wait_recv()
            kv_copy(h, 1).wait_recv()

        scores = jnp.where(allowed, mm_nt(query[:, part], keys[:, part]) * scale, NEG)
        top = jnp.max(scores, axis=1, keepdims=True)
        shifted = jnp.exp(scores - top)
        total = jnp.sum(shifted, axis=1, keepdims=True)
        weights = (shifted * (1.0 / total)).astype(BF16)
        attn[:, part] = mm(weights, values[:, part]).astype(BF16)
        lse[:, h : h + 1] = top + jnp.log(total)

    for h in range(heads):

        @pl.when(y == 0)
        def _(h=h):
            kv_copy(h, 0).wait_send()
            kv_copy(h, 1).wait_send()

    for c in range(chunks):
        for s in range(n):

            @pl.when((s <= me) & (me < n - 1))
            def _(c=c, s=s):
                x_copy(c, s, True).wait_send()

            @pl.when((s >= me) & (me > 0))
            def _(c=c, s=s):
                x_copy(c, s, False).wait_send()

    own_grads.wait()
    for d, copy in enumerate(c_copies, 1):

        if handed and d == 2:

            @pl.when(jnp.logical_not(inner))
            def _(copy=copy):
                copy.wait_recv()

        else:
            copy.wait_recv()

        @pl.when(((me + d) % n - me != n - 1) & (me - (me + d) % n != n - 1) if handed else me >= 0)
        def _(copy=copy):
            copy.wait_send()

    if handed:

        @pl.when(inner)
        def _():
            hand_on().wait_send()

    for copy in g_copies:
        copy.wait_send()


def front(tokens, gains, cotangent, w_query, w_key, w_value, segments, freq):
    rows, own = tokens.shape
    n = lax.axis_size("tp")
    width = n * own
    mine = w_query.shape[1]
    heads = mine // HD
    chunks = 8 if n <= 4 else 2
    far = pl.BlockSpec(memory_space=pl.ANY)
    vmem = pl.BlockSpec(memory_space=pltpu.VMEM)
    dma = pltpu.SemaphoreType.DMA

    def shape(*dims, kind=BF16):
        return jax.ShapeDtypeStruct(dims, kind)

    return pl.pallas_call(
        functools.partial(front_kernel, 1.0 / math.sqrt(HD), chunks),
        out_shape=[
            shape(rows, width), shape(rows, width), shape(rows, 1, kind=F32), shape(1, width, kind=F32),
            shape(rows, width), shape(rows, mine), shape(2 * rows, mine), shape(2 * rows, mine), shape(rows, mine),
            shape(rows, heads, kind=F32), shape(rows, 1, kind=F32), shape(1, 2 * rows, kind=F32),
            shape(rows, HD, kind=F32), shape(rows, HD, kind=F32),
        ],
        in_specs=[vmem] * 2 + [far] * 4 + [vmem] * 2,
        out_specs=[vmem] * 4 + [far] + [vmem] * 9,
        scratch_shapes=[pltpu.VMEM((width, mine), BF16)] * 3
        + [pltpu.VMEM((n, 16, own), BF16), dma((4,)), dma((chunks, n, 2)), dma((chunks, n))]
        + [dma((2 * n,)), dma((2 * n,)), dma((heads, 2)), dma((heads, 2))],
        compiler_params=pltpu.CompilerParams(
            collective_id=7, has_side_effects=True, vmem_limit_bytes=62 << 20
        ),
        cost_estimate=pl.CostEstimate(flops=0, bytes_accessed=0, transcendentals=0),
    )(tokens, gains, cotangent, w_query, w_key, w_value, segments, freq)


def tail_kernel(
    scale,
    sgu, sd, egu, ed, flat, normed, w_query, w_key, w_value, attn, ffn,
    tokens, inv_one, low, w_out, query, keys, values, lse, query_seg, key_seg, cos, sin,
    sgu_f, sd_f, egu_f, ed_f, qkv_f, wo_f, flat_f, ffn_own, normed_own, row_total, gain_f,
    normed_v, wq_v, wk_v, wv_v, attn_v, grad_attn, grad_key, grad_value, early, came, grad_qkv,
    q_sent, q_half, q_in, q_in2, q_out, w_sent, w_half, w_in, w_in2, w_out_v,
    e_own, e_in, flat_in, ffn_in, grad_normed, normed_in, row_in, gain_in, l_sem, s_sem, r_sem,
):
    core, x, y, (to_core, to_x, to_y) = places()
    used = [0, 0]
    sent = []

    def here(source, target):
        k = used[0]
        used[0] += 1
        copy = pltpu.make_async_copy(source, target, l_sem.at[k])
        copy.start()
        return copy

    def remote(source, target, where):
        k = used[1]
        used[1] += 1
        return pltpu.make_async_remote_copy(
            src_ref=source, dst_ref=target, send_sem=s_sem.at[k], recv_sem=r_sem.at[k],
            device_id=where, device_id_type=pl.DeviceIdType.MESH,
        )

    def there(source, target, where):
        copy = remote(source, target, where)
        copy.start()
        sent.append(copy)
        return copy

    rows = query.shape[0]
    heads = query.shape[1] // HD
    mine = heads * HD
    q_rows, w_rows = q_in.shape[0], w_in.shape[0]
    e_rows = e_own.shape[0]
    n, me = lax.axis_size("tp"), lax.axis_index("tp")
    tp = [{"tp": (me + d) % n} for d in range(1, n)]
    own_width = ffn_own.shape[1]

    def columns(d):
        return pl.ds(pl.multiple_of(((me + d) % n) * own_width, own_width), own_width)

    greet_all([to_core, to_x, to_y] + tp)

    b3 = there(egu.at[pl.ds((1 - x) * e_rows, e_rows)], e_in, to_x)
    b6 = there(ed, ed_f.at[core, x], to_x)
    d3 = [there(sd.at[0], sd_f.at[core, 0, y], to_y)]
    f1 = there(flat, flat_in.at[0], to_core)
    z_ffn = [there(ffn.at[:, columns(d)], ffn_in.at[d], tp[d - 1]) for d in range(1, n)]
    own_ffn = here(ffn.at[:, columns(0)], ffn_in.at[0])
    load_attn = here(attn, attn_v)
    load_normed = here(normed, normed_v)
    loads = [here(w_query, wq_v), here(w_key, wk_v), here(w_value, wv_v)]
    load_e = here(egu.at[pl.ds(x * e_rows, e_rows)], e_own)
    own_ed = here(ed, ed_f.at[core, x])
    own_s = here(sgu, sgu_f.at[core, y])
    own_sd = [here(sd.at[p], sd_f.at[core, p, y]) for p in range(2)]

    grad_attn[...] = mm_nt(low[...], w_out[...]).astype(BF16)
    key_at = (y - 1) * rows + lax.broadcasted_iota(jnp.int32, (1, 2 * rows), 1)
    query_at = y * rows + lax.broadcasted_iota(jnp.int32, (rows, 1), 0)
    allowed = (query_seg[...] == key_seg[...]) & (key_at <= query_at)
    sums_of = jnp.zeros((rows, 1), F32)
    early_copies = []
    for h in range(heads):
        own = slice(h * HD, (h + 1) * HD)
        q, k, v, g = query[:, own], keys[:, own], values[:, own], grad_attn[:, own]
        scores = jnp.where(allowed, mm_nt(q, k) * scale, NEG)
        probs = jnp.exp(scores - lse[:, h : h + 1])
        grad_probs = mm_nt(g, v)
        weighted = probs * grad_probs
        grad_scores = (weighted - probs * jnp.sum(weighted, axis=1, keepdims=True)).astype(BF16)
        grad_q = mm(grad_scores, k) * scale
        grad_k = mm_tn(grad_scores, q) * scale
        grad_v = mm_tn(probs.astype(BF16), g)
        grad_key[:, own] = grad_k[rows:]
        grad_value[:, own] = grad_v[rows:]
        early[h, 0] = grad_k[:rows].astype(BF16)
        early[h, 1] = grad_v[:rows].astype(BF16)
        copy = remote(early.at[h], came.at[h], to_y)
        early_copies.append(copy)

        @pl.when(y == 1)
        def _(copy=copy):
            copy.start()

        sums_of = sums_of + jnp.sum(grad_q * q.astype(F32), axis=1, keepdims=True)
        turned = grad_q * cos[...] + pltpu.roll(grad_q, HD // 2, 1) * sin[...]
        grad_qkv[:, own] = turned.astype(BF16)

    d1 = there(sgu.at[0], sgu_f.at[core, y, 0], to_y)
    load_attn.wait()
    half_of = low.shape[1] // 2
    w_sent[...] = mm_tn(attn_v[...], low[:, pl.ds(pl.multiple_of((1 - core) * half_of, half_of), half_of)]).astype(BF16)
    a0 = there(w_sent, w_half, to_core)
    w_own = mm_tn(attn_v[...], low[:, pl.ds(pl.multiple_of(core * half_of, half_of), half_of)])
    f1.wait_recv()
    flat_f[...] = flat[...] + flat_in[0]
    f2 = there(flat_f, flat_in.at[1], to_x)
    a0.wait_recv()
    w_half[...] = (w_own + w_half[...].astype(F32)).astype(BF16)
    a2 = there(w_half.at[pl.ds((1 - y) * w_rows, w_rows)], w_in, to_y)

    for h in range(heads):
        own = slice(h * HD, (h + 1) * HD)

        @pl.when(y == 0)
        def _(h=h, own=own):
            early_copies[h].wait_recv()
            grad_key[:, own] = grad_key[:, own] + came[h, 0].astype(F32)
            grad_value[:, own] = grad_value[:, own] + came[h, 1].astype(F32)

        @pl.when(y == 1)
        def _(h=h):
            early_copies[h].wait_send()

        grad_k, grad_v = grad_key[:, own], grad_value[:, own]
        sums_of = sums_of + jnp.sum(
            grad_k * keys[rows:, own].astype(F32) + grad_v * values[rows:, own].astype(F32),
            axis=1, keepdims=True,
        )
        turned = grad_k * cos[...] + pltpu.roll(grad_k, HD // 2, 1) * sin[...]
        grad_qkv[:, mine + h * HD : mine + (h + 1) * HD] = turned.astype(BF16)
        grad_qkv[:, 2 * mine + h * HD : 2 * mine + (h + 1) * HD] = grad_v.astype(BF16)
    row_in[0] = jnp.broadcast_to(sums_of, (rows, 128)).T[:8]
    z_rows = [there(row_in.at[0], row_in.at[d], tp[d - 1]) for d in range(1, n)]

    load_normed.wait()
    tall = q_half.shape[0]
    step = tall // 4

    def product(i, which):
        start = pl.multiple_of(which * tall + i * step, step)
        return mm_tn(normed_v[:, pl.ds(start, step)], grad_qkv[...])

    a0q = []
    for i in range(4):
        q_sent[i * step : (i + 1) * step, :] = product(i, 1 - core).astype(BF16)
        a0q.append(there(q_sent.at[pl.ds(i * step, step)], q_half.at[pl.ds(i * step, step)], to_core))
    for i in range(4):
        value = product(i, core)
        a0q[i].wait_recv()
        here_rows = slice(i * step, (i + 1) * step)
        q_half[here_rows, :] = (value + q_half[here_rows, :].astype(F32)).astype(BF16)
    a1 = there(q_half.at[pl.ds((1 - y) * q_rows, q_rows)], q_in, to_y)
    d2 = there(sgu.at[1], sgu_f.at[core, y, 1], to_y)
    for copy in loads:
        copy.wait()
    grad_normed[...] = (
        mm_nt(grad_qkv[:, :mine], wq_v[...])
        + mm_nt(grad_qkv[:, mine : 2 * mine], wk_v[...])
        + mm_nt(grad_qkv[:, 2 * mine :], wv_v[...])
    ).astype(BF16)
    z_normed = [there(grad_normed.at[:, columns(d)], normed_in.at[d], tp[d - 1]) for d in range(1, n)]

    load_e.wait()
    b3.wait_recv()
    add_rows(e_own, e_in, 0, e_rows)
    cut, cut_b = e_rows // 64 * 16, e_rows * 5 // 128 * 16
    b5a = there(e_own.at[pl.ds(0, cut)], egu_f.at[core, x, pl.ds(0, cut)], to_x)
    f2.wait_recv()
    f2.wait_send()
    flat_f[...] = flat_f[...] + flat_in[1]
    f3 = there(flat_f, flat_in.at[2], to_y)
    a2.wait_recv()
    add_rows(w_half, w_in, y * w_rows, w_rows)
    a4 = there(w_half.at[pl.ds(y * w_rows + (1 - x) * (w_rows // 2), w_rows // 2)], w_in2, to_x)
    a1.wait_recv()
    add_rows(q_half, q_in, y * q_rows, q_rows)
    a3 = there(q_half.at[pl.ds(y * q_rows + (1 - x) * (q_rows // 2), q_rows // 2)], q_in2, to_x)
    own_e = here(e_own, egu_f.at[core, x])
    d3.append(there(sd.at[1], sd_f.at[core, 1, y], to_y))
    for copy in z_normed + z_rows:
        copy.wait_recv()
    total = grad_normed[:, columns(0)].astype(F32)
    row_sum = row_in[0]
    for d in range(1, n):
        total = total + normed_in[d].astype(F32)
        row_sum = row_sum + row_in[d]
    normed_own[...] = total
    row_total[...] = row_sum
    gain = jnp.sum(total * tokens[...].astype(F32) * inv_one[...], axis=0, keepdims=True)
    gain_f[...] = jnp.broadcast_to(gain, gain_f.shape)
    g1 = there(gain_f, gain_in.at[0], to_core)
    a4.wait_recv()
    add_rows(w_half, w_in2, y * w_rows + x * (w_rows // 2), w_rows // 2, w_out_v)
    a6 = there(w_out_v, wo_f.at[core, y, x], to_x)
    own_w = here(w_out_v, wo_f.at[core, y, x])
    g1.wait_recv()
    g1.wait_send()
    gain_f[...] = gain_f[...] + gain_in[0]
    g2 = there(gain_f, gain_in.at[1], to_x)
    a3.wait_recv()
    add_rows(q_half, q_in2, y * q_rows + x * (q_rows // 2), q_rows // 2, q_out)
    a5 = there(q_out, qkv_f.at[core, y, x], to_x)
    own_q = here(q_out, qkv_f.at[core, y, x])
    b5 = there(e_own.at[pl.ds(cut, cut_b - cut)], egu_f.at[core, x, pl.ds(cut, cut_b - cut)], to_x)
    b7 = there(e_own.at[pl.ds(cut_b, e_rows - cut_b)], egu_f.at[core, x, pl.ds(cut_b, e_rows - cut_b)], to_x)
    own_ffn.wait()
    for copy in z_ffn:
        copy.wait_recv()
    total = ffn_in[0].astype(F32)
    for d in range(1, n):
        total = total + ffn_in[d].astype(F32)
    ffn_own[...] = total
    own_ed.wait()
    b6.wait_recv()
    c6 = there(ed_f.at[core], ed_f.at[core], to_core)
    own_s.wait()
    d1.wait_recv()
    d2.wait_recv()
    c1 = there(sgu_f.at[core], sgu_f.at[core], to_core)
    g2.wait_recv()
    g2.wait_send()
    gain_f[...] = gain_f[...] + gain_in[1]
    g3 = there(gain_f, gain_in.at[2], to_y)
    a6.wait_recv()
    own_w.wait()
    a8 = there(wo_f.at[core, y], wo_f.at[core, y], to_y)
    a5.wait_recv()
    own_q.wait()
    a7 = there(qkv_f.at[core, y], qkv_f.at[core, y], to_y)
    for copy in own_sd:
        copy.wait()
    for copy in d3:
        copy.wait_recv()
    c2 = there(sd_f.at[core], sd_f.at[core], to_core)
    f3.wait_recv()
    f3.wait_send()
    flat_f[...] = flat_f[...] + flat_in[2]
    own_e.wait()
    b5a.wait_recv()
    b5.wait_recv()
    c3 = there(egu_f.at[core, :, pl.ds(0, cut_b)], egu_f.at[core, :, pl.ds(0, cut_b)], to_core)
    b7.wait_recv()
    rest = pl.ds(cut_b, e_rows - cut_b)
    c7 = there(egu_f.at[core, :, rest], egu_f.at[core, :, rest], to_core)
    a8.wait_recv()
    c5 = there(wo_f.at[core], wo_f.at[core], to_core)
    a7.wait_recv()
    c4 = there(qkv_f.at[core], qkv_f.at[core], to_core)
    g3.wait_recv()
    g3.wait_send()
    gain_f[...] = gain_f[...] + gain_in[2]
    for copy in (c1, c2, c3, c4, c5, c6, c7):
        copy.wait_recv()
    for copy in sent:
        if all(copy is not other for other in (f2, f3, g1, g2, g3)):
            copy.wait_send()


def tail(sgu, sd, egu, ed, flat, normed, w_query, w_key, w_value, attn, ffn, tokens, inv_one, low, w_out, query, keys, values, lse, query_seg, key_seg, cos, sin):
    rows, width = low.shape
    mine = query.shape[1]
    heads = mine // HD

    def pieces(count, height, wide):
        return jax.ShapeDtypeStruct((2,) * count + (height, wide), BF16)

    far = pl.BlockSpec(memory_space=pl.ANY)
    vmem = pl.BlockSpec(memory_space=pltpu.VMEM)

    def room(*shape, kind=BF16):
        return pltpu.VMEM(shape, kind)

    half_of = width // 2
    n = lax.axis_size("tp")
    dma = pltpu.SemaphoreType.DMA
    return pl.pallas_call(
        functools.partial(tail_kernel, 1.0 / math.sqrt(HD)),
        out_shape=[
            pieces(3, *sgu.shape[1:]), pieces(3, *sd.shape[1:]),
            pieces(2, egu.shape[0] // 2, egu.shape[1]), pieces(2, *ed.shape),
            pieces(3, half_of // 4, 3 * mine), pieces(3, mine // 4, half_of),
            jax.ShapeDtypeStruct(flat.shape, F32), jax.ShapeDtypeStruct(tokens.shape, F32),
            jax.ShapeDtypeStruct(tokens.shape, F32), jax.ShapeDtypeStruct((8, rows), F32),
            jax.ShapeDtypeStruct((8, tokens.shape[1]), F32),
        ],
        in_specs=[far] * 4 + [vmem] + [far] * 6 + [vmem] * 12,
        out_specs=[far] * 6 + [vmem] * 5,
        scratch_shapes=[
            room(rows, width), room(width, mine), room(width, mine), room(width, mine), room(rows, mine),
            room(rows, mine), room(rows, mine, kind=F32), room(rows, mine, kind=F32),
            room(heads, 2, rows, HD), room(heads, 2, rows, HD), room(rows, 3 * mine),
            room(half_of, 3 * mine), room(half_of, 3 * mine), room(half_of // 2, 3 * mine),
            room(half_of // 4, 3 * mine), room(half_of // 4, 3 * mine),
            room(mine, half_of), room(mine, half_of), room(mine // 2, half_of),
            room(mine // 4, half_of), room(mine // 4, half_of),
            room(egu.shape[0] // 2, egu.shape[1]), room(egu.shape[0] // 2, egu.shape[1]),
            room(3, *flat.shape, kind=F32), room(n, *tokens.shape), room(rows, width), room(n, *tokens.shape),
            room(n, 8, rows, kind=F32), room(3, 8, tokens.shape[1], kind=F32),
            dma((16,)), dma((38 + heads + 3 * n,)), dma((38 + heads + 3 * n,)),
        ],
        compiler_params=pltpu.CompilerParams(
            collective_id=3, has_side_effects=True, vmem_limit_bytes=62 << 20
        ),
        cost_estimate=pl.CostEstimate(flops=0, bytes_accessed=0, transcendentals=0),
    )(sgu, sd, egu, ed, flat, normed, w_query, w_key, w_value, attn, ffn, tokens, inv_one, low, w_out, query, keys, values, lse, query_seg, key_seg, cos, sin)


def widen_kernel(source, *outputs):
    value = source[...]
    value = value.reshape(value.shape[-2:])
    start = 0
    for out in outputs:
        width = out.shape[1]
        out[...] = value[:, start : start + width].astype(F32)
        start += width


def widen(value, widths=(), kinds=1, kind=0, across=2):
    columns = value.shape[-1]
    if widths:
        value = value.reshape(-1, columns)
        rows = value.shape[0]
        step = min(rows, 256)
        source = pl.BlockSpec((step, columns), lambda i: (i, 0))
        grid = (rows // step,)
        specs = [pl.BlockSpec((step, width), lambda i: (i, 0)) for width in widths]
        shapes = [jax.ShapeDtypeStruct((rows, width), F32) for width in widths]
    else:
        value = value.reshape(across, kinds, -1, columns)
        rows = value.shape[2]
        step = rows
        while step * columns > (1 << 19) and step % 32 == 0:
            step //= 2
        steps = rows // step
        source = pl.BlockSpec((1, 1, step, columns), lambda i, c: (c, kind, i, 0))
        grid = (steps, across)
        specs = [pl.BlockSpec((step, columns), lambda i, c: (i, c))]
        shapes = [jax.ShapeDtypeStruct((rows, across * columns), F32)]
    return pl.pallas_call(
        widen_kernel,
        grid=grid,
        in_specs=[source],
        out_specs=specs,
        out_shape=shapes,
        compiler_params=pltpu.CompilerParams(vmem_limit_bytes=32 << 20),
        cost_estimate=pl.CostEstimate(flops=0, bytes_accessed=0, transcendentals=0),
    )(value)


def weight_kernel(added, part, left, right, *refs):
    total = mm_tn(left[...], right[...])
    if added:
        total = total + refs[0][...].astype(F32)
    refs[-1][...] = total.astype(BF16)


def weight_half(left, right, which, columns, got=None, rows=None, block=1408):
    rows = rows or left.shape[0]
    height, wide = left.shape[1], right.shape[1]
    if columns:
        wide = wide // 2
    else:
        height = height // 2
    step = height
    while step > block and step % 256 == 0:
        step //= 2
    steps = height // step
    extra = [] if got is None else [got]
    out_spec = pl.BlockSpec((step, wide), lambda i, part: (i, 0))
    if columns:
        left_at, right_at = (lambda i, part: (0, i)), (lambda i, part: (0, part[0]))
    else:
        left_at, right_at = (lambda i, part: (0, part[0] * steps + i)), (lambda i, part: (0, 0))
    return pl.pallas_call(
        functools.partial(weight_kernel, bool(extra)),
        grid_spec=pltpu.PrefetchScalarGridSpec(
            num_scalar_prefetch=1,
            grid=(steps,),
            in_specs=[pl.BlockSpec((rows, step), left_at), pl.BlockSpec((rows, wide), right_at)]
            + [out_spec] * len(extra),
            out_specs=out_spec,
        ),
        out_shape=jax.ShapeDtypeStruct((height, wide), BF16),
        compiler_params=pltpu.CompilerParams(vmem_limit_bytes=48 << 20),
        cost_estimate=pl.CostEstimate(flops=0, bytes_accessed=0, transcendentals=0),
    )(which.reshape(1).astype(jnp.int32), left, right, *extra)


def ffn_kernel(groups, base, into, flipped, carry, *refs):
    rows, grads, scale, *stored = refs[:6]
    refs = refs[6:]
    if base:
        base_out, base_dx = refs[:2]
        refs = refs[2:]
    if into:
        refs = refs[2:]
    sources, refs = refs[: len(carry)], refs[len(carry) :]
    hid_ref, dgu_ref, out_ref, dx_ref, small_ref, *refs = refs
    *refs, gate_w, up_w, down_w, w_sem = refs
    weights = [
        pltpu.make_async_copy(source, target, w_sem.at[m])
        for m, (source, target) in enumerate(zip(stored, (gate_w, up_w, down_w)))
    ]

    @pl.when(pl.program_id(0) == 0)
    def _():
        for copy in weights:
            copy.start()

    copies = []
    if carry:
        send_sem, recv_sem = refs[-2:]
        _, x, y, where = places()
        for m, (link, count, start, stride) in enumerate(carry):
            first = start + (1 - (x, y)[link - 1]) * stride
            copies.append(
                pltpu.make_async_remote_copy(
                    src_ref=sources[m].at[pl.ds(first, count)], dst_ref=refs[m],
                    send_sem=send_sem.at[m], recv_sem=recv_sem.at[m],
                    device_id=where[link], device_id_type=pl.DeviceIdType.MESH,
                )
            )
        links = sorted({link for link, _, _, _ in carry})

        @pl.when(pl.program_id(0) == 0)
        def _():
            greet_all([where[link] for link in links])
            for copy in copies:
                copy.start()

    @pl.when(pl.program_id(0) == 0)
    def _():
        for copy in weights:
            copy.wait()

    width = down_w.shape[0]
    to, back = (mm_nt, mm) if flipped else (mm, mm_nt)
    gate_pre = to(rows[...], gate_w[...])
    up_pre = to(rows[...], up_w[...])
    grad_hidden = mm_nt(grads[...], down_w[...])
    sig = 1.0 / (1.0 + jnp.exp(-gate_pre))
    act = gate_pre * sig
    slope = sig + act * (1.0 - sig)
    hidden = (act * up_pre).astype(BF16).astype(F32)
    each = width // groups
    column = lax.broadcasted_iota(jnp.int32, (1, width), 1)
    wide = scale[:, 0:1]
    for e in range(1, groups):
        wide = jnp.where(column >= e * each, scale[:, e : e + 1], wide)
    prod = hidden * grad_hidden
    for e in range(groups):
        part = prod
        if groups > 1:
            part = jnp.where((column >= e * each) & (column < (e + 1) * each), prod, 0.0)
        small_ref[:, e : e + 1] = jnp.sum(part, axis=1, keepdims=True)
    hid = (hidden * wide).astype(BF16)
    hid_ref[...] = hid
    scaled = grad_hidden * wide
    dgate = (scaled * up_pre * slope).astype(BF16)
    dup = (scaled * act).astype(BF16)
    dgu_ref[:, :width] = dgate
    dgu_ref[:, width:] = dup
    small_ref[:, groups : groups + 1] = jnp.sum(
        dgate.astype(F32) * gate_pre + dup.astype(F32) * up_pre, axis=1, keepdims=True
    )
    out = mm(hid, down_w[...])
    dx = back(dgate, gate_w[...]) + back(dup, up_w[...])
    if base:
        out = out + base_out[...].astype(F32)
        dx = dx + base_dx[...].astype(F32)
    out_ref[...] = out.astype(BF16)
    dx_ref[...] = dx.astype(BF16)
    if carry:

        @pl.when(pl.program_id(0) == pl.num_programs(0) - 1)
        def _():
            for copy in copies:
                copy.wait()


def ffn(rows, grads, scale, gate_w, up_w, down_w, start=0, total=0, base=(), into=(), flipped=False, carry=(), number=None):
    count, groups = scale.shape
    width = rows.shape[1]
    hidden = down_w.shape[0]
    block = min(256, count)
    first = start // block
    total = total or count
    place = first if total > count else 0

    def at(n, offset):
        return pl.BlockSpec((block, n), lambda i: (i + offset, 0))

    far = pl.BlockSpec(memory_space=pl.ANY)
    return pl.pallas_call(
        functools.partial(
            ffn_kernel, groups, bool(base), bool(into), flipped, tuple(c[1:] for c in carry)
        ),
        grid=(count // block,),
        in_specs=[at(width, first), at(width, first), at(groups, 0)]
        + [far] * 3
        + [at(width, 0)] * len(base)
        + [far] * (len(into) + len(carry)),
        out_specs=[
            at(hidden, place),
            at(2 * hidden, place),
            at(width, 0),
            at(width, 0),
            at(groups + 1, 0),
        ]
        + [far] * len(carry),
        out_shape=[
            jax.ShapeDtypeStruct((total, hidden), BF16),
            jax.ShapeDtypeStruct((total, 2 * hidden), BF16),
            jax.ShapeDtypeStruct((count, width), BF16),
            jax.ShapeDtypeStruct((count, width), BF16),
            jax.ShapeDtypeStruct((count, groups + 1), F32),
        ]
        + [jax.ShapeDtypeStruct((c[2], c[0].shape[1]), BF16) for c in carry],
        scratch_shapes=([pltpu.SemaphoreType.DMA((len(carry),))] * 2 if carry else [])
        + [pltpu.VMEM(w.shape, BF16) for w in (gate_w, up_w, down_w)]
        + [pltpu.SemaphoreType.DMA((3,))],
        input_output_aliases={6 + len(base) + k: k for k in range(len(into))},
        compiler_params=pltpu.CompilerParams(
            vmem_limit_bytes=62 << 20, collective_id=number, has_side_effects=bool(carry)
        ),
        cost_estimate=pl.CostEstimate(flops=0, bytes_accessed=0, transcendentals=0),
    )(rows, grads, scale, gate_w, up_w, down_w, *base, *into, *[c[0] for c in carry])


def line_sum(depth, prepare, settle, gathered, beside, part, came, came_two, spread, sems):
    n = lax.axis_size("tp")
    me = lax.axis_index("tp")
    chunks, _, step, _ = part.shape
    sum_send, sum_recv, two_recv, out_send, out_recv = sems

    def send(source, target, send_sem, recv_sem, to):
        return pltpu.make_async_remote_copy(
            src_ref=source, dst_ref=target, send_sem=send_sem, recv_sem=recv_sem,
            device_id={"tp": to}, device_id_type=pl.DeviceIdType.MESH,
        )

    def sum_copy(c, s, to_right, two):
        target = came_two.at[c] if two else came.at[c, s]
        sem = two_recv.at[c] if two else sum_recv.at[c, s]
        return send(part.at[c, s], target, sum_send.at[c, s], sem, me + 1 if to_right else me - 1)

    def out_copy(c, s, to_right):
        return send(
            spread.at[c, s], spread.at[c, s], out_send.at[c, s, 1 if to_right else 0],
            out_recv.at[c, s], me + 1 if to_right else me - 1,
        )

    def within(c):
        return (c >= 0) & (c < chunks)

    def pass_sums(t):
        @pl.when(within(t))
        def _():
            prepare(t)

        for s in range(n):
            c = t - me * depth

            @pl.when((me < s) & within(c))
            def _(s=s, c=c):
                @pl.when(me > 0)
                def _():
                    sum_copy(c, s, True, False).wait_recv()
                    part[c, s] = (part[c, s].astype(F32) + came[c, s].astype(F32)).astype(BF16)

                sum_copy(c, s, True, False).start()

        for s in range(n):
            c = t - (n - 1 - me) * depth

            @pl.when((me > s) & within(c))
            def _(s=s, c=c):
                @pl.when(me < n - 1)
                def _():
                    sum_copy(c, s, False, False).wait_recv()
                    part[c, s] = (part[c, s].astype(F32) + came[c, s].astype(F32)).astype(BF16)

                @pl.when(me - 1 == s)
                def _():
                    sum_copy(c, s, False, True).start()

                @pl.when(me - 1 > s)
                def _():
                    sum_copy(c, s, False, False).start()

    def pass_own(t):
        c = t - (n - 1) * depth
        for s in range(n):

            @pl.when((me == s) & within(c))
            def _(s=s):
                if s > 0:
                    sum_copy(c, s, True, False).wait_recv()
                if s < n - 1:
                    sum_copy(c, s, False, True).wait_recv()
                total = part[c, s].astype(F32)
                if s > 0:
                    total = total + came[c, s].astype(F32)
                if s < n - 1:
                    total = total + came_two[c].astype(F32)
                spread[c, s] = settle(c, total)
                if s > 0:
                    out_copy(c, s, False).start()
                if s < n - 1:
                    out_copy(c, s, True).start()

    def pass_out(t):
        for s in range(n):
            right = t - (n - 1 + me - s) * depth
            left = t - (n - 1 + s - me) * depth

            @pl.when((me > s) & within(right))
            def _(s=s, c=right):
                out_copy(c, s, True).wait_recv()

                @pl.when(me < n - 1)
                def _():
                    out_copy(c, s, True).start()

            @pl.when((me < s) & within(left))
            def _(s=s, c=left):
                out_copy(c, s, False).wait_recv()

                @pl.when(me > 0)
                def _():
                    out_copy(c, s, False).start()

        last = t - 2 * (n - 1) * depth

        @pl.when(within(last))
        def _():
            gathered(last)

    def turn(t, carry):
        pass_sums(t)
        pass_own(t)
        pass_out(t)
        if beside is not None:
            beside(t)
        return carry

    lax.fori_loop(0, chunks + 2 * (n - 1) * depth, turn, 0)

    def drain(c, carry):
        for s in range(n):

            @pl.when(me != s)
            def _(s=s):
                sum_copy(c, s, True, False).wait_send()

            @pl.when((me < n - 1) & (s <= me))
            def _(s=s):
                out_copy(c, s, True).wait_send()

            @pl.when((me > 0) & (s >= me))
            def _(s=s):
                out_copy(c, s, False).wait_send()

        return carry

    lax.fori_loop(0, chunks, drain, 0)


def line_scratch(rows, width_own):
    n = lax.axis_size("tp")
    chunks = max(1, min(16, 128 // n))
    step = rows // chunks
    slots = pltpu.VMEM((chunks, n, step, width_own), BF16)
    dma = pltpu.SemaphoreType.DMA
    return chunks, step, [
        slots, slots, pltpu.VMEM((chunks, step, width_own), BF16), slots,
        dma((chunks, n)), dma((chunks, n)), dma((chunks,)), dma((chunks, n, 2)), dma((chunks, n)),
    ]


def greet(peers):
    n = lax.axis_size("tp")
    me = lax.axis_index("tp")
    barrier = pltpu.get_barrier_semaphore()

    def signal(where):
        pl.semaphore_signal(barrier, inc=1, device_id=where, device_id_type=pl.DeviceIdType.MESH)

    @pl.when(me > 0)
    def _():
        signal({"tp": me - 1})

    @pl.when(me < n - 1)
    def _():
        signal({"tp": me + 1})

    for where in peers:
        signal(where)

    beside = jnp.where(me > 0, 1, 0) + jnp.where(me < n - 1, 1, 0)
    pl.semaphore_wait(barrier, beside + len(peers))


def attend_out_kernel(
    chunks, step, depth, eps, attn, w_out, x, gain, grads,
    mixed, resid_own, inv_out, grads_peer,
    part, came, came_two, spread, s0, s1, s2, s3, s4, y_send, y_recv, g_send, g_recv,
):
    n = lax.axis_size("tp")
    me = lax.axis_index("tp")
    own = part.shape[3]
    rows = attn.shape[0]
    other = {"ep": 1 - lax.axis_index("ep")}
    greet([other])
    grads_copy = pltpu.make_async_remote_copy(
        src_ref=grads.at[pl.ds(0, grads_peer.shape[0])], dst_ref=grads_peer, send_sem=g_send, recv_sem=g_recv,
        device_id=other, device_id_type=pl.DeviceIdType.MESH,
    )
    grads_copy.start()
    block = max(step, min(rows, 128))

    def product(b, carry):
        start = pl.multiple_of(b * block, block)
        value = mm(attn[pl.ds(start, block), :], w_out[...]).astype(BF16)
        for s in range(n):
            for k in range(block // step):
                part[b * (block // step) + k, s] = value[k * step:(k + 1) * step, s * own:(s + 1) * own]
        return carry

    lax.fori_loop(0, rows // block, product, 0)

    def at(c):
        return pl.ds(pl.multiple_of(c * step, step), step)

    def peer_copy(c):
        return pltpu.make_async_remote_copy(
            src_ref=mixed.at[at(c)], dst_ref=mixed.at[pl.ds(pl.multiple_of(rows + c * step, step), step)], send_sem=y_send.at[c], recv_sem=y_recv.at[c],
            device_id=other, device_id_type=pl.DeviceIdType.MESH,
        )

    def prepare(c):
        pass

    def settle(c, total):
        return total.astype(BF16)

    def gathered(c):
        resid = []
        square = jnp.zeros((step, 1), F32)
        for s in range(n):
            piece = x[at(c), s * own:(s + 1) * own].astype(F32) + spread[c, s].astype(F32)
            resid.append(piece)
            square = square + jnp.sum(piece * piece, axis=1, keepdims=True)
        inv = lax.rsqrt(square / (n * own) + eps)
        inv_out[at(c), :] = inv
        for s in range(n):
            mixed[at(c), s * own:(s + 1) * own] = (resid[s] * inv * gain[:, s * own:(s + 1) * own]).astype(BF16)

            @pl.when(me == s)
            def _(s=s):
                resid_own[at(c), :] = resid[s]

        peer_copy(c).start()

    line_sum(depth, prepare, settle, gathered, None, part, came, came_two, spread, (s0, s1, s2, s3, s4))

    def last(c, carry):
        peer_copy(c).wait_recv()
        peer_copy(c).wait_send()
        return carry

    lax.fori_loop(0, chunks, last, 0)
    grads_copy.wait()


def attend_out(attn, w_out, x, gain, grads, width_own, depth=1):
    rows, width = x.shape
    chunks, step, scratch = line_scratch(rows, width_own)
    vmem = pl.BlockSpec(memory_space=pltpu.VMEM)
    far = pl.BlockSpec(memory_space=pl.ANY)
    dma = pltpu.SemaphoreType.DMA
    return pl.pallas_call(
        functools.partial(attend_out_kernel, chunks, step, depth, EPS),
        out_shape=[
            jax.ShapeDtypeStruct((2 * rows, width), BF16),
            jax.ShapeDtypeStruct((rows, width_own), F32), jax.ShapeDtypeStruct((rows, 1), F32),
            jax.ShapeDtypeStruct((rows // 2, width), BF16),
        ],
        in_specs=[vmem] * 4 + [far],
        out_specs=[vmem] * 3 + [far],
        scratch_shapes=scratch + [dma((chunks,)), dma((chunks,)), dma, dma],
        compiler_params=pltpu.CompilerParams(collective_id=1, has_side_effects=True, vmem_limit_bytes=40 << 20),
        cost_estimate=pl.CostEstimate(flops=0, bytes_accessed=0, transcendentals=0),
    )(attn, w_out, x, gain, grads)


def resid_grad_kernel(
    chunks, step, depth, tiles, grad, grad_p, out_p, dgu, hid, both, both_grad, sgu, sd,
    small_e, small_p, small_s, prob, hot, logits, switch, w_small, g_own, resid_own, inv_two, gain,
    low, grad_resid, gain_grad, out_back, sum_egu, sum_ed, sgu_x, sd_x, grad_small,
    part, came, came_two, spread, s0, s1, s2, s3, s4, back, y_send, y_recv, o_send, o_recv,
    dgu_v, hid_v, both_v, both_grad_v, sent_egu, sent_ed, came_egu, came_ed,
    s_own, s_in, d_own, d_in, l_sem, w_send, w_recv, w_out, r_send, r_recv, r_out,
    router, along, small_y, small_z, ed_in, ed_out, t_send, t_recv, e_send, e_recv, e_out,
):
    n = lax.axis_size("tp")
    own = part.shape[3]
    rows = grad.shape[0]
    core, x, y, (to_core, to_x, other) = places()

    def at(c):
        return pl.ds(pl.multiple_of(c * step, step), step)

    def peer_copy(c):
        return pltpu.make_async_remote_copy(
            src_ref=grad_p.at[at(c)], dst_ref=back.at[at(c)], send_sem=y_send.at[c], recv_sem=y_recv.at[c],
            device_id=other, device_id_type=pl.DeviceIdType.MESH,
        )

    def out_copy():
        return pltpu.make_async_remote_copy(
            src_ref=out_p, dst_ref=out_back, send_sem=o_send, recv_sem=o_recv,
            device_id=other, device_id_type=pl.DeviceIdType.MESH,
        )

    loads = [
        pltpu.make_async_copy(source, target, l_sem.at[m])
        for m, (source, target) in enumerate(
            (
                (dgu, dgu_v),
                (both, both_v),
                (hid, hid_v),
                (both_grad, both_grad_v),
                (sgu.at[pl.ds(x * s_own.shape[0], s_own.shape[0])], s_own),
                (sd.at[pl.ds(y * d_own.shape[0], d_own.shape[0])], d_own),
            )
        )
    ]
    kinds = ((dgu_v, both_v, sent_egu, came_egu, sum_egu), (hid_v, both_grad_v, sent_ed, came_ed, sum_ed))

    def sum_copies(m):
        source, target, where = (
            (sgu.at[pl.ds((1 - x) * s_own.shape[0], s_own.shape[0])], s_in, to_x),
            (sd.at[pl.ds((1 - y) * d_own.shape[0], d_own.shape[0])], d_in, other),
            (s_own, sgu_x.at[x], to_x),
            (d_own, sd_x.at[x], to_x),
        )[m]
        return pltpu.make_async_remote_copy(
            src_ref=source, dst_ref=target, send_sem=r_send.at[m], recv_sem=r_recv.at[m],
            device_id=where, device_id_type=pl.DeviceIdType.MESH,
        )

    def own_out(m):
        return pltpu.make_async_copy((s_own, d_own)[m], (sgu_x, sd_x)[m].at[x], r_out.at[m])

    def shared(m):
        sum_copies(m).wait_recv()
        add_rows((s_own, d_own)[m], (s_in, d_in)[m], 0, (s_own, d_own)[m].shape[0])
        sum_copies(2 + m).start()
        own_out(m).start()

    def tile_copy(m, b):
        return pltpu.make_async_remote_copy(
            src_ref=kinds[m][2].at[b], dst_ref=kinds[m][3].at[b], send_sem=w_send.at[b, m], recv_sem=w_recv.at[b, m],
            device_id=to_core, device_id_type=pl.DeviceIdType.MESH,
        )

    def x_copy(b):
        wide = ed_in.shape[2]
        return pltpu.make_async_remote_copy(
            src_ref=came_ed.at[b, :, pl.ds(pl.multiple_of((1 - x) * wide, wide), wide)], dst_ref=ed_in.at[b],
            send_sem=e_send.at[b], recv_sem=e_recv.at[b],
            device_id=to_x, device_id_type=pl.DeviceIdType.MESH,
        )

    def x_out(b):
        tall = ed_in.shape[1]
        return pltpu.make_async_copy(
            ed_out.at[b], sum_ed.at[pl.ds(pl.multiple_of(b * tall, tall), tall)], e_out.at[b]
        )

    def tile_out(m, b):
        tall = kinds[m][3].shape[1]
        return pltpu.make_async_copy(
            kinds[m][3].at[b], kinds[m][4].at[pl.ds(pl.multiple_of(b * tall, tall), tall)], w_out.at[b, m]
        )

    def tile(m, b, which):
        left, right = kinds[m][:2]
        tall, wide = kinds[m][3].shape[1:]
        return mm_tn(
            left[...] if tiles == 1 else left[:, pl.ds(pl.multiple_of(b * tall, tall), tall)],
            right[:, pl.ds(pl.multiple_of(which * wide, wide), wide)],
        )

    def weights(t):
        @pl.when(t == 0)
        def _():
            for copy in loads:
                copy.wait()

        @pl.when(t == 1)
        def _():
            gates()

        @pl.when(t < tiles)
        def _():
            for m in range(2):
                kinds[m][2][t] = tile(m, t, 1 - core).astype(BF16)
                tile_copy(m, t).start()

        @pl.when(t == tiles * 8 // 11)
        def _():
            shared(0)

        @pl.when(t == tiles * 14 // 11)
        def _():
            shared(1)

        @pl.when((t >= tiles) & (t < 2 * tiles))
        def _():
            b = t - tiles
            for m in range(2):
                value = tile(m, b, core)
                tile_copy(m, b).wait_recv()
                kinds[m][3][b] = (value + kinds[m][3][b].astype(F32)).astype(BF16)
                if m == 0:
                    tile_out(m, b).start()
                else:
                    x_copy(b).start()

    for copy in loads:
        copy.start()
    me = lax.axis_index("tp")

    def small_copy(d):
        return pltpu.make_async_remote_copy(
            src_ref=small_z.at[0] if d else small_p, dst_ref=small_z.at[d] if d else small_y,
            send_sem=t_send.at[d], recv_sem=t_recv.at[d],
            device_id={"tp": (me + d) % n} if d else other, device_id_type=pl.DeviceIdType.MESH,
        )

    greet_all([other, to_core, to_x] + [{"tp": (me + d) % n} for d in range(1, n)])
    small_copy(0).start()
    sum_copies(0).start()

    def begin(c, carry):
        peer_copy(c).start()
        return carry

    lax.fori_loop(0, chunks, begin, 0)
    sum_copies(1).start()
    out_copy().start()
    gain_grad[...] = jnp.zeros_like(gain_grad)
    experts_own = small_e.shape[0] - 1
    experts = 2 * experts_own
    small_copy(0).wait_recv()
    here, there = small_e[:experts_own, :], small_y[:experts_own, :]
    small_z[0] = jnp.zeros_like(small_z[0])
    small_z[0, :experts_own] = jnp.where(y == 0, here, there)
    small_z[0, experts_own:experts] = jnp.where(y == 0, there, here)
    small_z[0, experts : experts + 1] = small_s[:1, :]
    small_z[0, experts + 1 : experts + 2] = small_s[1:, :] + small_e[experts_own:, :] + small_y[experts_own:, :]
    for d in range(1, n):
        small_copy(d).start()

    def gates():
        total = small_z[0]
        for d in range(1, n):
            small_copy(d).wait_recv()
            total = total + small_z[d]
        slots = prob.shape[1]
        total = jnp.concatenate([total, jnp.zeros((128 - total.shape[0], rows), F32)], axis=0).T
        grad_prob = total[:, :slots] * hot[...]
        inner = jnp.sum(prob[...] * grad_prob, axis=1, keepdims=True)
        sw = switch[...]
        grad_switch = total[:, experts : experts + 1] * sw * (1.0 - sw)
        place = lax.broadcasted_iota(jnp.int32, (1, slots), 1)
        grads = jnp.where(place == experts, grad_switch, prob[...] * (grad_prob - inner)).astype(BF16)
        router[...] = mm_nt(grads, w_small[...])
        along[...] = total[:, experts + 1 : experts + 2] + jnp.sum(
            grads.astype(F32) * logits[...], axis=1, keepdims=True
        )
        grad_small[...] = mm_tn(grads, both_v[:rows, :])

    def prepare(c):
        peer_copy(c).wait_recv()
        for s in range(n):
            columns = slice(s * own, (s + 1) * own)
            part[c, s] = (grad[at(c), columns].astype(F32) + back[at(c), columns].astype(F32)).astype(BF16)

    def settle(c, total):
        total = total + router[at(c), :]
        inv = inv_two[at(c), :]
        resid = resid_own[at(c), :]
        gain_grad[...] += jnp.sum(total * resid * inv, axis=0, keepdims=True)
        result = g_own[at(c), :].astype(F32) + inv * gain[...] * total - resid * (inv * inv * along[at(c), :] / (n * own))
        grad_resid[at(c), :] = result
        return result.astype(BF16)

    def gathered(c):
        for s in range(n):
            low[at(c), s * own:(s + 1) * own] = spread[c, s]

    line_sum(depth, prepare, settle, gathered, weights, part, came, came_two, spread, (s0, s1, s2, s3, s4))

    def last(c, carry):
        peer_copy(c).wait_send()
        return carry

    lax.fori_loop(0, chunks, last, 0)
    out_copy().wait()

    def done(b, carry):
        x_copy(b).wait_recv()
        wide = ed_in.shape[2]
        own = came_ed[b, :, pl.ds(pl.multiple_of(x * wide, wide), wide)]
        ed_out[b] = (own.astype(F32) + ed_in[b].astype(F32)).astype(BF16)
        x_out(b).start()
        tile_copy(0, b).wait_send()
        tile_copy(1, b).wait_send()
        tile_out(0, b).wait()
        x_copy(b).wait_send()
        return carry

    lax.fori_loop(0, tiles, done, 0)

    def written(b, carry):
        x_out(b).wait()
        return carry

    lax.fori_loop(0, tiles, written, 0)
    for m in range(2):
        sum_copies(m).wait_send()
        sum_copies(2 + m).wait()
        own_out(m).wait()
    for d in range(n):
        small_copy(d).wait_send()


def resid_grad(grad, grad_p, out_p, dgu, hid, both, both_grad, sgu, sd, small_e, small_p, small_s, prob, hot, logits, switch, w_small, g_own, resid_own, inv_two, gain, depth=1):
    rows, width = grad.shape
    width_own = g_own.shape[1]
    chunks, step, scratch = line_scratch(rows, width_own)
    hidden = hid.shape[1]
    tiles = 11 if hidden % (11 * 128) == 0 else 1
    vmem = pl.BlockSpec(memory_space=pltpu.VMEM)
    far = pl.BlockSpec(memory_space=pl.ANY)
    dma = pltpu.SemaphoreType.DMA
    return pl.pallas_call(
        functools.partial(resid_grad_kernel, chunks, step, depth, tiles),
        out_shape=[
            jax.ShapeDtypeStruct((rows, width), BF16), jax.ShapeDtypeStruct((rows, width_own), F32),
            jax.ShapeDtypeStruct((1, width_own), F32), jax.ShapeDtypeStruct((rows, width), BF16),
        ]
        + [jax.ShapeDtypeStruct((2 * hidden, width // 2), BF16), jax.ShapeDtypeStruct((hidden, width // 4), BF16)]
        + [jax.ShapeDtypeStruct((2, v.shape[0] // 2, v.shape[1]), BF16) for v in (sgu, sd)]
        + [jax.ShapeDtypeStruct((prob.shape[1], width), F32)],
        in_specs=[vmem] + [far] * 8 + [vmem] * 12,
        out_specs=[vmem] * 3 + [far] * 5 + [vmem],
        scratch_shapes=scratch + [pltpu.VMEM((rows, width), BF16), dma((chunks,)), dma((chunks,)), dma, dma]
        + [pltpu.VMEM(v.shape, BF16) for v in (dgu, hid, both, both_grad)]
        + [pltpu.VMEM((tiles, k * hidden // tiles, width // 2), BF16) for k in (2, 1, 2, 1)]
        + [pltpu.VMEM((v.shape[0] // 2, v.shape[1]), BF16) for v in (sgu, sgu, sd, sd)]
        + [dma((6,)), dma((tiles, 2)), dma((tiles, 2)), dma((tiles, 2)), dma((4,)), dma((4,)), dma((2,))]
        + [pltpu.VMEM((rows, width_own), F32), pltpu.VMEM((rows, 1), F32)]
        + [pltpu.VMEM(small_e.shape, F32), pltpu.VMEM((lax.axis_size("tp"), 16, rows), F32)]
        + [pltpu.VMEM((tiles, hidden // tiles, width // 4), BF16)] * 2
        + [dma((lax.axis_size("tp"),))] * 2 + [dma((tiles,))] * 3,
        compiler_params=pltpu.CompilerParams(collective_id=2, has_side_effects=True, vmem_limit_bytes=63 << 20),
        cost_estimate=pl.CostEstimate(flops=0, bytes_accessed=0, transcendentals=0),
    )(grad, grad_p, out_p, dgu, hid, both, both_grad, sgu, sd, small_e, small_p, small_s, prob, hot, logits, switch, w_small, g_own, resid_own, inv_two, gain)


def body(
    tokens,
    norm_attn,
    w_query,
    w_key,
    w_value,
    w_output,
    norm_ffn,
    w_router,
    shared_switch,
    shared_gate,
    shared_up,
    shared_down,
    expert_gate,
    expert_up,
    expert_down,
    routes,
    segments,
    output_gradient,
):
    tp_count = lax.axis_size("tp")
    ep_count = lax.axis_size("ep")
    dp_count = lax.axis_size("dp")
    tp_rank = lax.axis_index("tp")
    ep_rank = lax.axis_index("ep")
    rows = tokens.shape[0]
    width_own = tokens.shape[1]
    width = width_own * tp_count
    heads = w_query.shape[1] // HD
    experts_own = expert_gate.shape[0]
    experts = experts_own * ep_count
    expert_width = expert_gate.shape[2]
    score_scale = 1.0 / math.sqrt(HD)
    far_bits = [1 << b for b in range(1, dp_count.bit_length() - 1)]

    def own_columns(value):
        return lax.dynamic_slice_in_dim(value, tp_rank * width_own, width_own, value.ndim - 1)

    near = bit_of("dp", 1)

    def pair_send(left, right, columns, used=None):
        sent = weight_half(left, right, 1 - near, columns, rows=used)
        return sent, swap(sent, "dp", 1)

    def pair_keep(left, right, columns, got, used=None):
        return weight_half(left, right, near, columns, got, rows=used)

    core = ("dp", 1)
    far = [("dp", b) for b in far_bits]
    line = [("ep", 1)]
    x_link, y_link = far[0], line[0]

    def over_tp(value):
        if tp_count <= 4:
            others = [
                lax.ppermute(value, "tp", [(i, (i + d) % tp_count) for i in range(tp_count)])
                for d in range(1, tp_count)
            ]
            return sum(others, value)
        bit = 1
        while bit < tp_count:
            value = value + swap(value, "tp", bit)
            bit *= 2
        return value

    def over_rows(value):
        for axis, bit in [core] + far + line:
            value = value + swap(value, axis, bit)
        return value

    qkv = heads * HD
    freq = ROPE_BASE ** (-(np.arange(HD // 2, dtype=np.float64) * 2.0) / HD)
    freq = jnp.asarray(np.concatenate([freq, freq])[None, :], F32)
    gains = jnp.pad(jnp.stack([norm_attn, norm_ffn]), ((0, 14), (0, 0)))
    (
        x_full, normed, inv_one, gain_two, grad_rows, query, key_rows, value_rows, attn_rows, log_norm,
        query_seg, key_seg, cos_table, sin_table,
    ) = front(
        tokens, gains, output_gradient, w_query, w_key, w_value, segments.reshape(1, -1), freq
    )
    route_hot = jnp.sum(
        (routes[:, :, None] == jnp.arange(experts, dtype=jnp.int32)[None, None, :]).astype(F32),
        axis=1,
    )
    route_hot_peer = swap(route_hot, "ep", 1)

    both, resid_own, inv_two, grad_peer_a = attend_out(
        attn_rows, w_output, x_full, gain_two, grad_rows, width_own
    )
    mixed = both[:rows]

    def router(values):
        logits = mm(values, w_router)
        return logits, jax.nn.softmax(logits, axis=1)

    logits, router_prob = router(mixed)
    combine = router_prob * route_hot
    combine_peer = router(both[rows:])[1] * route_hot_peer
    switch_logit = mm(mixed, shared_switch[:, None])
    switch = jax.nn.sigmoid(switch_logit)

    def own_experts(value):
        return lax.dynamic_slice_in_dim(value, ep_rank * experts_own, experts_own, 1)

    hid_s, dgu_s, out_s, grad_s, small_s, grad_peer_b = ffn(
        both,
        grad_rows,
        switch,
        shared_gate,
        shared_up,
        shared_down,
        carry=[(grad_rows, 2, rows // 2, rows // 2, 0)],
        number=4,
    )
    both_grad = jnp.concatenate([grad_rows, grad_peer_a, grad_peer_b], axis=0)
    sent, got_sgu = pair_send(both, dgu_s, False, rows)
    sent, got_sd = pair_send(hid_s, after(grad_rows, sent), True)
    sum_sgu = pair_keep(both, after(dgu_s, sent, both_grad), False, got_sgu, rows)
    sum_sd = pair_keep(hid_s, after(grad_rows, sum_sgu), True, got_sd)
    quarter = sum_sgu.shape[0] // 4

    hidden_width = experts_own * expert_width
    gate_w = jnp.transpose(expert_gate, (0, 2, 1)).reshape(hidden_width, width)
    up_w = jnp.transpose(expert_up, (0, 2, 1)).reshape(hidden_width, width)
    down_w = expert_down.reshape(hidden_width, width)
    hid_p, dgu_p, out_p, grad_p, small_p, got_sgu_a, got_sd = ffn(
        both,
        after(both_grad, sum_sd),
        own_experts(combine_peer),
        gate_w,
        up_w,
        down_w,
        start=rows,
        total=2 * rows,
        flipped=True,
        carry=[
            (sum_sgu, 2, quarter, 0, 2 * quarter),
            (sum_sd, 1, sum_sd.shape[0] // 2, 0, sum_sd.shape[0] // 2),
        ],
        number=5,
    )
    hid_e, dgu_e, out_e, grad_e, small_e, got_sgu_b = ffn(
        both,
        both_grad,
        after(own_experts(combine), grad_p),
        gate_w,
        up_w,
        down_w,
        total=2 * rows,
        base=(out_s, grad_s),
        into=(hid_p, dgu_p),
        flipped=True,
        carry=[(sum_sgu, 2, quarter, quarter, 2 * quarter)],
        number=6,
    )
    got_sgu = jnp.concatenate([got_sgu_a, got_sgu_b], axis=0)

    sum_sgu = reduce_add(sum_sgu, got_sgu, *y_link)
    sum_sd = reduce_add(sum_sd, got_sd, *x_link)

    tp_rows = lax.dynamic_slice_in_dim(w_router, tp_rank * width_own, width_own, 0)
    spare = 16 - experts - 1

    def slots(value, more=None):
        more = jnp.zeros((value.shape[0], 1), value.dtype) if more is None else more
        return jnp.pad(jnp.concatenate([value, more], axis=1), ((0, 0), (0, spare)))

    resid_low, grad_resid, grad_gain_two, out_back, sum_egu, sum_ed, sgu_x, sd_x, grad_small = resid_grad(
        grad_e,
        grad_p,
        out_p,
        dgu_e,
        hid_e,
        both,
        both_grad,
        sum_sgu,
        sum_sd,
        small_e.T,
        small_p.T,
        small_s.T,
        slots(router_prob),
        slots(route_hot),
        slots(logits, switch_logit),
        switch,
        slots(tp_rows, own_columns(shared_switch)[:, None]),
        output_gradient,
        resid_own,
        inv_two,
        norm_ffn.astype(F32)[None, :],
    )

    flat = jnp.concatenate(
        [grad_gain_two.reshape(-1), grad_small[: experts + 1].reshape(-1)]
    ).reshape(-1, 128)
    inner = shared_gate.shape[1]
    ffn_part = (out_e.astype(F32) + out_back.astype(F32)).astype(BF16)
    sgu_f, sd_f, egu_f, ed_f, qkv_f, wo_f, flat, ffn_own, normed_own, row_total, grad_gain_one = tail(
        sgu_x,
        sd_x,
        sum_egu,
        sum_ed,
        flat,
        normed,
        w_query,
        w_key,
        w_value,
        attn_rows,
        ffn_part,
        tokens,
        inv_one,
        resid_low,
        w_output,
        query,
        key_rows,
        value_rows,
        log_norm,
        query_seg,
        key_seg,
        cos_table,
        sin_table,
    )

    sg_grad, su_grad = widen(sgu_f, (inner, inner))
    (sd_grad,) = widen(sd_f)
    (eg_grad,) = widen(egu_f, kinds=2, kind=0)
    (eu_grad,) = widen(egu_f, kinds=2, kind=1)
    (ed_grad,) = widen(ed_f, across=4)
    wq_grad, wk_grad, wv_grad = widen(qkv_f, (qkv,) * 3)
    (wo_grad,) = widen(wo_f)

    x_own = tokens.astype(F32)
    grad_tokens = (
        grad_resid
        + inv_one * norm_attn.astype(F32) * normed_own
        - x_own * (inv_one * inv_one) * (row_total[0][:, None] / width)
    )
    grad_gain_one = grad_gain_one[0]
    layer_out = (resid_own + ffn_own).astype(BF16)
    flat = flat.reshape(-1)
    grad_gain_two = flat[:width_own]
    grad_router = flat[width_own : width_own + width * experts].reshape(experts, width).T
    grad_switch_w = flat[width_own + width * experts :]

    def per_expert(value):
        return value.reshape(experts_own, expert_width, width)

    return (
        layer_out,
        grad_tokens,
        grad_gain_one,
        wq_grad,
        wk_grad,
        wv_grad,
        wo_grad,
        grad_gain_two,
        grad_router,
        grad_switch_w,
        sg_grad,
        su_grad,
        sd_grad,
        jnp.transpose(per_expert(eg_grad), (0, 2, 1)),
        jnp.transpose(per_expert(eu_grad), (0, 2, 1)),
        per_expert(ed_grad),
    )


def solution(mesh):
    placed = (
        P(("dp", "ep"), "tp"),
        P("tp"),
        P(None, "tp"),
        P(None, "tp"),
        P(None, "tp"),
        P("tp", None),
        P("tp"),
        P(),
        P(),
        P(None, "tp"),
        P(None, "tp"),
        P("tp", None),
        P("ep", None, "tp"),
        P("ep", None, "tp"),
        P("ep", "tp", None),
        P(("dp", "ep"), None),
        P("dp"),
        P(("dp", "ep"), "tp"),
    )
    return jax.shard_map(
        body,
        mesh=mesh,
        in_specs=placed,
        out_specs=(
            P(("dp", "ep"), "tp"),
            P(("dp", "ep"), "tp"),
            P("tp"),
            P(None, "tp"),
            P(None, "tp"),
            P(None, "tp"),
            P("tp", None),
            P("tp"),
            P(),
            P(),
            P(None, "tp"),
            P(None, "tp"),
            P("tp", None),
            P("ep", None, "tp"),
            P("ep", None, "tp"),
            P("ep", "tp", None),
        ),
        check_vma=False,
    )
```

```python
import functools
import math

import jax
import jax.numpy as jnp
import numpy as np
from jax import lax
from jax.experimental import pallas as pl
from jax.experimental.pallas import tpu as pltpu
from jax.sharding import PartitionSpec as P

HD = 128
EPS = 1e-06
ROPE_BASE = 1000000.0
NEG = -1e30
F32 = jnp.float32
BF16 = jnp.bfloat16


def mm(left, right):
    return lax.dot_general(left, right, (((1,), (0,)), ((), ())), preferred_element_type=F32)


def mm_nt(left, right):
    return lax.dot_general(left, right, (((1,), (1,)), ((), ())), preferred_element_type=F32)


def mm_tn(left, right):
    return lax.dot_general(left, right, (((0,), (0,)), ((), ())), preferred_element_type=F32)


def swap(value, axis, bit):
    count = lax.axis_size(axis)
    return lax.ppermute(value, axis, [(i, i ^ bit) for i in range(count)])


def bit_of(axis, bit):
    return (lax.axis_index(axis) // bit) % 2


def half(value, which, dim):
    size = value.shape[dim] // 2
    return lax.dynamic_slice_in_dim(value, which * size, size, dim)


def after(value, *others):
    return lax.optimization_barrier((value, *others))[0]


def reduce_send(value, axis, bit):
    return swap(half(value, 1 - bit_of(axis, bit), 0), axis, bit)


def reduce_add(value, got, axis, bit):
    return (half(value, bit_of(axis, bit), 0).astype(F32) + got.astype(F32)).astype(BF16)


def places():
    count = lax.axis_size("dp")
    dp, ep = lax.axis_index("dp"), lax.axis_index("ep")
    core, x = dp % 2, dp // (count // 2)
    where = (
        {"dp": dp + 1 - 2 * core},
        {"dp": (dp + count // 2) % count},
        {"ep": 1 - ep},
    )
    return core, x, ep, where


def greet_all(peers):
    barrier = pltpu.get_barrier_semaphore()
    for where in peers:
        pl.semaphore_signal(
            barrier, inc=1, device_id=where, device_id_type=pl.DeviceIdType.MESH
        )
    pl.semaphore_wait(barrier, len(peers))


def add_rows(total, more, start, count, out=None):
    step = 32 if count % 32 == 0 else 16

    def turn(k, carry):
        here = pl.ds(pl.multiple_of(k * step, step), step)
        there = pl.ds(pl.multiple_of(start + k * step, step), step)
        value = (total[there, :].astype(F32) + more[here, :].astype(F32)).astype(BF16)
        if out is None:
            total[there, :] = value
        else:
            out[here, :] = value
        return carry

    lax.fori_loop(0, count // step, turn, 0)


def front_kernel(
    scale, chunks, tokens, gains, cotangent, w_query, w_key, w_value, segments, freq, routes,
    x, normed, inv_one, gain_two, grads, query, keys, values, attn, lse, query_seg, key_seg, cos, sin, hot, hot_peer,
    hot_low, wq_v, wk_v, wv_v, gains_in, l_sem, x_send, x_recv, s_sem, r_sem, kv_send, kv_recv,
):
    n, me = lax.axis_size("tp"), lax.axis_index("tp")
    y = lax.axis_index("ep")
    rows, own = tokens.shape
    heads = query.shape[1] // HD
    step = rows // chunks
    to_y = {"ep": 1 - y}
    tp = [{"tp": (me + d) % n} for d in range(1, n)]

    def remote(source, target, send_sem, recv_sem, where):
        return pltpu.make_async_remote_copy(
            src_ref=source, dst_ref=target, send_sem=send_sem, recv_sem=recv_sem,
            device_id=where, device_id_type=pl.DeviceIdType.MESH,
        )

    def piece(c, s):
        return (pl.ds(c * step, step), pl.ds(pl.multiple_of(s * own, own), own))

    def x_copy(c, s, to_right):
        return remote(
            x.at[piece(c, s)], x.at[piece(c, s)], x_send.at[c, s, 1 if to_right else 0], x_recv.at[c, s],
            {"tp": me + 1 if to_right else me - 1},
        )

    loads = [
        pltpu.make_async_copy(a, b, l_sem.at[m])
        for m, (a, b) in enumerate(((w_key, wk_v), (w_value, wv_v), (w_query, wq_v)))
    ]
    for copy in loads:
        copy.start()
    x[:, pl.ds(pl.multiple_of(me * own, own), own)] = tokens[...]
    gains_in[0] = gains[...]
    greet_all([to_y] + tp)
    for c in range(chunks):

        @pl.when(me > 0)
        def _(c=c):
            x_copy(c, me, False).start()

        @pl.when(me < n - 1)
        def _(c=c):
            x_copy(c, me, True).start()

    g_copies = [remote(gains_in.at[0], gains_in.at[d], s_sem.at[d - 1], r_sem.at[d - 1], tp[d - 1]) for d in range(1, n)]
    for copy in g_copies:
        copy.start()

    top = routes.shape[0]
    chosen = jnp.concatenate([routes[...].astype(F32), jnp.zeros((128 - top, rows), F32)], axis=0).T
    slot = lax.broadcasted_iota(jnp.int32, (1, hot.shape[1]), 1).astype(F32)
    used = jnp.zeros(hot.shape, F32)
    for k in range(top):
        used = used + jnp.where(chosen[:, k : k + 1] == slot, 1.0, 0.0)
    hot[...] = used
    hot_low[...] = used.astype(BF16)
    hot_copy = remote(hot_low, hot_peer, s_sem.at[2 * n - 1], r_sem.at[2 * n - 1], to_y)
    hot_copy.start()

    at = (y * rows + lax.broadcasted_iota(jnp.int32, (rows, 1), 0)).astype(F32)
    angle = at * freq[...]
    cos[...] = jnp.cos(angle)
    lane = lax.broadcasted_iota(jnp.int32, (1, HD), 1)
    sin[...] = jnp.where(lane < HD // 2, 1.0, -1.0) * jnp.sin(angle)
    whole = segments[...].astype(F32)
    mine = jnp.where(y == 0, whole[:, :rows], whole[:, rows : 2 * rows])
    query_seg[...] = jnp.broadcast_to(mine, (128, rows)).T[:, :1]
    key_seg[:, :rows] = jnp.where(y == 0, -1.0, whole[:, :rows])
    key_seg[:, rows:] = mine

    for d in range(1, n):
        for c in range(chunks):

            @pl.when(me >= d)
            def _(c=c, d=d):
                x_copy(c, me - d, True).wait_recv()

                @pl.when(me < n - 1)
                def _():
                    x_copy(c, me - d, True).start()

            @pl.when(me + d < n)
            def _(c=c, d=d):
                x_copy(c, me + d, False).wait_recv()

                @pl.when(me > 0)
                def _():
                    x_copy(c, me + d, False).start()

    mine_at = pl.ds(pl.multiple_of(me * own, own), own)
    c_copies = [
        remote(cotangent, grads.at[:, mine_at], s_sem.at[n - 2 + d], r_sem.at[n - 2 + d], tp[d - 1]) for d in range(1, n)
    ]
    handed = n == 4
    for d, copy in enumerate(c_copies, 1):

        @pl.when(((me + d) % n - me != n - 1) & (me - (me + d) % n != n - 1) if handed else me >= 0)
        def _(copy=copy):
            copy.start()

    inner = (me > 0) & (me < n - 1)

    def hand_on():
        upward = me == n - 2
        origin = pl.ds(pl.multiple_of(jnp.where(upward, 0, n - 1) * own, own), own)
        arrival = jnp.where(upward, n - 2 + n - 1, n - 2 + 1)
        return remote(
            grads.at[:, origin], grads.at[:, origin], s_sem.at[2 * n - 2], r_sem.at[arrival],
            {"tp": jnp.where(upward, n - 1, 0)},
        )
    own_grads = pltpu.make_async_copy(cotangent, grads.at[:, mine_at], l_sem.at[3])
    own_grads.start()
    for copy in g_copies:
        copy.wait_recv()
    gain_one = []
    for s in range(n):
        row = gains_in[0, :2, :].astype(F32) * jnp.where(me == s, 1.0, 0.0)
        for d in range(1, n):
            row = row + gains_in[d, :2, :].astype(F32) * jnp.where((me - d + n) % n == s, 1.0, 0.0)
        gain_one.append(row[:1])
        gain_two[:, s * own : (s + 1) * own] = row[1:]

    block = min(rows, 128)
    for b in range(rows // block):
        here = slice(b * block, (b + 1) * block)
        square = jnp.zeros((block, 1), F32)
        for s in range(n):
            part = x[here, s * own : (s + 1) * own].astype(F32)
            square = square + jnp.sum(part * part, axis=1, keepdims=True)
        inv = lax.rsqrt(square / (n * own) + EPS)
        inv_one[here, :] = inv
        for s in range(n):
            columns = slice(s * own, (s + 1) * own)
            normed[here, columns] = (x[here, columns].astype(F32) * inv * gain_one[s]).astype(BF16)

    def rope(value):
        return value * cos[...] - pltpu.roll(value, HD // 2, 1) * sin[...]

    loads[0].wait()
    loads[1].wait()
    key_pre = mm(normed[...], wk_v[...])
    value_pre = mm(normed[...], wv_v[...])

    @pl.when(y == 0)
    def _():
        keys[:rows, :] = jnp.zeros((rows, heads * HD), BF16)
        values[:rows, :] = jnp.zeros((rows, heads * HD), BF16)

    def kv_copy(h, m):
        array = (keys, values)[m]
        part = pl.ds(h * HD, HD)
        return remote(
            array.at[pl.ds(rows, rows), part], array.at[pl.ds(0, rows), part], kv_send.at[h, m], kv_recv.at[h, m], to_y
        )

    for h in range(heads):
        part = slice(h * HD, (h + 1) * HD)
        keys[rows:, part] = rope(key_pre[:, part]).astype(BF16)
        values[rows:, part] = value_pre[:, part].astype(BF16)

        @pl.when(y == 0)
        def _(h=h):
            kv_copy(h, 0).start()
            kv_copy(h, 1).start()

    loads[2].wait()
    query_pre = mm(normed[...], wq_v[...])
    for h in range(heads):
        part = slice(h * HD, (h + 1) * HD)
        query[:, part] = rope(query_pre[:, part]).astype(BF16)

    if handed:

        @pl.when(inner)
        def _():
            c_copies[1].wait_recv()
            hand_on().start()

    key_at = (y - 1) * rows + lax.broadcasted_iota(jnp.int32, (1, 2 * rows), 1)
    query_at = y * rows + lax.broadcasted_iota(jnp.int32, (rows, 1), 0)
    allowed = (query_seg[...] == key_seg[...]) & (key_at <= query_at)
    for h in range(heads):
        part = slice(h * HD, (h + 1) * HD)

        @pl.when(y == 1)
        def _(h=h):
            kv_copy(h, 0).wait_recv()
            kv_copy(h, 1).wait_recv()

        scores = jnp.where(allowed, mm_nt(query[:, part], keys[:, part]) * scale, NEG)
        top = jnp.max(scores, axis=1, keepdims=True)
        shifted = jnp.exp(scores - top)
        total = jnp.sum(shifted, axis=1, keepdims=True)
        weights = (shifted * (1.0 / total)).astype(BF16)
        attn[:, part] = mm(weights, values[:, part]).astype(BF16)
        lse[:, h : h + 1] = top + jnp.log(total)

    for h in range(heads):

        @pl.when(y == 0)
        def _(h=h):
            kv_copy(h, 0).wait_send()
            kv_copy(h, 1).wait_send()

    for c in range(chunks):
        for s in range(n):

            @pl.when((s <= me) & (me < n - 1))
            def _(c=c, s=s):
                x_copy(c, s, True).wait_send()

            @pl.when((s >= me) & (me > 0))
            def _(c=c, s=s):
                x_copy(c, s, False).wait_send()

    own_grads.wait()
    for d, copy in enumerate(c_copies, 1):

        if handed and d == 2:

            @pl.when(jnp.logical_not(inner))
            def _(copy=copy):
                copy.wait_recv()

        else:
            copy.wait_recv()

        @pl.when(((me + d) % n - me != n - 1) & (me - (me + d) % n != n - 1) if handed else me >= 0)
        def _(copy=copy):
            copy.wait_send()

    if handed:

        @pl.when(inner)
        def _():
            hand_on().wait_send()

    for copy in g_copies:
        copy.wait_send()
    hot_copy.wait()


def front(tokens, gains, cotangent, w_query, w_key, w_value, segments, freq, routes, slots):
    rows, own = tokens.shape
    n = lax.axis_size("tp")
    width = n * own
    mine = w_query.shape[1]
    heads = mine // HD
    chunks = 8 if n <= 4 else 2
    far = pl.BlockSpec(memory_space=pl.ANY)
    vmem = pl.BlockSpec(memory_space=pltpu.VMEM)
    dma = pltpu.SemaphoreType.DMA

    def shape(*dims, kind=BF16):
        return jax.ShapeDtypeStruct(dims, kind)

    return pl.pallas_call(
        functools.partial(front_kernel, 1.0 / math.sqrt(HD), chunks),
        out_shape=[
            shape(rows, width), shape(rows, width), shape(rows, 1, kind=F32), shape(1, width, kind=F32),
            shape(rows, width), shape(rows, mine), shape(2 * rows, mine), shape(2 * rows, mine), shape(rows, mine),
            shape(rows, heads, kind=F32), shape(rows, 1, kind=F32), shape(1, 2 * rows, kind=F32),
            shape(rows, HD, kind=F32), shape(rows, HD, kind=F32), shape(rows, slots, kind=F32), shape(rows, slots),
        ],
        in_specs=[vmem] * 2 + [far] * 4 + [vmem] * 3,
        out_specs=[vmem] * 4 + [far] + [vmem] * 11,
        scratch_shapes=[pltpu.VMEM((rows, slots), BF16)]
        + [pltpu.VMEM((width, mine), BF16)] * 3
        + [pltpu.VMEM((n, 16, own), BF16), dma((4,)), dma((chunks, n, 2)), dma((chunks, n))]
        + [dma((2 * n,)), dma((2 * n,)), dma((heads, 2)), dma((heads, 2))],
        compiler_params=pltpu.CompilerParams(
            collective_id=7, has_side_effects=True, vmem_limit_bytes=44 << 20
        ),
        cost_estimate=pl.CostEstimate(flops=0, bytes_accessed=0, transcendentals=0),
    )(tokens, gains, cotangent, w_query, w_key, w_value, segments, freq, routes)


def tail_kernel(
    scale,
    _sgu, _sd, egu, _ed, flat, normed, w_query, w_key, w_value, attn, ffn,
    tokens, inv_one, low, w_out, query, keys, values, lse, query_seg, key_seg, cos, sin,
    sgu_f, sd_f, egu_f, ed_f, qkv_f, wo_f, flat_f, ffn_own, normed_own, row_total, gain_f,
    normed_v, wq_v, wk_v, wv_v, attn_v, grad_attn, grad_key, grad_value, early, came, grad_qkv,
    q_sent, q_half, q_in, q_in2, q_out, w_sent, w_half, w_in, w_in2, w_out_v,
    e_own, e_in, flat_in, ffn_in, ffn_sent, ffn_came, grad_normed, normed_in, row_in, gain_in, l_sem, s_sem, r_sem,
):
    core, x, y, (to_core, to_x, to_y) = places()
    used = [0, 0]
    sent = []

    def here(source, target):
        k = used[0]
        used[0] += 1
        copy = pltpu.make_async_copy(source, target, l_sem.at[k])
        copy.start()
        return copy

    def remote(source, target, where):
        k = used[1]
        used[1] += 1
        return pltpu.make_async_remote_copy(
            src_ref=source, dst_ref=target, send_sem=s_sem.at[k], recv_sem=r_sem.at[k],
            device_id=where, device_id_type=pl.DeviceIdType.MESH,
        )

    def there(source, target, where):
        copy = remote(source, target, where)
        copy.start()
        sent.append(copy)
        return copy

    rows = query.shape[0]
    heads = query.shape[1] // HD
    mine = heads * HD
    q_rows, w_rows = q_in.shape[0], w_in.shape[0]
    e_rows = e_own.shape[0]
    n, me = lax.axis_size("tp"), lax.axis_index("tp")
    tp = [{"tp": (me + d) % n} for d in range(1, n)]
    own_width = ffn_own.shape[1]

    def columns(d):
        return pl.ds(pl.multiple_of(((me + d) % n) * own_width, own_width), own_width)

    greet_all([to_core, to_x, to_y] + tp)

    b3 = there(egu.at[pl.ds((1 - x) * e_rows, e_rows)], e_in, to_x)
    b6 = there(ed_f.at[core, x], ed_f.at[core, x], to_x)
    d3 = [there(sd_f.at[core, 0, y], sd_f.at[core, 0, y], to_y)]
    f1 = there(flat, flat_in.at[0], to_core)
    z_ffn = [
        there(ffn.at[pl.ds(rows, rows), columns(d)], ffn_in.at[n + d], tp[d - 1]) for d in range(1, n)
    ]
    own_ffn = [here(ffn.at[pl.ds(m * rows, rows), columns(0)], ffn_in.at[m * n]) for m in (1, 0)]
    load_attn = here(attn, attn_v)
    load_normed = here(normed, normed_v)
    loads = [here(w_query, wq_v), here(w_key, wk_v), here(w_value, wv_v)]
    load_e = here(egu.at[pl.ds(x * e_rows, e_rows)], e_own)

    grad_attn[...] = mm_nt(low[...], w_out[...]).astype(BF16)
    key_at = (y - 1) * rows + lax.broadcasted_iota(jnp.int32, (1, 2 * rows), 1)
    query_at = y * rows + lax.broadcasted_iota(jnp.int32, (rows, 1), 0)
    allowed = (query_seg[...] == key_seg[...]) & (key_at <= query_at)
    sums_of = jnp.zeros((rows, 1), F32)
    early_copies = []
    for h in range(heads):
        own = slice(h * HD, (h + 1) * HD)
        q, k, v, g = query[:, own], keys[:, own], values[:, own], grad_attn[:, own]
        scores = jnp.where(allowed, mm_nt(q, k) * scale, NEG)
        probs = jnp.exp(scores - lse[:, h : h + 1])
        grad_probs = mm_nt(g, v)
        weighted = probs * grad_probs
        grad_scores = (weighted - probs * jnp.sum(weighted, axis=1, keepdims=True)).astype(BF16)
        grad_q = mm(grad_scores, k) * scale
        grad_k = mm_tn(grad_scores, q) * scale
        grad_v = mm_tn(probs.astype(BF16), g)
        grad_key[:, own] = grad_k[rows:]
        grad_value[:, own] = grad_v[rows:]
        early[h, 0] = grad_k[:rows].astype(BF16)
        early[h, 1] = grad_v[:rows].astype(BF16)
        copy = remote(early.at[h], came.at[h], to_y)
        early_copies.append(copy)

        @pl.when(y == 1)
        def _(copy=copy):
            copy.start()

        sums_of = sums_of + jnp.sum(grad_q * q.astype(F32), axis=1, keepdims=True)
        turned = grad_q * cos[...] + pltpu.roll(grad_q, HD // 2, 1) * sin[...]
        grad_qkv[:, own] = turned.astype(BF16)

    d1 = there(sgu_f.at[core, y, 1 - x], sgu_f.at[core, y, 1 - x], to_y)
    load_attn.wait()
    half_of = low.shape[1] // 2
    w_sent[...] = mm_tn(attn_v[...], low[:, pl.ds(pl.multiple_of((1 - core) * half_of, half_of), half_of)]).astype(BF16)
    a0 = there(w_sent, w_half, to_core)
    w_own = mm_tn(attn_v[...], low[:, pl.ds(pl.multiple_of(core * half_of, half_of), half_of)])
    f1.wait_recv()
    flat_f[...] = flat[...] + flat_in[0]
    f2 = there(flat_f, flat_in.at[1], to_x)
    a0.wait_recv()
    w_half[...] = (w_own + w_half[...].astype(F32)).astype(BF16)
    a2 = there(w_half.at[pl.ds((1 - y) * w_rows, w_rows)], w_in, to_y)

    for h in range(heads):
        own = slice(h * HD, (h + 1) * HD)

        @pl.when(y == 0)
        def _(h=h, own=own):
            early_copies[h].wait_recv()
            grad_key[:, own] = grad_key[:, own] + came[h, 0].astype(F32)
            grad_value[:, own] = grad_value[:, own] + came[h, 1].astype(F32)

        @pl.when(y == 1)
        def _(h=h):
            early_copies[h].wait_send()

        grad_k, grad_v = grad_key[:, own], grad_value[:, own]
        sums_of = sums_of + jnp.sum(
            grad_k * keys[rows:, own].astype(F32) + grad_v * values[rows:, own].astype(F32),
            axis=1, keepdims=True,
        )
        turned = grad_k * cos[...] + pltpu.roll(grad_k, HD // 2, 1) * sin[...]
        grad_qkv[:, mine + h * HD : mine + (h + 1) * HD] = turned.astype(BF16)
        grad_qkv[:, 2 * mine + h * HD : 2 * mine + (h + 1) * HD] = grad_v.astype(BF16)
    row_in[0] = jnp.broadcast_to(sums_of, (rows, 128)).T[:8]
    z_rows = [there(row_in.at[0], row_in.at[d], tp[d - 1]) for d in range(1, n)]

    load_normed.wait()
    tall = q_half.shape[0]
    step = tall // 4

    def product(i, which):
        start = pl.multiple_of(which * tall + i * step, step)
        return mm_tn(normed_v[:, pl.ds(start, step)], grad_qkv[...])

    a0q = []
    for i in range(4):
        q_sent[i * step : (i + 1) * step, :] = product(i, 1 - core).astype(BF16)
        a0q.append(there(q_sent.at[pl.ds(i * step, step)], q_half.at[pl.ds(i * step, step)], to_core))
    for i in range(4):
        value = product(i, core)
        a0q[i].wait_recv()
        here_rows = slice(i * step, (i + 1) * step)
        q_half[here_rows, :] = (value + q_half[here_rows, :].astype(F32)).astype(BF16)
    a1 = there(q_half.at[pl.ds((1 - y) * q_rows, q_rows)], q_in, to_y)
    for copy in loads:
        copy.wait()
    grad_normed[...] = (
        mm_nt(grad_qkv[:, :mine], wq_v[...])
        + mm_nt(grad_qkv[:, mine : 2 * mine], wk_v[...])
        + mm_nt(grad_qkv[:, 2 * mine :], wv_v[...])
    ).astype(BF16)
    z_normed = [there(grad_normed.at[:, columns(d)], normed_in.at[d], tp[d - 1]) for d in range(1, n)]
    z_own = [there(ffn.at[pl.ds(0, rows), columns(d)], ffn_in.at[d], tp[d - 1]) for d in range(1, n)]

    load_e.wait()
    b3.wait_recv()
    add_rows(e_own, e_in, 0, e_rows)
    cut, cut_b = e_rows // 64 * 16, e_rows * 5 // 128 * 16
    b5a = there(e_own.at[pl.ds(0, cut)], egu_f.at[core, x, pl.ds(0, cut)], to_x)
    f2.wait_recv()
    f2.wait_send()
    flat_f[...] = flat_f[...] + flat_in[1]
    f3 = there(flat_f, flat_in.at[2], to_y)
    a2.wait_recv()
    add_rows(w_half, w_in, y * w_rows, w_rows)
    a4 = there(w_half.at[pl.ds(y * w_rows + (1 - x) * (w_rows // 2), w_rows // 2)], w_in2, to_x)
    a1.wait_recv()
    add_rows(q_half, q_in, y * q_rows, q_rows)
    a3 = there(q_half.at[pl.ds(y * q_rows + (1 - x) * (q_rows // 2), q_rows // 2)], q_in2, to_x)
    own_e = here(e_own, egu_f.at[core, x])
    d3.append(there(sd_f.at[core, 1, y], sd_f.at[core, 1, y], to_y))
    for copy in own_ffn:
        copy.wait()
    for copy in z_ffn:
        copy.wait_recv()
    total = ffn_in[n].astype(F32)
    for m in range(n + 1, 2 * n):
        total = total + ffn_in[m].astype(F32)
    ffn_sent[...] = total.astype(BF16)
    o1 = there(ffn_sent, ffn_came, to_y)
    for copy in z_normed + z_rows:
        copy.wait_recv()
    total = grad_normed[:, columns(0)].astype(F32)
    row_sum = row_in[0]
    for d in range(1, n):
        total = total + normed_in[d].astype(F32)
        row_sum = row_sum + row_in[d]
    normed_own[...] = total
    row_total[...] = row_sum
    gain = jnp.sum(total * tokens[...].astype(F32) * inv_one[...], axis=0, keepdims=True)
    gain_f[...] = jnp.broadcast_to(gain, gain_f.shape)
    g1 = there(gain_f, gain_in.at[0], to_core)
    a4.wait_recv()
    add_rows(w_half, w_in2, y * w_rows + x * (w_rows // 2), w_rows // 2, w_out_v)
    a6 = there(w_out_v, wo_f.at[core, y, x], to_x)
    own_w = here(w_out_v, wo_f.at[core, y, x])
    g1.wait_recv()
    g1.wait_send()
    gain_f[...] = gain_f[...] + gain_in[0]
    g2 = there(gain_f, gain_in.at[1], to_x)
    a3.wait_recv()
    add_rows(q_half, q_in2, y * q_rows + x * (q_rows // 2), q_rows // 2, q_out)
    a5 = there(q_out, qkv_f.at[core, y, x], to_x)
    own_q = here(q_out, qkv_f.at[core, y, x])
    b5 = there(e_own.at[pl.ds(cut, cut_b - cut)], egu_f.at[core, x, pl.ds(cut, cut_b - cut)], to_x)
    b7 = there(e_own.at[pl.ds(cut_b, e_rows - cut_b)], egu_f.at[core, x, pl.ds(cut_b, e_rows - cut_b)], to_x)
    b6.wait_recv()
    c6 = there(ed_f.at[core], ed_f.at[core], to_core)
    d1.wait_recv()
    c1 = there(sgu_f.at[core], sgu_f.at[core], to_core)
    g2.wait_recv()
    g2.wait_send()
    gain_f[...] = gain_f[...] + gain_in[1]
    g3 = there(gain_f, gain_in.at[2], to_y)
    a6.wait_recv()
    own_w.wait()
    a8 = there(wo_f.at[core, y], wo_f.at[core, y], to_y)
    a5.wait_recv()
    own_q.wait()
    a7 = there(qkv_f.at[core, y], qkv_f.at[core, y], to_y)
    for copy in d3:
        copy.wait_recv()
    c2 = there(sd_f.at[core], sd_f.at[core], to_core)
    f3.wait_recv()
    f3.wait_send()
    flat_f[...] = flat_f[...] + flat_in[2]
    own_e.wait()
    b5a.wait_recv()
    b5.wait_recv()
    c3 = there(egu_f.at[core, :, pl.ds(0, cut_b)], egu_f.at[core, :, pl.ds(0, cut_b)], to_core)
    b7.wait_recv()
    rest = pl.ds(cut_b, e_rows - cut_b)
    c7 = there(egu_f.at[core, :, rest], egu_f.at[core, :, rest], to_core)
    a8.wait_recv()
    c5 = there(wo_f.at[core], wo_f.at[core], to_core)
    a7.wait_recv()
    c4 = there(qkv_f.at[core], qkv_f.at[core], to_core)
    g3.wait_recv()
    g3.wait_send()
    gain_f[...] = gain_f[...] + gain_in[2]
    for copy in z_own:
        copy.wait_recv()
    o1.wait_recv()
    total = ffn_came[...].astype(F32)
    for m in range(n):
        total = total + ffn_in[m].astype(F32)
    ffn_own[...] = total
    for copy in (c1, c2, c3, c4, c5, c6, c7):
        copy.wait_recv()
    for copy in sent:
        if all(copy is not other for other in (f2, f3, g1, g2, g3)):
            copy.wait_send()


def tail(sgu, sd, egu, ed, flat, normed, w_query, w_key, w_value, attn, ffn, tokens, inv_one, low, w_out, query, keys, values, lse, query_seg, key_seg, cos, sin):
    rows, width = low.shape
    mine = query.shape[1]
    heads = mine // HD

    def pieces(count, height, wide):
        return jax.ShapeDtypeStruct((2,) * count + (height, wide), BF16)

    far = pl.BlockSpec(memory_space=pl.ANY)
    vmem = pl.BlockSpec(memory_space=pltpu.VMEM)

    def room(*shape, kind=BF16):
        return pltpu.VMEM(shape, kind)

    half_of = width // 2
    n = lax.axis_size("tp")
    dma = pltpu.SemaphoreType.DMA
    return pl.pallas_call(
        functools.partial(tail_kernel, 1.0 / math.sqrt(HD)),
        out_shape=[
            jax.ShapeDtypeStruct(sgu.shape, BF16), jax.ShapeDtypeStruct(sd.shape, BF16),
            pieces(2, egu.shape[0] // 2, egu.shape[1]), jax.ShapeDtypeStruct(ed.shape, BF16),
            pieces(3, half_of // 4, 3 * mine), pieces(3, mine // 4, half_of),
            jax.ShapeDtypeStruct(flat.shape, F32), jax.ShapeDtypeStruct(tokens.shape, F32),
            jax.ShapeDtypeStruct(tokens.shape, F32), jax.ShapeDtypeStruct((8, rows), F32),
            jax.ShapeDtypeStruct((8, tokens.shape[1]), F32),
        ],
        in_specs=[far] * 4 + [vmem] + [far] * 6 + [vmem] * 12,
        out_specs=[far] * 6 + [vmem] * 5,
        scratch_shapes=[
            room(rows, width), room(width, mine), room(width, mine), room(width, mine), room(rows, mine),
            room(rows, mine), room(rows, mine, kind=F32), room(rows, mine, kind=F32),
            room(heads, 2, rows, HD), room(heads, 2, rows, HD), room(rows, 3 * mine),
            room(half_of, 3 * mine), room(half_of, 3 * mine), room(half_of // 2, 3 * mine),
            room(half_of // 4, 3 * mine), room(half_of // 4, 3 * mine),
            room(mine, half_of), room(mine, half_of), room(mine // 2, half_of),
            room(mine // 4, half_of), room(mine // 4, half_of),
            room(egu.shape[0] // 2, egu.shape[1]), room(egu.shape[0] // 2, egu.shape[1]),
            room(3, *flat.shape, kind=F32), room(2 * n, *tokens.shape), room(*tokens.shape), room(*tokens.shape), room(rows, width), room(n, *tokens.shape),
            room(n, 8, rows, kind=F32), room(3, 8, tokens.shape[1], kind=F32),
            dma((18,)), dma((38 + heads + 4 * n,)), dma((38 + heads + 4 * n,)),
        ],
        input_output_aliases={0: 0, 1: 1, 3: 3},
        compiler_params=pltpu.CompilerParams(
            collective_id=3, has_side_effects=True, vmem_limit_bytes=62 << 20
        ),
        cost_estimate=pl.CostEstimate(flops=0, bytes_accessed=0, transcendentals=0),
    )(sgu, sd, egu, ed, flat, normed, w_query, w_key, w_value, attn, ffn, tokens, inv_one, low, w_out, query, keys, values, lse, query_seg, key_seg, cos, sin)


def widen_kernel(source, *outputs):
    value = source[...]
    value = value.reshape(value.shape[-2:])
    start = 0
    for out in outputs:
        width = out.shape[1]
        out[...] = value[:, start : start + width].astype(F32)
        start += width


def widen(value, widths=(), kinds=1, kind=0, across=2):
    columns = value.shape[-1]
    if widths:
        value = value.reshape(-1, columns)
        rows = value.shape[0]
        step = min(rows, 256)
        source = pl.BlockSpec((step, columns), lambda i: (i, 0))
        grid = (rows // step,)
        specs = [pl.BlockSpec((step, width), lambda i: (i, 0)) for width in widths]
        shapes = [jax.ShapeDtypeStruct((rows, width), F32) for width in widths]
    else:
        value = value.reshape(across, kinds, -1, columns)
        rows = value.shape[2]
        step = rows
        while step * columns > (1 << 20) and step % 32 == 0:
            step //= 2
        steps = rows // step
        source = pl.BlockSpec((1, 1, step, columns), lambda i, c: (c, kind, i, 0))
        grid = (steps, across)
        specs = [pl.BlockSpec((step, columns), lambda i, c: (i, c))]
        shapes = [jax.ShapeDtypeStruct((rows, across * columns), F32)]
    return pl.pallas_call(
        widen_kernel,
        grid=grid,
        in_specs=[source],
        out_specs=specs,
        out_shape=shapes,
        compiler_params=pltpu.CompilerParams(vmem_limit_bytes=24 << 20),
        cost_estimate=pl.CostEstimate(flops=0, bytes_accessed=0, transcendentals=0),
    )(value)


def weight_kernel(added, part, left, right, *refs):
    total = mm_tn(left[...], right[...])
    if added:
        total = total + refs[0][...].astype(F32)
    refs[-1][...] = total.astype(BF16)


def weight_half(left, right, which, columns, got=None, rows=None, block=1408):
    rows = rows or left.shape[0]
    height, wide = left.shape[1], right.shape[1]
    if columns:
        wide = wide // 2
    else:
        height = height // 2
    step = height
    while step > block and step % 256 == 0:
        step //= 2
    steps = height // step
    extra = [] if got is None else [got]
    out_spec = pl.BlockSpec((step, wide), lambda i, part: (i, 0))
    if columns:
        left_at, right_at = (lambda i, part: (0, i)), (lambda i, part: (0, part[0]))
    else:
        left_at, right_at = (lambda i, part: (0, part[0] * steps + i)), (lambda i, part: (0, 0))
    return pl.pallas_call(
        functools.partial(weight_kernel, bool(extra)),
        grid_spec=pltpu.PrefetchScalarGridSpec(
            num_scalar_prefetch=1,
            grid=(steps,),
            in_specs=[pl.BlockSpec((rows, step), left_at), pl.BlockSpec((rows, wide), right_at)]
            + [out_spec] * len(extra),
            out_specs=out_spec,
        ),
        out_shape=jax.ShapeDtypeStruct((height, wide), BF16),
        compiler_params=pltpu.CompilerParams(vmem_limit_bytes=48 << 20),
        cost_estimate=pl.CostEstimate(flops=0, bytes_accessed=0, transcendentals=0),
    )(which.reshape(1).astype(jnp.int32), left, right, *extra)


def ffn_kernel(groups, base, flipped, carry, *refs):
    rows, grads, scale, *stored = refs[:6]
    refs = refs[6:]
    if base:
        base_out, base_dx = refs[:2]
        refs = refs[2:]
    sources, refs = refs[: len(carry)], refs[len(carry) :]
    hid_ref, dgu_ref, out_ref, dx_ref, small_ref, *refs = refs
    *refs, gate_w, up_w, down_w, w_sem = refs
    weights = [
        pltpu.make_async_copy(source, target, w_sem.at[m])
        for m, (source, target) in enumerate(zip(stored, (gate_w, up_w, down_w)))
    ]

    @pl.when(pl.program_id(0) == 0)
    def _():
        for copy in weights:
            copy.start()

    copies = []
    if carry:
        send_sem, recv_sem = refs[-2:]
        _, x, y, where = places()
        for m, (link, count, start, stride) in enumerate(carry):
            first = start + (1 - (x, y)[link - 1]) * stride
            copies.append(
                pltpu.make_async_remote_copy(
                    src_ref=sources[m].at[pl.ds(first, count)], dst_ref=refs[m],
                    send_sem=send_sem.at[m], recv_sem=recv_sem.at[m],
                    device_id=where[link], device_id_type=pl.DeviceIdType.MESH,
                )
            )
        links = sorted({link for link, _, _, _ in carry})

        @pl.when(pl.program_id(0) == 0)
        def _():
            greet_all([where[link] for link in links])
            for copy in copies:
                copy.start()

    @pl.when(pl.program_id(0) == 0)
    def _():
        for copy in weights:
            copy.wait()

    width = down_w.shape[0]
    to, back = (mm_nt, mm) if flipped else (mm, mm_nt)
    gate_pre = to(rows[...], gate_w[...])
    up_pre = to(rows[...], up_w[...])
    grad_hidden = mm_nt(grads[...], down_w[...])
    sig = 1.0 / (1.0 + jnp.exp(-gate_pre))
    act = gate_pre * sig
    slope = sig + act * (1.0 - sig)
    hidden = (act * up_pre).astype(BF16).astype(F32)
    each = width // groups
    column = lax.broadcasted_iota(jnp.int32, (1, width), 1)
    wide = scale[:, 0:1]
    for e in range(1, groups):
        wide = jnp.where(column >= e * each, scale[:, e : e + 1], wide)
    prod = hidden * grad_hidden
    for e in range(groups):
        part = prod
        if groups > 1:
            part = jnp.where((column >= e * each) & (column < (e + 1) * each), prod, 0.0)
        small_ref[:, e : e + 1] = jnp.sum(part, axis=1, keepdims=True)
    hid = (hidden * wide).astype(BF16)
    hid_ref[...] = hid
    scaled = grad_hidden * wide
    dgate = (scaled * up_pre * slope).astype(BF16)
    dup = (scaled * act).astype(BF16)
    dgu_ref[:, :width] = dgate
    dgu_ref[:, width:] = dup
    small_ref[:, groups : groups + 1] = jnp.sum(
        dgate.astype(F32) * gate_pre + dup.astype(F32) * up_pre, axis=1, keepdims=True
    )
    out = mm(hid, down_w[...])
    dx = back(dgate, gate_w[...]) + back(dup, up_w[...])
    if base:
        own = jnp.where(2 * pl.program_id(0) >= pl.num_programs(0), 1.0, 0.0)
        out = out + own * base_out[...].astype(F32)
        dx = dx + own * base_dx[...].astype(F32)
    out_ref[...] = out.astype(BF16)
    dx_ref[...] = dx.astype(BF16)
    if carry:

        @pl.when(pl.program_id(0) == pl.num_programs(0) - 1)
        def _():
            for copy in copies:
                copy.wait()


def ffn(rows, grads, scale, gate_w, up_w, down_w, count, base=(), flipped=False, carry=(), number=None):
    groups = scale.shape[1]
    width = rows.shape[1]
    hidden = down_w.shape[0]
    block = min(256, count)
    steps = count // block

    def at(n):
        if base:
            return pl.BlockSpec((block, n), lambda i: ((i + steps // 2) % steps, 0))
        return pl.BlockSpec((block, n), lambda i: (i, 0))

    def late(n):
        return pl.BlockSpec((block, n), lambda i: (jnp.maximum(i - steps // 2, 0), 0))

    far = pl.BlockSpec(memory_space=pl.ANY)
    return pl.pallas_call(
        functools.partial(
            ffn_kernel, groups, bool(base), flipped, tuple(c[1:] for c in carry)
        ),
        grid=(steps,),
        in_specs=[at(width), at(width), at(groups)]
        + [far] * 3
        + [late(width)] * len(base)
        + [far] * len(carry),
        out_specs=[
            at(hidden),
            at(2 * hidden),
            at(width),
            at(width),
            at(groups + 1),
        ]
        + [far] * len(carry),
        out_shape=[
            jax.ShapeDtypeStruct((count, hidden), BF16),
            jax.ShapeDtypeStruct((count, 2 * hidden), BF16),
            jax.ShapeDtypeStruct((count, width), BF16),
            jax.ShapeDtypeStruct((count, width), BF16),
            jax.ShapeDtypeStruct((count, groups + 1), F32),
        ]
        + [jax.ShapeDtypeStruct((c[2], c[0].shape[1]), BF16) for c in carry],
        scratch_shapes=([pltpu.SemaphoreType.DMA((len(carry),))] * 2 if carry else [])
        + [pltpu.VMEM(w.shape, BF16) for w in (gate_w, up_w, down_w)]
        + [pltpu.SemaphoreType.DMA((3,))],
        compiler_params=pltpu.CompilerParams(
            vmem_limit_bytes=62 << 20, collective_id=number, has_side_effects=bool(carry)
        ),
        cost_estimate=pl.CostEstimate(flops=0, bytes_accessed=0, transcendentals=0),
    )(rows, grads, scale, gate_w, up_w, down_w, *base, *[c[0] for c in carry])


def line_sum(depth, prepare, settle, gathered, beside, part, came, came_two, spread, sems):
    n = lax.axis_size("tp")
    me = lax.axis_index("tp")
    chunks, _, step, _ = part.shape
    sum_send, sum_recv, two_recv, out_send, out_recv = sems

    def send(source, target, send_sem, recv_sem, to):
        return pltpu.make_async_remote_copy(
            src_ref=source, dst_ref=target, send_sem=send_sem, recv_sem=recv_sem,
            device_id={"tp": to}, device_id_type=pl.DeviceIdType.MESH,
        )

    def sum_copy(c, s, to_right, two):
        target = came_two.at[c] if two else came.at[c, s]
        sem = two_recv.at[c] if two else sum_recv.at[c, s]
        return send(part.at[c, s], target, sum_send.at[c, s], sem, me + 1 if to_right else me - 1)

    def out_copy(c, s, to_right):
        return send(
            spread.at[c, s], spread.at[c, s], out_send.at[c, s, 1 if to_right else 0],
            out_recv.at[c, s], me + 1 if to_right else me - 1,
        )

    def within(c):
        return (c >= 0) & (c < chunks)

    def pass_sums(t):
        @pl.when(within(t))
        def _():
            prepare(t)

        for s in range(n):
            c = t - me * depth

            @pl.when((me < s) & within(c))
            def _(s=s, c=c):
                @pl.when(me > 0)
                def _():
                    sum_copy(c, s, True, False).wait_recv()
                    part[c, s] = (part[c, s].astype(F32) + came[c, s].astype(F32)).astype(BF16)

                sum_copy(c, s, True, False).start()

        for s in range(n):
            c = t - (n - 1 - me) * depth

            @pl.when((me > s) & within(c))
            def _(s=s, c=c):
                @pl.when(me < n - 1)
                def _():
                    sum_copy(c, s, False, False).wait_recv()
                    part[c, s] = (part[c, s].astype(F32) + came[c, s].astype(F32)).astype(BF16)

                @pl.when(me - 1 == s)
                def _():
                    sum_copy(c, s, False, True).start()

                @pl.when(me - 1 > s)
                def _():
                    sum_copy(c, s, False, False).start()

    def pass_own(t):
        c = t - (n - 1) * depth
        for s in range(n):

            @pl.when((me == s) & within(c))
            def _(s=s):
                if s > 0:
                    sum_copy(c, s, True, False).wait_recv()
                if s < n - 1:
                    sum_copy(c, s, False, True).wait_recv()
                total = part[c, s].astype(F32)
                if s > 0:
                    total = total + came[c, s].astype(F32)
                if s < n - 1:
                    total = total + came_two[c].astype(F32)
                spread[c, s] = settle(c, total)
                if s > 0:
                    out_copy(c, s, False).start()
                if s < n - 1:
                    out_copy(c, s, True).start()

    def pass_out(t):
        for s in range(n):
            right = t - (n - 1 + me - s) * depth
            left = t - (n - 1 + s - me) * depth

            @pl.when((me > s) & within(right))
            def _(s=s, c=right):
                out_copy(c, s, True).wait_recv()

                @pl.when(me < n - 1)
                def _():
                    out_copy(c, s, True).start()

            @pl.when((me < s) & within(left))
            def _(s=s, c=left):
                out_copy(c, s, False).wait_recv()

                @pl.when(me > 0)
                def _():
                    out_copy(c, s, False).start()

        last = t - 2 * (n - 1) * depth

        @pl.when(within(last))
        def _():
            gathered(last)

    def turn(t, carry):
        pass_sums(t)
        pass_own(t)
        pass_out(t)
        if beside is not None:
            beside(t)
        return carry

    lax.fori_loop(0, chunks + 2 * (n - 1) * depth, turn, 0)

    def drain(c, carry):
        for s in range(n):

            @pl.when(me != s)
            def _(s=s):
                sum_copy(c, s, True, False).wait_send()

            @pl.when((me < n - 1) & (s <= me))
            def _(s=s):
                out_copy(c, s, True).wait_send()

            @pl.when((me > 0) & (s >= me))
            def _(s=s):
                out_copy(c, s, False).wait_send()

        return carry

    lax.fori_loop(0, chunks, drain, 0)


def line_scratch(rows, width_own):
    n = lax.axis_size("tp")
    chunks = max(1, min(16, 128 // n))
    step = rows // chunks
    slots = pltpu.VMEM((chunks, n, step, width_own), BF16)
    dma = pltpu.SemaphoreType.DMA
    return chunks, step, [
        slots, slots, pltpu.VMEM((chunks, step, width_own), BF16), slots,
        dma((chunks, n)), dma((chunks, n)), dma((chunks,)), dma((chunks, n, 2)), dma((chunks, n)),
    ]


def greet(peers):
    n = lax.axis_size("tp")
    me = lax.axis_index("tp")
    barrier = pltpu.get_barrier_semaphore()

    def signal(where):
        pl.semaphore_signal(barrier, inc=1, device_id=where, device_id_type=pl.DeviceIdType.MESH)

    @pl.when(me > 0)
    def _():
        signal({"tp": me - 1})

    @pl.when(me < n - 1)
    def _():
        signal({"tp": me + 1})

    for where in peers:
        signal(where)

    beside = jnp.where(me > 0, 1, 0) + jnp.where(me < n - 1, 1, 0)
    pl.semaphore_wait(barrier, beside + len(peers))


def attend_out_kernel(
    chunks, step, depth, experts, attn, w_out, x, gain, grads, w_small, hot, hot_peer,
    mixed, resid_own, inv_out, grads_peer, logits, prob, switch, gates,
    part, came, came_two, spread, s0, s1, s2, s3, s4, y_send, y_recv, g_send, g_recv,
):
    n = lax.axis_size("tp")
    me = lax.axis_index("tp")
    own = part.shape[3]
    rows = attn.shape[0]
    other = {"ep": 1 - lax.axis_index("ep")}
    greet([other])
    grads_copy = pltpu.make_async_remote_copy(
        src_ref=grads.at[pl.ds(0, grads_peer.shape[0])], dst_ref=grads_peer, send_sem=g_send, recv_sem=g_recv,
        device_id=other, device_id_type=pl.DeviceIdType.MESH,
    )
    grads_copy.start()
    block = max(step, min(rows, 128))

    def product(b, carry):
        start = pl.multiple_of(b * block, block)
        value = mm(attn[pl.ds(start, block), :], w_out[...]).astype(BF16)
        for s in range(n):
            for k in range(block // step):
                part[b * (block // step) + k, s] = value[k * step:(k + 1) * step, s * own:(s + 1) * own]
        return carry

    lax.fori_loop(0, rows // block, product, 0)

    def at(c):
        return pl.ds(pl.multiple_of(c * step, step), step)

    def peer_copy(c):
        return pltpu.make_async_remote_copy(
            src_ref=mixed.at[at(c)], dst_ref=mixed.at[pl.ds(pl.multiple_of(rows + c * step, step), step)], send_sem=y_send.at[c], recv_sem=y_recv.at[c],
            device_id=other, device_id_type=pl.DeviceIdType.MESH,
        )

    def prepare(c):
        pass

    def settle(c, total):
        return total.astype(BF16)

    place = lax.broadcasted_iota(jnp.int32, (1, w_small.shape[0]), 1)
    here = lax.axis_index("ep") == 0

    def chances(scores):
        scores = jnp.where(place < experts, scores, NEG)
        raised = jnp.exp(scores - jnp.max(scores, axis=1, keepdims=True))
        return jnp.where(place < experts, raised / jnp.sum(raised, axis=1, keepdims=True), 0.0)

    def own_gates(value):
        return jnp.where(here, value[:, : experts // 2], value[:, experts // 2 : experts])

    def gathered(c):
        resid = []
        square = jnp.zeros((step, 1), F32)
        for s in range(n):
            piece = x[at(c), s * own:(s + 1) * own].astype(F32) + spread[c, s].astype(F32)
            resid.append(piece)
            square = square + jnp.sum(piece * piece, axis=1, keepdims=True)
        inv = lax.rsqrt(square / (n * own) + EPS)
        inv_out[at(c), :] = inv
        for s in range(n):
            mixed[at(c), s * own:(s + 1) * own] = (resid[s] * inv * gain[:, s * own:(s + 1) * own]).astype(BF16)

            @pl.when(me == s)
            def _(s=s):
                resid_own[at(c), :] = resid[s]

        peer_copy(c).start()

    line_sum(depth, prepare, settle, gathered, None, part, came, came_two, spread, (s0, s1, s2, s3, s4))

    scores = mm_nt(mixed[:rows, :], w_small[...])
    chance = chances(scores)
    logits[...] = scores
    prob[...] = chance
    switch[...] = 1.0 / (1.0 + jnp.exp(-scores[:, experts : experts + 1]))
    gates[:rows, :] = own_gates(chance * hot[...])

    def last(c, carry):
        peer_copy(c).wait_recv()
        peer_copy(c).wait_send()
        return carry

    lax.fori_loop(0, chunks, last, 0)
    chance = chances(mm_nt(mixed[rows:, :], w_small[...]))
    gates[rows:, :] = own_gates(chance * hot_peer[...].astype(F32))
    grads_copy.wait()


def attend_out(attn, w_out, x, gain, grads, w_small, hot, hot_peer, experts, width_own, depth=1):
    rows, width = x.shape
    chunks, step, scratch = line_scratch(rows, width_own)
    vmem = pl.BlockSpec(memory_space=pltpu.VMEM)
    far = pl.BlockSpec(memory_space=pl.ANY)
    dma = pltpu.SemaphoreType.DMA
    return pl.pallas_call(
        functools.partial(attend_out_kernel, chunks, step, depth, experts),
        out_shape=[
            jax.ShapeDtypeStruct((2 * rows, width), BF16),
            jax.ShapeDtypeStruct((rows, width_own), F32), jax.ShapeDtypeStruct((rows, 1), F32),
            jax.ShapeDtypeStruct((rows // 2, width), BF16),
            jax.ShapeDtypeStruct(hot.shape, F32), jax.ShapeDtypeStruct(hot.shape, F32),
            jax.ShapeDtypeStruct((rows, 1), F32), jax.ShapeDtypeStruct((2 * rows, experts // 2), F32),
        ],
        in_specs=[vmem] * 4 + [far] + [vmem] * 3,
        out_specs=[vmem] * 3 + [far] + [vmem] * 4,
        scratch_shapes=scratch + [dma((chunks,)), dma((chunks,)), dma, dma],
        compiler_params=pltpu.CompilerParams(collective_id=1, has_side_effects=True, vmem_limit_bytes=40 << 20),
        cost_estimate=pl.CostEstimate(flops=0, bytes_accessed=0, transcendentals=0),
    )(attn, w_out, x, gain, grads, w_small, hot, hot_peer)


def resid_grad_kernel(
    chunks, step, depth, tiles, grads_all, dgu, hid, both, both_grad, sgu, sd,
    small_e, small_p, small_s, prob, hot, logits, switch, w_small, g_own, resid_own, inv_two, gain,
    low, grad_resid, gain_grad, sum_egu, ed_f, sgu_f, sd_f, grad_small,
    part, came, came_two, spread, s0, s1, s2, s3, s4, back, y_send, y_recv, grad,
    dgu_v, hid_v, both_v, both_grad_v, sent_egu, sent_ed, came_egu, came_ed,
    s_own, s_in, d_own, d_in, l_sem, w_send, w_recv, w_out, r_send, r_recv, r_out,
    router, along, small_y, small_z, ed_in, ed_out, t_send, t_recv, e_send, e_recv, e_out,
):
    n = lax.axis_size("tp")
    own = part.shape[3]
    rows = grad.shape[0]
    load_grad = pltpu.make_async_copy(grads_all.at[pl.ds(0, rows)], grad, l_sem.at[6])
    core, x, y, (to_core, to_x, other) = places()

    def at(c):
        return pl.ds(pl.multiple_of(c * step, step), step)

    def peer_copy(c):
        return pltpu.make_async_remote_copy(
            src_ref=grads_all.at[pl.ds(pl.multiple_of(rows + c * step, step), step)], dst_ref=back.at[at(c)], send_sem=y_send.at[c], recv_sem=y_recv.at[c],
            device_id=other, device_id_type=pl.DeviceIdType.MESH,
        )

    loads = [
        pltpu.make_async_copy(source, target, l_sem.at[m])
        for m, (source, target) in enumerate(
            (
                (dgu, dgu_v),
                (both, both_v),
                (hid, hid_v),
                (both_grad, both_grad_v),
                (sgu.at[pl.ds(x * s_own.shape[0], s_own.shape[0])], s_own),
                (sd.at[pl.ds(y * d_own.shape[0], d_own.shape[0])], d_own),
            )
        )
    ]
    kinds = ((dgu_v, both_v, sent_egu, came_egu, sum_egu), (hid_v, both_grad_v, sent_ed, came_ed, None))

    def sum_copies(m):
        source, target, where = (
            (sgu.at[pl.ds((1 - x) * s_own.shape[0], s_own.shape[0])], s_in, to_x),
            (sd.at[pl.ds((1 - y) * d_own.shape[0], d_own.shape[0])], d_in, other),
            (s_own, sgu_f.at[core, y, x], to_x),
            (d_own, sd_f.at[core, x, y], to_x),
            (s_own, sgu_f.at[core, y, x], other),
        )[m]
        return pltpu.make_async_remote_copy(
            src_ref=source, dst_ref=target, send_sem=r_send.at[m], recv_sem=r_recv.at[m],
            device_id=where, device_id_type=pl.DeviceIdType.MESH,
        )

    def own_out(m):
        target = (sgu_f.at[core, y, x], sd_f.at[core, x, y])[m]
        return pltpu.make_async_copy((s_own, d_own)[m], target, r_out.at[m])

    def shared(m):
        sum_copies(m).wait_recv()
        add_rows((s_own, d_own)[m], (s_in, d_in)[m], 0, (s_own, d_own)[m].shape[0])
        sum_copies(2 + m).start()
        if m == 0:
            sum_copies(4).start()
        own_out(m).start()

    def tile_copy(m, b):
        return pltpu.make_async_remote_copy(
            src_ref=kinds[m][2].at[b], dst_ref=kinds[m][3].at[b], send_sem=w_send.at[b, m], recv_sem=w_recv.at[b, m],
            device_id=to_core, device_id_type=pl.DeviceIdType.MESH,
        )

    def x_copy(b):
        wide = ed_in.shape[2]
        return pltpu.make_async_remote_copy(
            src_ref=came_ed.at[b, :, pl.ds(pl.multiple_of((1 - x) * wide, wide), wide)], dst_ref=ed_in.at[b],
            send_sem=e_send.at[b], recv_sem=e_recv.at[b],
            device_id=to_x, device_id_type=pl.DeviceIdType.MESH,
        )

    def x_out(b):
        tall = ed_in.shape[1]
        return pltpu.make_async_copy(
            ed_out.at[b], ed_f.at[core, x, pl.ds(pl.multiple_of(b * tall, tall), tall)], e_out.at[b]
        )

    def tile_out(m, b):
        tall = kinds[m][3].shape[1]
        return pltpu.make_async_copy(
            kinds[m][3].at[b], kinds[m][4].at[pl.ds(pl.multiple_of(b * tall, tall), tall)], w_out.at[b, m]
        )

    def tile(m, b, which):
        left, right = kinds[m][:2]
        tall, wide = kinds[m][3].shape[1:]
        return mm_tn(
            left[...] if tiles == 1 else left[:, pl.ds(pl.multiple_of(b * tall, tall), tall)],
            right[:, pl.ds(pl.multiple_of(which * wide, wide), wide)],
        )

    def weights(t):
        @pl.when(t == 0)
        def _():
            for copy in loads:
                copy.wait()

        @pl.when(t == 1)
        def _():
            gates()

        @pl.when(t < tiles)
        def _():
            for m in range(2):
                kinds[m][2][t] = tile(m, t, 1 - core).astype(BF16)
                tile_copy(m, t).start()

        @pl.when(t == tiles * 8 // 11)
        def _():
            shared(0)

        @pl.when(t == tiles * 14 // 11)
        def _():
            shared(1)

        @pl.when((t >= tiles) & (t < 2 * tiles))
        def _():
            b = t - tiles
            for m in range(2):
                value = tile(m, b, core)
                tile_copy(m, b).wait_recv()
                kinds[m][3][b] = (value + kinds[m][3][b].astype(F32)).astype(BF16)
                if m == 0:
                    tile_out(m, b).start()
                else:
                    x_copy(b).start()

    load_grad.start()
    for copy in loads:
        copy.start()
    me = lax.axis_index("tp")

    def small_copy(d):
        return pltpu.make_async_remote_copy(
            src_ref=small_z.at[0] if d else small_p, dst_ref=small_z.at[d] if d else small_y,
            send_sem=t_send.at[d], recv_sem=t_recv.at[d],
            device_id={"tp": (me + d) % n} if d else other, device_id_type=pl.DeviceIdType.MESH,
        )

    greet_all([other, to_core, to_x] + [{"tp": (me + d) % n} for d in range(1, n)])
    small_copy(0).start()
    sum_copies(0).start()

    def begin(c, carry):
        peer_copy(c).start()
        return carry

    lax.fori_loop(0, chunks, begin, 0)
    sum_copies(1).start()
    gain_grad[...] = jnp.zeros_like(gain_grad)
    experts_own = small_e.shape[0] - 1
    experts = 2 * experts_own
    small_copy(0).wait_recv()
    here, there = small_e[:experts_own, :], small_y[:experts_own, :]
    small_z[0] = jnp.zeros_like(small_z[0])
    small_z[0, :experts_own] = jnp.where(y == 0, here, there)
    small_z[0, experts_own:experts] = jnp.where(y == 0, there, here)
    small_z[0, experts : experts + 1] = small_s[:1, :]
    small_z[0, experts + 1 : experts + 2] = small_s[1:, :] + small_e[experts_own:, :] + small_y[experts_own:, :]
    for d in range(1, n):
        small_copy(d).start()

    def gates():
        total = small_z[0]
        for d in range(1, n):
            small_copy(d).wait_recv()
            total = total + small_z[d]
        slots = prob.shape[1]
        total = jnp.concatenate([total, jnp.zeros((128 - total.shape[0], rows), F32)], axis=0).T
        grad_prob = total[:, :slots] * hot[...]
        inner = jnp.sum(prob[...] * grad_prob, axis=1, keepdims=True)
        sw = switch[...]
        grad_switch = total[:, experts : experts + 1] * sw * (1.0 - sw)
        place = lax.broadcasted_iota(jnp.int32, (1, slots), 1)
        grads = jnp.where(place == experts, grad_switch, prob[...] * (grad_prob - inner)).astype(BF16)
        width = w_small.shape[1] // n
        router[...] = mm(grads, w_small[:, pl.ds(pl.multiple_of(me * width, width), width)])
        along[...] = total[:, experts + 1 : experts + 2] + jnp.sum(
            grads.astype(F32) * logits[...], axis=1, keepdims=True
        )
        grad_small[...] = mm_tn(grads, both_v[:rows, :])

    def prepare(c):
        @pl.when(c == 0)
        def _():
            load_grad.wait()

        peer_copy(c).wait_recv()
        for s in range(n):
            columns = slice(s * own, (s + 1) * own)
            part[c, s] = (grad[at(c), columns].astype(F32) + back[at(c), columns].astype(F32)).astype(BF16)

    def settle(c, total):
        total = total + router[at(c), :]
        inv = inv_two[at(c), :]
        resid = resid_own[at(c), :]
        gain_grad[...] += jnp.sum(total * resid * inv, axis=0, keepdims=True)
        result = g_own[at(c), :].astype(F32) + inv * gain[...] * total - resid * (inv * inv * along[at(c), :] / (n * own))
        grad_resid[at(c), :] = result
        return result.astype(BF16)

    def gathered(c):
        for s in range(n):
            low[at(c), s * own:(s + 1) * own] = spread[c, s]

    line_sum(depth, prepare, settle, gathered, weights, part, came, came_two, spread, (s0, s1, s2, s3, s4))

    def last(c, carry):
        peer_copy(c).wait_send()
        return carry

    lax.fori_loop(0, chunks, last, 0)

    def done(b, carry):
        x_copy(b).wait_recv()
        wide = ed_in.shape[2]
        own = came_ed[b, :, pl.ds(pl.multiple_of(x * wide, wide), wide)]
        ed_out[b] = (own.astype(F32) + ed_in[b].astype(F32)).astype(BF16)
        x_out(b).start()
        tile_copy(0, b).wait_send()
        tile_copy(1, b).wait_send()
        tile_out(0, b).wait()
        x_copy(b).wait_send()
        return carry

    lax.fori_loop(0, tiles, done, 0)

    def written(b, carry):
        x_out(b).wait()
        return carry

    lax.fori_loop(0, tiles, written, 0)
    for m in range(2):
        sum_copies(m).wait_send()
        sum_copies(2 + m).wait()
        own_out(m).wait()
    sum_copies(4).wait()
    for d in range(n):
        small_copy(d).wait_send()


def resid_grad(grads_all, dgu, hid, both, both_grad, sgu, sd, small_e, small_p, small_s, prob, hot, logits, switch, w_small, g_own, resid_own, inv_two, gain, depth=1):
    rows, width = grads_all.shape[0] // 2, grads_all.shape[1]
    width_own = g_own.shape[1]
    chunks, step, scratch = line_scratch(rows, width_own)
    hidden = hid.shape[1]
    tiles = 11 if hidden % (11 * 128) == 0 else 1
    vmem = pl.BlockSpec(memory_space=pltpu.VMEM)
    far = pl.BlockSpec(memory_space=pl.ANY)
    dma = pltpu.SemaphoreType.DMA
    return pl.pallas_call(
        functools.partial(resid_grad_kernel, chunks, step, depth, tiles),
        out_shape=[
            jax.ShapeDtypeStruct((rows, width), BF16), jax.ShapeDtypeStruct((rows, width_own), F32),
            jax.ShapeDtypeStruct((1, width_own), F32),
        ]
        + [jax.ShapeDtypeStruct((2 * hidden, width // 2), BF16), jax.ShapeDtypeStruct((2, 2, hidden, width // 4), BF16)]
        + [
            jax.ShapeDtypeStruct((2, 2, 2, sgu.shape[0] // 2, sgu.shape[1]), BF16),
            jax.ShapeDtypeStruct((2, 2, 2, sd.shape[0] // 2, sd.shape[1]), BF16),
        ]
        + [jax.ShapeDtypeStruct((prob.shape[1], width), F32)],
        in_specs=[far] * 7 + [vmem] * 12,
        out_specs=[vmem] * 3 + [far] * 4 + [vmem],
        scratch_shapes=scratch + [pltpu.VMEM((rows, width), BF16), dma((chunks,)), dma((chunks,)), pltpu.VMEM((rows, width), BF16)]
        + [pltpu.VMEM(v.shape, BF16) for v in (dgu, hid, both, both_grad)]
        + [pltpu.VMEM((tiles, k * hidden // tiles, width // 2), BF16) for k in (2, 1, 2, 1)]
        + [pltpu.VMEM((v.shape[0] // 2, v.shape[1]), BF16) for v in (sgu, sgu, sd, sd)]
        + [dma((7,)), dma((tiles, 2)), dma((tiles, 2)), dma((tiles, 2)), dma((5,)), dma((5,)), dma((2,))]
        + [pltpu.VMEM((rows, width_own), F32), pltpu.VMEM((rows, 1), F32)]
        + [pltpu.VMEM(small_e.shape, F32), pltpu.VMEM((lax.axis_size("tp"), 16, rows), F32)]
        + [pltpu.VMEM((tiles, hidden // tiles, width // 4), BF16)] * 2
        + [dma((lax.axis_size("tp"),))] * 2 + [dma((tiles,))] * 3,
        compiler_params=pltpu.CompilerParams(collective_id=2, has_side_effects=True, vmem_limit_bytes=63 << 20),
        cost_estimate=pl.CostEstimate(flops=0, bytes_accessed=0, transcendentals=0),
    )(grads_all, dgu, hid, both, both_grad, sgu, sd, small_e, small_p, small_s, prob, hot, logits, switch, w_small, g_own, resid_own, inv_two, gain)


def body(
    tokens,
    norm_attn,
    w_query,
    w_key,
    w_value,
    w_output,
    norm_ffn,
    w_router,
    shared_switch,
    shared_gate,
    shared_up,
    shared_down,
    expert_gate,
    expert_up,
    expert_down,
    routes,
    segments,
    output_gradient,
):
    tp_count = lax.axis_size("tp")
    ep_count = lax.axis_size("ep")
    dp_count = lax.axis_size("dp")
    tp_rank = lax.axis_index("tp")
    ep_rank = lax.axis_index("ep")
    rows = tokens.shape[0]
    width_own = tokens.shape[1]
    width = width_own * tp_count
    heads = w_query.shape[1] // HD
    experts_own = expert_gate.shape[0]
    experts = experts_own * ep_count
    expert_width = expert_gate.shape[2]
    score_scale = 1.0 / math.sqrt(HD)
    far_bits = [1 << b for b in range(1, dp_count.bit_length() - 1)]

    def own_columns(value):
        return lax.dynamic_slice_in_dim(value, tp_rank * width_own, width_own, value.ndim - 1)

    near = bit_of("dp", 1)

    def pair_send(left, right, columns, used=None):
        sent = weight_half(left, right, 1 - near, columns, rows=used)
        return sent, swap(sent, "dp", 1)

    def pair_keep(left, right, columns, got, used=None):
        return weight_half(left, right, near, columns, got, rows=used)

    core = ("dp", 1)
    far = [("dp", b) for b in far_bits]
    line = [("ep", 1)]
    x_link, y_link = far[0], line[0]

    def over_tp(value):
        if tp_count <= 4:
            others = [
                lax.ppermute(value, "tp", [(i, (i + d) % tp_count) for i in range(tp_count)])
                for d in range(1, tp_count)
            ]
            return sum(others, value)
        bit = 1
        while bit < tp_count:
            value = value + swap(value, "tp", bit)
            bit *= 2
        return value

    def over_rows(value):
        for axis, bit in [core] + far + line:
            value = value + swap(value, axis, bit)
        return value

    qkv = heads * HD
    freq = ROPE_BASE ** (-(np.arange(HD // 2, dtype=np.float64) * 2.0) / HD)
    freq = jnp.asarray(np.concatenate([freq, freq])[None, :], F32)
    gains = jnp.pad(jnp.stack([norm_attn, norm_ffn]), ((0, 14), (0, 0)))
    slots = 16
    w_small = jnp.concatenate(
        [w_router.T, shared_switch[None, :], jnp.zeros((slots - experts - 1, width), BF16)], axis=0
    )
    (
        x_full, normed, inv_one, gain_two, grad_rows, query, key_rows, value_rows, attn_rows, log_norm,
        query_seg, key_seg, cos_table, sin_table, hot, hot_peer,
    ) = front(
        tokens, gains, output_gradient, w_query, w_key, w_value, segments.reshape(1, -1), freq, routes.T, slots
    )
    both, resid_own, inv_two, grad_peer_a, logits, router_prob, switch, gates = attend_out(
        attn_rows, w_output, x_full, gain_two, grad_rows, w_small, hot, hot_peer, experts, width_own
    )

    hid_s, dgu_s, out_s, grad_s, small_s, grad_peer_b = ffn(
        both,
        grad_rows,
        switch,
        shared_gate,
        shared_up,
        shared_down,
        rows,
        carry=[(grad_rows, 2, rows // 2, rows // 2, 0)],
        number=4,
    )
    both_grad = jnp.concatenate([grad_rows, grad_peer_a, grad_peer_b], axis=0)
    sent, got_sgu = pair_send(both, dgu_s, False, rows)
    sent, got_sd = pair_send(hid_s, after(grad_rows, sent), True)
    sum_sgu = pair_keep(both, after(dgu_s, sent, both_grad), False, got_sgu, rows)
    sum_sd = pair_keep(hid_s, after(grad_rows, sum_sgu), True, got_sd)

    hidden_width = experts_own * expert_width
    gate_w = jnp.transpose(expert_gate, (0, 2, 1)).reshape(hidden_width, width)
    up_w = jnp.transpose(expert_up, (0, 2, 1)).reshape(hidden_width, width)
    down_w = expert_down.reshape(hidden_width, width)
    hid_e, dgu_e, out_e, grad_e, small_e, got_sgu, got_sd = ffn(
        both,
        after(both_grad, sum_sd),
        gates,
        gate_w,
        up_w,
        down_w,
        2 * rows,
        base=(out_s, grad_s),
        flipped=True,
        carry=[
            (sum_sgu, 2, sum_sgu.shape[0] // 2, 0, sum_sgu.shape[0] // 2),
            (sum_sd, 1, sum_sd.shape[0] // 2, 0, sum_sd.shape[0] // 2),
        ],
        number=5,
    )

    sum_sgu = reduce_add(sum_sgu, got_sgu, *y_link)
    sum_sd = reduce_add(sum_sd, got_sd, *x_link)

    small_t = small_e.T
    resid_low, grad_resid, grad_gain_two, sum_egu, ed_f, sgu_f, sd_f, grad_small = resid_grad(
        grad_e,
        dgu_e,
        hid_e,
        both,
        both_grad,
        sum_sgu,
        sum_sd,
        small_t[:, :rows],
        small_t[:, rows:],
        small_s.T,
        router_prob,
        hot,
        logits,
        switch,
        w_small,
        output_gradient,
        resid_own,
        inv_two,
        norm_ffn.astype(F32)[None, :],
    )

    flat = jnp.concatenate(
        [grad_gain_two.reshape(-1), grad_small[: experts + 1].reshape(-1)]
    ).reshape(-1, 128)
    inner = shared_gate.shape[1]
    sgu_f, sd_f, egu_f, ed_f, qkv_f, wo_f, flat, ffn_own, normed_own, row_total, grad_gain_one = tail(
        sgu_f,
        sd_f,
        sum_egu,
        ed_f,
        flat,
        normed,
        w_query,
        w_key,
        w_value,
        attn_rows,
        out_e,
        tokens,
        inv_one,
        resid_low,
        w_output,
        query,
        key_rows,
        value_rows,
        log_norm,
        query_seg,
        key_seg,
        cos_table,
        sin_table,
    )

    sg_grad, su_grad = widen(sgu_f, (inner, inner))
    (sd_grad,) = widen(sd_f)
    (eg_grad,) = widen(egu_f, kinds=2, kind=0)
    (eu_grad,) = widen(egu_f, kinds=2, kind=1)
    (ed_grad,) = widen(ed_f, across=4)
    wq_grad, wk_grad, wv_grad = widen(qkv_f, (qkv,) * 3)
    (wo_grad,) = widen(wo_f)

    x_own = tokens.astype(F32)
    grad_tokens = (
        grad_resid
        + inv_one * norm_attn.astype(F32) * normed_own
        - x_own * (inv_one * inv_one) * (row_total[0][:, None] / width)
    )
    grad_gain_one = grad_gain_one[0]
    layer_out = (resid_own + ffn_own).astype(BF16)
    flat = flat.reshape(-1)
    grad_gain_two = flat[:width_own]
    grad_router = flat[width_own : width_own + width * experts].reshape(experts, width).T
    grad_switch_w = flat[width_own + width * experts :]

    def per_expert(value):
        return value.reshape(experts_own, expert_width, width)

    return (
        layer_out,
        grad_tokens,
        grad_gain_one,
        wq_grad,
        wk_grad,
        wv_grad,
        wo_grad,
        grad_gain_two,
        grad_router,
        grad_switch_w,
        sg_grad,
        su_grad,
        sd_grad,
        jnp.transpose(per_expert(eg_grad), (0, 2, 1)),
        jnp.transpose(per_expert(eu_grad), (0, 2, 1)),
        per_expert(ed_grad),
    )


def solution(mesh):
    placed = (
        P(("dp", "ep"), "tp"),
        P("tp"),
        P(None, "tp"),
        P(None, "tp"),
        P(None, "tp"),
        P("tp", None),
        P("tp"),
        P(),
        P(),
        P(None, "tp"),
        P(None, "tp"),
        P("tp", None),
        P("ep", None, "tp"),
        P("ep", None, "tp"),
        P("ep", "tp", None),
        P(("dp", "ep"), None),
        P("dp"),
        P(("dp", "ep"), "tp"),
    )
    return jax.shard_map(
        body,
        mesh=mesh,
        in_specs=placed,
        out_specs=(
            P(("dp", "ep"), "tp"),
            P(("dp", "ep"), "tp"),
            P("tp"),
            P(None, "tp"),
            P(None, "tp"),
            P(None, "tp"),
            P("tp", None),
            P("tp"),
            P(),
            P(),
            P(None, "tp"),
            P(None, "tp"),
            P("tp", None),
            P("ep", None, "tp"),
            P("ep", None, "tp"),
            P("ep", "tp", None),
        ),
        check_vma=False,
    )
```

```python
import functools
import math

import jax
import jax.numpy as jnp
import numpy as np
from jax import lax
from jax.experimental import pallas as pl
from jax.experimental.pallas import tpu as pltpu
from jax.sharding import PartitionSpec as P

HD = 128
EPS = 1e-06
ROPE_BASE = 1000000.0
NEG = -1e30
F32 = jnp.float32
BF16 = jnp.bfloat16


def mm(left, right):
    return lax.dot_general(left, right, (((1,), (0,)), ((), ())), preferred_element_type=F32)


def mm_nt(left, right):
    return lax.dot_general(left, right, (((1,), (1,)), ((), ())), preferred_element_type=F32)


def mm_tn(left, right):
    return lax.dot_general(left, right, (((0,), (0,)), ((), ())), preferred_element_type=F32)


def swap(value, axis, bit):
    count = lax.axis_size(axis)
    return lax.ppermute(value, axis, [(i, i ^ bit) for i in range(count)])


def bit_of(axis, bit):
    return (lax.axis_index(axis) // bit) % 2


def half(value, which, dim):
    size = value.shape[dim] // 2
    return lax.dynamic_slice_in_dim(value, which * size, size, dim)


def after(value, *others):
    return lax.optimization_barrier((value, *others))[0]


def reduce_send(value, axis, bit):
    return swap(half(value, 1 - bit_of(axis, bit), 0), axis, bit)


def reduce_add(value, got, axis, bit):
    return (half(value, bit_of(axis, bit), 0).astype(F32) + got.astype(F32)).astype(BF16)


def places():
    count = lax.axis_size("dp")
    dp, ep = lax.axis_index("dp"), lax.axis_index("ep")
    core, x = dp % 2, dp // (count // 2)
    where = (
        {"dp": dp + 1 - 2 * core},
        {"dp": (dp + count // 2) % count},
        {"ep": 1 - ep},
    )
    return core, x, ep, where


def greet_all(peers):
    barrier = pltpu.get_barrier_semaphore()
    for where in peers:
        pl.semaphore_signal(
            barrier, inc=1, device_id=where, device_id_type=pl.DeviceIdType.MESH
        )
    pl.semaphore_wait(barrier, len(peers))


def add_rows(total, more, start, count, out=None):
    step = 32 if count % 32 == 0 else 16

    def turn(k, carry):
        here = pl.ds(pl.multiple_of(k * step, step), step)
        there = pl.ds(pl.multiple_of(start + k * step, step), step)
        value = (total[there, :].astype(F32) + more[here, :].astype(F32)).astype(BF16)
        if out is None:
            total[there, :] = value
        else:
            out[here, :] = value
        return carry

    lax.fori_loop(0, count // step, turn, 0)


def front_kernel(
    scale, chunks, tokens, gains, cotangent, w_query, w_key, w_value, segments, freq, routes,
    x, normed, inv_one, gain_two, grads, query, keys, values, attn, lse, query_seg, key_seg, cos, sin, hot, hot_peer,
    hot_low, wq_v, wk_v, wv_v, gains_in, l_sem, x_send, x_recv, s_sem, r_sem, kv_send, kv_recv,
):
    n, me = lax.axis_size("tp"), lax.axis_index("tp")
    y = lax.axis_index("ep")
    rows, own = tokens.shape
    heads = query.shape[1] // HD
    step = rows // chunks
    to_y = {"ep": 1 - y}
    tp = [{"tp": (me + d) % n} for d in range(1, n)]

    def remote(source, target, send_sem, recv_sem, where):
        return pltpu.make_async_remote_copy(
            src_ref=source, dst_ref=target, send_sem=send_sem, recv_sem=recv_sem,
            device_id=where, device_id_type=pl.DeviceIdType.MESH,
        )

    def piece(c, s):
        return (pl.ds(c * step, step), pl.ds(pl.multiple_of(s * own, own), own))

    def x_copy(c, s, to_right):
        return remote(
            x.at[piece(c, s)], x.at[piece(c, s)], x_send.at[c, s, 1 if to_right else 0], x_recv.at[c, s],
            {"tp": me + 1 if to_right else me - 1},
        )

    loads = [
        pltpu.make_async_copy(a, b, l_sem.at[m])
        for m, (a, b) in enumerate(((w_key, wk_v), (w_value, wv_v), (w_query, wq_v)))
    ]
    for copy in loads:
        copy.start()
    x[:, pl.ds(pl.multiple_of(me * own, own), own)] = tokens[...]
    gains_in[0] = gains[...]
    greet_all([to_y] + tp)
    for c in range(chunks):

        @pl.when(me > 0)
        def _(c=c):
            x_copy(c, me, False).start()

        @pl.when(me < n - 1)
        def _(c=c):
            x_copy(c, me, True).start()

    g_copies = [remote(gains_in.at[0], gains_in.at[d], s_sem.at[d - 1], r_sem.at[d - 1], tp[d - 1]) for d in range(1, n)]
    for copy in g_copies:
        copy.start()

    top = routes.shape[0]
    chosen = jnp.concatenate([routes[...].astype(F32), jnp.zeros((128 - top, rows), F32)], axis=0).T
    slot = lax.broadcasted_iota(jnp.int32, (1, hot.shape[1]), 1).astype(F32)
    used = jnp.zeros(hot.shape, F32)
    for k in range(top):
        used = used + jnp.where(chosen[:, k : k + 1] == slot, 1.0, 0.0)
    hot[...] = used
    hot_low[...] = used.astype(BF16)
    hot_copy = remote(hot_low, hot_peer, s_sem.at[2 * n - 1], r_sem.at[2 * n - 1], to_y)
    hot_copy.start()

    at = (y * rows + lax.broadcasted_iota(jnp.int32, (rows, 1), 0)).astype(F32)
    angle = at * freq[...]
    cos[...] = jnp.cos(angle)
    lane = lax.broadcasted_iota(jnp.int32, (1, HD), 1)
    sin[...] = jnp.where(lane < HD // 2, 1.0, -1.0) * jnp.sin(angle)
    whole = segments[...].astype(F32)
    mine = jnp.where(y == 0, whole[:, :rows], whole[:, rows : 2 * rows])
    query_seg[...] = jnp.broadcast_to(mine, (128, rows)).T[:, :1]
    key_seg[:, :rows] = jnp.where(y == 0, -1.0, whole[:, :rows])
    key_seg[:, rows:] = mine

    for d in range(1, n):
        for c in range(chunks):

            @pl.when(me >= d)
            def _(c=c, d=d):
                x_copy(c, me - d, True).wait_recv()

                @pl.when(me < n - 1)
                def _():
                    x_copy(c, me - d, True).start()

            @pl.when(me + d < n)
            def _(c=c, d=d):
                x_copy(c, me + d, False).wait_recv()

                @pl.when(me > 0)
                def _():
                    x_copy(c, me + d, False).start()

    mine_at = pl.ds(pl.multiple_of(me * own, own), own)
    c_copies = [
        remote(cotangent, grads.at[:, mine_at], s_sem.at[n - 2 + d], r_sem.at[n - 2 + d], tp[d - 1]) for d in range(1, n)
    ]
    handed = n == 4
    for d, copy in enumerate(c_copies, 1):

        @pl.when(((me + d) % n - me != n - 1) & (me - (me + d) % n != n - 1) if handed else me >= 0)
        def _(copy=copy):
            copy.start()

    inner = (me > 0) & (me < n - 1)

    def hand_on():
        upward = me == n - 2
        origin = pl.ds(pl.multiple_of(jnp.where(upward, 0, n - 1) * own, own), own)
        arrival = jnp.where(upward, n - 2 + n - 1, n - 2 + 1)
        return remote(
            grads.at[:, origin], grads.at[:, origin], s_sem.at[2 * n - 2], r_sem.at[arrival],
            {"tp": jnp.where(upward, n - 1, 0)},
        )
    own_grads = pltpu.make_async_copy(cotangent, grads.at[:, mine_at], l_sem.at[3])
    own_grads.start()
    for copy in g_copies:
        copy.wait_recv()
    gain_one = []
    for s in range(n):
        row = gains_in[0, :2, :].astype(F32) * jnp.where(me == s, 1.0, 0.0)
        for d in range(1, n):
            row = row + gains_in[d, :2, :].astype(F32) * jnp.where((me - d + n) % n == s, 1.0, 0.0)
        gain_one.append(row[:1])
        gain_two[:, s * own : (s + 1) * own] = row[1:]

    block = min(rows, 128)
    for b in range(rows // block):
        here = slice(b * block, (b + 1) * block)
        square = jnp.zeros((block, 1), F32)
        for s in range(n):
            part = x[here, s * own : (s + 1) * own].astype(F32)
            square = square + jnp.sum(part * part, axis=1, keepdims=True)
        inv = lax.rsqrt(square / (n * own) + EPS)
        inv_one[here, :] = inv
        for s in range(n):
            columns = slice(s * own, (s + 1) * own)
            normed[here, columns] = (x[here, columns].astype(F32) * inv * gain_one[s]).astype(BF16)

    def rope(value):
        return value * cos[...] - pltpu.roll(value, HD // 2, 1) * sin[...]

    loads[0].wait()
    loads[1].wait()
    key_pre = mm(normed[...], wk_v[...])
    value_pre = mm(normed[...], wv_v[...])

    @pl.when(y == 0)
    def _():
        keys[:rows, :] = jnp.zeros((rows, heads * HD), BF16)
        values[:rows, :] = jnp.zeros((rows, heads * HD), BF16)

    def kv_copy(h, m):
        array = (keys, values)[m]
        part = pl.ds(h * HD, HD)
        return remote(
            array.at[pl.ds(rows, rows), part], array.at[pl.ds(0, rows), part], kv_send.at[h, m], kv_recv.at[h, m], to_y
        )

    for h in range(heads):
        part = slice(h * HD, (h + 1) * HD)
        keys[rows:, part] = rope(key_pre[:, part]).astype(BF16)
        values[rows:, part] = value_pre[:, part].astype(BF16)

        @pl.when(y == 0)
        def _(h=h):
            kv_copy(h, 0).start()
            kv_copy(h, 1).start()

    loads[2].wait()
    query_pre = mm(normed[...], wq_v[...])
    for h in range(heads):
        part = slice(h * HD, (h + 1) * HD)
        query[:, part] = rope(query_pre[:, part]).astype(BF16)

    if handed:

        @pl.when(inner)
        def _():
            c_copies[1].wait_recv()
            hand_on().start()

    key_at = (y - 1) * rows + lax.broadcasted_iota(jnp.int32, (1, 2 * rows), 1)
    query_at = y * rows + lax.broadcasted_iota(jnp.int32, (rows, 1), 0)
    allowed = (query_seg[...] == key_seg[...]) & (key_at <= query_at)
    for h in range(heads):
        part = slice(h * HD, (h + 1) * HD)

        @pl.when(y == 1)
        def _(h=h):
            kv_copy(h, 0).wait_recv()
            kv_copy(h, 1).wait_recv()

        scores = jnp.where(allowed, mm_nt(query[:, part], keys[:, part]) * scale, NEG)
        top = jnp.max(scores, axis=1, keepdims=True)
        shifted = jnp.exp(scores - top)
        total = jnp.sum(shifted, axis=1, keepdims=True)
        weights = (shifted * (1.0 / total)).astype(BF16)
        attn[:, part] = mm(weights, values[:, part]).astype(BF16)
        lse[:, h : h + 1] = top + jnp.log(total)

    for h in range(heads):

        @pl.when(y == 0)
        def _(h=h):
            kv_copy(h, 0).wait_send()
            kv_copy(h, 1).wait_send()

    for c in range(chunks):
        for s in range(n):

            @pl.when((s <= me) & (me < n - 1))
            def _(c=c, s=s):
                x_copy(c, s, True).wait_send()

            @pl.when((s >= me) & (me > 0))
            def _(c=c, s=s):
                x_copy(c, s, False).wait_send()

    own_grads.wait()
    for d, copy in enumerate(c_copies, 1):

        if handed and d == 2:

            @pl.when(jnp.logical_not(inner))
            def _(copy=copy):
                copy.wait_recv()

        else:
            copy.wait_recv()

        @pl.when(((me + d) % n - me != n - 1) & (me - (me + d) % n != n - 1) if handed else me >= 0)
        def _(copy=copy):
            copy.wait_send()

    if handed:

        @pl.when(inner)
        def _():
            hand_on().wait_send()

    for copy in g_copies:
        copy.wait_send()
    hot_copy.wait()


def front(tokens, gains, cotangent, w_query, w_key, w_value, segments, freq, routes, slots):
    rows, own = tokens.shape
    n = lax.axis_size("tp")
    width = n * own
    mine = w_query.shape[1]
    heads = mine // HD
    chunks = 8 if n <= 4 else 2
    far = pl.BlockSpec(memory_space=pl.ANY)
    vmem = pl.BlockSpec(memory_space=pltpu.VMEM)
    dma = pltpu.SemaphoreType.DMA

    def shape(*dims, kind=BF16):
        return jax.ShapeDtypeStruct(dims, kind)

    return pl.pallas_call(
        functools.partial(front_kernel, 1.0 / math.sqrt(HD), chunks),
        out_shape=[
            shape(rows, width), shape(rows, width), shape(rows, 1, kind=F32), shape(1, width, kind=F32),
            shape(rows, width), shape(rows, mine), shape(2 * rows, mine), shape(2 * rows, mine), shape(rows, mine),
            shape(rows, heads, kind=F32), shape(rows, 1, kind=F32), shape(1, 2 * rows, kind=F32),
            shape(rows, HD, kind=F32), shape(rows, HD, kind=F32), shape(rows, slots, kind=F32), shape(rows, slots),
        ],
        in_specs=[vmem] * 2 + [far] * 4 + [vmem] * 3,
        out_specs=[vmem] * 4 + [far] + [vmem] * 11,
        scratch_shapes=[pltpu.VMEM((rows, slots), BF16)]
        + [pltpu.VMEM((width, mine), BF16)] * 3
        + [pltpu.VMEM((n, 16, own), BF16), dma((4,)), dma((chunks, n, 2)), dma((chunks, n))]
        + [dma((2 * n,)), dma((2 * n,)), dma((heads, 2)), dma((heads, 2))],
        compiler_params=pltpu.CompilerParams(
            collective_id=7, has_side_effects=True, vmem_limit_bytes=44 << 20
        ),
        cost_estimate=pl.CostEstimate(flops=0, bytes_accessed=0, transcendentals=0),
    )(tokens, gains, cotangent, w_query, w_key, w_value, segments, freq, routes)


def tail_kernel(
    scale,
    _sgu, _sd, egu, _ed, flat, normed, w_query, w_key, w_value, attn, ffn,
    tokens, inv_one, low, w_out, query, keys, values, lse, query_seg, key_seg, cos, sin,
    sgu_f, sd_f, egu_f, ed_f, qkv_f, wo_f, flat_f, ffn_own, normed_own, row_total, gain_f,
    normed_v, wq_v, wk_v, wv_v, attn_v, grad_attn, grad_key, grad_value, early, came, grad_qkv,
    q_sent, q_half, q_in, q_in2, q_out, w_sent, w_half, w_in, w_in2, w_out_v,
    e_own, e_in, flat_in, ffn_in, ffn_sent, ffn_came, grad_normed, normed_in, row_in, gain_in, l_sem, s_sem, r_sem,
):
    core, x, y, (to_core, to_x, to_y) = places()
    used = [0, 0]
    sent = []

    def here(source, target):
        k = used[0]
        used[0] += 1
        copy = pltpu.make_async_copy(source, target, l_sem.at[k])
        copy.start()
        return copy

    def remote(source, target, where):
        k = used[1]
        used[1] += 1
        return pltpu.make_async_remote_copy(
            src_ref=source, dst_ref=target, send_sem=s_sem.at[k], recv_sem=r_sem.at[k],
            device_id=where, device_id_type=pl.DeviceIdType.MESH,
        )

    def there(source, target, where):
        copy = remote(source, target, where)
        copy.start()
        sent.append(copy)
        return copy

    rows = query.shape[0]
    heads = query.shape[1] // HD
    mine = heads * HD
    q_rows, w_rows = q_in.shape[0], w_in.shape[0]
    e_rows = e_own.shape[0]
    n, me = lax.axis_size("tp"), lax.axis_index("tp")
    tp = [{"tp": (me + d) % n} for d in range(1, n)]
    own_width = ffn_own.shape[1]

    def columns(d):
        return pl.ds(pl.multiple_of(((me + d) % n) * own_width, own_width), own_width)

    greet_all([to_core, to_x, to_y] + tp)

    b3 = there(egu.at[pl.ds((1 - x) * e_rows, e_rows)], e_in, to_x)
    b6 = there(ed_f.at[core, x], ed_f.at[core, x], to_x)
    d3 = [there(sd_f.at[core, 0, y], sd_f.at[core, 0, y], to_y)]
    f1 = there(flat, flat_in.at[0], to_core)
    z_ffn = [
        there(ffn.at[pl.ds(rows, rows), columns(d)], ffn_in.at[n + d], tp[d - 1]) for d in range(1, n)
    ]
    own_ffn = [here(ffn.at[pl.ds(m * rows, rows), columns(0)], ffn_in.at[m * n]) for m in (1, 0)]
    load_attn = here(attn, attn_v)
    load_normed = here(normed, normed_v)
    loads = [here(w_query, wq_v), here(w_key, wk_v), here(w_value, wv_v)]
    load_e = here(egu.at[pl.ds(x * e_rows, e_rows)], e_own)

    grad_attn[...] = mm_nt(low[...], w_out[...]).astype(BF16)
    key_at = (y - 1) * rows + lax.broadcasted_iota(jnp.int32, (1, 2 * rows), 1)
    query_at = y * rows + lax.broadcasted_iota(jnp.int32, (rows, 1), 0)
    allowed = (query_seg[...] == key_seg[...]) & (key_at <= query_at)
    sums_of = jnp.zeros((rows, 1), F32)
    early_copies = []
    for h in range(heads):
        own = slice(h * HD, (h + 1) * HD)
        q, k, v, g = query[:, own], keys[:, own], values[:, own], grad_attn[:, own]
        scores = jnp.where(allowed, mm_nt(q, k) * scale, NEG)
        probs = jnp.exp(scores - lse[:, h : h + 1])
        grad_probs = mm_nt(g, v)
        weighted = probs * grad_probs
        grad_scores = (weighted - probs * jnp.sum(weighted, axis=1, keepdims=True)).astype(BF16)
        grad_q = mm(grad_scores, k) * scale
        grad_k = mm_tn(grad_scores, q) * scale
        grad_v = mm_tn(probs.astype(BF16), g)
        grad_key[:, own] = grad_k[rows:]
        grad_value[:, own] = grad_v[rows:]
        early[h, 0] = grad_k[:rows].astype(BF16)
        early[h, 1] = grad_v[:rows].astype(BF16)
        copy = remote(early.at[h], came.at[h], to_y)
        early_copies.append(copy)

        @pl.when(y == 1)
        def _(copy=copy):
            copy.start()

        sums_of = sums_of + jnp.sum(grad_q * q.astype(F32), axis=1, keepdims=True)
        turned = grad_q * cos[...] + pltpu.roll(grad_q, HD // 2, 1) * sin[...]
        grad_qkv[:, own] = turned.astype(BF16)

    load_attn.wait()
    half_of = low.shape[1] // 2
    w_sent[...] = mm_tn(attn_v[...], low[:, pl.ds(pl.multiple_of((1 - core) * half_of, half_of), half_of)]).astype(BF16)
    a0 = there(w_sent, w_half, to_core)
    w_own = mm_tn(attn_v[...], low[:, pl.ds(pl.multiple_of(core * half_of, half_of), half_of)])
    f1.wait_recv()
    flat_f[...] = flat[...] + flat_in[0]
    f2 = there(flat_f, flat_in.at[1], to_x)
    a0.wait_recv()
    w_half[...] = (w_own + w_half[...].astype(F32)).astype(BF16)
    a2 = there(w_half.at[pl.ds((1 - y) * w_rows, w_rows)], w_in, to_y)

    for h in range(heads):
        own = slice(h * HD, (h + 1) * HD)

        @pl.when(y == 0)
        def _(h=h, own=own):
            early_copies[h].wait_recv()
            grad_key[:, own] = grad_key[:, own] + came[h, 0].astype(F32)
            grad_value[:, own] = grad_value[:, own] + came[h, 1].astype(F32)

        @pl.when(y == 1)
        def _(h=h):
            early_copies[h].wait_send()

        grad_k, grad_v = grad_key[:, own], grad_value[:, own]
        sums_of = sums_of + jnp.sum(
            grad_k * keys[rows:, own].astype(F32) + grad_v * values[rows:, own].astype(F32),
            axis=1, keepdims=True,
        )
        turned = grad_k * cos[...] + pltpu.roll(grad_k, HD // 2, 1) * sin[...]
        grad_qkv[:, mine + h * HD : mine + (h + 1) * HD] = turned.astype(BF16)
        grad_qkv[:, 2 * mine + h * HD : 2 * mine + (h + 1) * HD] = grad_v.astype(BF16)
    row_in[0] = jnp.broadcast_to(sums_of, (rows, 128)).T[:8]
    z_rows = [there(row_in.at[0], row_in.at[d], tp[d - 1]) for d in range(1, n)]

    load_normed.wait()
    tall = q_half.shape[0]
    step = tall // 4

    def product(i, which):
        start = pl.multiple_of(which * tall + i * step, step)
        return mm_tn(normed_v[:, pl.ds(start, step)], grad_qkv[...])

    a0q = []
    for i in range(4):
        q_sent[i * step : (i + 1) * step, :] = product(i, 1 - core).astype(BF16)
        a0q.append(there(q_sent.at[pl.ds(i * step, step)], q_half.at[pl.ds(i * step, step)], to_core))
    for i in range(4):
        value = product(i, core)
        a0q[i].wait_recv()
        here_rows = slice(i * step, (i + 1) * step)
        q_half[here_rows, :] = (value + q_half[here_rows, :].astype(F32)).astype(BF16)
    a1 = there(q_half.at[pl.ds((1 - y) * q_rows, q_rows)], q_in, to_y)
    d1 = there(sgu_f.at[core, y, 1 - x], sgu_f.at[core, y, 1 - x], to_y)
    for copy in loads:
        copy.wait()
    grad_normed[...] = (
        mm_nt(grad_qkv[:, :mine], wq_v[...])
        + mm_nt(grad_qkv[:, mine : 2 * mine], wk_v[...])
        + mm_nt(grad_qkv[:, 2 * mine :], wv_v[...])
    ).astype(BF16)
    z_normed = [there(grad_normed.at[:, columns(d)], normed_in.at[d], tp[d - 1]) for d in range(1, n)]
    z_own = [there(ffn.at[pl.ds(0, rows), columns(d)], ffn_in.at[d], tp[d - 1]) for d in range(1, n)]

    load_e.wait()
    b3.wait_recv()
    add_rows(e_own, e_in, 0, e_rows)
    cut, cut_b = e_rows // 64 * 16, e_rows * 5 // 128 * 16
    b5a = there(e_own.at[pl.ds(0, cut)], egu_f.at[core, x, pl.ds(0, cut)], to_x)
    f2.wait_recv()
    f2.wait_send()
    flat_f[...] = flat_f[...] + flat_in[1]
    f3 = there(flat_f, flat_in.at[2], to_y)
    a2.wait_recv()
    add_rows(w_half, w_in, y * w_rows, w_rows)
    a4 = there(w_half.at[pl.ds(y * w_rows + (1 - x) * (w_rows // 2), w_rows // 2)], w_in2, to_x)
    a1.wait_recv()
    add_rows(q_half, q_in, y * q_rows, q_rows)
    a3 = there(q_half.at[pl.ds(y * q_rows + (1 - x) * (q_rows // 2), q_rows // 2)], q_in2, to_x)
    own_e = here(e_own, egu_f.at[core, x])
    d3.append(there(sd_f.at[core, 1, y], sd_f.at[core, 1, y], to_y))
    for copy in own_ffn:
        copy.wait()
    for copy in z_ffn:
        copy.wait_recv()
    total = ffn_in[n].astype(F32)
    for m in range(n + 1, 2 * n):
        total = total + ffn_in[m].astype(F32)
    ffn_sent[...] = total.astype(BF16)
    o1 = there(ffn_sent, ffn_came, to_y)
    for copy in z_normed + z_rows:
        copy.wait_recv()
    total = grad_normed[:, columns(0)].astype(F32)
    row_sum = row_in[0]
    for d in range(1, n):
        total = total + normed_in[d].astype(F32)
        row_sum = row_sum + row_in[d]
    normed_own[...] = total
    row_total[...] = row_sum
    gain = jnp.sum(total * tokens[...].astype(F32) * inv_one[...], axis=0, keepdims=True)
    gain_f[...] = jnp.broadcast_to(gain, gain_f.shape)
    g1 = there(gain_f, gain_in.at[0], to_core)
    a4.wait_recv()
    add_rows(w_half, w_in2, y * w_rows + x * (w_rows // 2), w_rows // 2, w_out_v)
    a6 = there(w_out_v, wo_f.at[core, y, x], to_x)
    own_w = here(w_out_v, wo_f.at[core, y, x])
    g1.wait_recv()
    g1.wait_send()
    gain_f[...] = gain_f[...] + gain_in[0]
    g2 = there(gain_f, gain_in.at[1], to_x)
    a3.wait_recv()
    add_rows(q_half, q_in2, y * q_rows + x * (q_rows // 2), q_rows // 2, q_out)
    a5 = there(q_out, qkv_f.at[core, y, x], to_x)
    own_q = here(q_out, qkv_f.at[core, y, x])
    b5 = there(e_own.at[pl.ds(cut, cut_b - cut)], egu_f.at[core, x, pl.ds(cut, cut_b - cut)], to_x)
    b7 = there(e_own.at[pl.ds(cut_b, e_rows - cut_b)], egu_f.at[core, x, pl.ds(cut_b, e_rows - cut_b)], to_x)
    b6.wait_recv()
    c6 = there(ed_f.at[core], ed_f.at[core], to_core)
    d1.wait_recv()
    c1 = there(sgu_f.at[core], sgu_f.at[core], to_core)
    g2.wait_recv()
    g2.wait_send()
    gain_f[...] = gain_f[...] + gain_in[1]
    g3 = there(gain_f, gain_in.at[2], to_y)
    a6.wait_recv()
    own_w.wait()
    a8 = there(wo_f.at[core, y], wo_f.at[core, y], to_y)
    a5.wait_recv()
    own_q.wait()
    a7 = there(qkv_f.at[core, y], qkv_f.at[core, y], to_y)
    for copy in d3:
        copy.wait_recv()
    c2 = there(sd_f.at[core], sd_f.at[core], to_core)
    f3.wait_recv()
    f3.wait_send()
    flat_f[...] = flat_f[...] + flat_in[2]
    own_e.wait()
    b5a.wait_recv()
    b5.wait_recv()
    c3 = there(egu_f.at[core, :, pl.ds(0, cut_b)], egu_f.at[core, :, pl.ds(0, cut_b)], to_core)
    b7.wait_recv()
    rest = pl.ds(cut_b, e_rows - cut_b)
    c7 = there(egu_f.at[core, :, rest], egu_f.at[core, :, rest], to_core)
    a8.wait_recv()
    c5 = there(wo_f.at[core], wo_f.at[core], to_core)
    a7.wait_recv()
    c4 = there(qkv_f.at[core], qkv_f.at[core], to_core)
    g3.wait_recv()
    g3.wait_send()
    gain_f[...] = gain_f[...] + gain_in[2]
    for copy in z_own:
        copy.wait_recv()
    o1.wait_recv()
    total = ffn_came[...].astype(F32)
    for m in range(n):
        total = total + ffn_in[m].astype(F32)
    ffn_own[...] = total
    for copy in (c1, c2, c3, c4, c5, c6, c7):
        copy.wait_recv()
    for copy in sent:
        if all(copy is not other for other in (f2, f3, g1, g2, g3)):
            copy.wait_send()


def tail(sgu, sd, egu, ed, flat, normed, w_query, w_key, w_value, attn, ffn, tokens, inv_one, low, w_out, query, keys, values, lse, query_seg, key_seg, cos, sin):
    rows, width = low.shape
    mine = query.shape[1]
    heads = mine // HD

    def pieces(count, height, wide):
        return jax.ShapeDtypeStruct((2,) * count + (height, wide), BF16)

    far = pl.BlockSpec(memory_space=pl.ANY)
    vmem = pl.BlockSpec(memory_space=pltpu.VMEM)

    def room(*shape, kind=BF16):
        return pltpu.VMEM(shape, kind)

    half_of = width // 2
    n = lax.axis_size("tp")
    dma = pltpu.SemaphoreType.DMA
    return pl.pallas_call(
        functools.partial(tail_kernel, 1.0 / math.sqrt(HD)),
        out_shape=[
            jax.ShapeDtypeStruct(sgu.shape, BF16), jax.ShapeDtypeStruct(sd.shape, BF16),
            pieces(2, egu.shape[0] // 2, egu.shape[1]), jax.ShapeDtypeStruct(ed.shape, BF16),
            pieces(3, half_of // 4, 3 * mine), pieces(3, mine // 4, half_of),
            jax.ShapeDtypeStruct(flat.shape, F32), jax.ShapeDtypeStruct(tokens.shape, F32),
            jax.ShapeDtypeStruct(tokens.shape, F32), jax.ShapeDtypeStruct((8, rows), F32),
            jax.ShapeDtypeStruct((8, tokens.shape[1]), F32),
        ],
        in_specs=[far] * 4 + [vmem] + [far] * 6 + [vmem] * 12,
        out_specs=[far] * 6 + [vmem] * 5,
        scratch_shapes=[
            room(rows, width), room(width, mine), room(width, mine), room(width, mine), room(rows, mine),
            room(rows, mine), room(rows, mine, kind=F32), room(rows, mine, kind=F32),
            room(heads, 2, rows, HD), room(heads, 2, rows, HD), room(rows, 3 * mine),
            room(half_of, 3 * mine), room(half_of, 3 * mine), room(half_of // 2, 3 * mine),
            room(half_of // 4, 3 * mine), room(half_of // 4, 3 * mine),
            room(mine, half_of), room(mine, half_of), room(mine // 2, half_of),
            room(mine // 4, half_of), room(mine // 4, half_of),
            room(egu.shape[0] // 2, egu.shape[1]), room(egu.shape[0] // 2, egu.shape[1]),
            room(3, *flat.shape, kind=F32), room(2 * n, *tokens.shape), room(*tokens.shape), room(*tokens.shape), room(rows, width), room(n, *tokens.shape),
            room(n, 8, rows, kind=F32), room(3, 8, tokens.shape[1], kind=F32),
            dma((18,)), dma((38 + heads + 4 * n,)), dma((38 + heads + 4 * n,)),
        ],
        input_output_aliases={0: 0, 1: 1, 3: 3},
        compiler_params=pltpu.CompilerParams(
            collective_id=3, has_side_effects=True, vmem_limit_bytes=62 << 20
        ),
        cost_estimate=pl.CostEstimate(flops=0, bytes_accessed=0, transcendentals=0),
    )(sgu, sd, egu, ed, flat, normed, w_query, w_key, w_value, attn, ffn, tokens, inv_one, low, w_out, query, keys, values, lse, query_seg, key_seg, cos, sin)


def widen_kernel(source, *outputs):
    value = source[...]
    value = value.reshape(value.shape[-2:])
    start = 0
    for out in outputs:
        width = out.shape[1]
        out[...] = value[:, start : start + width].astype(F32)
        start += width


def widen(value, widths=(), kinds=1, kind=0, across=2):
    columns = value.shape[-1]
    if widths:
        value = value.reshape(-1, columns)
        rows = value.shape[0]
        step = min(rows, 256)
        source = pl.BlockSpec((step, columns), lambda i: (i, 0))
        grid = (rows // step,)
        specs = [pl.BlockSpec((step, width), lambda i: (i, 0)) for width in widths]
        shapes = [jax.ShapeDtypeStruct((rows, width), F32) for width in widths]
    else:
        value = value.reshape(across, kinds, -1, columns)
        rows = value.shape[2]
        step = rows
        while step * columns > (1 << 20) and step % 32 == 0:
            step //= 2
        steps = rows // step
        source = pl.BlockSpec((1, 1, step, columns), lambda i, c: (c, kind, i, 0))
        grid = (steps, across)
        specs = [pl.BlockSpec((step, columns), lambda i, c: (i, c))]
        shapes = [jax.ShapeDtypeStruct((rows, across * columns), F32)]
    return pl.pallas_call(
        widen_kernel,
        grid=grid,
        in_specs=[source],
        out_specs=specs,
        out_shape=shapes,
        compiler_params=pltpu.CompilerParams(vmem_limit_bytes=24 << 20),
        cost_estimate=pl.CostEstimate(flops=0, bytes_accessed=0, transcendentals=0),
    )(value)


def weight_kernel(added, part, left, right, *refs):
    total = mm_tn(left[...], right[...])
    if added:
        total = total + refs[0][...].astype(F32)
    refs[-1][...] = total.astype(BF16)


def weight_half(left, right, which, columns, got=None, rows=None, block=1408):
    rows = rows or left.shape[0]
    height, wide = left.shape[1], right.shape[1]
    if columns:
        wide = wide // 2
    else:
        height = height // 2
    step = height
    while step > block and step % 256 == 0:
        step //= 2
    steps = height // step
    extra = [] if got is None else [got]
    out_spec = pl.BlockSpec((step, wide), lambda i, part: (i, 0))
    if columns:
        left_at, right_at = (lambda i, part: (0, i)), (lambda i, part: (0, part[0]))
    else:
        left_at, right_at = (lambda i, part: (0, part[0] * steps + i)), (lambda i, part: (0, 0))
    return pl.pallas_call(
        functools.partial(weight_kernel, bool(extra)),
        grid_spec=pltpu.PrefetchScalarGridSpec(
            num_scalar_prefetch=1,
            grid=(steps,),
            in_specs=[pl.BlockSpec((rows, step), left_at), pl.BlockSpec((rows, wide), right_at)]
            + [out_spec] * len(extra),
            out_specs=out_spec,
        ),
        out_shape=jax.ShapeDtypeStruct((height, wide), BF16),
        compiler_params=pltpu.CompilerParams(vmem_limit_bytes=48 << 20),
        cost_estimate=pl.CostEstimate(flops=0, bytes_accessed=0, transcendentals=0),
    )(which.reshape(1).astype(jnp.int32), left, right, *extra)


def ffn_kernel(groups, base, flipped, carry, *refs):
    rows, grads, scale, *stored = refs[:6]
    refs = refs[6:]
    if base:
        base_out, base_dx = refs[:2]
        refs = refs[2:]
    sources, refs = refs[: len(carry)], refs[len(carry) :]
    hid_ref, dgu_ref, out_ref, dx_ref, small_ref, *refs = refs
    *refs, gate_w, up_w, down_w, w_sem = refs
    weights = [
        pltpu.make_async_copy(source, target, w_sem.at[m])
        for m, (source, target) in enumerate(zip(stored, (gate_w, up_w, down_w)))
    ]

    @pl.when(pl.program_id(0) == 0)
    def _():
        for copy in weights:
            copy.start()

    copies = []
    if carry:
        send_sem, recv_sem = refs[-2:]
        _, x, y, where = places()
        for m, (link, count, start, stride) in enumerate(carry):
            first = start + (1 - (x, y)[link - 1]) * stride
            copies.append(
                pltpu.make_async_remote_copy(
                    src_ref=sources[m].at[pl.ds(first, count)], dst_ref=refs[m],
                    send_sem=send_sem.at[m], recv_sem=recv_sem.at[m],
                    device_id=where[link], device_id_type=pl.DeviceIdType.MESH,
                )
            )
        links = sorted({link for link, _, _, _ in carry})

        @pl.when(pl.program_id(0) == 0)
        def _():
            greet_all([where[link] for link in links])
            for copy in copies:
                copy.start()

    def stored_is_here(m):
        @pl.when(pl.program_id(0) == 0)
        def _():
            weights[m].wait()

    stored_is_here(0)
    width = down_w.shape[0]
    to, back = (mm_nt, mm) if flipped else (mm, mm_nt)
    gate_pre = to(rows[...], gate_w[...])
    stored_is_here(1)
    up_pre = to(rows[...], up_w[...])
    stored_is_here(2)
    grad_hidden = mm_nt(grads[...], down_w[...])
    sig = 1.0 / (1.0 + jnp.exp(-gate_pre))
    act = gate_pre * sig
    slope = sig + act * (1.0 - sig)
    hidden = (act * up_pre).astype(BF16).astype(F32)
    each = width // groups
    column = lax.broadcasted_iota(jnp.int32, (1, width), 1)
    wide = scale[:, 0:1]
    for e in range(1, groups):
        wide = jnp.where(column >= e * each, scale[:, e : e + 1], wide)
    prod = hidden * grad_hidden
    for e in range(groups):
        part = prod
        if groups > 1:
            part = jnp.where((column >= e * each) & (column < (e + 1) * each), prod, 0.0)
        small_ref[:, e : e + 1] = jnp.sum(part, axis=1, keepdims=True)
    hid = (hidden * wide).astype(BF16)
    hid_ref[...] = hid
    scaled = grad_hidden * wide
    dgate = (scaled * up_pre * slope).astype(BF16)
    dup = (scaled * act).astype(BF16)
    dgu_ref[:, :width] = dgate
    dgu_ref[:, width:] = dup
    small_ref[:, groups : groups + 1] = jnp.sum(
        dgate.astype(F32) * gate_pre + dup.astype(F32) * up_pre, axis=1, keepdims=True
    )
    out = mm(hid, down_w[...])
    dx = back(dgate, gate_w[...]) + back(dup, up_w[...])
    if base:
        own = jnp.where(2 * pl.program_id(0) >= pl.num_programs(0), 1.0, 0.0)
        out = out + own * base_out[...].astype(F32)
        dx = dx + own * base_dx[...].astype(F32)
    out_ref[...] = out.astype(BF16)
    dx_ref[...] = dx.astype(BF16)
    if carry:

        @pl.when(pl.program_id(0) == pl.num_programs(0) - 1)
        def _():
            for copy in copies:
                copy.wait()


def ffn(rows, grads, scale, gate_w, up_w, down_w, count, base=(), flipped=False, carry=(), number=None):
    groups = scale.shape[1]
    width = rows.shape[1]
    hidden = down_w.shape[0]
    block = min(256, count)
    steps = count // block

    def at(n):
        if base:
            return pl.BlockSpec((block, n), lambda i: ((i + steps // 2) % steps, 0))
        return pl.BlockSpec((block, n), lambda i: (i, 0))

    def late(n):
        return pl.BlockSpec((block, n), lambda i: (jnp.maximum(i - steps // 2, 0), 0))

    far = pl.BlockSpec(memory_space=pl.ANY)
    return pl.pallas_call(
        functools.partial(
            ffn_kernel, groups, bool(base), flipped, tuple(c[1:] for c in carry)
        ),
        grid=(steps,),
        in_specs=[at(width), at(width), at(groups)]
        + [far] * 3
        + [late(width)] * len(base)
        + [far] * len(carry),
        out_specs=[
            at(hidden),
            at(2 * hidden),
            at(width),
            at(width),
            at(groups + 1),
        ]
        + [far] * len(carry),
        out_shape=[
            jax.ShapeDtypeStruct((count, hidden), BF16),
            jax.ShapeDtypeStruct((count, 2 * hidden), BF16),
            jax.ShapeDtypeStruct((count, width), BF16),
            jax.ShapeDtypeStruct((count, width), BF16),
            jax.ShapeDtypeStruct((count, groups + 1), F32),
        ]
        + [jax.ShapeDtypeStruct((c[2], c[0].shape[1]), BF16) for c in carry],
        scratch_shapes=([pltpu.SemaphoreType.DMA((len(carry),))] * 2 if carry else [])
        + [pltpu.VMEM(w.shape, BF16) for w in (gate_w, up_w, down_w)]
        + [pltpu.SemaphoreType.DMA((3,))],
        compiler_params=pltpu.CompilerParams(
            vmem_limit_bytes=62 << 20, collective_id=number, has_side_effects=bool(carry)
        ),
        cost_estimate=pl.CostEstimate(flops=0, bytes_accessed=0, transcendentals=0),
    )(rows, grads, scale, gate_w, up_w, down_w, *base, *[c[0] for c in carry])


def line_sum(depth, prepare, settle, gathered, beside, part, came, came_two, spread, sems):
    n = lax.axis_size("tp")
    me = lax.axis_index("tp")
    chunks, _, step, _ = part.shape
    sum_send, sum_recv, two_recv, out_send, out_recv = sems

    def send(source, target, send_sem, recv_sem, to):
        return pltpu.make_async_remote_copy(
            src_ref=source, dst_ref=target, send_sem=send_sem, recv_sem=recv_sem,
            device_id={"tp": to}, device_id_type=pl.DeviceIdType.MESH,
        )

    def sum_copy(c, s, to_right, two):
        target = came_two.at[c] if two else came.at[c, s]
        sem = two_recv.at[c] if two else sum_recv.at[c, s]
        return send(part.at[c, s], target, sum_send.at[c, s], sem, me + 1 if to_right else me - 1)

    def out_copy(c, s, to_right):
        return send(
            spread.at[c, s], spread.at[c, s], out_send.at[c, s, 1 if to_right else 0],
            out_recv.at[c, s], me + 1 if to_right else me - 1,
        )

    def within(c):
        return (c >= 0) & (c < chunks)

    def pass_sums(t):
        @pl.when(within(t))
        def _():
            prepare(t)

        for s in range(n):
            c = t - me * depth

            @pl.when((me < s) & within(c))
            def _(s=s, c=c):
                @pl.when(me > 0)
                def _():
                    sum_copy(c, s, True, False).wait_recv()
                    part[c, s] = (part[c, s].astype(F32) + came[c, s].astype(F32)).astype(BF16)

                sum_copy(c, s, True, False).start()

        for s in range(n):
            c = t - (n - 1 - me) * depth

            @pl.when((me > s) & within(c))
            def _(s=s, c=c):
                @pl.when(me < n - 1)
                def _():
                    sum_copy(c, s, False, False).wait_recv()
                    part[c, s] = (part[c, s].astype(F32) + came[c, s].astype(F32)).astype(BF16)

                @pl.when(me - 1 == s)
                def _():
                    sum_copy(c, s, False, True).start()

                @pl.when(me - 1 > s)
                def _():
                    sum_copy(c, s, False, False).start()

    def pass_own(t):
        c = t - (n - 1) * depth
        for s in range(n):

            @pl.when((me == s) & within(c))
            def _(s=s):
                if s > 0:
                    sum_copy(c, s, True, False).wait_recv()
                if s < n - 1:
                    sum_copy(c, s, False, True).wait_recv()
                total = part[c, s].astype(F32)
                if s > 0:
                    total = total + came[c, s].astype(F32)
                if s < n - 1:
                    total = total + came_two[c].astype(F32)
                spread[c, s] = settle(c, total)
                if s > 0:
                    out_copy(c, s, False).start()
                if s < n - 1:
                    out_copy(c, s, True).start()

    def pass_out(t):
        for s in range(n):
            right = t - (n - 1 + me - s) * depth
            left = t - (n - 1 + s - me) * depth

            @pl.when((me > s) & within(right))
            def _(s=s, c=right):
                out_copy(c, s, True).wait_recv()

                @pl.when(me < n - 1)
                def _():
                    out_copy(c, s, True).start()

            @pl.when((me < s) & within(left))
            def _(s=s, c=left):
                out_copy(c, s, False).wait_recv()

                @pl.when(me > 0)
                def _():
                    out_copy(c, s, False).start()

        last = t - 2 * (n - 1) * depth

        @pl.when(within(last))
        def _():
            gathered(last)

    def turn(t, carry):
        pass_sums(t)
        pass_own(t)
        pass_out(t)
        if beside is not None:
            beside(t)
        return carry

    lax.fori_loop(0, chunks + 2 * (n - 1) * depth, turn, 0)

    def drain(c, carry):
        for s in range(n):

            @pl.when(me != s)
            def _(s=s):
                sum_copy(c, s, True, False).wait_send()

            @pl.when((me < n - 1) & (s <= me))
            def _(s=s):
                out_copy(c, s, True).wait_send()

            @pl.when((me > 0) & (s >= me))
            def _(s=s):
                out_copy(c, s, False).wait_send()

        return carry

    lax.fori_loop(0, chunks, drain, 0)


def line_scratch(rows, width_own):
    n = lax.axis_size("tp")
    chunks = max(1, min(16, 128 // n))
    step = rows // chunks
    slots = pltpu.VMEM((chunks, n, step, width_own), BF16)
    dma = pltpu.SemaphoreType.DMA
    return chunks, step, [
        slots, slots, pltpu.VMEM((chunks, step, width_own), BF16), slots,
        dma((chunks, n)), dma((chunks, n)), dma((chunks,)), dma((chunks, n, 2)), dma((chunks, n)),
    ]


def greet(peers):
    n = lax.axis_size("tp")
    me = lax.axis_index("tp")
    barrier = pltpu.get_barrier_semaphore()

    def signal(where):
        pl.semaphore_signal(barrier, inc=1, device_id=where, device_id_type=pl.DeviceIdType.MESH)

    @pl.when(me > 0)
    def _():
        signal({"tp": me - 1})

    @pl.when(me < n - 1)
    def _():
        signal({"tp": me + 1})

    for where in peers:
        signal(where)

    beside = jnp.where(me > 0, 1, 0) + jnp.where(me < n - 1, 1, 0)
    pl.semaphore_wait(barrier, beside + len(peers))


def attend_out_kernel(
    chunks, step, depth, experts, attn, w_out, x, gain, grads, w_small, hot, hot_peer,
    mixed, resid_own, inv_out, grads_peer, logits, prob, switch, gates,
    part, came, came_two, spread, s0, s1, s2, s3, s4, y_send, y_recv, g_send, g_recv,
):
    n = lax.axis_size("tp")
    me = lax.axis_index("tp")
    own = part.shape[3]
    rows = attn.shape[0]
    other = {"ep": 1 - lax.axis_index("ep")}
    greet([other])
    grads_copy = pltpu.make_async_remote_copy(
        src_ref=grads.at[pl.ds(0, grads_peer.shape[0])], dst_ref=grads_peer, send_sem=g_send, recv_sem=g_recv,
        device_id=other, device_id_type=pl.DeviceIdType.MESH,
    )
    grads_copy.start()
    block = max(step, min(rows, 128))

    def product(b, carry):
        start = pl.multiple_of(b * block, block)
        value = mm(attn[pl.ds(start, block), :], w_out[...]).astype(BF16)
        for s in range(n):
            for k in range(block // step):
                part[b * (block // step) + k, s] = value[k * step:(k + 1) * step, s * own:(s + 1) * own]
        return carry

    lax.fori_loop(0, rows // block, product, 0)

    def at(c):
        return pl.ds(pl.multiple_of(c * step, step), step)

    def peer_copy(c):
        return pltpu.make_async_remote_copy(
            src_ref=mixed.at[at(c)], dst_ref=mixed.at[pl.ds(pl.multiple_of(rows + c * step, step), step)], send_sem=y_send.at[c], recv_sem=y_recv.at[c],
            device_id=other, device_id_type=pl.DeviceIdType.MESH,
        )

    def prepare(c):
        pass

    def settle(c, total):
        return total.astype(BF16)

    place = lax.broadcasted_iota(jnp.int32, (1, w_small.shape[0]), 1)
    here = lax.axis_index("ep") == 0

    def chances(scores):
        scores = jnp.where(place < experts, scores, NEG)
        raised = jnp.exp(scores - jnp.max(scores, axis=1, keepdims=True))
        return jnp.where(place < experts, raised / jnp.sum(raised, axis=1, keepdims=True), 0.0)

    def own_gates(value):
        return jnp.where(here, value[:, : experts // 2], value[:, experts // 2 : experts])

    def gathered(c):
        resid = []
        square = jnp.zeros((step, 1), F32)
        for s in range(n):
            piece = x[at(c), s * own:(s + 1) * own].astype(F32) + spread[c, s].astype(F32)
            resid.append(piece)
            square = square + jnp.sum(piece * piece, axis=1, keepdims=True)
        inv = lax.rsqrt(square / (n * own) + EPS)
        inv_out[at(c), :] = inv
        for s in range(n):
            mixed[at(c), s * own:(s + 1) * own] = (resid[s] * inv * gain[:, s * own:(s + 1) * own]).astype(BF16)

            @pl.when(me == s)
            def _(s=s):
                resid_own[at(c), :] = resid[s]

        peer_copy(c).start()

    line_sum(depth, prepare, settle, gathered, None, part, came, came_two, spread, (s0, s1, s2, s3, s4))

    scores = mm_nt(mixed[:rows, :], w_small[...])
    chance = chances(scores)
    logits[...] = scores
    prob[...] = chance
    switch[...] = 1.0 / (1.0 + jnp.exp(-scores[:, experts : experts + 1]))
    gates[:rows, :] = own_gates(chance * hot[...])

    def last(c, carry):
        peer_copy(c).wait_recv()
        peer_copy(c).wait_send()
        return carry

    lax.fori_loop(0, chunks, last, 0)
    chance = chances(mm_nt(mixed[rows:, :], w_small[...]))
    gates[rows:, :] = own_gates(chance * hot_peer[...].astype(F32))
    grads_copy.wait()


def attend_out(attn, w_out, x, gain, grads, w_small, hot, hot_peer, experts, width_own, depth=1):
    rows, width = x.shape
    chunks, step, scratch = line_scratch(rows, width_own)
    vmem = pl.BlockSpec(memory_space=pltpu.VMEM)
    far = pl.BlockSpec(memory_space=pl.ANY)
    dma = pltpu.SemaphoreType.DMA
    return pl.pallas_call(
        functools.partial(attend_out_kernel, chunks, step, depth, experts),
        out_shape=[
            jax.ShapeDtypeStruct((2 * rows, width), BF16),
            jax.ShapeDtypeStruct((rows, width_own), F32), jax.ShapeDtypeStruct((rows, 1), F32),
            jax.ShapeDtypeStruct((rows // 2, width), BF16),
            jax.ShapeDtypeStruct(hot.shape, F32), jax.ShapeDtypeStruct(hot.shape, F32),
            jax.ShapeDtypeStruct((rows, 1), F32), jax.ShapeDtypeStruct((2 * rows, experts // 2), F32),
        ],
        in_specs=[vmem] * 4 + [far] + [vmem] * 3,
        out_specs=[vmem] * 3 + [far] + [vmem] * 4,
        scratch_shapes=scratch + [dma((chunks,)), dma((chunks,)), dma, dma],
        compiler_params=pltpu.CompilerParams(collective_id=1, has_side_effects=True, vmem_limit_bytes=40 << 20),
        cost_estimate=pl.CostEstimate(flops=0, bytes_accessed=0, transcendentals=0),
    )(attn, w_out, x, gain, grads, w_small, hot, hot_peer)


def resid_grad_kernel(
    chunks, step, depth, tiles, grads_all, dgu, hid, both, both_grad, sgu, sd,
    small_e, small_p, small_s, prob, hot, logits, switch, w_small, g_own, resid_own, inv_two, gain,
    low, grad_resid, gain_grad, sum_egu, ed_f, sgu_f, sd_f, grad_small,
    part, came, came_two, spread, s0, s1, s2, s3, s4, back, y_send, y_recv, grad,
    dgu_v, hid_v, both_v, both_grad_v, sent_egu, sent_ed, came_egu, came_ed,
    s_own, s_in, d_own, d_in, l_sem, w_send, w_recv, w_out, r_send, r_recv, r_out,
    router, along, small_y, small_z, ed_in, ed_out, t_send, t_recv, e_send, e_recv, e_out,
):
    n = lax.axis_size("tp")
    own = part.shape[3]
    rows = grad.shape[0]
    load_grad = pltpu.make_async_copy(grads_all.at[pl.ds(0, rows)], grad, l_sem.at[6])
    core, x, y, (to_core, to_x, other) = places()

    def at(c):
        return pl.ds(pl.multiple_of(c * step, step), step)

    def peer_copy(c):
        return pltpu.make_async_remote_copy(
            src_ref=grads_all.at[pl.ds(pl.multiple_of(rows + c * step, step), step)], dst_ref=back.at[at(c)], send_sem=y_send.at[c], recv_sem=y_recv.at[c],
            device_id=other, device_id_type=pl.DeviceIdType.MESH,
        )

    loads = [
        pltpu.make_async_copy(source, target, l_sem.at[m])
        for m, (source, target) in enumerate(
            (
                (dgu, dgu_v),
                (both, both_v),
                (hid, hid_v),
                (both_grad, both_grad_v),
                (sgu.at[pl.ds(x * s_own.shape[0], s_own.shape[0])], s_own),
                (sd.at[pl.ds(y * d_own.shape[0], d_own.shape[0])], d_own),
            )
        )
    ]
    kinds = ((dgu_v, both_v, sent_egu, came_egu, sum_egu), (hid_v, both_grad_v, sent_ed, came_ed, None))

    def sum_copies(m):
        source, target, where = (
            (sgu.at[pl.ds((1 - x) * s_own.shape[0], s_own.shape[0])], s_in, to_x),
            (sd.at[pl.ds((1 - y) * d_own.shape[0], d_own.shape[0])], d_in, other),
            (s_own, sgu_f.at[core, y, x], to_x),
            (d_own, sd_f.at[core, x, y], to_x),
            (s_own, sgu_f.at[core, y, x], other),
        )[m]
        return pltpu.make_async_remote_copy(
            src_ref=source, dst_ref=target, send_sem=r_send.at[m], recv_sem=r_recv.at[m],
            device_id=where, device_id_type=pl.DeviceIdType.MESH,
        )

    def own_out(m):
        target = (sgu_f.at[core, y, x], sd_f.at[core, x, y])[m]
        return pltpu.make_async_copy((s_own, d_own)[m], target, r_out.at[m])

    def shared(m):
        sum_copies(m).wait_recv()
        add_rows((s_own, d_own)[m], (s_in, d_in)[m], 0, (s_own, d_own)[m].shape[0])
        sum_copies(2 + m).start()
        if m == 0:
            sum_copies(4).start()
        own_out(m).start()

    def tile_copy(m, b):
        return pltpu.make_async_remote_copy(
            src_ref=kinds[m][2].at[b], dst_ref=kinds[m][3].at[b], send_sem=w_send.at[b, m], recv_sem=w_recv.at[b, m],
            device_id=to_core, device_id_type=pl.DeviceIdType.MESH,
        )

    def x_copy(b):
        wide = ed_in.shape[2]
        return pltpu.make_async_remote_copy(
            src_ref=came_ed.at[b, :, pl.ds(pl.multiple_of((1 - x) * wide, wide), wide)], dst_ref=ed_in.at[b],
            send_sem=e_send.at[b], recv_sem=e_recv.at[b],
            device_id=to_x, device_id_type=pl.DeviceIdType.MESH,
        )

    def x_out(b):
        tall = ed_in.shape[1]
        return pltpu.make_async_copy(
            ed_out.at[b], ed_f.at[core, x, pl.ds(pl.multiple_of(b * tall, tall), tall)], e_out.at[b]
        )

    def tile_out(m, b):
        tall = kinds[m][3].shape[1]
        return pltpu.make_async_copy(
            kinds[m][3].at[b], kinds[m][4].at[pl.ds(pl.multiple_of(b * tall, tall), tall)], w_out.at[b, m]
        )

    def tile(m, b, which):
        left, right = kinds[m][:2]
        tall, wide = kinds[m][3].shape[1:]
        return mm_tn(
            left[...] if tiles == 1 else left[:, pl.ds(pl.multiple_of(b * tall, tall), tall)],
            right[:, pl.ds(pl.multiple_of(which * wide, wide), wide)],
        )

    def weights(t):
        @pl.when(t == 0)
        def _():
            for copy in loads:
                copy.wait()

        @pl.when(t == 1)
        def _():
            gates()

        @pl.when(t < tiles)
        def _():
            for m in range(2):
                kinds[m][2][t] = tile(m, t, 1 - core).astype(BF16)
                tile_copy(m, t).start()

        @pl.when(t == tiles * 8 // 11)
        def _():
            shared(0)

        @pl.when(t == tiles * 14 // 11)
        def _():
            shared(1)

        @pl.when((t >= tiles) & (t < 2 * tiles))
        def _():
            b = t - tiles
            for m in range(2):
                value = tile(m, b, core)
                tile_copy(m, b).wait_recv()
                kinds[m][3][b] = (value + kinds[m][3][b].astype(F32)).astype(BF16)
                if m == 0:
                    tile_out(m, b).start()
                else:
                    x_copy(b).start()

    load_grad.start()
    for copy in loads:
        copy.start()
    me = lax.axis_index("tp")

    def small_copy(d):
        return pltpu.make_async_remote_copy(
            src_ref=small_z.at[0] if d else small_p, dst_ref=small_z.at[d] if d else small_y,
            send_sem=t_send.at[d], recv_sem=t_recv.at[d],
            device_id={"tp": (me + d) % n} if d else other, device_id_type=pl.DeviceIdType.MESH,
        )

    greet_all([other, to_core, to_x] + [{"tp": (me + d) % n} for d in range(1, n)])
    small_copy(0).start()
    sum_copies(0).start()

    def begin(c, carry):
        peer_copy(c).start()
        return carry

    lax.fori_loop(0, chunks, begin, 0)
    sum_copies(1).start()
    gain_grad[...] = jnp.zeros_like(gain_grad)
    experts_own = small_e.shape[0] - 1
    experts = 2 * experts_own
    small_copy(0).wait_recv()
    here, there = small_e[:experts_own, :], small_y[:experts_own, :]
    small_z[0] = jnp.zeros_like(small_z[0])
    small_z[0, :experts_own] = jnp.where(y == 0, here, there)
    small_z[0, experts_own:experts] = jnp.where(y == 0, there, here)
    small_z[0, experts : experts + 1] = small_s[:1, :]
    small_z[0, experts + 1 : experts + 2] = small_s[1:, :] + small_e[experts_own:, :] + small_y[experts_own:, :]
    for d in range(1, n):
        small_copy(d).start()

    def gates():
        total = small_z[0]
        for d in range(1, n):
            small_copy(d).wait_recv()
            total = total + small_z[d]
        slots = prob.shape[1]
        total = jnp.concatenate([total, jnp.zeros((128 - total.shape[0], rows), F32)], axis=0).T
        grad_prob = total[:, :slots] * hot[...]
        inner = jnp.sum(prob[...] * grad_prob, axis=1, keepdims=True)
        sw = switch[...]
        grad_switch = total[:, experts : experts + 1] * sw * (1.0 - sw)
        place = lax.broadcasted_iota(jnp.int32, (1, slots), 1)
        grads = jnp.where(place == experts, grad_switch, prob[...] * (grad_prob - inner)).astype(BF16)
        width = w_small.shape[1] // n
        router[...] = mm(grads, w_small[:, pl.ds(pl.multiple_of(me * width, width), width)])
        along[...] = total[:, experts + 1 : experts + 2] + jnp.sum(
            grads.astype(F32) * logits[...], axis=1, keepdims=True
        )
        grad_small[...] = mm_tn(grads, both_v[:rows, :])

    def prepare(c):
        @pl.when(c == 0)
        def _():
            load_grad.wait()

        peer_copy(c).wait_recv()
        for s in range(n):
            columns = slice(s * own, (s + 1) * own)
            part[c, s] = (grad[at(c), columns].astype(F32) + back[at(c), columns].astype(F32)).astype(BF16)

    def settle(c, total):
        total = total + router[at(c), :]
        inv = inv_two[at(c), :]
        resid = resid_own[at(c), :]
        gain_grad[...] += jnp.sum(total * resid * inv, axis=0, keepdims=True)
        result = g_own[at(c), :].astype(F32) + inv * gain[...] * total - resid * (inv * inv * along[at(c), :] / (n * own))
        grad_resid[at(c), :] = result
        return result.astype(BF16)

    def gathered(c):
        for s in range(n):
            low[at(c), s * own:(s + 1) * own] = spread[c, s]

    line_sum(depth, prepare, settle, gathered, weights, part, came, came_two, spread, (s0, s1, s2, s3, s4))

    def last(c, carry):
        peer_copy(c).wait_send()
        return carry

    lax.fori_loop(0, chunks, last, 0)

    def done(b, carry):
        x_copy(b).wait_recv()
        wide = ed_in.shape[2]
        own = came_ed[b, :, pl.ds(pl.multiple_of(x * wide, wide), wide)]
        ed_out[b] = (own.astype(F32) + ed_in[b].astype(F32)).astype(BF16)
        x_out(b).start()
        tile_copy(0, b).wait_send()
        tile_copy(1, b).wait_send()
        tile_out(0, b).wait()
        x_copy(b).wait_send()
        return carry

    lax.fori_loop(0, tiles, done, 0)

    def written(b, carry):
        x_out(b).wait()
        return carry

    lax.fori_loop(0, tiles, written, 0)
    for m in range(2):
        sum_copies(m).wait_send()
        sum_copies(2 + m).wait()
        own_out(m).wait()
    sum_copies(4).wait()
    for d in range(n):
        small_copy(d).wait_send()


def resid_grad(grads_all, dgu, hid, both, both_grad, sgu, sd, small_e, small_p, small_s, prob, hot, logits, switch, w_small, g_own, resid_own, inv_two, gain, depth=1):
    rows, width = grads_all.shape[0] // 2, grads_all.shape[1]
    width_own = g_own.shape[1]
    chunks, step, scratch = line_scratch(rows, width_own)
    hidden = hid.shape[1]
    tiles = 11 if hidden % (11 * 128) == 0 else 1
    vmem = pl.BlockSpec(memory_space=pltpu.VMEM)
    far = pl.BlockSpec(memory_space=pl.ANY)
    dma = pltpu.SemaphoreType.DMA
    return pl.pallas_call(
        functools.partial(resid_grad_kernel, chunks, step, depth, tiles),
        out_shape=[
            jax.ShapeDtypeStruct((rows, width), BF16), jax.ShapeDtypeStruct((rows, width_own), F32),
            jax.ShapeDtypeStruct((1, width_own), F32),
        ]
        + [jax.ShapeDtypeStruct((2 * hidden, width // 2), BF16), jax.ShapeDtypeStruct((2, 2, hidden, width // 4), BF16)]
        + [
            jax.ShapeDtypeStruct((2, 2, 2, sgu.shape[0] // 2, sgu.shape[1]), BF16),
            jax.ShapeDtypeStruct((2, 2, 2, sd.shape[0] // 2, sd.shape[1]), BF16),
        ]
        + [jax.ShapeDtypeStruct((prob.shape[1], width), F32)],
        in_specs=[far] * 7 + [vmem] * 12,
        out_specs=[vmem] * 3 + [far] * 4 + [vmem],
        scratch_shapes=scratch + [pltpu.VMEM((rows, width), BF16), dma((chunks,)), dma((chunks,)), pltpu.VMEM((rows, width), BF16)]
        + [pltpu.VMEM(v.shape, BF16) for v in (dgu, hid, both, both_grad)]
        + [pltpu.VMEM((tiles, k * hidden // tiles, width // 2), BF16) for k in (2, 1, 2, 1)]
        + [pltpu.VMEM((v.shape[0] // 2, v.shape[1]), BF16) for v in (sgu, sgu, sd, sd)]
        + [dma((7,)), dma((tiles, 2)), dma((tiles, 2)), dma((tiles, 2)), dma((5,)), dma((5,)), dma((2,))]
        + [pltpu.VMEM((rows, width_own), F32), pltpu.VMEM((rows, 1), F32)]
        + [pltpu.VMEM(small_e.shape, F32), pltpu.VMEM((lax.axis_size("tp"), 16, rows), F32)]
        + [pltpu.VMEM((tiles, hidden // tiles, width // 4), BF16)] * 2
        + [dma((lax.axis_size("tp"),))] * 2 + [dma((tiles,))] * 3,
        compiler_params=pltpu.CompilerParams(collective_id=2, has_side_effects=True, vmem_limit_bytes=63 << 20),
        cost_estimate=pl.CostEstimate(flops=0, bytes_accessed=0, transcendentals=0),
    )(grads_all, dgu, hid, both, both_grad, sgu, sd, small_e, small_p, small_s, prob, hot, logits, switch, w_small, g_own, resid_own, inv_two, gain)


def body(
    tokens,
    norm_attn,
    w_query,
    w_key,
    w_value,
    w_output,
    norm_ffn,
    w_router,
    shared_switch,
    shared_gate,
    shared_up,
    shared_down,
    expert_gate,
    expert_up,
    expert_down,
    routes,
    segments,
    output_gradient,
):
    tp_count = lax.axis_size("tp")
    ep_count = lax.axis_size("ep")
    dp_count = lax.axis_size("dp")
    tp_rank = lax.axis_index("tp")
    ep_rank = lax.axis_index("ep")
    rows = tokens.shape[0]
    width_own = tokens.shape[1]
    width = width_own * tp_count
    heads = w_query.shape[1] // HD
    experts_own = expert_gate.shape[0]
    experts = experts_own * ep_count
    expert_width = expert_gate.shape[2]
    score_scale = 1.0 / math.sqrt(HD)
    far_bits = [1 << b for b in range(1, dp_count.bit_length() - 1)]

    def own_columns(value):
        return lax.dynamic_slice_in_dim(value, tp_rank * width_own, width_own, value.ndim - 1)

    near = bit_of("dp", 1)

    def pair_send(left, right, columns, used=None):
        sent = weight_half(left, right, 1 - near, columns, rows=used)
        return sent, swap(sent, "dp", 1)

    def pair_keep(left, right, columns, got, used=None):
        return weight_half(left, right, near, columns, got, rows=used)

    core = ("dp", 1)
    far = [("dp", b) for b in far_bits]
    line = [("ep", 1)]
    x_link, y_link = far[0], line[0]

    def over_tp(value):
        if tp_count <= 4:
            others = [
                lax.ppermute(value, "tp", [(i, (i + d) % tp_count) for i in range(tp_count)])
                for d in range(1, tp_count)
            ]
            return sum(others, value)
        bit = 1
        while bit < tp_count:
            value = value + swap(value, "tp", bit)
            bit *= 2
        return value

    def over_rows(value):
        for axis, bit in [core] + far + line:
            value = value + swap(value, axis, bit)
        return value

    qkv = heads * HD
    freq = ROPE_BASE ** (-(np.arange(HD // 2, dtype=np.float64) * 2.0) / HD)
    freq = jnp.asarray(np.concatenate([freq, freq])[None, :], F32)
    gains = jnp.pad(jnp.stack([norm_attn, norm_ffn]), ((0, 14), (0, 0)))
    slots = 16
    w_small = jnp.concatenate(
        [w_router.T, shared_switch[None, :], jnp.zeros((slots - experts - 1, width), BF16)], axis=0
    )
    (
        x_full, normed, inv_one, gain_two, grad_rows, query, key_rows, value_rows, attn_rows, log_norm,
        query_seg, key_seg, cos_table, sin_table, hot, hot_peer,
    ) = front(
        tokens, gains, output_gradient, w_query, w_key, w_value, segments.reshape(1, -1), freq, routes.T, slots
    )
    both, resid_own, inv_two, grad_peer_a, logits, router_prob, switch, gates = attend_out(
        attn_rows, w_output, x_full, gain_two, grad_rows, w_small, hot, hot_peer, experts, width_own
    )

    hid_s, dgu_s, out_s, grad_s, small_s, grad_peer_b = ffn(
        both,
        grad_rows,
        switch,
        shared_gate,
        shared_up,
        shared_down,
        rows,
        carry=[(grad_rows, 2, rows // 2, rows // 2, 0)],
        number=4,
    )
    both_grad = jnp.concatenate([grad_rows, grad_peer_a, grad_peer_b], axis=0)
    sent, got_sgu = pair_send(both, dgu_s, False, rows)
    sent, got_sd = pair_send(hid_s, after(grad_rows, sent), True)
    sum_sgu = pair_keep(both, after(dgu_s, sent, both_grad), False, got_sgu, rows)
    sum_sd = pair_keep(hid_s, after(grad_rows, sum_sgu), True, got_sd)

    hidden_width = experts_own * expert_width
    gate_w = jnp.transpose(expert_gate, (0, 2, 1)).reshape(hidden_width, width)
    up_w = jnp.transpose(expert_up, (0, 2, 1)).reshape(hidden_width, width)
    down_w = expert_down.reshape(hidden_width, width)
    hid_e, dgu_e, out_e, grad_e, small_e, got_sgu, got_sd = ffn(
        both,
        after(both_grad, sum_sd),
        gates,
        gate_w,
        up_w,
        down_w,
        2 * rows,
        base=(out_s, grad_s),
        flipped=True,
        carry=[
            (sum_sgu, 2, sum_sgu.shape[0] // 2, 0, sum_sgu.shape[0] // 2),
            (sum_sd, 1, sum_sd.shape[0] // 2, 0, sum_sd.shape[0] // 2),
        ],
        number=5,
    )

    sum_sgu = reduce_add(sum_sgu, got_sgu, *y_link)
    sum_sd = reduce_add(sum_sd, got_sd, *x_link)

    small_t = small_e.T
    resid_low, grad_resid, grad_gain_two, sum_egu, ed_f, sgu_f, sd_f, grad_small = resid_grad(
        grad_e,
        dgu_e,
        hid_e,
        both,
        both_grad,
        sum_sgu,
        sum_sd,
        small_t[:, :rows],
        small_t[:, rows:],
        small_s.T,
        router_prob,
        hot,
        logits,
        switch,
        w_small,
        output_gradient,
        resid_own,
        inv_two,
        norm_ffn.astype(F32)[None, :],
    )

    flat = jnp.concatenate(
        [grad_gain_two.reshape(-1), grad_small[: experts + 1].reshape(-1)]
    ).reshape(-1, 128)
    inner = shared_gate.shape[1]
    sgu_f, sd_f, egu_f, ed_f, qkv_f, wo_f, flat, ffn_own, normed_own, row_total, grad_gain_one = tail(
        sgu_f,
        sd_f,
        sum_egu,
        ed_f,
        flat,
        normed,
        w_query,
        w_key,
        w_value,
        attn_rows,
        out_e,
        tokens,
        inv_one,
        resid_low,
        w_output,
        query,
        key_rows,
        value_rows,
        log_norm,
        query_seg,
        key_seg,
        cos_table,
        sin_table,
    )

    sg_grad, su_grad = widen(sgu_f, (inner, inner))
    (sd_grad,) = widen(sd_f)
    (eg_grad,) = widen(egu_f, kinds=2, kind=0)
    (eu_grad,) = widen(egu_f, kinds=2, kind=1)
    (ed_grad,) = widen(ed_f, across=4)
    wq_grad, wk_grad, wv_grad = widen(qkv_f, (qkv,) * 3)
    (wo_grad,) = widen(wo_f)

    x_own = tokens.astype(F32)
    grad_tokens = (
        grad_resid
        + inv_one * norm_attn.astype(F32) * normed_own
        - x_own * (inv_one * inv_one) * (row_total[0][:, None] / width)
    )
    grad_gain_one = grad_gain_one[0]
    layer_out = (resid_own + ffn_own).astype(BF16)
    flat = flat.reshape(-1)
    grad_gain_two = flat[:width_own]
    grad_router = flat[width_own : width_own + width * experts].reshape(experts, width).T
    grad_switch_w = flat[width_own + width * experts :]

    def per_expert(value):
        return value.reshape(experts_own, expert_width, width)

    return (
        layer_out,
        grad_tokens,
        grad_gain_one,
        wq_grad,
        wk_grad,
        wv_grad,
        wo_grad,
        grad_gain_two,
        grad_router,
        grad_switch_w,
        sg_grad,
        su_grad,
        sd_grad,
        jnp.transpose(per_expert(eg_grad), (0, 2, 1)),
        jnp.transpose(per_expert(eu_grad), (0, 2, 1)),
        per_expert(ed_grad),
    )


def solution(mesh):
    placed = (
        P(("dp", "ep"), "tp"),
        P("tp"),
        P(None, "tp"),
        P(None, "tp"),
        P(None, "tp"),
        P("tp", None),
        P("tp"),
        P(),
        P(),
        P(None, "tp"),
        P(None, "tp"),
        P("tp", None),
        P("ep", None, "tp"),
        P("ep", None, "tp"),
        P("ep", "tp", None),
        P(("dp", "ep"), None),
        P("dp"),
        P(("dp", "ep"), "tp"),
    )
    return jax.shard_map(
        body,
        mesh=mesh,
        in_specs=placed,
        out_specs=(
            P(("dp", "ep"), "tp"),
            P(("dp", "ep"), "tp"),
            P("tp"),
            P(None, "tp"),
            P(None, "tp"),
            P(None, "tp"),
            P("tp", None),
            P("tp"),
            P(),
            P(),
            P(None, "tp"),
            P(None, "tp"),
            P("tp", None),
            P("ep", None, "tp"),
            P("ep", None, "tp"),
            P("ep", "tp", None),
        ),
        check_vma=False,
    )
```
